32 devices in a mesh: seq: 32 (over z, y, x, core), head: 1.
Axes of the slice: x: 2, y: 2, z: 4, core: 2. Of those that a mesh axis runs over, the one named last changes fastest.
Arguments:
- queries: bfloat16 [2048, 1536], P('seq', 'head'), may hold values from -6 to 6
- key_vectors: bfloat16 [2048, 512], P('seq', 'head'), may hold values from -6 to 6
- value_vectors: bfloat16 [2048, 512], P('seq', 'head'), may hold values from -6 to 6
- lengths: int32 [16], replicated, may hold values from 1 to 256, 2048 in all
- out_weight: bfloat16 [1536, 1536], P('head', 'seq'), may hold values from -0.15625 to 0.15625
- residual: bfloat16 [2048, 1536], P(('seq', 'head')), may hold values from -6 to 6
- norm_gain: float32 [1536], replicated, may hold values from 0.1 to 1.9
- route_ids: int32 [2048, 6], P(('seq', 'head')), may hold values from 0 to 63, all different within a row; in each aligned block of 64 rows (0 to 63, 64 to 127, ...) at most 6 rows name the same one
- route_logits: float32 [2048, 6], P(('seq', 'head')), may hold values from -8 to 340
- shared_gate_up: bfloat16 [1536, 2, 1024], P(None, None, ('seq', 'head')), may hold values from -0.15625 to 0.15625
- shared_down: bfloat16 [1024, 1536], P(('seq', 'head')), may hold values from -0.1875 to 0.1875
- expert_gate_up: bfloat16 [128, 1536, 2, 256], P('seq'), may hold values from -0.15625 to 0.15625
- expert_down: bfloat16 [128, 256, 1536], P('seq'), may hold values from -0.25 to 0.25
- cache_blocks: bfloat16 [32, 128, 8, 4, 128], P('seq', None, None, 'head'), may hold values from -6 to 6
- block_table: int32 [32], replicated, may hold values from 0 to 31, each once
Outputs:
- layer_out: bfloat16 [2048, 1536], P(('seq', 'head'))
- cache_out: bfloat16 [32, 128, 8, 4, 128], P(None, 'seq', None, 'head')
The draws below stay inside these ranges and needn't reach their ends.
Inputs may be any that keep to these rules, and one draw needn't show every extreme that they name: The lengths sum to 2048. `route_ids`: each token names 6 different experts; among the tokens of one device no expert is named more than 6 times. `block_table`: every block appears once.
All inputs are finite; a program needn't handle non-finite values.
Results may differ from the reference program's by a relative error of at most 0.0095.
Values may be sent and summed in bfloat16 or wider, within the bound.
No kernel may reach another device: no remote copies, remote signals or barrier semaphores. Data moves between devices by JAX's collectives and lax.ppermute only.
A program may use at most 64 MiB of HBM per device.

```python
import math
import jax
import jax.numpy as jnp
import numpy as np
from jax import lax

D = 1536
QH = 12
KVH = 4
HD = 128
EXPERTS = 64
TOP = 6
EFF = 512
SFF = 1024
TOK_DEV = 64
BLK = 128
CLAYERS = 4
TOKENS = 2048
REQS = 16
MOST = 256
HALF_FF = 256
HALVES = 128
CAP = 6
BLOCKS = 32
N_HEAD = 1
DEVICES = 32


def draw_queries(key, part):
    sample = jax.random.truncated_normal(jax.random.fold_in(key, 1), -6.0, 6.0, (TOKENS, QH * HD), jnp.float32)
    return sample.astype(jnp.bfloat16)


def draw_key_vectors(key, part):
    sample = jax.random.truncated_normal(jax.random.fold_in(key, 3), -6.0, 6.0, (TOKENS, KVH * HD), jnp.float32)
    return sample.astype(jnp.bfloat16)


def draw_route_logits(key, part):
    sample = 2.0 * jax.random.truncated_normal(jax.random.fold_in(key, 26), -4.0, 4.0, (TOKENS, TOP), jnp.float32)
    return sample


def level_of(rng, shape, shards, low, high):
    loudness = 1.0
    for axis_at, parts in shards:
        steps = jax.random.uniform(jax.random.fold_in(jax.random.fold_in(rng, 6), axis_at), (parts,), jnp.float32, low / len(shards), high / len(shards))
        loudness = loudness * jnp.repeat(jnp.exp(steps), shape[axis_at] // parts).reshape((-1,) + (1,) * (len(shape) - 1 - axis_at))
    return loudness


def split_up(amount, total, reach, slope):
    loads = [(1 << 20) // math.isqrt(rank ** slope) + 1 for rank in range(2, amount + 1)]
    spare, counts = total - reach - (amount - 1), [1] * (amount - 1)
    while spare > 0:
        free = [i for i in range(amount - 1) if counts[i] < reach]
        pool, left = sum([loads[i] for i in free]), spare
        for i in free:
            addition = min(reach - counts[i], max(1, left * loads[i] // pool), spare)
            counts[i] = counts[i] + addition
            spare = spare - addition
    return np.array([reach] + counts)


def ragged(stream_key, amount, total, reach, skew):
    if amount == 2:
        one = jax.random.randint(stream_key, (), max(1, total - reach), min(reach, total - 1) + 1)
        return jnp.stack([one, total - one])
    sizes = jnp.asarray(split_up(amount, total, reach, skew), jnp.int32)
    twos = (amount - 1) // 2
    donor, taker = sizes[1:1 + 2 * twos:2], sizes[2:2 + 2 * twos:2]
    room = jnp.minimum(donor - 1, reach - taker)
    moved = jax.random.randint(jax.random.fold_in(stream_key, 1), (twos,), 0, 1 << 20) % (room + 1)
    sizes = sizes.at[1:1 + 2 * twos:2].set(donor - moved).at[2:2 + 2 * twos:2].set(taker + moved)
    return sizes[jax.random.permutation(jax.random.fold_in(stream_key, 2), amount)]


def routed_block(own_key, own, number, rows, amount, top, bound, slope):
    order = jax.random.permutation(own_key, amount)
    heavy_load, ordinary = load_shares(amount, rows * top, bound, slope, True), load_shares(amount, rows * top, bound, slope, False)
    places = jnp.arange(amount)

    def named(sizes, offset_by):
        used = int((sizes > 0).sum())
        fixed = max(1, used // 4)
        moved = fixed + (places - fixed + offset_by * (used - fixed)) % max(1, amount - fixed)
        return jnp.zeros((amount,), jnp.int32).at[order[jnp.where(places < fixed, places, moved)]].set(jnp.asarray(sizes, jnp.int32))

    sizes = jnp.where(number % 4 == 0, named(heavy_load, number // 4), named(ordinary, number - number // 4 - 1))
    mixed = jax.random.permutation(jax.random.fold_in(own, 3), amount)
    source_of, sink = mixed[0:amount // 2 * 2:2], mixed[1:amount // 2 * 2:2]
    slack = jnp.minimum(sizes[source_of] - 1, bound - sizes[sink]) // 2
    slack = jnp.where((source_of == order[0]) | (sink == order[0]) | (sizes[sink] == 0), 0, jnp.maximum(slack, 0))
    moved = jax.random.randint(jax.random.fold_in(own, 4), (amount // 2,), 0, 1 << 20) % (slack + 1)
    sizes = sizes.at[source_of].add(-moved).at[sink].add(moved)
    members = jnp.searchsorted(jnp.cumsum(sizes), jnp.arange(rows * top), side="right").astype(jnp.int32)
    grid = members.reshape(top, rows).T
    grid = grid[jax.random.permutation(jax.random.fold_in(own, 1), rows)]
    offset_by = jax.random.randint(jax.random.fold_in(own, 2), (rows, 1), 0, top)
    return jnp.take_along_axis(grid, (jnp.arange(top)[None, :] + offset_by) % top, axis=1)


def load_shares(amount, total, reach, slope, full):
    portions = [(1 << 20) // math.isqrt(grade ** slope) + 1 for grade in range(1, amount + 1)]
    largest = reach if full else min(reach, max(-(-total // amount), total * portions[0] // sum(portions)))
    least = 1 if total - largest >= amount - 1 else 0
    counts, surplus = [largest] + [least] * (amount - 1), total - largest - least * (amount - 1)
    while surplus > 0:
        movable = [i for i in range(1, amount) if counts[i] < largest] or [i for i in range(1, amount) if counts[i] < reach]
        pool, remaining = sum([portions[i] for i in movable]), surplus
        for i in movable:
            addition = min(reach - counts[i], max(1, remaining * portions[i] // pool), surplus)
            counts[i] = counts[i] + addition
            surplus = surplus - addition
    return np.array(counts)


def bell_draw(key, shape, width, most, pieces=(), kind=jnp.bfloat16):
    level = level_of(key, shape, pieces, -0.22, 0.18) if pieces else 1.0
    drawn = jax.random.normal(key, shape, jnp.float32) * width * level
    return jnp.minimum(jnp.maximum(drawn, -most), most).astype(kind)


def setup_inputs(seed: int = 0) -> dict:
    arg_keys = jax.random.split(jax.random.key(seed), 16)
    queries = draw_queries(jax.random.fold_in(arg_keys[15], 71), 0)
    key_vectors = draw_key_vectors(jax.random.fold_in(arg_keys[15], 71), 0)
    value_vectors = bell_draw(arg_keys[2], (TOKENS, KVH * HD), 1.0, 6.0, ((0, 32),))
    lengths = ragged(arg_keys[3], REQS, TOKENS, MOST, 2).astype(jnp.int32)
    out_weight = bell_draw(arg_keys[4], (QH * HD, D), (QH * HD) ** -0.5, 0.15625, ((1, 32),))
    residual = bell_draw(arg_keys[5], (TOKENS, D), 1.0, 6.0, ((0, 32),))
    norm_gain = jnp.clip(1.0 + 0.18 * jax.random.normal(arg_keys[6], (D,), jnp.float32), 0.1, 1.9)
    route_ids_keys = jax.random.split(jax.random.fold_in(arg_keys[7], 1), TOKENS // (TOK_DEV // N_HEAD))
    route_ids_turns = jax.random.permutation(jax.random.fold_in(arg_keys[7], 3), TOKENS // (TOK_DEV // N_HEAD))
    route_ids = jax.vmap(lambda own, number: routed_block(jax.random.fold_in(arg_keys[7], 2), own, number, TOK_DEV // N_HEAD, EXPERTS, TOP, CAP, 2))(route_ids_keys, route_ids_turns).reshape((TOKENS, TOP))
    route_logits = draw_route_logits(jax.random.fold_in(arg_keys[15], 71), 0)
    shared_gate_up = bell_draw(arg_keys[9], (D, 2, SFF), D ** -0.5, 0.15625, ((2, 32),))
    shared_down = bell_draw(arg_keys[10], (SFF, D), SFF ** -0.5, 0.1875, ((0, 32),))
    expert_gate_up = bell_draw(arg_keys[11], (HALVES, D, 2, HALF_FF), D ** -0.5, 0.15625, ((0, 32),))
    expert_down = bell_draw(arg_keys[12], (HALVES, HALF_FF, D), EFF ** -0.5, 0.25, ((0, 32),))
    cache_blocks = bell_draw(arg_keys[13], (BLOCKS, BLK, 2 * CLAYERS, KVH, HD), 1.0, 6.0, ((0, 32),))
    block_table = jax.random.permutation(arg_keys[14], BLOCKS).astype(jnp.int32)
    return dict(queries=queries, key_vectors=key_vectors, value_vectors=value_vectors, lengths=lengths, out_weight=out_weight, residual=residual, norm_gain=norm_gain, route_ids=route_ids, route_logits=route_logits, shared_gate_up=shared_gate_up, shared_down=shared_down, expert_gate_up=expert_gate_up, expert_down=expert_down, cache_blocks=cache_blocks, block_table=block_table)


NEGATIVE = -1e+30
EPSILON = 1e-05

def segment_of(positions, lengths):
    request_ends = jnp.cumsum(lengths).astype(jnp.int32)
    passed = (request_ends[None, :] <= positions[:, None]).astype(jnp.int32)
    return lax.optimization_barrier(jnp.sum(passed, axis=1)).astype(jnp.int32)

def attend(queries, key_vectors, value_vectors, lengths):
    group_size = QH // KVH
    block_rows = 512
    pad_keys = jnp.concatenate([jnp.zeros((MOST, KVH * HD), key_vectors.dtype), key_vectors], axis=0)
    pad_values = jnp.concatenate([jnp.zeros((MOST, KVH * HD), value_vectors.dtype), value_vectors], axis=0)

    def one_block(block_index):
        first_row = (block_index * block_rows).astype(jnp.int32)
        query_part = lax.dynamic_slice_in_dim(queries, first_row, block_rows, 0)
        query_part = query_part.reshape(block_rows, KVH, group_size, HD).astype(jnp.float32)
        key_part = lax.dynamic_slice_in_dim(pad_keys, first_row, MOST + block_rows, 0)
        key_part = key_part.reshape(MOST + block_rows, KVH, HD).astype(jnp.float32)
        value_part = lax.dynamic_slice_in_dim(pad_values, first_row, MOST + block_rows, 0)
        value_part = value_part.reshape(MOST + block_rows, KVH, HD).astype(jnp.float32)
        query_pos = first_row + jnp.arange(block_rows, dtype=jnp.int32)
        key_pos = first_row - MOST + jnp.arange(MOST + block_rows, dtype=jnp.int32)
        visible = (key_pos[None, :] >= 0) & (key_pos[None, :] <= query_pos[:, None])
        visible = visible & (segment_of(key_pos, lengths)[None, :] == segment_of(query_pos, lengths)[:, None])
        scores = jnp.einsum('tkgd,wkd->kgtw', query_part, key_part) * (1.0 / math.sqrt(HD))
        scores = jnp.where(visible[None, None], scores, NEGATIVE)
        row_max = lax.optimization_barrier(jnp.max(scores, axis=-1, keepdims=True))
        weights = jnp.exp(scores - row_max)
        row_total = lax.optimization_barrier(jnp.sum(weights, axis=-1))
        rounded = lax.optimization_barrier(weights.astype(jnp.bfloat16)).astype(jnp.float32)
        weighted = jnp.einsum('kgtw,wkd->tkgd', rounded, value_part)
        heads = weighted / jnp.transpose(row_total, (2, 0, 1))[..., None]
        return heads.astype(jnp.bfloat16).reshape(block_rows, QH * HD)
    blocks = lax.map(one_block, jnp.arange(TOKENS // block_rows, dtype=jnp.int32))
    return blocks.reshape(TOKENS, QH * HD)

def reference(queries, key_vectors, value_vectors, lengths, out_weight, residual, norm_gain, route_ids, route_logits, shared_gate_up, shared_down, expert_gate_up, expert_down, cache_blocks, block_table):
    heads = attend(queries, key_vectors, value_vectors, lengths)
    attn_out = jnp.dot(heads, out_weight, preferred_element_type=jnp.float32)
    mixed = residual.astype(jnp.float32) + attn_out
    mean_square = lax.optimization_barrier(jnp.mean(mixed * mixed, axis=-1, keepdims=True))
    normed = (mixed * lax.rsqrt(mean_square + EPSILON) * norm_gain).astype(jnp.bfloat16)
    shared_both = jnp.einsum('td,dcf->tcf', normed.astype(jnp.float32), shared_gate_up.astype(jnp.float32))
    shared_act = (jax.nn.silu(shared_both[:, 0]) * shared_both[:, 1]).astype(jnp.bfloat16)
    shared_part = jnp.dot(shared_act, shared_down, preferred_element_type=jnp.float32)
    route_probs = jax.nn.softmax(route_logits, axis=-1)
    rows_block = TOK_DEV // N_HEAD
    flat_ids = route_ids.reshape(-1).astype(jnp.int32)
    onehot = (flat_ids.reshape(DEVICES, rows_block * TOP)[:, :, None] == jnp.arange(EXPERTS, dtype=jnp.int32)[None, None, :]).astype(jnp.int32)
    slot_rank = lax.optimization_barrier(jnp.sum((jnp.cumsum(onehot, axis=1) - 1) * onehot, axis=2)).reshape(-1).astype(jnp.int32)
    block_of = (jnp.arange(TOKENS * TOP, dtype=jnp.int32) // (rows_block * TOP)).astype(jnp.int32)
    slot_of = (block_of * CAP + slot_rank).astype(jnp.int32)
    token_of = (jnp.arange(TOKENS * TOP, dtype=jnp.int32) // TOP).astype(jnp.int32)
    weight_of = route_probs.reshape(-1)
    slot_count = DEVICES * CAP
    padded = jnp.concatenate([normed, jnp.zeros((1, D), normed.dtype)], axis=0)

    def one_expert(accumulated, expert):
        chosen = flat_ids == expert
        target = jnp.where(chosen, slot_of, slot_count).astype(jnp.int32)
        row_index = jnp.full((slot_count,), TOKENS, jnp.int32).at[target].set(token_of, mode='drop')
        row_scale = jnp.zeros((slot_count,), jnp.float32).at[target].set(weight_of, mode='drop')
        rows_in = padded[row_index]
        summed = jnp.zeros((slot_count, D), jnp.float32)
        for half_index in range(2):
            weight_row = half_index * EXPERTS + expert
            gate_up = jnp.dot(rows_in, expert_gate_up[weight_row].reshape(D, 2 * HALF_FF), preferred_element_type=jnp.float32)
            expert_act = (jax.nn.silu(gate_up[:, :HALF_FF]) * gate_up[:, HALF_FF:]).astype(jnp.bfloat16)
            half_out = jnp.dot(expert_act, expert_down[weight_row], preferred_element_type=jnp.float32)
            summed = summed + lax.optimization_barrier(half_out.astype(jnp.bfloat16)).astype(jnp.float32)
        accumulated = accumulated.at[row_index].add(row_scale[:, None] * summed, mode='drop')
        return (accumulated, None)
    routed, _ = lax.scan(one_expert, jnp.zeros((TOKENS, D), jnp.float32), jnp.arange(EXPERTS, dtype=jnp.int32))
    layer_out = (mixed + shared_part + routed).astype(jnp.bfloat16)
    cache_out = jnp.take(cache_blocks, block_table, axis=0)
    return (layer_out, cache_out)
```

```python
import math

import jax
import jax.numpy as jnp
from jax import lax
from jax.experimental import pallas as pl
from jax.experimental.pallas import tpu as pltpu
from jax.sharding import PartitionSpec as P

HD = 128
EXPERTS = 64
TOP = 6
REACH = 4
HALVES = 128
CAP = 6
Z_SIZE = 4
PLANE = 8
MIB = 1024 * 1024


NEGATIVE = -1e30
EPSILON = 1e-05


def from_behind(shard, axis, by):
    devices = lax.axis_size(axis)
    pairs = [(i, i + by) for i in range(devices) if 0 <= i + by < devices]
    return lax.ppermute(shard, axis, pairs)


def segment_of(positions, lengths):
    request_ends = jnp.cumsum(lengths)
    passed = (request_ends[None, :] <= positions[:, None]).astype(jnp.int32)
    return jnp.sum(passed, axis=1)


def shared_ffn(rows_in, gate_up_part, down_part):
    shared_both = jnp.einsum(
        "td,dcf->tcf", rows_in, gate_up_part, preferred_element_type=jnp.float32
    )
    shared_act = (jax.nn.silu(shared_both[:, 0]) * shared_both[:, 1]).astype(jnp.bfloat16)
    return jnp.dot(shared_act, down_part, preferred_element_type=jnp.float32)


def general_shards(
    queries,
    key_vectors,
    value_vectors,
    lengths,
    out_weight,
    residual,
    norm_gain,
    route_ids,
    route_logits,
    shared_gate_up,
    shared_down,
    expert_gate_up,
    expert_down,
    cache_blocks,
    block_table,
):
    handed = lax.all_to_all(cache_blocks, "seq", split_axis=1, concat_axis=0, tiled=True)
    cache_out = jnp.take(handed, block_table, axis=0)
    tok_rows = queries.shape[0]
    seq_index = lax.axis_index("seq")
    earlier = [
        from_behind((key_vectors, value_vectors), "seq", offset) for offset in range(REACH, 0, -1)
    ]
    window_keys = jnp.concatenate([member[0] for member in earlier] + [key_vectors], axis=0)
    window_values = jnp.concatenate([member[1] for member in earlier] + [value_vectors], axis=0)
    key_count = window_keys.shape[0]
    kv_heads = key_vectors.shape[1] // HD
    query_heads = queries.shape[1] // HD
    group_size = query_heads // kv_heads
    query_pos = seq_index * tok_rows + jnp.arange(tok_rows, dtype=jnp.int32)
    key_pos = (seq_index - REACH) * tok_rows + jnp.arange(key_count, dtype=jnp.int32)
    visible = (key_pos[None, :] >= 0) & (key_pos[None, :] <= query_pos[:, None])
    visible = visible & (
        segment_of(key_pos, lengths)[None, :] == segment_of(query_pos, lengths)[:, None]
    )
    query_part = queries.reshape(tok_rows, kv_heads, group_size, HD)
    key_part = window_keys.reshape(key_count, kv_heads, HD)
    value_part = window_values.reshape(key_count, kv_heads, HD)
    scores = jnp.einsum(
        "tkgd,wkd->kgtw", query_part, key_part, preferred_element_type=jnp.float32
    ) * (1.0 / math.sqrt(HD))
    scores = jnp.where(visible[None, None], scores, NEGATIVE)
    row_max = jnp.max(scores, axis=-1, keepdims=True)
    weights = jnp.exp(scores - row_max)
    row_total = jnp.sum(weights, axis=-1)
    weighted = jnp.einsum(
        "kgtw,wkd->tkgd",
        weights.astype(jnp.bfloat16),
        value_part,
        preferred_element_type=jnp.float32,
    )
    heads = (weighted / jnp.transpose(row_total, (2, 0, 1))[..., None]).astype(jnp.bfloat16)
    heads = heads.reshape(tok_rows, query_heads * HD)
    partial_out = jnp.dot(
        heads,
        lax.all_gather(out_weight, "seq", axis=1, tiled=True),
        preferred_element_type=jnp.float32,
    )
    attn_out = lax.psum_scatter(partial_out, "head", scatter_dimension=0, tiled=True)
    mixed = residual.astype(jnp.float32) + attn_out
    mean_square = jnp.mean(mixed * mixed, axis=-1, keepdims=True)
    normed = (mixed * lax.rsqrt(mean_square + EPSILON) * norm_gain).astype(jnp.bfloat16)
    gate_up_all, down_all = (
        lax.all_gather(shared_gate_up, ("seq", "head"), axis=2, tiled=True),
        lax.all_gather(shared_down, ("seq", "head"), axis=0, tiled=True),
    )
    shared_part = shared_ffn(normed, gate_up_all, down_all)
    own_tokens = normed.shape[0]
    width_model = normed.shape[1]
    flat_ids = route_ids.reshape(-1)
    onehot = (flat_ids[:, None] == jnp.arange(EXPERTS, dtype=jnp.int32)[None, :]).astype(jnp.int32)
    slot_rank = jnp.sum((jnp.cumsum(onehot, axis=0) - 1) * onehot, axis=1)
    first_slot = flat_ids * CAP + slot_rank
    second_slot = (flat_ids + EXPERTS) * CAP + slot_rank
    token_of = jnp.arange(flat_ids.shape[0], dtype=jnp.int32) // TOP
    routed_rows = normed[token_of]
    outgoing = jnp.zeros((HALVES * CAP, width_model), jnp.bfloat16)
    outgoing = outgoing.at[jnp.concatenate([first_slot, second_slot])].set(
        jnp.concatenate([routed_rows, routed_rows], axis=0)
    )
    local_halves = expert_gate_up.shape[0]
    outgoing = outgoing.reshape(HALVES // local_halves, local_halves, CAP, width_model)
    gate_up = jnp.einsum(
        "nsjd,sdcf->nsjcf",
        lax.all_to_all(outgoing, "seq", split_axis=0, concat_axis=0, tiled=True),
        expert_gate_up,
        preferred_element_type=jnp.float32,
    )
    expert_act = (jax.nn.silu(gate_up[:, :, :, 0]) * gate_up[:, :, :, 1]).astype(jnp.bfloat16)
    half_out = jnp.einsum(
        "nsjf,sfd->nsjd", expert_act, expert_down, preferred_element_type=jnp.float32
    ).astype(jnp.bfloat16)
    returned = lax.all_to_all(half_out, "seq", split_axis=0, concat_axis=0, tiled=True)
    returned = returned.reshape(HALVES * CAP, width_model)
    pair_sum = returned[first_slot].astype(jnp.float32) + returned[second_slot].astype(jnp.float32)
    route_probs = jax.nn.softmax(route_logits, axis=-1)
    routed = jnp.sum(
        route_probs[:, :, None] * pair_sum.reshape(own_tokens, TOP, width_model), axis=1
    )
    layer_out = (mixed + shared_part + routed).astype(jnp.bfloat16)
    return (layer_out, cache_out)


VMEM = pl.BlockSpec(memory_space=pltpu.VMEM)
SMEM = pl.BlockSpec(memory_space=pltpu.SMEM)
ANY = pl.BlockSpec(memory_space=pl.ANY)


def dot_rows(left, right):
    return lax.dot_general(left, right, (((1,), (1,)), ((), ())), preferred_element_type=jnp.float32)


def dot(left, right):
    return jnp.dot(left, right, preferred_element_type=jnp.float32)


def silu_times(gate, up):
    return (gate / (1.0 + jnp.exp(-gate)) * up).astype(jnp.bfloat16)


def attention_kernel(first_ref, lengths_ref, q_ref, k4_ref, k3_ref, k2_ref, k1_ref, own_ref, out_ref):
    tokens = q_ref.shape[0]
    kv_width = own_ref.shape[1] // 2
    kv_heads = kv_width // HD
    group = q_ref.shape[1] // HD // kv_heads
    blocks = [k4_ref, k3_ref, k2_ref, k1_ref, own_ref]
    keys = len(blocks) * tokens
    first = first_ref[0]
    query_pos = first + lax.broadcasted_iota(jnp.int32, (tokens, keys), 0)
    key_pos = first - (keys - tokens) + lax.broadcasted_iota(jnp.int32, (tokens, keys), 1)
    start = jnp.zeros((tokens, keys), jnp.int32)
    end = jnp.int32(0)
    for request in range(lengths_ref.shape[0]):
        end = end + lengths_ref[request]
        start = jnp.maximum(start, jnp.where(query_pos >= end, end, 0))
    hidden = jnp.where((key_pos >= start) & (key_pos <= query_pos), 0.0, NEGATIVE)
    hidden = jnp.concatenate([hidden] * group, axis=0)
    scale = 1.0 / math.sqrt(HD)
    for kv in range(kv_heads):
        at = slice(kv * HD, (kv + 1) * HD)
        value_at = slice(kv_width + kv * HD, kv_width + (kv + 1) * HD)
        key = jnp.concatenate([block[:, at] for block in blocks], axis=0)
        value = jnp.concatenate([block[:, value_at] for block in blocks], axis=0)
        heads = [kv * group + member for member in range(group)]
        query = jnp.concatenate([q_ref[:, h * HD : (h + 1) * HD] for h in heads], axis=0)
        scores = dot_rows(query, key) * scale + hidden
        weights = jnp.exp(scores - jnp.max(scores, axis=-1, keepdims=True))
        total = jnp.sum(weights, axis=-1, keepdims=True)
        result = (dot(weights.astype(jnp.bfloat16), value) / total).astype(jnp.bfloat16)
        for member, h in enumerate(heads):
            out_ref[:, h * HD : (h + 1) * HD] = result[member * tokens : (member + 1) * tokens]


def project_kernel(core_ref, mine_ref, other_ref, weight_ref, own_ref, send_ref, *, chunk):
    tokens = mine_ref.shape[0]
    heads = jnp.concatenate([mine_ref[...], other_ref[...]], axis=0)
    turned = dot_rows(weight_ref[...], heads)
    is_first = core_ref[0] == 0
    pieces = []
    for at in range(0, weight_ref.shape[0], chunk):
        piece = turned[at : at + chunk]
        pieces.append(jnp.where(is_first, piece, 0.0))
        pieces.append(jnp.where(is_first, 0.0, piece))
    out = jnp.concatenate(pieces, axis=0).T
    own_ref[...] = out[:tokens]
    send_ref[...] = out[tokens:]


def norm_kernel(residual_ref, own_ref, received_ref, gain_ref, mixed_ref, normed_ref):
    mixed = residual_ref[...].astype(jnp.float32) + (own_ref[...] + received_ref[...])
    mixed_ref[...] = mixed
    mean_square = jnp.mean(mixed * mixed, axis=-1, keepdims=True)
    normed = (mixed * lax.rsqrt(mean_square + EPSILON) * gain_ref[...]).astype(jnp.bfloat16)
    for z in range(normed_ref.shape[0]):
        normed_ref[z] = normed


def pick_kernel(code_ref, rows_ref, out_ref):
    _, picked, _ = out_ref.shape
    tokens = rows_ref.shape[0]
    row = pl.program_id(0) * picked + lax.broadcasted_iota(jnp.int32, (picked, tokens), 0)
    chosen = code_ref[0:1, :] == row
    for choice in range(1, TOP):
        chosen = chosen | (code_ref[choice : choice + 1, :] == row)
    onehot = jnp.where(chosen, 1.0, 0.0).astype(jnp.bfloat16)
    out_ref[0] = dot(onehot, rows_ref[...]).astype(jnp.bfloat16)


def shared_kernel(code_ref, prob_ref, rows_ref, gate_up_ref, down_ref, out_ref, mix_ref):
    parts = gate_up_ref.shape[0]
    gate_weight = jnp.concatenate([gate_up_ref[p, 0] for p in range(parts)], axis=0)
    up_weight = jnp.concatenate([gate_up_ref[p, 1] for p in range(parts)], axis=0)
    rows = rows_ref[...]
    act = silu_times(dot_rows(rows, gate_weight), dot_rows(rows, up_weight))
    out_ref[...] = dot(act, down_ref[...])
    column = lax.broadcasted_iota(jnp.int32, mix_ref.shape, 1)
    mix = jnp.zeros(mix_ref.shape, jnp.float32)
    for choice in range(TOP):
        one = slice(choice, choice + 1)
        mix = jnp.where(code_ref[:, one] == column, prob_ref[:, one], mix)
    mix_ref[...] = mix.astype(jnp.bfloat16)


def experts_kernel(rows_ref, gate_up_ref, down_ref, out_ref):
    sources, both, width = rows_ref.shape
    per_half = both // 2
    rows = rows_ref[...].astype(jnp.float32)
    results = []
    for half in range(2):
        own = rows[:, half * per_half : (half + 1) * per_half]
        own = own.reshape(sources * per_half, width).astype(jnp.bfloat16)
        act = silu_times(dot(own, gate_up_ref[half, 0]), dot(own, gate_up_ref[half, 1]))
        results.append(dot(act, down_ref[half]).reshape(sources, per_half, width))
    out_ref[...] = jnp.concatenate(results, axis=1).astype(jnp.bfloat16)


def combine_kernel(mix_ref, rows_ref, shared_ref, out_ref):
    out_ref[...] = (dot(mix_ref[...], rows_ref[...]) + shared_ref[...]).astype(jnp.bfloat16)


def final_kernel(mixed_ref, parts_ref, out_ref):
    total = mixed_ref[...]
    for z in range(parts_ref.shape[0]):
        total = total + parts_ref[z].astype(jnp.float32)
    out_ref[...] = total.astype(jnp.bfloat16)


def reorder_kernel(table_ref, from_ref, to_ref, sems):
    copies = []
    for block in range(to_ref.shape[0]):
        copy = pltpu.make_async_copy(from_ref.at[table_ref[block]], to_ref.at[block], sems.at[block])
        copy.start()
        copies.append(copy)
    for copy in copies:
        copy.wait()


def params(mib):
    return pltpu.CompilerParams(vmem_limit_bytes=mib * MIB)


def cost(flops, moved):
    return pl.CostEstimate(flops=int(flops), bytes_accessed=int(moved), transcendentals=0)


def route_codes(route_ids, z_index):
    tokens = route_ids.shape[0]
    experts = jnp.arange(EXPERTS, dtype=jnp.int32)
    named = route_ids[:, :, None] == experts[None, None, :]
    member = jnp.any(named, axis=1).astype(jnp.float32)
    order = jnp.arange(tokens, dtype=jnp.int32)
    before = (order[None, :] < order[:, None]).astype(jnp.float32)
    ahead = dot(before, member)
    rank = jnp.sum(jnp.where(named, ahead[:, None, :], 0.0), axis=2).astype(jnp.int32)
    half_experts = EXPERTS // 2
    per_device = half_experts // PLANE
    plane_at = (route_ids % half_experts) // per_device
    in_device = (route_ids % per_device) * Z_SIZE + z_index
    code = (plane_at * per_device * Z_SIZE + in_device) * CAP + rank
    return code + (route_ids // half_experts) * (PLANE * per_device * Z_SIZE * CAP)


def shards(
    queries,
    key_vectors,
    value_vectors,
    lengths,
    out_weight,
    residual,
    norm_gain,
    route_ids,
    route_logits,
    shared_gate_up,
    shared_down,
    expert_gate_up,
    expert_down,
    cache_blocks,
    block_table,
):
    tokens, width = residual.shape
    devices = lax.axis_size("seq")
    me = lax.axis_index("seq")
    z_index = me // PLANE
    z_groups = [[p + PLANE * z for z in range(Z_SIZE)] for p in range(PLANE)]
    planes = [[p + PLANE * z for p in range(PLANE)] for z in range(Z_SIZE)]
    same_core = [[core + 2 * chip for chip in range(devices // 2)] for core in range(2)]
    partner = [(i, i ^ 1) for i in range(devices)]
    bf16, f32 = jnp.bfloat16, jnp.float32
    shape = jax.ShapeDtypeStruct

    turned_weight = lax.all_gather(
        out_weight.T, "seq", axis=0, tiled=True, axis_index_groups=same_core
    )

    own_kv = jnp.concatenate([key_vectors, value_vectors], axis=1)
    behind = [from_behind(own_kv, "seq", offset) for offset in range(REACH, 0, -1)]

    _, block_tokens, layers, kv_heads, head_size = cache_blocks.shape
    per_device = block_tokens // devices
    outgoing_cache = cache_blocks.reshape(devices, per_device * layers, kv_heads, head_size)
    handed = lax.all_to_all(outgoing_cache, "seq", split_axis=0, concat_axis=0, tiled=True)
    cache_out = pl.pallas_call(
        reorder_kernel,
        out_shape=shape(handed.shape, bf16),
        in_specs=[SMEM, ANY],
        out_specs=ANY,
        scratch_shapes=[pltpu.SemaphoreType.DMA((devices,))],
        cost_estimate=cost(0, 2 * handed.size * 2),
        name="reorder",
    )(block_table, handed)
    cache_out = cache_out.reshape(devices, per_device, layers, kv_heads, head_size)

    code = route_codes(route_ids, z_index).astype(f32)
    probs = jax.nn.softmax(route_logits, axis=-1)
    pad = ((0, 0), (0, 2))
    packed = jnp.concatenate([jnp.pad(code, pad), jnp.pad(probs, pad)], axis=1).T
    packed = lax.all_gather(packed, "seq", axis=0, axis_index_groups=z_groups)
    gathered_codes = packed[:, :8].astype(jnp.int32) - (z_index % 2) * (PLANE * 4 * Z_SIZE * CAP)
    all_tokens = Z_SIZE * tokens
    code_rows = jnp.transpose(gathered_codes, (1, 0, 2)).reshape(8, all_tokens)
    code_columns = jnp.transpose(gathered_codes, (0, 2, 1)).reshape(all_tokens, 8)
    prob_columns = jnp.transpose(packed[:, 8:], (0, 2, 1)).reshape(all_tokens, 8)

    shared_both = lax.all_gather(
        jnp.transpose(shared_gate_up, (1, 2, 0)), "seq", axis=0, axis_index_groups=planes
    )
    shared_back = lax.all_gather(
        shared_down, "seq", axis=0, tiled=True, axis_index_groups=planes
    )

    first_token = jnp.reshape(me * tokens, (1,)).astype(jnp.int32)
    heads = pl.pallas_call(
        attention_kernel,
        out_shape=shape((tokens, width), bf16),
        in_specs=[SMEM, SMEM] + [VMEM] * 6,
        out_specs=VMEM,
        compiler_params=params(24),
        cost_estimate=cost(4 * tokens * 5 * tokens * width, 2 * MIB),
        name="attention",
    )(first_token, lengths, queries, *behind, own_kv)

    other_heads = lax.ppermute(heads, "seq", partner)
    core = jnp.reshape(me % 2, (1,)).astype(jnp.int32)
    steps = 4
    half_columns = turned_weight.shape[0]
    own_out, other_out = pl.pallas_call(
        lambda *refs: project_kernel(*refs, chunk=out_weight.shape[1]),
        grid=(steps,),
        out_shape=[shape((tokens, width), f32)] * 2,
        in_specs=[
            SMEM,
            pl.BlockSpec((tokens, width), lambda i: (0, 0)),
            pl.BlockSpec((tokens, width), lambda i: (0, 0)),
            pl.BlockSpec((half_columns // steps, width), lambda i: (i, 0)),
        ],
        out_specs=[pl.BlockSpec((tokens, width // steps), lambda i: (0, i))] * 2,
        compiler_params=params(24),
        cost_estimate=cost(4 * tokens * width * half_columns, 3 * MIB),
        name="project",
    )(core, heads, other_heads, turned_weight)
    received_out = lax.ppermute(other_out, "seq", partner)

    mixed, normed = pl.pallas_call(
        norm_kernel,
        out_shape=[shape((tokens, width), f32), shape((Z_SIZE, tokens, width), bf16)],
        in_specs=[VMEM] * 4,
        out_specs=[VMEM] * 2,
        compiler_params=params(16),
        cost_estimate=cost(8 * tokens * width, 2 * MIB),
        name="norm",
    )(residual, own_out, received_out, norm_gain.reshape(1, width))

    rows = lax.all_to_all(
        normed, "seq", split_axis=0, concat_axis=0, tiled=True, axis_index_groups=z_groups
    ).reshape(all_tokens, width)

    local_halves, _, _, half_ff = expert_gate_up.shape
    per_half = Z_SIZE * CAP
    picked = local_halves * per_half
    outgoing = pl.pallas_call(
        pick_kernel,
        grid=(PLANE,),
        out_shape=shape((PLANE, picked, width), bf16),
        in_specs=[
            pl.BlockSpec((8, all_tokens), lambda i: (0, 0)),
            pl.BlockSpec((all_tokens, width), lambda i: (0, 0)),
        ],
        out_specs=pl.BlockSpec((1, picked, width), lambda i: (i, 0, 0)),
        compiler_params=params(16),
        cost_estimate=cost(2 * PLANE * picked * all_tokens * width, 3 * MIB),
        name="pick",
    )(code_rows, rows)

    arrived = lax.all_to_all(
        outgoing, "seq", split_axis=0, concat_axis=0, tiled=True, axis_index_groups=planes
    )
    shared_part, mix = pl.pallas_call(
        shared_kernel,
        out_shape=[shape((all_tokens, width), f32), shape((all_tokens, PLANE * picked), bf16)],
        in_specs=[VMEM] * 5,
        out_specs=[VMEM] * 2,
        compiler_params=params(32),
        cost_estimate=cost(6 * all_tokens * 256 * width, 5 * MIB),
        name="shared_expert",
    )(code_columns, prob_columns, rows, shared_both, shared_back)

    gate_up = jnp.transpose(expert_gate_up, (0, 2, 1, 3))
    returning = pl.pallas_call(
        experts_kernel,
        grid=(local_halves // 2,),
        out_shape=shape((PLANE, picked, width), bf16),
        in_specs=[
            pl.BlockSpec((PLANE, 2 * per_half, width), lambda i: (0, i, 0)),
            pl.BlockSpec((2, 2, width, half_ff), lambda i: (i, 0, 0, 0)),
            pl.BlockSpec((2, half_ff, width), lambda i: (i, 0, 0)),
        ],
        out_specs=pl.BlockSpec((PLANE, 2 * per_half, width), lambda i: (0, i, 0)),
        compiler_params=params(40),
        cost_estimate=cost(6 * PLANE * picked * half_ff * width, 14 * MIB),
        name="experts",
    )(arrived, gate_up, expert_down)
    returned = lax.all_to_all(
        returning, "seq", split_axis=0, concat_axis=0, tiled=True, axis_index_groups=planes
    ).reshape(PLANE * picked, width)

    column_steps = 2
    part_width = width // column_steps
    parts = pl.pallas_call(
        combine_kernel,
        grid=(column_steps,),
        out_shape=shape((all_tokens, width), bf16),
        in_specs=[
            pl.BlockSpec((all_tokens, PLANE * picked), lambda i: (0, 0)),
            pl.BlockSpec((PLANE * picked, part_width), lambda i: (0, i)),
            pl.BlockSpec((all_tokens, part_width), lambda i: (0, i)),
        ],
        out_specs=pl.BlockSpec((all_tokens, part_width), lambda i: (0, i)),
        compiler_params=params(24),
        cost_estimate=cost(2 * all_tokens * PLANE * picked * width, 5 * MIB),
        name="combine",
    )(mix, returned, shared_part)
    parts = lax.all_to_all(
        parts.reshape(Z_SIZE, tokens, width),
        "seq",
        split_axis=0,
        concat_axis=0,
        tiled=True,
        axis_index_groups=z_groups,
    )
    layer_out = pl.pallas_call(
        final_kernel,
        out_shape=shape((tokens, width), bf16),
        in_specs=[VMEM] * 2,
        out_specs=VMEM,
        compiler_params=params(16),
        cost_estimate=cost(5 * tokens * width, MIB),
        name="final",
    )(mixed, parts)
    return (layer_out, cache_out)


def solution(mesh):
    in_specs = (
        P("seq", "head"),
        P("seq", "head"),
        P("seq", "head"),
        P(),
        P("head", "seq"),
        P(("seq", "head"), None),
        P(),
        P(("seq", "head"), None),
        P(("seq", "head"), None),
        P(None, None, ("seq", "head")),
        P(("seq", "head"), None),
        P("seq", None, None, None),
        P("seq", None, None),
        P("seq", None, None, "head", None),
        P(),
    )
    out_specs = (P(("seq", "head"), None), P(None, "seq", None, "head", None))
    planes_fit = mesh.shape["seq"] == Z_SIZE * PLANE and mesh.shape["head"] == 1
    body = shards if planes_fit else general_shards
    return jax.shard_map(body, mesh=mesh, in_specs=in_specs, out_specs=out_specs, check_vma=False)
```

```python
import math

import jax
import jax.numpy as jnp
from jax import lax
from jax.experimental import pallas as pl
from jax.experimental.pallas import tpu as pltpu
from jax.sharding import PartitionSpec as P

HD = 128
EXPERTS = 64
TOP = 6
REACH = 4
HALVES = 128
CAP = 6
Z_SIZE = 4
PLANE = 8
MIB = 1024 * 1024


NEGATIVE = -1e30
EPSILON = 1e-05


def from_behind(shard, axis, by):
    devices = lax.axis_size(axis)
    pairs = [(i, i + by) for i in range(devices) if 0 <= i + by < devices]
    return lax.ppermute(shard, axis, pairs)


def segment_of(positions, lengths):
    request_ends = jnp.cumsum(lengths)
    passed = (request_ends[None, :] <= positions[:, None]).astype(jnp.int32)
    return jnp.sum(passed, axis=1)


def shared_ffn(rows_in, gate_up_part, down_part):
    shared_both = jnp.einsum(
        "td,dcf->tcf", rows_in, gate_up_part, preferred_element_type=jnp.float32
    )
    shared_act = (jax.nn.silu(shared_both[:, 0]) * shared_both[:, 1]).astype(jnp.bfloat16)
    return jnp.dot(shared_act, down_part, preferred_element_type=jnp.float32)


def general_shards(
    queries,
    key_vectors,
    value_vectors,
    lengths,
    out_weight,
    residual,
    norm_gain,
    route_ids,
    route_logits,
    shared_gate_up,
    shared_down,
    expert_gate_up,
    expert_down,
    cache_blocks,
    block_table,
):
    handed = lax.all_to_all(cache_blocks, "seq", split_axis=1, concat_axis=0, tiled=True)
    cache_out = jnp.take(handed, block_table, axis=0)
    tok_rows = queries.shape[0]
    seq_index = lax.axis_index("seq")
    earlier = [
        from_behind((key_vectors, value_vectors), "seq", offset) for offset in range(REACH, 0, -1)
    ]
    window_keys = jnp.concatenate([member[0] for member in earlier] + [key_vectors], axis=0)
    window_values = jnp.concatenate([member[1] for member in earlier] + [value_vectors], axis=0)
    key_count = window_keys.shape[0]
    kv_heads = key_vectors.shape[1] // HD
    query_heads = queries.shape[1] // HD
    group_size = query_heads // kv_heads
    query_pos = seq_index * tok_rows + jnp.arange(tok_rows, dtype=jnp.int32)
    key_pos = (seq_index - REACH) * tok_rows + jnp.arange(key_count, dtype=jnp.int32)
    visible = (key_pos[None, :] >= 0) & (key_pos[None, :] <= query_pos[:, None])
    visible = visible & (
        segment_of(key_pos, lengths)[None, :] == segment_of(query_pos, lengths)[:, None]
    )
    query_part = queries.reshape(tok_rows, kv_heads, group_size, HD)
    key_part = window_keys.reshape(key_count, kv_heads, HD)
    value_part = window_values.reshape(key_count, kv_heads, HD)
    scores = jnp.einsum(
        "tkgd,wkd->kgtw", query_part, key_part, preferred_element_type=jnp.float32
    ) * (1.0 / math.sqrt(HD))
    scores = jnp.where(visible[None, None], scores, NEGATIVE)
    row_max = jnp.max(scores, axis=-1, keepdims=True)
    weights = jnp.exp(scores - row_max)
    row_total = jnp.sum(weights, axis=-1)
    weighted = jnp.einsum(
        "kgtw,wkd->tkgd",
        weights.astype(jnp.bfloat16),
        value_part,
        preferred_element_type=jnp.float32,
    )
    heads = (weighted / jnp.transpose(row_total, (2, 0, 1))[..., None]).astype(jnp.bfloat16)
    heads = heads.reshape(tok_rows, query_heads * HD)
    partial_out = jnp.dot(
        heads,
        lax.all_gather(out_weight, "seq", axis=1, tiled=True),
        preferred_element_type=jnp.float32,
    )
    attn_out = lax.psum_scatter(partial_out, "head", scatter_dimension=0, tiled=True)
    mixed = residual.astype(jnp.float32) + attn_out
    mean_square = jnp.mean(mixed * mixed, axis=-1, keepdims=True)
    normed = (mixed * lax.rsqrt(mean_square + EPSILON) * norm_gain).astype(jnp.bfloat16)
    gate_up_all, down_all = (
        lax.all_gather(shared_gate_up, ("seq", "head"), axis=2, tiled=True),
        lax.all_gather(shared_down, ("seq", "head"), axis=0, tiled=True),
    )
    shared_part = shared_ffn(normed, gate_up_all, down_all)
    own_tokens = normed.shape[0]
    width_model = normed.shape[1]
    flat_ids = route_ids.reshape(-1)
    onehot = (flat_ids[:, None] == jnp.arange(EXPERTS, dtype=jnp.int32)[None, :]).astype(jnp.int32)
    slot_rank = jnp.sum((jnp.cumsum(onehot, axis=0) - 1) * onehot, axis=1)
    first_slot = flat_ids * CAP + slot_rank
    second_slot = (flat_ids + EXPERTS) * CAP + slot_rank
    token_of = jnp.arange(flat_ids.shape[0], dtype=jnp.int32) // TOP
    routed_rows = normed[token_of]
    outgoing = jnp.zeros((HALVES * CAP, width_model), jnp.bfloat16)
    outgoing = outgoing.at[jnp.concatenate([first_slot, second_slot])].set(
        jnp.concatenate([routed_rows, routed_rows], axis=0)
    )
    local_halves = expert_gate_up.shape[0]
    outgoing = outgoing.reshape(HALVES // local_halves, local_halves, CAP, width_model)
    gate_up = jnp.einsum(
        "nsjd,sdcf->nsjcf",
        lax.all_to_all(outgoing, "seq", split_axis=0, concat_axis=0, tiled=True),
        expert_gate_up,
        preferred_element_type=jnp.float32,
    )
    expert_act = (jax.nn.silu(gate_up[:, :, :, 0]) * gate_up[:, :, :, 1]).astype(jnp.bfloat16)
    half_out = jnp.einsum(
        "nsjf,sfd->nsjd", expert_act, expert_down, preferred_element_type=jnp.float32
    ).astype(jnp.bfloat16)
    returned = lax.all_to_all(half_out, "seq", split_axis=0, concat_axis=0, tiled=True)
    returned = returned.reshape(HALVES * CAP, width_model)
    pair_sum = returned[first_slot].astype(jnp.float32) + returned[second_slot].astype(jnp.float32)
    route_probs = jax.nn.softmax(route_logits, axis=-1)
    routed = jnp.sum(
        route_probs[:, :, None] * pair_sum.reshape(own_tokens, TOP, width_model), axis=1
    )
    layer_out = (mixed + shared_part + routed).astype(jnp.bfloat16)
    return (layer_out, cache_out)


VMEM = pl.BlockSpec(memory_space=pltpu.VMEM)
SMEM = pl.BlockSpec(memory_space=pltpu.SMEM)
ANY = pl.BlockSpec(memory_space=pl.ANY)


def dot_rows(left, right):
    return lax.dot_general(left, right, (((1,), (1,)), ((), ())), preferred_element_type=jnp.float32)


def dot(left, right):
    return jnp.dot(left, right, preferred_element_type=jnp.float32)


def silu_times(gate, up):
    return (gate / (1.0 + jnp.exp(-gate)) * up).astype(jnp.bfloat16)


def attention_kernel(
    first_ref, lengths_ref, q_ref, k4_ref, k3_ref, k2_ref, k1_ref, own_ref, residual_ref, info_ref, out_ref
):
    tokens, width = q_ref.shape
    copies = out_ref.shape[0]
    kv_width = own_ref.shape[1] // 2
    kv_heads = kv_width // HD
    group = width // HD // kv_heads
    blocks = [k4_ref, k3_ref, k2_ref, k1_ref, own_ref]
    keys = len(blocks) * tokens
    first = first_ref[0]
    query_pos = first + lax.broadcasted_iota(jnp.int32, (tokens, keys), 0)
    key_pos = first - (keys - tokens) + lax.broadcasted_iota(jnp.int32, (tokens, keys), 1)
    start = jnp.zeros((tokens, keys), jnp.int32)
    end = jnp.int32(0)
    for request in range(lengths_ref.shape[0]):
        end = end + lengths_ref[request]
        start = jnp.maximum(start, jnp.where(query_pos >= end, end, 0))
    hidden = jnp.where((key_pos >= start) & (key_pos <= query_pos), 0.0, NEGATIVE)
    hidden = jnp.concatenate([hidden] * group, axis=0)
    scale = 1.0 / math.sqrt(HD)
    part = width // copies
    for z in range(copies):
        out_ref[z, :, width : width + part] = residual_ref[:, z * part : (z + 1) * part]
        out_ref[z, :, width + part :] = info_ref[...]
    for kv in range(kv_heads):
        at = slice(kv * HD, (kv + 1) * HD)
        value_at = slice(kv_width + kv * HD, kv_width + (kv + 1) * HD)
        key = jnp.concatenate([block[:, at] for block in blocks], axis=0)
        value = jnp.concatenate([block[:, value_at] for block in blocks], axis=0)
        heads = [kv * group + member for member in range(group)]
        query = jnp.concatenate([q_ref[:, h * HD : (h + 1) * HD] for h in heads], axis=0)
        scores = dot_rows(query, key) * scale + hidden
        weights = jnp.exp(scores - jnp.max(scores, axis=-1, keepdims=True))
        total = jnp.sum(weights, axis=-1, keepdims=True)
        result = (dot(weights.astype(jnp.bfloat16), value) / total).astype(jnp.bfloat16)
        for member, h in enumerate(heads):
            for z in range(copies):
                out_ref[z, :, h * HD : (h + 1) * HD] = result[member * tokens : (member + 1) * tokens]


def project_kernel(heads_ref, residual_ref, weight_ref, out_ref):
    out = dot_rows(heads_ref[...], weight_ref[...]) + residual_ref[...].astype(jnp.float32)
    out = out.astype(jnp.bfloat16)
    for z in range(out_ref.shape[0]):
        out_ref[z] = out


def row_codes(info, first, parity, per_device):
    where_to = info(first).astype(jnp.int32) - PLANE * parity
    inside = info(first + 8).astype(jnp.int32)
    fits = (where_to >= 0) & (where_to < PLANE)
    return jnp.where(fits, where_to * per_device + inside, -1)


def pick_kernel(parity_ref, mixed_ref, gain_ref, info_ref, normed_ref, out_ref, code_ref):
    _, picked, _ = out_ref.shape
    tokens = normed_ref.shape[0]

    @pl.when(pl.program_id(0) == 0)
    def _():
        columns = mixed_ref.shape[2]
        mixed = [mixed_ref[z].astype(jnp.float32) for z in range(mixed_ref.shape[0])]
        square = sum(jnp.sum(m * m, axis=-1, keepdims=True) for m in mixed)
        factor = lax.rsqrt(square / normed_ref.shape[1] + EPSILON)
        for z, m in enumerate(mixed):
            at = slice(z * columns, (z + 1) * columns)
            normed_ref[:, at] = (m * factor * gain_ref[:, at]).astype(jnp.bfloat16)
        info = info_ref[...].astype(jnp.float32).T
        code_ref[...] = row_codes(lambda at: info[at : at + 8], 0, parity_ref[0], picked)

    row = pl.program_id(0) * picked + lax.broadcasted_iota(jnp.int32, (picked, tokens), 0)
    chosen = code_ref[0:1, :] == row
    for choice in range(1, TOP):
        chosen = chosen | (code_ref[choice : choice + 1, :] == row)
    onehot = jnp.where(chosen, 1.0, 0.0).astype(jnp.bfloat16)
    out_ref[0] = dot(onehot, normed_ref[...]).astype(jnp.bfloat16)


def shared_kernel(parity_ref, info_ref, rows_ref, weight_ref, out_ref, mix_ref):
    parts, units, _ = weight_ref.shape
    units = units // 3
    gate_weight, up_weight, down_weight = [
        jnp.concatenate([weight_ref[p, at * units : (at + 1) * units] for p in range(parts)], axis=0)
        for at in range(3)
    ]
    rows = rows_ref[...]
    act = silu_times(dot_rows(rows, gate_weight), dot_rows(rows, up_weight))
    out_ref[...] = dot(act, down_weight)
    info = info_ref[...].astype(jnp.float32)
    column = lax.broadcasted_iota(jnp.int32, mix_ref.shape, 1)
    mix = jnp.zeros(mix_ref.shape, jnp.float32)
    for choice in range(TOP):
        code = row_codes(lambda at: info[:, at : at + 1], choice, parity_ref[0], mix_ref.shape[1] // PLANE)
        mix = jnp.where(code == column, info[:, 16 + choice : 17 + choice], mix)
    mix_ref[...] = mix.astype(jnp.bfloat16)


def experts_kernel(rows_ref, gate_up_ref, down_ref, out_ref):
    sources, both, width = rows_ref.shape
    per_half = both // 2
    rows = rows_ref[...].astype(jnp.float32)
    results = []
    for half in range(2):
        own = rows[:, half * per_half : (half + 1) * per_half]
        own = own.reshape(sources * per_half, width).astype(jnp.bfloat16)
        act = silu_times(dot(own, gate_up_ref[half, 0]), dot(own, gate_up_ref[half, 1]))
        results.append(dot(act, down_ref[half]).reshape(sources, per_half, width))
    out_ref[...] = jnp.concatenate(results, axis=1).astype(jnp.bfloat16)


def combine_kernel(mix_ref, rows_ref, shared_ref, out_ref):
    out_ref[...] = (dot(mix_ref[...], rows_ref[...]) + shared_ref[...]).astype(jnp.bfloat16)


def final_kernel(z_ref, mixed_ref, parts_ref, out_ref):
    tokens = out_ref.shape[0]
    columns = mixed_ref.shape[2]
    own = pl.ds(pl.multiple_of(z_ref[0] * tokens, tokens), tokens)
    for block in range(mixed_ref.shape[0]):
        at = slice(block * columns, (block + 1) * columns)
        total = mixed_ref[block, own, :].astype(jnp.float32)
        for z in range(parts_ref.shape[0]):
            total = total + parts_ref[z, :, at].astype(jnp.float32)
        out_ref[:, at] = total.astype(jnp.bfloat16)


def reorder_kernel(me_ref, table_ref, from_ref, to_ref):
    me = me_ref[0]
    for block in range(to_ref.shape[0]):
        source = table_ref[block]
        z_steps = (me // PLANE - source // PLANE + Z_SIZE) % Z_SIZE
        steps = (me % PLANE - source % PLANE + PLANE) % PLANE
        to_ref[block] = from_ref[z_steps * PLANE + steps]


def params(mib):
    return pltpu.CompilerParams(vmem_limit_bytes=mib * MIB)


def cost(flops, moved):
    return pl.CostEstimate(flops=int(flops), bytes_accessed=int(moved), transcendentals=0)


def route_info(route_ids, route_logits, z_index):
    tokens = route_ids.shape[0]
    experts = jnp.arange(EXPERTS, dtype=jnp.int32)
    named = route_ids[:, :, None] == experts[None, None, :]
    member = jnp.any(named, axis=1).astype(jnp.float32)
    order = jnp.arange(tokens, dtype=jnp.int32)
    before = (order[None, :] < order[:, None]).astype(jnp.float32)
    ahead = dot(before, member)
    rank = jnp.sum(jnp.where(named, ahead[:, None, :], 0.0), axis=2).astype(jnp.int32)
    per_device = EXPERTS // 2 // PLANE
    where_to = route_ids // per_device
    inside = ((route_ids % per_device) * Z_SIZE + z_index) * CAP + rank
    probs = jax.nn.softmax(route_logits, axis=-1)
    pad = ((0, 0), (0, 8 - TOP))
    columns = [jnp.pad(c.astype(jnp.bfloat16), pad) for c in (where_to, inside, probs)]
    return jnp.concatenate(columns + [jnp.zeros((tokens, 104), jnp.bfloat16)], axis=1)


def shards(
    queries,
    key_vectors,
    value_vectors,
    lengths,
    out_weight,
    residual,
    norm_gain,
    route_ids,
    route_logits,
    shared_gate_up,
    shared_down,
    expert_gate_up,
    expert_down,
    cache_blocks,
    block_table,
):
    tokens, width = residual.shape
    devices = lax.axis_size("seq")
    me = lax.axis_index("seq")
    z_index, plane_index = me // PLANE, me % PLANE
    z_groups = [[p + PLANE * z for z in range(Z_SIZE)] for p in range(PLANE)]
    planes = [[p + PLANE * z for p in range(PLANE)] for z in range(Z_SIZE)]
    bf16, f32 = jnp.bfloat16, jnp.float32
    shape = jax.ShapeDtypeStruct
    scalar = lambda value: jnp.reshape(value, (1,)).astype(jnp.int32)
    all_tokens = Z_SIZE * tokens
    part = width // Z_SIZE

    def exchange(array, groups):
        return lax.all_to_all(
            array, "seq", split_axis=0, concat_axis=0, tiled=True, axis_index_groups=groups
        )

    own_kv = jnp.concatenate([key_vectors, value_vectors], axis=1)
    behind = [from_behind(own_kv, "seq", offset) for offset in range(REACH, 0, -1)]

    turned_weight = lax.all_gather(
        out_weight.T, "seq", axis=0, tiled=True, axis_index_groups=planes
    )
    own_shared = jnp.concatenate(
        [jnp.transpose(shared_gate_up, (1, 2, 0)).reshape(-1, width), shared_down], axis=0
    )
    shared_weight = lax.all_gather(own_shared, "seq", axis=0, axis_index_groups=planes)

    info = route_info(route_ids, route_logits, z_index)
    sent_width = width + part + info.shape[1]
    sent = pl.pallas_call(
        attention_kernel,
        out_shape=shape((Z_SIZE, tokens, sent_width), bf16),
        in_specs=[SMEM, SMEM] + [VMEM] * 8,
        out_specs=VMEM,
        compiler_params=params(24),
        cost_estimate=cost(4 * tokens * 5 * tokens * width, 3 * MIB),
        name="attention",
    )(scalar(me * tokens), lengths, queries, *behind, own_kv, residual, info)

    sent, cache_blocks = lax.optimization_barrier((sent, cache_blocks))
    _, block_tokens, layers, kv_heads, head_size = cache_blocks.shape
    per_device = block_tokens // devices
    cache_view = cache_blocks.reshape(Z_SIZE, PLANE, per_device * layers, kv_heads, head_size)
    in_plane = []
    for step in range(PLANE):
        piece = lax.dynamic_index_in_dim(
            cache_view, (plane_index + step) % PLANE, axis=1, keepdims=False
        )
        if step:
            pairs = [
                (z * PLANE + p, z * PLANE + (p + step) % PLANE)
                for z in range(Z_SIZE)
                for p in range(PLANE)
            ]
            piece = lax.ppermute(piece, "seq", pairs)
        in_plane.append(piece)

    gathered = exchange(sent, z_groups).reshape(all_tokens, sent_width)
    mixed_part = pl.pallas_call(
        project_kernel,
        grid=(1,),
        out_shape=shape((Z_SIZE, all_tokens, part), bf16),
        in_specs=[
            pl.BlockSpec((all_tokens, width), lambda i: (0, 0)),
            pl.BlockSpec((all_tokens, part), lambda i: (0, width // part)),
            pl.BlockSpec((part, width), lambda i: (0, 0)),
        ],
        out_specs=pl.BlockSpec((Z_SIZE, all_tokens, part), lambda i: (0, 0, 0)),
        compiler_params=params(24),
        cost_estimate=cost(2 * all_tokens * width * part, 3 * MIB),
        name="project",
    )(gathered, gathered, turned_weight)
    mixed = exchange(mixed_part, z_groups)

    local_halves, _, _, half_ff = expert_gate_up.shape
    per_half = Z_SIZE * CAP
    picked = local_halves * per_half
    info_at = sent_width // 128 - 1
    parity = scalar(z_index % 2)
    normed, outgoing = pl.pallas_call(
        pick_kernel,
        grid=(PLANE,),
        out_shape=[shape((all_tokens, width), bf16), shape((PLANE, picked, width), bf16)],
        in_specs=[
            SMEM,
            pl.BlockSpec((Z_SIZE, all_tokens, part), lambda i: (0, 0, 0)),
            pl.BlockSpec((1, width), lambda i: (0, 0)),
            pl.BlockSpec((all_tokens, 128), lambda i: (0, info_at)),
        ],
        out_specs=[
            pl.BlockSpec((all_tokens, width), lambda i: (0, 0)),
            pl.BlockSpec((1, picked, width), lambda i: (i, 0, 0)),
        ],
        scratch_shapes=[pltpu.VMEM((8, all_tokens), jnp.int32)],
        compiler_params=params(24),
        cost_estimate=cost(2 * PLANE * picked * all_tokens * width, 4 * MIB),
        name="pick",
    )(parity, mixed, norm_gain.reshape(1, width), gathered)

    outgoing, in_plane = lax.optimization_barrier((outgoing, in_plane))
    stacked = jnp.stack(in_plane)
    arrived_cache = []
    for step in range(Z_SIZE):
        piece = lax.dynamic_index_in_dim(stacked, (z_index + step) % Z_SIZE, axis=1, keepdims=False)
        if step:
            pairs = [
                (z * PLANE + p, (z + step) % Z_SIZE * PLANE + p)
                for z in range(Z_SIZE)
                for p in range(PLANE)
            ]
            piece = lax.ppermute(piece, "seq", pairs)
        arrived_cache.append(piece)
    arrived_cache = jnp.concatenate(arrived_cache)
    cache_out = pl.pallas_call(
        reorder_kernel,
        out_shape=shape(arrived_cache.shape, bf16),
        in_specs=[SMEM, SMEM, VMEM],
        out_specs=VMEM,
        compiler_params=params(16),
        cost_estimate=cost(0, 2 * arrived_cache.size * 2),
        name="reorder",
    )(scalar(me), block_table, arrived_cache)
    cache_out = cache_out.reshape(devices, per_device, layers, kv_heads, head_size)

    arrived = exchange(outgoing, planes)
    shared_part, mix = pl.pallas_call(
        shared_kernel,
        grid=(1,),
        out_shape=[shape((all_tokens, width), f32), shape((all_tokens, PLANE * picked), bf16)],
        in_specs=[
            SMEM,
            pl.BlockSpec((all_tokens, 128), lambda i: (0, info_at)),
            pl.BlockSpec((all_tokens, width), lambda i: (0, 0)),
            pl.BlockSpec(shared_weight.shape, lambda i: (0, 0, 0)),
        ],
        out_specs=[
            pl.BlockSpec((all_tokens, width), lambda i: (0, 0)),
            pl.BlockSpec((all_tokens, PLANE * picked), lambda i: (0, 0)),
        ],
        compiler_params=params(32),
        cost_estimate=cost(6 * all_tokens * 256 * width, 5 * MIB),
        name="shared_expert",
    )(parity, gathered, normed, shared_weight)

    gate_up = jnp.transpose(expert_gate_up, (0, 2, 1, 3))
    returning = pl.pallas_call(
        experts_kernel,
        grid=(local_halves // 2,),
        out_shape=shape((PLANE, picked, width), bf16),
        in_specs=[
            pl.BlockSpec((PLANE, 2 * per_half, width), lambda i: (0, i, 0)),
            pl.BlockSpec((2, 2, width, half_ff), lambda i: (i, 0, 0, 0)),
            pl.BlockSpec((2, half_ff, width), lambda i: (i, 0, 0)),
        ],
        out_specs=pl.BlockSpec((PLANE, 2 * per_half, width), lambda i: (0, i, 0)),
        compiler_params=params(40),
        cost_estimate=cost(6 * PLANE * picked * half_ff * width, 14 * MIB),
        name="experts",
    )(arrived, gate_up, expert_down)
    returned = exchange(returning, planes).reshape(PLANE * picked, width)

    column_steps = 2
    part_width = width // column_steps
    parts = pl.pallas_call(
        combine_kernel,
        grid=(column_steps,),
        out_shape=shape((all_tokens, width), bf16),
        in_specs=[
            pl.BlockSpec((all_tokens, PLANE * picked), lambda i: (0, 0)),
            pl.BlockSpec((PLANE * picked, part_width), lambda i: (0, i)),
            pl.BlockSpec((all_tokens, part_width), lambda i: (0, i)),
        ],
        out_specs=pl.BlockSpec((all_tokens, part_width), lambda i: (0, i)),
        compiler_params=params(24),
        cost_estimate=cost(2 * all_tokens * PLANE * picked * width, 5 * MIB),
        name="combine",
    )(mix, returned, shared_part)
    parts = exchange(parts.reshape(Z_SIZE, tokens, width), z_groups)
    layer_out = pl.pallas_call(
        final_kernel,
        out_shape=shape((tokens, width), bf16),
        in_specs=[SMEM] + [VMEM] * 2,
        out_specs=VMEM,
        compiler_params=params(16),
        cost_estimate=cost(5 * tokens * width, 2 * MIB),
        name="final",
    )(scalar(z_index), mixed, parts)
    return (layer_out, cache_out)


def solution(mesh):
    in_specs = (
        P("seq", "head"),
        P("seq", "head"),
        P("seq", "head"),
        P(),
        P("head", "seq"),
        P(("seq", "head"), None),
        P(),
        P(("seq", "head"), None),
        P(("seq", "head"), None),
        P(None, None, ("seq", "head")),
        P(("seq", "head"), None),
        P("seq", None, None, None),
        P("seq", None, None),
        P("seq", None, None, "head", None),
        P(),
    )
    out_specs = (P(("seq", "head"), None), P(None, "seq", None, "head", None))
    planes_fit = mesh.shape["seq"] == Z_SIZE * PLANE and mesh.shape["head"] == 1
    body = shards if planes_fit else general_shards
    return jax.shard_map(body, mesh=mesh, in_specs=in_specs, out_specs=out_specs, check_vma=False)
```

```python
import math

import jax
import jax.numpy as jnp
from jax import lax
from jax.experimental import pallas as pl
from jax.experimental.pallas import tpu as pltpu
from jax.sharding import PartitionSpec as P

HD = 128
EXPERTS = 64
TOP = 6
REACH = 4
HALVES = 128
CAP = 6
Z_SIZE = 4
PLANE = 8
MIB = 1024 * 1024


NEGATIVE = -1e30
EPSILON = 1e-05


def from_behind(shard, axis, by):
    devices = lax.axis_size(axis)
    pairs = [(i, i + by) for i in range(devices) if 0 <= i + by < devices]
    return lax.ppermute(shard, axis, pairs)


def segment_of(positions, lengths):
    request_ends = jnp.cumsum(lengths)
    passed = (request_ends[None, :] <= positions[:, None]).astype(jnp.int32)
    return jnp.sum(passed, axis=1)


def shared_ffn(rows_in, gate_up_part, down_part):
    shared_both = jnp.einsum(
        "td,dcf->tcf", rows_in, gate_up_part, preferred_element_type=jnp.float32
    )
    shared_act = (jax.nn.silu(shared_both[:, 0]) * shared_both[:, 1]).astype(jnp.bfloat16)
    return jnp.dot(shared_act, down_part, preferred_element_type=jnp.float32)


def general_shards(
    queries,
    key_vectors,
    value_vectors,
    lengths,
    out_weight,
    residual,
    norm_gain,
    route_ids,
    route_logits,
    shared_gate_up,
    shared_down,
    expert_gate_up,
    expert_down,
    cache_blocks,
    block_table,
):
    handed = lax.all_to_all(cache_blocks, "seq", split_axis=1, concat_axis=0, tiled=True)
    cache_out = jnp.take(handed, block_table, axis=0)
    tok_rows = queries.shape[0]
    seq_index = lax.axis_index("seq")
    earlier = [
        from_behind((key_vectors, value_vectors), "seq", offset) for offset in range(REACH, 0, -1)
    ]
    window_keys = jnp.concatenate([member[0] for member in earlier] + [key_vectors], axis=0)
    window_values = jnp.concatenate([member[1] for member in earlier] + [value_vectors], axis=0)
    key_count = window_keys.shape[0]
    kv_heads = key_vectors.shape[1] // HD
    query_heads = queries.shape[1] // HD
    group_size = query_heads // kv_heads
    query_pos = seq_index * tok_rows + jnp.arange(tok_rows, dtype=jnp.int32)
    key_pos = (seq_index - REACH) * tok_rows + jnp.arange(key_count, dtype=jnp.int32)
    visible = (key_pos[None, :] >= 0) & (key_pos[None, :] <= query_pos[:, None])
    visible = visible & (
        segment_of(key_pos, lengths)[None, :] == segment_of(query_pos, lengths)[:, None]
    )
    query_part = queries.reshape(tok_rows, kv_heads, group_size, HD)
    key_part = window_keys.reshape(key_count, kv_heads, HD)
    value_part = window_values.reshape(key_count, kv_heads, HD)
    scores = jnp.einsum(
        "tkgd,wkd->kgtw", query_part, key_part, preferred_element_type=jnp.float32
    ) * (1.0 / math.sqrt(HD))
    scores = jnp.where(visible[None, None], scores, NEGATIVE)
    row_max = jnp.max(scores, axis=-1, keepdims=True)
    weights = jnp.exp(scores - row_max)
    row_total = jnp.sum(weights, axis=-1)
    weighted = jnp.einsum(
        "kgtw,wkd->tkgd",
        weights.astype(jnp.bfloat16),
        value_part,
        preferred_element_type=jnp.float32,
    )
    heads = (weighted / jnp.transpose(row_total, (2, 0, 1))[..., None]).astype(jnp.bfloat16)
    heads = heads.reshape(tok_rows, query_heads * HD)
    partial_out = jnp.dot(
        heads,
        lax.all_gather(out_weight, "seq", axis=1, tiled=True),
        preferred_element_type=jnp.float32,
    )
    attn_out = lax.psum_scatter(partial_out, "head", scatter_dimension=0, tiled=True)
    mixed = residual.astype(jnp.float32) + attn_out
    mean_square = jnp.mean(mixed * mixed, axis=-1, keepdims=True)
    normed = (mixed * lax.rsqrt(mean_square + EPSILON) * norm_gain).astype(jnp.bfloat16)
    gate_up_all, down_all = (
        lax.all_gather(shared_gate_up, ("seq", "head"), axis=2, tiled=True),
        lax.all_gather(shared_down, ("seq", "head"), axis=0, tiled=True),
    )
    shared_part = shared_ffn(normed, gate_up_all, down_all)
    own_tokens = normed.shape[0]
    width_model = normed.shape[1]
    flat_ids = route_ids.reshape(-1)
    onehot = (flat_ids[:, None] == jnp.arange(EXPERTS, dtype=jnp.int32)[None, :]).astype(jnp.int32)
    slot_rank = jnp.sum((jnp.cumsum(onehot, axis=0) - 1) * onehot, axis=1)
    first_slot = flat_ids * CAP + slot_rank
    second_slot = (flat_ids + EXPERTS) * CAP + slot_rank
    token_of = jnp.arange(flat_ids.shape[0], dtype=jnp.int32) // TOP
    routed_rows = normed[token_of]
    outgoing = jnp.zeros((HALVES * CAP, width_model), jnp.bfloat16)
    outgoing = outgoing.at[jnp.concatenate([first_slot, second_slot])].set(
        jnp.concatenate([routed_rows, routed_rows], axis=0)
    )
    local_halves = expert_gate_up.shape[0]
    outgoing = outgoing.reshape(HALVES // local_halves, local_halves, CAP, width_model)
    gate_up = jnp.einsum(
        "nsjd,sdcf->nsjcf",
        lax.all_to_all(outgoing, "seq", split_axis=0, concat_axis=0, tiled=True),
        expert_gate_up,
        preferred_element_type=jnp.float32,
    )
    expert_act = (jax.nn.silu(gate_up[:, :, :, 0]) * gate_up[:, :, :, 1]).astype(jnp.bfloat16)
    half_out = jnp.einsum(
        "nsjf,sfd->nsjd", expert_act, expert_down, preferred_element_type=jnp.float32
    ).astype(jnp.bfloat16)
    returned = lax.all_to_all(half_out, "seq", split_axis=0, concat_axis=0, tiled=True)
    returned = returned.reshape(HALVES * CAP, width_model)
    pair_sum = returned[first_slot].astype(jnp.float32) + returned[second_slot].astype(jnp.float32)
    route_probs = jax.nn.softmax(route_logits, axis=-1)
    routed = jnp.sum(
        route_probs[:, :, None] * pair_sum.reshape(own_tokens, TOP, width_model), axis=1
    )
    layer_out = (mixed + shared_part + routed).astype(jnp.bfloat16)
    return (layer_out, cache_out)


VMEM = pl.BlockSpec(memory_space=pltpu.VMEM)
SMEM = pl.BlockSpec(memory_space=pltpu.SMEM)
ANY = pl.BlockSpec(memory_space=pl.ANY)


def dot_rows(left, right):
    return lax.dot_general(left, right, (((1,), (1,)), ((), ())), preferred_element_type=jnp.float32)


def dot(left, right):
    return jnp.dot(left, right, preferred_element_type=jnp.float32)


def silu_times(gate, up):
    return (gate / (1.0 + jnp.exp(-gate)) * up).astype(jnp.bfloat16)


def attention_kernel(
    first_ref, lengths_ref, q_ref, k4_ref, k3_ref, k2_ref, k1_ref, own_ref, residual_ref, info_ref, out_ref
):
    tokens, width = q_ref.shape
    copies = out_ref.shape[0]
    kv_width = own_ref.shape[1] // 2
    kv_heads = kv_width // HD
    group = width // HD // kv_heads
    blocks = [k4_ref, k3_ref, k2_ref, k1_ref, own_ref]
    keys = len(blocks) * tokens
    first = first_ref[0]
    query_pos = first + lax.broadcasted_iota(jnp.int32, (tokens, keys), 0)
    key_pos = first - (keys - tokens) + lax.broadcasted_iota(jnp.int32, (tokens, keys), 1)
    start = jnp.zeros((tokens, keys), jnp.int32)
    end = jnp.int32(0)
    for request in range(lengths_ref.shape[0]):
        end = end + lengths_ref[request]
        start = jnp.maximum(start, jnp.where(query_pos >= end, end, 0))
    hidden = jnp.where((key_pos >= start) & (key_pos <= query_pos), 0.0, NEGATIVE)
    hidden = jnp.concatenate([hidden] * group, axis=0)
    scale = 1.0 / math.sqrt(HD)
    part = width // copies
    for z in range(copies):
        out_ref[z, :, width : width + part] = residual_ref[:, z * part : (z + 1) * part]
        out_ref[z, :, width + part :] = info_ref[...]
    for kv in range(kv_heads):
        at = slice(kv * HD, (kv + 1) * HD)
        value_at = slice(kv_width + kv * HD, kv_width + (kv + 1) * HD)
        key = jnp.concatenate([block[:, at] for block in blocks], axis=0)
        value = jnp.concatenate([block[:, value_at] for block in blocks], axis=0)
        heads = [kv * group + member for member in range(group)]
        query = jnp.concatenate([q_ref[:, h * HD : (h + 1) * HD] for h in heads], axis=0)
        scores = dot_rows(query, key) * scale + hidden
        weights = jnp.exp(scores - jnp.max(scores, axis=-1, keepdims=True))
        total = jnp.sum(weights, axis=-1, keepdims=True)
        result = (dot(weights.astype(jnp.bfloat16), value) / total).astype(jnp.bfloat16)
        for member, h in enumerate(heads):
            for z in range(copies):
                out_ref[z, :, h * HD : (h + 1) * HD] = result[member * tokens : (member + 1) * tokens]


def route_kernel(z_ref, ids_ref, logits_ref, out_ref, turned_ref):
    choices, tokens = ids_ref.shape
    turned_ref[...] = jnp.zeros(turned_ref.shape, jnp.float32)
    turned_ref[:choices, :tokens] = ids_ref[...].astype(jnp.float32)
    turned_ref[8 : 8 + choices, :tokens] = logits_ref[...]
    table = turned_ref[...].T[:tokens]
    lane = lax.broadcasted_iota(jnp.int32, table.shape, 1)
    ids = [table[:, c : c + 1].astype(jnp.int32) for c in range(choices)]
    logits = [table[:, 8 + c : 9 + c] for c in range(choices)]
    member = jnp.zeros(table.shape, jnp.float32)
    for one in ids:
        member = jnp.where(lane == one, 1.0, member)
    row = lax.broadcasted_iota(jnp.int32, (tokens, tokens), 0)
    earlier = jnp.where(lax.broadcasted_iota(jnp.int32, (tokens, tokens), 1) < row, 1.0, 0.0)
    ahead = dot(earlier.astype(jnp.bfloat16), member.astype(jnp.bfloat16))
    top = logits[0]
    for one in logits[1:]:
        top = jnp.maximum(top, one)
    powers = [jnp.exp(one - top) for one in logits]
    total = sum(powers[1:], powers[0])
    per_device = EXPERTS // 2 // PLANE
    out = jnp.zeros(table.shape, jnp.float32)
    for c, one in enumerate(ids):
        rank = jnp.sum(jnp.where(lane == one, ahead, 0.0), axis=1, keepdims=True)
        where_to = lax.div(one, per_device).astype(jnp.float32)
        first = (lax.rem(one, per_device) * Z_SIZE + z_ref[0]) * CAP
        out = jnp.where(lane == c, where_to, out)
        out = jnp.where(lane == 8 + c, first.astype(jnp.float32) + rank, out)
        out = jnp.where(lane == 16 + c, powers[c] / total, out)
    out_ref[...] = out.astype(jnp.bfloat16)


def regroup_kernel(z_ref, *refs):
    pieces, outs = refs[:PLANE], refs[PLANE:]
    for step, out in enumerate(outs):
        z = lax.rem(z_ref[0] + step, Z_SIZE)
        for at, piece in enumerate(pieces):
            out[at] = piece[z]


def project_kernel(heads_ref, residual_ref, weight_ref, out_ref):
    out = dot_rows(heads_ref[...], weight_ref[...]) + residual_ref[...].astype(jnp.float32)
    out = out.astype(jnp.bfloat16)
    for z in range(out_ref.shape[0]):
        out_ref[z] = out


def row_codes(info, first, parity, per_device):
    where_to = info(first).astype(jnp.int32) - PLANE * parity
    inside = info(first + 8).astype(jnp.int32)
    fits = (where_to >= 0) & (where_to < PLANE)
    return jnp.where(fits, where_to * per_device + inside, -1)


def pick_kernel(parity_ref, mixed_ref, gain_ref, info_ref, normed_ref, out_ref, code_ref):
    _, picked, _ = out_ref.shape
    tokens = normed_ref.shape[0]

    @pl.when(pl.program_id(0) == 0)
    def _():
        columns = mixed_ref.shape[2]
        mixed = [mixed_ref[z].astype(jnp.float32) for z in range(mixed_ref.shape[0])]
        square = sum(jnp.sum(m * m, axis=-1, keepdims=True) for m in mixed)
        factor = lax.rsqrt(square / normed_ref.shape[1] + EPSILON)
        for z, m in enumerate(mixed):
            at = slice(z * columns, (z + 1) * columns)
            normed_ref[:, at] = (m * factor * gain_ref[:, at]).astype(jnp.bfloat16)
        info = info_ref[...].astype(jnp.float32).T
        code_ref[...] = row_codes(lambda at: info[at : at + 8], 0, parity_ref[0], picked)

    row = pl.program_id(0) * picked + lax.broadcasted_iota(jnp.int32, (picked, tokens), 0)
    chosen = code_ref[0:1, :] == row
    for choice in range(1, TOP):
        chosen = chosen | (code_ref[choice : choice + 1, :] == row)
    onehot = jnp.where(chosen, 1.0, 0.0).astype(jnp.bfloat16)
    out_ref[0] = dot(onehot, normed_ref[...]).astype(jnp.bfloat16)


def shared_kernel(parity_ref, info_ref, rows_ref, weight_ref, out_ref, mix_ref):
    parts, units, _ = weight_ref.shape
    units = units // 3
    gate_weight, up_weight, down_weight = [
        jnp.concatenate([weight_ref[p, at * units : (at + 1) * units] for p in range(parts)], axis=0)
        for at in range(3)
    ]
    rows = rows_ref[...]
    act = silu_times(dot_rows(rows, gate_weight), dot_rows(rows, up_weight))
    out_ref[...] = dot(act, down_weight)
    info = info_ref[...].astype(jnp.float32)
    column = lax.broadcasted_iota(jnp.int32, mix_ref.shape, 1)
    mix = jnp.zeros(mix_ref.shape, jnp.float32)
    for choice in range(TOP):
        code = row_codes(lambda at: info[:, at : at + 1], choice, parity_ref[0], mix_ref.shape[1] // PLANE)
        mix = jnp.where(code == column, info[:, 16 + choice : 17 + choice], mix)
    mix_ref[...] = mix.astype(jnp.bfloat16)


def experts_kernel(rows_ref, gate_up_ref, down_ref, out_ref):
    sources, both, width = rows_ref.shape
    per_half = both // 2
    rows = rows_ref[...].astype(jnp.float32)
    results = []
    for half in range(2):
        own = rows[:, half * per_half : (half + 1) * per_half]
        own = own.reshape(sources * per_half, width).astype(jnp.bfloat16)
        act = silu_times(dot(own, gate_up_ref[half, 0]), dot(own, gate_up_ref[half, 1]))
        results.append(dot(act, down_ref[half]).reshape(sources, per_half, width))
    out_ref[...] = jnp.concatenate(results, axis=1).astype(jnp.bfloat16)


def combine_kernel(mix_ref, rows_ref, shared_ref, out_ref):
    out_ref[...] = (dot(mix_ref[...], rows_ref[...]) + shared_ref[...]).astype(jnp.bfloat16)


def final_kernel(z_ref, mixed_ref, parts_ref, out_ref):
    tokens = out_ref.shape[0]
    columns = mixed_ref.shape[2]
    own = pl.ds(pl.multiple_of(z_ref[0] * tokens, tokens), tokens)
    for block in range(mixed_ref.shape[0]):
        at = slice(block * columns, (block + 1) * columns)
        total = mixed_ref[block, own, :].astype(jnp.float32)
        for z in range(parts_ref.shape[0]):
            total = total + parts_ref[z, :, at].astype(jnp.float32)
        out_ref[:, at] = total.astype(jnp.bfloat16)


def reorder_kernel(me_ref, table_ref, from_ref, to_ref):
    me = me_ref[0]
    for block in range(to_ref.shape[0]):
        source = table_ref[block]
        z_steps = lax.rem(lax.div(me, PLANE) - lax.div(source, PLANE) + Z_SIZE, Z_SIZE)
        steps = lax.rem(lax.rem(me, PLANE) - lax.rem(source, PLANE) + PLANE, PLANE)
        to_ref[block] = from_ref[z_steps * PLANE + steps]


def params():
    return pltpu.CompilerParams(vmem_limit_bytes=58 * MIB)


def cost(flops, moved):
    return pl.CostEstimate(flops=int(flops), bytes_accessed=int(moved), transcendentals=0)


def shards(
    queries,
    key_vectors,
    value_vectors,
    lengths,
    out_weight,
    residual,
    norm_gain,
    route_ids,
    route_logits,
    shared_gate_up,
    shared_down,
    expert_gate_up,
    expert_down,
    cache_blocks,
    block_table,
):
    tokens, width = residual.shape
    devices = lax.axis_size("seq")
    me = lax.axis_index("seq")
    z_index, plane_index = lax.div(me, PLANE), lax.rem(me, PLANE)
    z_groups = [[p + PLANE * z for z in range(Z_SIZE)] for p in range(PLANE)]
    planes = [[p + PLANE * z for p in range(PLANE)] for z in range(Z_SIZE)]
    bf16, f32 = jnp.bfloat16, jnp.float32
    shape = jax.ShapeDtypeStruct
    scalar = lambda value: jnp.reshape(value, (1,)).astype(jnp.int32)
    all_tokens = Z_SIZE * tokens
    part = width // Z_SIZE

    def exchange(array, groups):
        return lax.all_to_all(
            array, "seq", split_axis=0, concat_axis=0, tiled=True, axis_index_groups=groups
        )

    own_kv = jnp.concatenate([key_vectors, value_vectors], axis=1)
    behind = [from_behind(own_kv, "seq", offset) for offset in range(REACH, 0, -1)]

    turned_weight = lax.all_gather(
        out_weight.T, "seq", axis=0, tiled=True, axis_index_groups=planes
    )
    own_shared = jnp.concatenate(
        [jnp.transpose(shared_gate_up, (1, 2, 0)).reshape(-1, width), shared_down], axis=0
    )

    info = pl.pallas_call(
        route_kernel,
        out_shape=shape((tokens, 128), bf16),
        in_specs=[SMEM] + [VMEM] * 2,
        out_specs=VMEM,
        scratch_shapes=[pltpu.VMEM((128, 128), f32)],
        compiler_params=params(),
        cost_estimate=cost(MIB, MIB),
        name="route",
    )(scalar(z_index), route_ids.T, route_logits.T)
    sent_width = width + part + info.shape[1]
    sent = pl.pallas_call(
        attention_kernel,
        out_shape=shape((Z_SIZE, tokens, sent_width), bf16),
        in_specs=[SMEM, SMEM] + [VMEM] * 8,
        out_specs=VMEM,
        compiler_params=params(),
        cost_estimate=cost(4 * tokens * 5 * tokens * width, 3 * MIB),
        name="attention",
    )(scalar(me * tokens), lengths, queries, *behind, own_kv, residual, info)

    sent, cache_blocks, own_shared, expert_gate_up = lax.optimization_barrier(
        (sent, cache_blocks, own_shared, expert_gate_up)
    )
    shared_weight = lax.all_gather(own_shared, "seq", axis=0, axis_index_groups=planes)
    _, block_tokens, layers, kv_heads, head_size = cache_blocks.shape
    per_device = block_tokens // devices
    cache_view = cache_blocks.reshape(Z_SIZE, PLANE, per_device * layers, kv_heads, head_size)
    in_plane = []
    for step in range(PLANE):
        piece = lax.dynamic_index_in_dim(
            cache_view, lax.rem(plane_index + step, PLANE), axis=1, keepdims=False
        )
        if step:
            pairs = [
                (z * PLANE + p, z * PLANE + (p + step) % PLANE)
                for z in range(Z_SIZE)
                for p in range(PLANE)
            ]
            piece = lax.ppermute(piece, "seq", pairs)
        in_plane.append(piece)

    gathered = exchange(sent, z_groups).reshape(all_tokens, sent_width)
    mixed_part = pl.pallas_call(
        project_kernel,
        grid=(1,),
        out_shape=shape((Z_SIZE, all_tokens, part), bf16),
        in_specs=[
            pl.BlockSpec((all_tokens, width), lambda i: (0, 0)),
            pl.BlockSpec((all_tokens, part), lambda i: (0, width // part)),
            pl.BlockSpec((part, width), lambda i: (0, 0)),
        ],
        out_specs=pl.BlockSpec((Z_SIZE, all_tokens, part), lambda i: (0, 0, 0)),
        compiler_params=params(),
        cost_estimate=cost(2 * all_tokens * width * part, 3 * MIB),
        name="project",
    )(gathered, gathered, turned_weight)
    gate_up = jnp.transpose(expert_gate_up, (0, 2, 1, 3))
    mixed = exchange(mixed_part, z_groups)

    local_halves, _, _, half_ff = expert_gate_up.shape
    per_half = Z_SIZE * CAP
    picked = local_halves * per_half
    info_at = sent_width // 128 - 1
    parity = scalar(lax.rem(z_index, 2))
    normed, outgoing = pl.pallas_call(
        pick_kernel,
        grid=(PLANE,),
        out_shape=[shape((all_tokens, width), bf16), shape((PLANE, picked, width), bf16)],
        in_specs=[
            SMEM,
            pl.BlockSpec((Z_SIZE, all_tokens, part), lambda i: (0, 0, 0)),
            pl.BlockSpec((1, width), lambda i: (0, 0)),
            pl.BlockSpec((all_tokens, 128), lambda i: (0, info_at)),
        ],
        out_specs=[
            pl.BlockSpec((all_tokens, width), lambda i: (0, 0)),
            pl.BlockSpec((1, picked, width), lambda i: (i, 0, 0)),
        ],
        scratch_shapes=[pltpu.VMEM((8, all_tokens), jnp.int32)],
        compiler_params=params(),
        cost_estimate=cost(2 * PLANE * picked * all_tokens * width, 4 * MIB),
        name="pick",
    )(parity, mixed, norm_gain.reshape(1, width), gathered)

    outgoing, in_plane, gate_up = lax.optimization_barrier((outgoing, in_plane, gate_up))
    along_z = pl.pallas_call(
        regroup_kernel,
        out_shape=[shape((PLANE,) + in_plane[0].shape[1:], bf16)] * Z_SIZE,
        in_specs=[SMEM] + [VMEM] * PLANE,
        out_specs=[VMEM] * Z_SIZE,
        compiler_params=params(),
        cost_estimate=cost(0, 2 * MIB),
        name="regroup",
    )(scalar(z_index), *in_plane)
    arrived_cache = []
    for step in range(Z_SIZE):
        piece = along_z[step]
        if step:
            pairs = [
                (z * PLANE + p, (z + step) % Z_SIZE * PLANE + p)
                for z in range(Z_SIZE)
                for p in range(PLANE)
            ]
            piece = lax.ppermute(piece, "seq", pairs)
        arrived_cache.append(piece)
    arrived = exchange(outgoing, planes)
    returning = pl.pallas_call(
        experts_kernel,
        grid=(local_halves // 2,),
        out_shape=shape((PLANE, picked, width), bf16),
        in_specs=[
            pl.BlockSpec((PLANE, 2 * per_half, width), lambda i: (0, i, 0)),
            pl.BlockSpec((2, 2, width, half_ff), lambda i: (i, 0, 0, 0)),
            pl.BlockSpec((2, half_ff, width), lambda i: (i, 0, 0)),
        ],
        out_specs=pl.BlockSpec((PLANE, 2 * per_half, width), lambda i: (0, i, 0)),
        compiler_params=params(),
        cost_estimate=cost(6 * PLANE * picked * half_ff * width, 14 * MIB),
        name="experts",
    )(arrived, gate_up, expert_down)
    returning, arrived_cache = lax.optimization_barrier((returning, arrived_cache))
    arrived_cache = jnp.concatenate(arrived_cache)
    cache_out = pl.pallas_call(
        reorder_kernel,
        out_shape=shape(arrived_cache.shape, bf16),
        in_specs=[SMEM, SMEM, VMEM],
        out_specs=VMEM,
        compiler_params=params(),
        cost_estimate=cost(0, 2 * arrived_cache.size * 2),
        name="reorder",
    )(scalar(me), block_table, arrived_cache)
    cache_out = cache_out.reshape(devices, per_device, layers, kv_heads, head_size)

    shared_part, mix = pl.pallas_call(
        shared_kernel,
        grid=(1,),
        out_shape=[shape((all_tokens, width), f32), shape((all_tokens, PLANE * picked), bf16)],
        in_specs=[
            SMEM,
            pl.BlockSpec((all_tokens, 128), lambda i: (0, info_at)),
            pl.BlockSpec((all_tokens, width), lambda i: (0, 0)),
            pl.BlockSpec(shared_weight.shape, lambda i: (0, 0, 0)),
        ],
        out_specs=[
            pl.BlockSpec((all_tokens, width), lambda i: (0, 0)),
            pl.BlockSpec((all_tokens, PLANE * picked), lambda i: (0, 0)),
        ],
        compiler_params=params(),
        cost_estimate=cost(6 * all_tokens * 256 * width, 5 * MIB),
        name="shared_expert",
    )(parity, gathered, normed, shared_weight)

    returned = exchange(returning, planes).reshape(PLANE * picked, width)

    column_steps = 2
    part_width = width // column_steps
    parts = pl.pallas_call(
        combine_kernel,
        grid=(column_steps,),
        out_shape=shape((all_tokens, width), bf16),
        in_specs=[
            pl.BlockSpec((all_tokens, PLANE * picked), lambda i: (0, 0)),
            pl.BlockSpec((PLANE * picked, part_width), lambda i: (0, i)),
            pl.BlockSpec((all_tokens, part_width), lambda i: (0, i)),
        ],
        out_specs=pl.BlockSpec((all_tokens, part_width), lambda i: (0, i)),
        compiler_params=params(),
        cost_estimate=cost(2 * all_tokens * PLANE * picked * width, 5 * MIB),
        name="combine",
    )(mix, returned, shared_part)
    parts = exchange(parts.reshape(Z_SIZE, tokens, width), z_groups)
    layer_out = pl.pallas_call(
        final_kernel,
        out_shape=shape((tokens, width), bf16),
        in_specs=[SMEM] + [VMEM] * 2,
        out_specs=VMEM,
        compiler_params=params(),
        cost_estimate=cost(5 * tokens * width, 2 * MIB),
        name="final",
    )(scalar(z_index), mixed, parts)
    return (layer_out, cache_out)


def solution(mesh):
    in_specs = (
        P("seq", "head"),
        P("seq", "head"),
        P("seq", "head"),
        P(),
        P("head", "seq"),
        P(("seq", "head"), None),
        P(),
        P(("seq", "head"), None),
        P(("seq", "head"), None),
        P(None, None, ("seq", "head")),
        P(("seq", "head"), None),
        P("seq", None, None, None),
        P("seq", None, None),
        P("seq", None, None, "head", None),
        P(),
    )
    out_specs = (P(("seq", "head"), None), P(None, "seq", None, "head", None))
    planes_fit = mesh.shape["seq"] == Z_SIZE * PLANE and mesh.shape["head"] == 1
    body = shards if planes_fit else general_shards
    return jax.shard_map(body, mesh=mesh, in_specs=in_specs, out_specs=out_specs, check_vma=False)
```

```python
import math

import jax
import jax.numpy as jnp
from jax import lax
from jax.experimental import pallas as pl
from jax.experimental.pallas import tpu as pltpu
from jax.sharding import PartitionSpec as P

HD = 128
EXPERTS = 64
TOP = 6
REACH = 4
HALVES = 128
CAP = 6
Z_SIZE = 4
PLANE = 8
MIB = 1024 * 1024


NEGATIVE = -1e30
EPSILON = 1e-05


def from_behind(shard, axis, by):
    devices = lax.axis_size(axis)
    pairs = [(i, i + by) for i in range(devices) if 0 <= i + by < devices]
    return lax.ppermute(shard, axis, pairs)


def segment_of(positions, lengths):
    request_ends = jnp.cumsum(lengths)
    passed = (request_ends[None, :] <= positions[:, None]).astype(jnp.int32)
    return jnp.sum(passed, axis=1)


def shared_ffn(rows_in, gate_up_part, down_part):
    shared_both = jnp.einsum(
        "td,dcf->tcf", rows_in, gate_up_part, preferred_element_type=jnp.float32
    )
    shared_act = (jax.nn.silu(shared_both[:, 0]) * shared_both[:, 1]).astype(jnp.bfloat16)
    return jnp.dot(shared_act, down_part, preferred_element_type=jnp.float32)


def general_shards(
    queries,
    key_vectors,
    value_vectors,
    lengths,
    out_weight,
    residual,
    norm_gain,
    route_ids,
    route_logits,
    shared_gate_up,
    shared_down,
    expert_gate_up,
    expert_down,
    cache_blocks,
    block_table,
):
    handed = lax.all_to_all(cache_blocks, "seq", split_axis=1, concat_axis=0, tiled=True)
    cache_out = jnp.take(handed, block_table, axis=0)
    tok_rows = queries.shape[0]
    seq_index = lax.axis_index("seq")
    earlier = [
        from_behind((key_vectors, value_vectors), "seq", offset) for offset in range(REACH, 0, -1)
    ]
    window_keys = jnp.concatenate([member[0] for member in earlier] + [key_vectors], axis=0)
    window_values = jnp.concatenate([member[1] for member in earlier] + [value_vectors], axis=0)
    key_count = window_keys.shape[0]
    kv_heads = key_vectors.shape[1] // HD
    query_heads = queries.shape[1] // HD
    group_size = query_heads // kv_heads
    query_pos = seq_index * tok_rows + jnp.arange(tok_rows, dtype=jnp.int32)
    key_pos = (seq_index - REACH) * tok_rows + jnp.arange(key_count, dtype=jnp.int32)
    visible = (key_pos[None, :] >= 0) & (key_pos[None, :] <= query_pos[:, None])
    visible = visible & (
        segment_of(key_pos, lengths)[None, :] == segment_of(query_pos, lengths)[:, None]
    )
    query_part = queries.reshape(tok_rows, kv_heads, group_size, HD)
    key_part = window_keys.reshape(key_count, kv_heads, HD)
    value_part = window_values.reshape(key_count, kv_heads, HD)
    scores = jnp.einsum(
        "tkgd,wkd->kgtw", query_part, key_part, preferred_element_type=jnp.float32
    ) * (1.0 / math.sqrt(HD))
    scores = jnp.where(visible[None, None], scores, NEGATIVE)
    row_max = jnp.max(scores, axis=-1, keepdims=True)
    weights = jnp.exp(scores - row_max)
    row_total = jnp.sum(weights, axis=-1)
    weighted = jnp.einsum(
        "kgtw,wkd->tkgd",
        weights.astype(jnp.bfloat16),
        value_part,
        preferred_element_type=jnp.float32,
    )
    heads = (weighted / jnp.transpose(row_total, (2, 0, 1))[..., None]).astype(jnp.bfloat16)
    heads = heads.reshape(tok_rows, query_heads * HD)
    partial_out = jnp.dot(
        heads,
        lax.all_gather(out_weight, "seq", axis=1, tiled=True),
        preferred_element_type=jnp.float32,
    )
    attn_out = lax.psum_scatter(partial_out, "head", scatter_dimension=0, tiled=True)
    mixed = residual.astype(jnp.float32) + attn_out
    mean_square = jnp.mean(mixed * mixed, axis=-1, keepdims=True)
    normed = (mixed * lax.rsqrt(mean_square + EPSILON) * norm_gain).astype(jnp.bfloat16)
    gate_up_all, down_all = (
        lax.all_gather(shared_gate_up, ("seq", "head"), axis=2, tiled=True),
        lax.all_gather(shared_down, ("seq", "head"), axis=0, tiled=True),
    )
    shared_part = shared_ffn(normed, gate_up_all, down_all)
    own_tokens = normed.shape[0]
    width_model = normed.shape[1]
    flat_ids = route_ids.reshape(-1)
    onehot = (flat_ids[:, None] == jnp.arange(EXPERTS, dtype=jnp.int32)[None, :]).astype(jnp.int32)
    slot_rank = jnp.sum((jnp.cumsum(onehot, axis=0) - 1) * onehot, axis=1)
    first_slot = flat_ids * CAP + slot_rank
    second_slot = (flat_ids + EXPERTS) * CAP + slot_rank
    token_of = jnp.arange(flat_ids.shape[0], dtype=jnp.int32) // TOP
    routed_rows = normed[token_of]
    outgoing = jnp.zeros((HALVES * CAP, width_model), jnp.bfloat16)
    outgoing = outgoing.at[jnp.concatenate([first_slot, second_slot])].set(
        jnp.concatenate([routed_rows, routed_rows], axis=0)
    )
    local_halves = expert_gate_up.shape[0]
    outgoing = outgoing.reshape(HALVES // local_halves, local_halves, CAP, width_model)
    gate_up = jnp.einsum(
        "nsjd,sdcf->nsjcf",
        lax.all_to_all(outgoing, "seq", split_axis=0, concat_axis=0, tiled=True),
        expert_gate_up,
        preferred_element_type=jnp.float32,
    )
    expert_act = (jax.nn.silu(gate_up[:, :, :, 0]) * gate_up[:, :, :, 1]).astype(jnp.bfloat16)
    half_out = jnp.einsum(
        "nsjf,sfd->nsjd", expert_act, expert_down, preferred_element_type=jnp.float32
    ).astype(jnp.bfloat16)
    returned = lax.all_to_all(half_out, "seq", split_axis=0, concat_axis=0, tiled=True)
    returned = returned.reshape(HALVES * CAP, width_model)
    pair_sum = returned[first_slot].astype(jnp.float32) + returned[second_slot].astype(jnp.float32)
    route_probs = jax.nn.softmax(route_logits, axis=-1)
    routed = jnp.sum(
        route_probs[:, :, None] * pair_sum.reshape(own_tokens, TOP, width_model), axis=1
    )
    layer_out = (mixed + shared_part + routed).astype(jnp.bfloat16)
    return (layer_out, cache_out)


VMEM = pl.BlockSpec(memory_space=pltpu.VMEM)
SMEM = pl.BlockSpec(memory_space=pltpu.SMEM)
ANY = pl.BlockSpec(memory_space=pl.ANY)


def dot_rows(left, right):
    return lax.dot_general(left, right, (((1,), (1,)), ((), ())), preferred_element_type=jnp.float32)


def dot(left, right):
    return jnp.dot(left, right, preferred_element_type=jnp.float32)


def silu_times(gate, up):
    return (gate / (1.0 + jnp.exp(-gate)) * up).astype(jnp.bfloat16)


def attention_kernel(
    first_ref, lengths_ref, q_ref, k4_ref, k3_ref, k2_ref, k1_ref, own_ref, info_ref, out_ref
):
    tokens, width = q_ref.shape
    kv_width = own_ref.shape[1] // 2
    kv_heads = kv_width // HD
    group = width // HD // kv_heads
    blocks = [k4_ref, k3_ref, k2_ref, k1_ref, own_ref]
    keys = len(blocks) * tokens
    first = first_ref[0]
    query_pos = first + lax.broadcasted_iota(jnp.int32, (tokens, keys), 0)
    key_pos = first - (keys - tokens) + lax.broadcasted_iota(jnp.int32, (tokens, keys), 1)
    start = jnp.zeros((tokens, keys), jnp.int32)
    end = jnp.int32(0)
    for request in range(lengths_ref.shape[0]):
        end = end + lengths_ref[request]
        start = jnp.maximum(start, jnp.where(query_pos >= end, end, 0))
    hidden = jnp.where((key_pos >= start) & (key_pos <= query_pos), 0.0, NEGATIVE)
    hidden = jnp.concatenate([hidden] * group, axis=0)
    scale = 1.0 / math.sqrt(HD)
    out_ref[:, width:] = info_ref[...]
    for kv in range(kv_heads):
        at = slice(kv * HD, (kv + 1) * HD)
        value_at = slice(kv_width + kv * HD, kv_width + (kv + 1) * HD)
        key = jnp.concatenate([block[:, at] for block in blocks], axis=0)
        value = jnp.concatenate([block[:, value_at] for block in blocks], axis=0)
        heads = [kv * group + member for member in range(group)]
        query = jnp.concatenate([q_ref[:, h * HD : (h + 1) * HD] for h in heads], axis=0)
        scores = dot_rows(query, key) * scale + hidden
        weights = jnp.exp(scores - jnp.max(scores, axis=-1, keepdims=True))
        total = jnp.sum(weights, axis=-1, keepdims=True)
        result = (dot(weights.astype(jnp.bfloat16), value) / total).astype(jnp.bfloat16)
        for member, h in enumerate(heads):
            out_ref[:, h * HD : (h + 1) * HD] = result[member * tokens : (member + 1) * tokens]


def route_kernel(z_ref, ids_ref, logits_ref, out_ref, turned_ref):
    choices, tokens = ids_ref.shape
    turned_ref[...] = jnp.zeros(turned_ref.shape, jnp.float32)
    turned_ref[:choices, :tokens] = ids_ref[...].astype(jnp.float32)
    turned_ref[8 : 8 + choices, :tokens] = logits_ref[...]
    table = turned_ref[...].T[:tokens]
    lane = lax.broadcasted_iota(jnp.int32, table.shape, 1)
    ids = [table[:, c : c + 1].astype(jnp.int32) for c in range(choices)]
    logits = [table[:, 8 + c : 9 + c] for c in range(choices)]
    member = jnp.zeros(table.shape, jnp.float32)
    for one in ids:
        member = jnp.where(lane == one, 1.0, member)
    row = lax.broadcasted_iota(jnp.int32, (tokens, tokens), 0)
    earlier = jnp.where(lax.broadcasted_iota(jnp.int32, (tokens, tokens), 1) < row, 1.0, 0.0)
    ahead = dot(earlier.astype(jnp.bfloat16), member.astype(jnp.bfloat16))
    top = logits[0]
    for one in logits[1:]:
        top = jnp.maximum(top, one)
    powers = [jnp.exp(one - top) for one in logits]
    total = sum(powers[1:], powers[0])
    per_device = EXPERTS // 2 // PLANE
    out = jnp.zeros(table.shape, jnp.float32)
    for c, one in enumerate(ids):
        rank = jnp.sum(jnp.where(lane == one, ahead, 0.0), axis=1, keepdims=True)
        where_to = lax.div(one, per_device).astype(jnp.float32)
        first = (lax.rem(one, per_device) * Z_SIZE + z_ref[0]) * CAP
        out = jnp.where(lane == c, where_to, out)
        out = jnp.where(lane == 8 + c, first.astype(jnp.float32) + rank, out)
        out = jnp.where(lane == 16 + c, powers[c] / total, out)
    out_ref[...] = out.astype(jnp.bfloat16)


def regroup_kernel(z_ref, *refs):
    pieces, outs = refs[:PLANE], refs[PLANE:]
    for step, out in enumerate(outs):
        z = lax.rem(z_ref[0] + step, Z_SIZE)
        for at, piece in enumerate(pieces):
            out[at] = piece[z]


def source_z(z_ref, step):
    return lax.rem(z_ref[0] + Z_SIZE - step, Z_SIZE)


def project_kernel(z_ref, *refs):
    sent = refs[:Z_SIZE]
    residual_ref, weight_ref, first_ref, second_ref, info_ref, heads_ref = refs[Z_SIZE:]
    width = heads_ref.shape[2]
    for step, sent_ref in enumerate(sent):
        z = source_z(z_ref, step)
        heads_ref[z] = sent_ref[:, :width]
        info_ref[z] = sent_ref[:, width:]
    heads = jnp.concatenate([heads_ref[z] for z in range(Z_SIZE)], axis=0)
    residual = jnp.concatenate([residual_ref[z] for z in range(Z_SIZE)], axis=0)
    cut = first_ref.shape[1]
    for at, out_ref in ((slice(0, cut), first_ref), (slice(cut, None), second_ref)):
        out = dot_rows(heads, weight_ref[at]) + residual[:, at].astype(jnp.float32)
        out_ref[...] = out.astype(jnp.bfloat16)


def row_codes(info, first, parity, per_device):
    where_to = info(first).astype(jnp.int32) - PLANE * parity
    inside = info(first + 8).astype(jnp.int32)
    fits = (where_to >= 0) & (where_to < PLANE)
    return jnp.where(fits, where_to * per_device + inside, -1)


def tables_kernel(parity_ref, info_ref, onehot_ref, mix_ref):
    rows, tokens = onehot_ref.shape
    info = info_ref[...].astype(jnp.float32)
    turned = info.T
    codes = row_codes(lambda at: turned[at : at + 8], 0, parity_ref[0], rows // PLANE)
    row = lax.broadcasted_iota(jnp.int32, (rows, tokens), 0)
    chosen = codes[0:1, :] == row
    for choice in range(1, TOP):
        chosen = chosen | (codes[choice : choice + 1, :] == row)
    onehot_ref[...] = jnp.where(chosen, 1.0, 0.0).astype(jnp.bfloat16)
    column = lax.broadcasted_iota(jnp.int32, mix_ref.shape, 1)
    mix = jnp.zeros(mix_ref.shape, jnp.float32)
    for choice in range(TOP):
        code = row_codes(lambda at: info[:, at : at + 1], choice, parity_ref[0], rows // PLANE)
        mix = jnp.where(code == column, info[:, 16 + choice : 17 + choice], mix)
    mix_ref[...] = mix.astype(jnp.bfloat16)


def pick_kernel(z_ref, onehot_ref, *refs):
    parts, out_ref, turned_ref = refs[:Z_SIZE], refs[Z_SIZE], refs[Z_SIZE + 1]
    for step, part_ref in enumerate(parts):
        turned_ref[source_z(z_ref, step)] = part_ref[...]
    rows = jnp.concatenate([turned_ref[z] for z in range(Z_SIZE)], axis=1)
    picked = out_ref.shape[1]
    for p in range(PLANE):
        onehot = onehot_ref[p * picked : (p + 1) * picked]
        out_ref[p] = dot(onehot, rows).astype(jnp.bfloat16)


def shared_kernel(z_ref, gain_ref, weight_ref, *refs):
    firsts, seconds = refs[:Z_SIZE], refs[Z_SIZE : 2 * Z_SIZE]
    out_ref, own_ref, mixed_ref = refs[2 * Z_SIZE :]
    cut = firsts[0].shape[1]
    for step in range(Z_SIZE):
        z = source_z(z_ref, step)
        mixed_ref[z, :, :cut] = firsts[step][...]
        mixed_ref[z, :, cut:] = seconds[step][...]
    tokens = own_ref.shape[0]
    own = pl.ds(pl.multiple_of(z_ref[0] * tokens, tokens), tokens)
    columns = mixed_ref.shape[2]
    for z in range(Z_SIZE):
        own_ref[:, z * columns : (z + 1) * columns] = mixed_ref[z, own, :].astype(jnp.float32)
    mixed = jnp.concatenate([mixed_ref[z] for z in range(Z_SIZE)], axis=1)
    normed = norm(mixed.astype(jnp.float32), gain_ref[...])
    parts, units, _ = weight_ref.shape
    units = units // 3
    gate_weight, up_weight, down_weight = [
        jnp.concatenate([weight_ref[p, at * units : (at + 1) * units] for p in range(parts)], axis=0)
        for at in range(3)
    ]
    act = silu_times(dot_rows(normed, gate_weight), dot_rows(normed, up_weight))
    out_ref[...] = dot(act, down_weight)


def norm(mixed, gain):
    mean_square = jnp.mean(mixed * mixed, axis=-1, keepdims=True)
    return (mixed * lax.rsqrt(mean_square + EPSILON) * gain).astype(jnp.bfloat16)


def experts_kernel(
    first_ref, second_ref, gain_ref, gate_up_hbm, down_hbm, out_ref, act_ref, gate_up_ref, down_ref, sems
):
    halves = gate_up_ref.shape[0]
    columns = out_ref.shape[2]
    fetches = []
    for half in range(halves):
        gate_up = pltpu.make_async_copy(gate_up_hbm.at[half], gate_up_ref.at[half], sems.at[0, half])
        down = pltpu.make_async_copy(
            down_hbm.at[half, :, pl.ds(0, columns)], down_ref.at[half], sems.at[1, half]
        )
        gate_up.start()
        down.start()
        fetches.append((gate_up, down))
    sources, rows, _ = first_ref.shape
    per_half = rows // halves
    cuts = [ref.shape[2] // Z_SIZE for ref in (first_ref, second_ref)]
    for pair in range(halves // 2):
        both = slice(2 * pair * per_half, 2 * (pair + 1) * per_half)
        parts = [ref[:, both, :].astype(jnp.float32) for ref in (first_ref, second_ref)]
        results = []
        for member in range(2):
            half = 2 * pair + member
            at = slice(member * per_half, (member + 1) * per_half)
            own = [p[:, at].reshape(sources * per_half, p.shape[2]) for p in parts]
            pieces = []
            for z in range(Z_SIZE):
                for cut, part in zip(cuts, own):
                    pieces.append(part[:, z * cut : (z + 1) * cut])
            normed = norm(jnp.concatenate(pieces, axis=1), gain_ref[...])
            fetches[half][0].wait()
            act = silu_times(dot(normed, gate_up_ref[half, 0]), dot(normed, gate_up_ref[half, 1]))
            act_ref[half] = act
            fetches[half][1].wait()
            results.append(dot(act, down_ref[half]).reshape(sources, per_half, columns))
        out_ref[:, both, :] = jnp.concatenate(results, axis=1).astype(jnp.bfloat16)


def rest_kernel(act_ref, down_ref, out_ref):
    halves = act_ref.shape[0]
    sources, rows, columns = out_ref.shape
    per_half = rows // halves
    for pair in range(halves // 2):
        both = slice(2 * pair * per_half, 2 * (pair + 1) * per_half)
        results = []
        for half in (2 * pair, 2 * pair + 1):
            results.append(dot(act_ref[half], down_ref[half]).reshape(sources, per_half, columns))
        out_ref[:, both, :] = jnp.concatenate(results, axis=1).astype(jnp.bfloat16)


def combine_kernel(z_ref, mix_ref, rows_ref, shared_ref, *refs):
    outs, sum_ref = refs[:Z_SIZE], refs[Z_SIZE]
    tokens = outs[0].shape[0]
    sum_ref[...] = dot(mix_ref[...], rows_ref[...]) + shared_ref[...]
    for step, out_ref in enumerate(outs):
        z = lax.rem(z_ref[0] + step, Z_SIZE)
        rows = pl.ds(pl.multiple_of(z * tokens, tokens), tokens)
        out_ref[...] = sum_ref[rows, :].astype(jnp.bfloat16)


def final_kernel(mixed_ref, *refs):
    firsts, seconds, out_ref = refs[:Z_SIZE], refs[Z_SIZE : 2 * Z_SIZE], refs[2 * Z_SIZE]
    cut = firsts[0].shape[1]
    for at, parts in ((slice(0, cut), firsts), (slice(cut, None), seconds)):
        total = mixed_ref[:, at]
        for part_ref in parts:
            total = total + part_ref[...].astype(jnp.float32)
        out_ref[:, at] = total.astype(jnp.bfloat16)


def reorder_kernel(me_ref, table_ref, from_ref, to_ref):
    me = me_ref[0]
    for block in range(to_ref.shape[0]):
        source = table_ref[block]
        z_steps = lax.rem(lax.div(me, PLANE) - lax.div(source, PLANE) + Z_SIZE, Z_SIZE)
        steps = lax.rem(lax.rem(me, PLANE) - lax.rem(source, PLANE) + PLANE, PLANE)
        to_ref[block] = from_ref[z_steps * PLANE + steps]


def params():
    return pltpu.CompilerParams(vmem_limit_bytes=58 * MIB)


def cost(flops, moved):
    return pl.CostEstimate(flops=int(flops), bytes_accessed=int(moved), transcendentals=0)


def shards(
    queries,
    key_vectors,
    value_vectors,
    lengths,
    out_weight,
    residual,
    norm_gain,
    route_ids,
    route_logits,
    shared_gate_up,
    shared_down,
    expert_gate_up,
    expert_down,
    cache_blocks,
    block_table,
):
    tokens, width = residual.shape
    devices = lax.axis_size("seq")
    me = lax.axis_index("seq")
    z_index, plane_index = lax.div(me, PLANE), lax.rem(me, PLANE)
    z_groups = [[p + PLANE * z for z in range(Z_SIZE)] for p in range(PLANE)]
    planes = [[p + PLANE * z for p in range(PLANE)] for z in range(Z_SIZE)]
    bf16, f32 = jnp.bfloat16, jnp.float32
    shape = jax.ShapeDtypeStruct
    scalar = lambda value: jnp.reshape(value, (1,)).astype(jnp.int32)
    all_tokens = Z_SIZE * tokens
    part = width // Z_SIZE

    def exchange(array, groups):
        return lax.all_to_all(
            array, "seq", split_axis=0, concat_axis=0, tiled=True, axis_index_groups=groups
        )

    own_kv = jnp.concatenate([key_vectors, value_vectors], axis=1)
    behind = [from_behind(own_kv, "seq", offset) for offset in range(REACH, 0, -1)]

    turned_weight = lax.all_gather(
        out_weight.T, "seq", axis=0, tiled=True, axis_index_groups=planes
    )
    info = pl.pallas_call(
        route_kernel,
        out_shape=shape((tokens, 128), bf16),
        in_specs=[SMEM] + [VMEM] * 2,
        out_specs=VMEM,
        scratch_shapes=[pltpu.VMEM((128, 128), f32)],
        compiler_params=params(),
        cost_estimate=cost(MIB, MIB),
        name="route",
    )(scalar(z_index), route_ids.T, route_logits.T)

    def along_z(array):
        arrays = [array]
        for step in range(1, Z_SIZE):
            arrays.append(lax.ppermute(array, "seq", z_pairs[step]))
        return arrays

    z_pairs = [
        [
            (z * PLANE + p, (z + step) % Z_SIZE * PLANE + p)
            for z in range(Z_SIZE)
            for p in range(PLANE)
        ]
        for step in range(Z_SIZE)
    ]
    z_scalar = scalar(z_index)
    gain = norm_gain.reshape(1, width)
    residual_parts = jnp.transpose(residual.reshape(tokens, Z_SIZE, part), (1, 0, 2))
    residual_parts = exchange(residual_parts, z_groups)

    sent_width = width + info.shape[1]
    sent = pl.pallas_call(
        attention_kernel,
        out_shape=shape((tokens, sent_width), bf16),
        in_specs=[SMEM, SMEM] + [VMEM] * 7,
        out_specs=VMEM,
        compiler_params=params(),
        cost_estimate=cost(4 * tokens * 5 * tokens * width, 3 * MIB),
        name="attention",
    )(scalar(me * tokens), lengths, queries, *behind, own_kv, info)

    gathered = along_z(sent)
    gathered[1], cache_blocks, shared_gate_up, shared_down, expert_gate_up = (
        lax.optimization_barrier(
            (gathered[1], cache_blocks, shared_gate_up, shared_down, expert_gate_up)
        )
    )

    own_shared = jnp.concatenate(
        [jnp.transpose(shared_gate_up, (1, 2, 0)).reshape(-1, width), shared_down], axis=0
    )
    shared_weight = lax.all_gather(own_shared, "seq", axis=0, axis_index_groups=planes)

    _, block_tokens, layers, kv_heads, head_size = cache_blocks.shape
    per_device = block_tokens // devices
    cache_view = cache_blocks.reshape(Z_SIZE, PLANE, per_device * layers, kv_heads, head_size)
    in_plane = []
    for step in range(PLANE):
        piece = lax.dynamic_index_in_dim(
            cache_view, lax.rem(plane_index + step, PLANE), axis=1, keepdims=False
        )
        if step:
            pairs = [
                (z * PLANE + p, z * PLANE + (p + step) % PLANE)
                for z in range(Z_SIZE)
                for p in range(PLANE)
            ]
            piece = lax.ppermute(piece, "seq", pairs)
        in_plane.append(piece)
    gate_up = jnp.transpose(expert_gate_up, (0, 2, 1, 3))

    first_part = part // 3
    second_part = part - first_part
    mixed_first, mixed_second, info = pl.pallas_call(
        project_kernel,
        out_shape=[
            shape((all_tokens, first_part), bf16),
            shape((all_tokens, second_part), bf16),
            shape((Z_SIZE, tokens, 128), bf16),
        ],
        in_specs=[SMEM] + [VMEM] * (Z_SIZE + 2),
        out_specs=[VMEM] * 3,
        scratch_shapes=[pltpu.VMEM((Z_SIZE, tokens, width), bf16)],
        compiler_params=params(),
        cost_estimate=cost(2 * all_tokens * width * part, 3 * MIB),
        name="project",
    )(z_scalar, *gathered, residual_parts, turned_weight)
    mixed_first = along_z(mixed_first)

    local_halves, _, _, half_ff = expert_gate_up.shape
    per_half = Z_SIZE * CAP
    picked = local_halves * per_half
    onehot, mix = pl.pallas_call(
        tables_kernel,
        out_shape=[
            shape((PLANE * picked, all_tokens), bf16),
            shape((all_tokens, PLANE * picked), bf16),
        ],
        in_specs=[SMEM, VMEM],
        out_specs=[VMEM] * 2,
        compiler_params=params(),
        cost_estimate=cost(20 * PLANE * picked * all_tokens, MIB),
        name="tables",
    )(scalar(lax.rem(z_index, 2)), info.reshape(all_tokens, 128))
    onehot, mixed_second = lax.optimization_barrier((onehot, mixed_second))
    mixed_second = along_z(mixed_second)

    def pick(parts):
        columns = parts[0].shape[1]
        return pl.pallas_call(
            pick_kernel,
            out_shape=shape((PLANE, picked, Z_SIZE * columns), bf16),
            in_specs=[SMEM] + [VMEM] * (1 + Z_SIZE),
            out_specs=VMEM,
            scratch_shapes=[pltpu.VMEM((Z_SIZE, all_tokens, columns), bf16)],
            compiler_params=params(),
            cost_estimate=cost(2 * PLANE * picked * all_tokens * columns * Z_SIZE, 3 * MIB),
            name="pick",
        )(z_scalar, onehot, *parts)

    arrived_first = exchange(pick(mixed_first), planes)
    outgoing = pick(mixed_second)

    outgoing, in_plane = lax.optimization_barrier((outgoing, in_plane))
    arrived_second = exchange(outgoing, planes)
    grouped = pl.pallas_call(
        regroup_kernel,
        out_shape=[shape((PLANE,) + in_plane[0].shape[1:], bf16)] * Z_SIZE,
        in_specs=[SMEM] + [VMEM] * PLANE,
        out_specs=[VMEM] * Z_SIZE,
        compiler_params=params(),
        cost_estimate=cost(0, 2 * MIB),
        name="regroup",
    )(z_scalar, *in_plane)
    arrived_cache = [grouped[0]]
    for step in range(1, Z_SIZE):
        arrived_cache.append(lax.ppermute(grouped[step], "seq", z_pairs[step]))

    arrived_second, shared_weight = lax.optimization_barrier((arrived_second, shared_weight))
    shared_part, own_mixed = pl.pallas_call(
        shared_kernel,
        out_shape=[shape((all_tokens, width), f32), shape((tokens, width), f32)],
        in_specs=[SMEM] + [VMEM] * (2 + 2 * Z_SIZE),
        out_specs=[VMEM] * 2,
        scratch_shapes=[pltpu.VMEM((Z_SIZE, all_tokens, part), bf16)],
        compiler_params=params(),
        cost_estimate=cost(6 * all_tokens * 256 * width, 5 * MIB),
        name="shared_expert",
    )(z_scalar, gain, shared_weight, *mixed_first, *mixed_second)

    first_width = 2 * width // 3
    second_width = width - first_width
    returning_first, act = pl.pallas_call(
        experts_kernel,
        out_shape=[
            shape((PLANE, picked, first_width), bf16),
            shape((local_halves, PLANE * per_half, half_ff), bf16),
        ],
        in_specs=[VMEM] * 3 + [ANY] * 2,
        out_specs=[VMEM] * 2,
        scratch_shapes=[
            pltpu.VMEM((local_halves, 2, width, half_ff), bf16),
            pltpu.VMEM((local_halves, half_ff, first_width), bf16),
            pltpu.SemaphoreType.DMA((2, local_halves)),
        ],
        compiler_params=params(),
        cost_estimate=cost(5 * PLANE * picked * half_ff * width, 13 * MIB),
        name="experts",
    )(arrived_first, arrived_second, gain, gate_up, expert_down)
    returning_first, arrived_cache = lax.optimization_barrier((returning_first, arrived_cache))
    returned_first = exchange(returning_first, planes).reshape(PLANE * picked, first_width)
    returning_second = pl.pallas_call(
        rest_kernel,
        grid=(1,),
        out_shape=shape((PLANE, picked, second_width), bf16),
        in_specs=[
            pl.BlockSpec(act.shape, lambda i: (0, 0, 0)),
            pl.BlockSpec(
                (local_halves, half_ff, second_width), lambda i: (0, 0, first_width // second_width)
            ),
        ],
        out_specs=pl.BlockSpec((PLANE, picked, second_width), lambda i: (0, 0, 0)),
        compiler_params=params(),
        cost_estimate=cost(PLANE * picked * half_ff * width, 2 * MIB),
        name="rest",
    )(act, expert_down)
    returned_second = exchange(returning_second, planes).reshape(PLANE * picked, second_width)

    arrived_cache = jnp.concatenate(arrived_cache)
    cache_out = pl.pallas_call(
        reorder_kernel,
        out_shape=shape(arrived_cache.shape, bf16),
        in_specs=[SMEM, SMEM, VMEM],
        out_specs=VMEM,
        compiler_params=params(),
        cost_estimate=cost(0, 2 * arrived_cache.size * 2),
        name="reorder",
    )(scalar(me), block_table, arrived_cache)
    cache_out = cache_out.reshape(devices, per_device, layers, kv_heads, head_size)

    def combine(returned, at):
        columns = returned.shape[1]
        block = at // columns
        sums = pl.pallas_call(
            combine_kernel,
            grid=(1,),
            out_shape=[shape((tokens, columns), bf16)] * Z_SIZE,
            in_specs=[
                SMEM,
                pl.BlockSpec(mix.shape, lambda i: (0, 0)),
                pl.BlockSpec(returned.shape, lambda i: (0, 0)),
                pl.BlockSpec((all_tokens, columns), lambda i: (0, block)),
            ],
            out_specs=[pl.BlockSpec((tokens, columns), lambda i: (0, 0))] * Z_SIZE,
            scratch_shapes=[pltpu.VMEM((all_tokens, columns), f32)],
            compiler_params=params(),
            cost_estimate=cost(2 * all_tokens * PLANE * picked * columns, 3 * MIB),
            name="combine",
        )(z_scalar, mix, returned, shared_part)
        arrivals = [lax.ppermute(sums[step], "seq", z_pairs[step]) for step in range(1, Z_SIZE)]
        return [sums[0]] + arrivals

    sums = combine(returned_first, 0) + combine(returned_second, first_width)
    layer_out = pl.pallas_call(
        final_kernel,
        out_shape=shape((tokens, width), bf16),
        in_specs=[VMEM] * (1 + 2 * Z_SIZE),
        out_specs=VMEM,
        compiler_params=params(),
        cost_estimate=cost(5 * tokens * width, 2 * MIB),
        name="final",
    )(own_mixed, *sums)
    return (layer_out, cache_out)


def solution(mesh):
    in_specs = (
        P("seq", "head"),
        P("seq", "head"),
        P("seq", "head"),
        P(),
        P("head", "seq"),
        P(("seq", "head"), None),
        P(),
        P(("seq", "head"), None),
        P(("seq", "head"), None),
        P(None, None, ("seq", "head")),
        P(("seq", "head"), None),
        P("seq", None, None, None),
        P("seq", None, None),
        P("seq", None, None, "head", None),
        P(),
    )
    out_specs = (P(("seq", "head"), None), P(None, "seq", None, "head", None))
    planes_fit = mesh.shape["seq"] == Z_SIZE * PLANE and mesh.shape["head"] == 1
    body = shards if planes_fit else general_shards
    return jax.shard_map(body, mesh=mesh, in_specs=in_specs, out_specs=out_specs, check_vma=False)
```

```python
import math

import jax
import jax.numpy as jnp
from jax import lax
from jax.experimental import pallas as pl
from jax.experimental.pallas import tpu as pltpu
from jax.sharding import PartitionSpec as P

HD = 128
EXPERTS = 64
TOP = 6
REACH = 4
HALVES = 128
CAP = 6
Z_SIZE = 4
PLANE = 8
MIB = 1024 * 1024


NEGATIVE = -1e30
EPSILON = 1e-05


def from_behind(shard, axis, by):
    devices = lax.axis_size(axis)
    pairs = [(i, i + by) for i in range(devices) if 0 <= i + by < devices]
    return lax.ppermute(shard, axis, pairs)


def segment_of(positions, lengths):
    request_ends = jnp.cumsum(lengths)
    passed = (request_ends[None, :] <= positions[:, None]).astype(jnp.int32)
    return jnp.sum(passed, axis=1)


def shared_ffn(rows_in, gate_up_part, down_part):
    shared_both = jnp.einsum(
        "td,dcf->tcf", rows_in, gate_up_part, preferred_element_type=jnp.float32
    )
    shared_act = (jax.nn.silu(shared_both[:, 0]) * shared_both[:, 1]).astype(jnp.bfloat16)
    return jnp.dot(shared_act, down_part, preferred_element_type=jnp.float32)


def general_shards(
    queries,
    key_vectors,
    value_vectors,
    lengths,
    out_weight,
    residual,
    norm_gain,
    route_ids,
    route_logits,
    shared_gate_up,
    shared_down,
    expert_gate_up,
    expert_down,
    cache_blocks,
    block_table,
):
    handed = lax.all_to_all(cache_blocks, "seq", split_axis=1, concat_axis=0, tiled=True)
    cache_out = jnp.take(handed, block_table, axis=0)
    tok_rows = queries.shape[0]
    seq_index = lax.axis_index("seq")
    earlier = [
        from_behind((key_vectors, value_vectors), "seq", offset) for offset in range(REACH, 0, -1)
    ]
    window_keys = jnp.concatenate([member[0] for member in earlier] + [key_vectors], axis=0)
    window_values = jnp.concatenate([member[1] for member in earlier] + [value_vectors], axis=0)
    key_count = window_keys.shape[0]
    kv_heads = key_vectors.shape[1] // HD
    query_heads = queries.shape[1] // HD
    group_size = query_heads // kv_heads
    query_pos = seq_index * tok_rows + jnp.arange(tok_rows, dtype=jnp.int32)
    key_pos = (seq_index - REACH) * tok_rows + jnp.arange(key_count, dtype=jnp.int32)
    visible = (key_pos[None, :] >= 0) & (key_pos[None, :] <= query_pos[:, None])
    visible = visible & (
        segment_of(key_pos, lengths)[None, :] == segment_of(query_pos, lengths)[:, None]
    )
    query_part = queries.reshape(tok_rows, kv_heads, group_size, HD)
    key_part = window_keys.reshape(key_count, kv_heads, HD)
    value_part = window_values.reshape(key_count, kv_heads, HD)
    scores = jnp.einsum(
        "tkgd,wkd->kgtw", query_part, key_part, preferred_element_type=jnp.float32
    ) * (1.0 / math.sqrt(HD))
    scores = jnp.where(visible[None, None], scores, NEGATIVE)
    row_max = jnp.max(scores, axis=-1, keepdims=True)
    weights = jnp.exp(scores - row_max)
    row_total = jnp.sum(weights, axis=-1)
    weighted = jnp.einsum(
        "kgtw,wkd->tkgd",
        weights.astype(jnp.bfloat16),
        value_part,
        preferred_element_type=jnp.float32,
    )
    heads = (weighted / jnp.transpose(row_total, (2, 0, 1))[..., None]).astype(jnp.bfloat16)
    heads = heads.reshape(tok_rows, query_heads * HD)
    partial_out = jnp.dot(
        heads,
        lax.all_gather(out_weight, "seq", axis=1, tiled=True),
        preferred_element_type=jnp.float32,
    )
    attn_out = lax.psum_scatter(partial_out, "head", scatter_dimension=0, tiled=True)
    mixed = residual.astype(jnp.float32) + attn_out
    mean_square = jnp.mean(mixed * mixed, axis=-1, keepdims=True)
    normed = (mixed * lax.rsqrt(mean_square + EPSILON) * norm_gain).astype(jnp.bfloat16)
    gate_up_all, down_all = (
        lax.all_gather(shared_gate_up, ("seq", "head"), axis=2, tiled=True),
        lax.all_gather(shared_down, ("seq", "head"), axis=0, tiled=True),
    )
    shared_part = shared_ffn(normed, gate_up_all, down_all)
    own_tokens = normed.shape[0]
    width_model = normed.shape[1]
    flat_ids = route_ids.reshape(-1)
    onehot = (flat_ids[:, None] == jnp.arange(EXPERTS, dtype=jnp.int32)[None, :]).astype(jnp.int32)
    slot_rank = jnp.sum((jnp.cumsum(onehot, axis=0) - 1) * onehot, axis=1)
    first_slot = flat_ids * CAP + slot_rank
    second_slot = (flat_ids + EXPERTS) * CAP + slot_rank
    token_of = jnp.arange(flat_ids.shape[0], dtype=jnp.int32) // TOP
    routed_rows = normed[token_of]
    outgoing = jnp.zeros((HALVES * CAP, width_model), jnp.bfloat16)
    outgoing = outgoing.at[jnp.concatenate([first_slot, second_slot])].set(
        jnp.concatenate([routed_rows, routed_rows], axis=0)
    )
    local_halves = expert_gate_up.shape[0]
    outgoing = outgoing.reshape(HALVES // local_halves, local_halves, CAP, width_model)
    gate_up = jnp.einsum(
        "nsjd,sdcf->nsjcf",
        lax.all_to_all(outgoing, "seq", split_axis=0, concat_axis=0, tiled=True),
        expert_gate_up,
        preferred_element_type=jnp.float32,
    )
    expert_act = (jax.nn.silu(gate_up[:, :, :, 0]) * gate_up[:, :, :, 1]).astype(jnp.bfloat16)
    half_out = jnp.einsum(
        "nsjf,sfd->nsjd", expert_act, expert_down, preferred_element_type=jnp.float32
    ).astype(jnp.bfloat16)
    returned = lax.all_to_all(half_out, "seq", split_axis=0, concat_axis=0, tiled=True)
    returned = returned.reshape(HALVES * CAP, width_model)
    pair_sum = returned[first_slot].astype(jnp.float32) + returned[second_slot].astype(jnp.float32)
    route_probs = jax.nn.softmax(route_logits, axis=-1)
    routed = jnp.sum(
        route_probs[:, :, None] * pair_sum.reshape(own_tokens, TOP, width_model), axis=1
    )
    layer_out = (mixed + shared_part + routed).astype(jnp.bfloat16)
    return (layer_out, cache_out)


VMEM = pl.BlockSpec(memory_space=pltpu.VMEM)
SMEM = pl.BlockSpec(memory_space=pltpu.SMEM)
HBM = pl.BlockSpec(memory_space=pltpu.HBM)


def dot_rows(left, right):
    return lax.dot_general(left, right, (((1,), (1,)), ((), ())), preferred_element_type=jnp.float32)


def dot(left, right):
    return jnp.dot(left, right, preferred_element_type=jnp.float32)


def silu_times(gate, up):
    return (gate / (1.0 + jnp.exp(-gate)) * up).astype(jnp.bfloat16)


def attention_kernel(
    z_ref,
    first_ref,
    lengths_ref,
    q_ref,
    k4_ref,
    k3_ref,
    k2_ref,
    k1_ref,
    own_ref,
    residual_ref,
    info_ref,
    *out_refs,
):
    tokens, width = q_ref.shape
    part = width // Z_SIZE
    kv_width = own_ref.shape[1] // 2
    kv_heads = kv_width // HD
    group = width // HD // kv_heads
    blocks = [k4_ref, k3_ref, k2_ref, k1_ref, own_ref]
    keys = len(blocks) * tokens
    first = first_ref[0]
    query_pos = first + lax.broadcasted_iota(jnp.int32, (tokens, keys), 0)
    key_pos = first - (keys - tokens) + lax.broadcasted_iota(jnp.int32, (tokens, keys), 1)
    start = jnp.zeros((tokens, keys), jnp.int32)
    end = jnp.int32(0)
    for request in range(lengths_ref.shape[0]):
        end = end + lengths_ref[request]
        start = jnp.maximum(start, jnp.where(query_pos >= end, end, 0))
    hidden = jnp.where((key_pos >= start) & (key_pos <= query_pos), 0.0, NEGATIVE)
    hidden = jnp.concatenate([hidden] * group, axis=0)
    scale = 1.0 / math.sqrt(HD)
    for step, out_ref in enumerate(out_refs):
        z = lax.rem(z_ref[0] + step, Z_SIZE)
        for column in range(Z_SIZE):

            @pl.when(z == column)
            def _(column=column, out_ref=out_ref):
                columns = slice(column * part, (column + 1) * part)
                out_ref[:, width : width + part] = residual_ref[:, columns]

        out_ref[:, width + part :] = info_ref[...]
    for kv in range(kv_heads):
        at = slice(kv * HD, (kv + 1) * HD)
        value_at = slice(kv_width + kv * HD, kv_width + (kv + 1) * HD)
        key = jnp.concatenate([block[:, at] for block in blocks], axis=0)
        value = jnp.concatenate([block[:, value_at] for block in blocks], axis=0)
        heads = [kv * group + member for member in range(group)]
        query = jnp.concatenate([q_ref[:, h * HD : (h + 1) * HD] for h in heads], axis=0)
        scores = dot_rows(query, key) * scale + hidden
        weights = jnp.exp(scores - jnp.max(scores, axis=-1, keepdims=True))
        total = jnp.sum(weights, axis=-1, keepdims=True)
        result = (dot(weights.astype(jnp.bfloat16), value) / total).astype(jnp.bfloat16)
        for member, h in enumerate(heads):
            for out_ref in out_refs:
                out_ref[:, h * HD : (h + 1) * HD] = result[member * tokens : (member + 1) * tokens]


def route_kernel(z_ref, ids_ref, logits_ref, out_ref, turned_ref):
    choices, tokens = ids_ref.shape
    turned_ref[...] = jnp.zeros(turned_ref.shape, jnp.float32)
    turned_ref[:choices, :tokens] = ids_ref[...].astype(jnp.float32)
    turned_ref[8 : 8 + choices, :tokens] = logits_ref[...]
    table = turned_ref[...].T[:tokens]
    lane = lax.broadcasted_iota(jnp.int32, table.shape, 1)
    ids = [table[:, c : c + 1].astype(jnp.int32) for c in range(choices)]
    logits = [table[:, 8 + c : 9 + c] for c in range(choices)]
    member = jnp.zeros(table.shape, jnp.float32)
    for one in ids:
        member = jnp.where(lane == one, 1.0, member)
    row = lax.broadcasted_iota(jnp.int32, (tokens, tokens), 0)
    earlier = jnp.where(lax.broadcasted_iota(jnp.int32, (tokens, tokens), 1) < row, 1.0, 0.0)
    ahead = dot(earlier.astype(jnp.bfloat16), member.astype(jnp.bfloat16))
    top = logits[0]
    for one in logits[1:]:
        top = jnp.maximum(top, one)
    powers = [jnp.exp(one - top) for one in logits]
    total = sum(powers[1:], powers[0])
    per_device = EXPERTS // 2 // PLANE
    out = jnp.zeros(table.shape, jnp.float32)
    for c, one in enumerate(ids):
        rank = jnp.sum(jnp.where(lane == one, ahead, 0.0), axis=1, keepdims=True)
        where_to = lax.div(one, per_device).astype(jnp.float32)
        first = (lax.rem(one, per_device) * Z_SIZE + z_ref[0]) * CAP
        out = jnp.where(lane == c, where_to, out)
        out = jnp.where(lane == 8 + c, first.astype(jnp.float32) + rank, out)
        out = jnp.where(lane == 16 + c, powers[c] / total, out)
    out_ref[...] = out.astype(jnp.bfloat16)


def regroup_kernel(z_ref, *refs):
    pieces, outs = refs[:PLANE], refs[PLANE:]
    for step, out in enumerate(outs):
        z = lax.rem(z_ref[0] + step, Z_SIZE)
        for at, piece in enumerate(pieces):
            out[at] = piece[z]


def source_z(z_ref, step):
    return lax.rem(z_ref[0] + Z_SIZE - step, Z_SIZE)


def project_kernel(z_ref, *refs):
    sent = refs[:Z_SIZE]
    weight_ref, mixed_ref, info_ref, rows_ref = refs[Z_SIZE:]
    for step, sent_ref in enumerate(sent):
        rows_ref[source_z(z_ref, step)] = sent_ref[...]
    rows = jnp.concatenate([rows_ref[z] for z in range(Z_SIZE)], axis=0)
    part, width = weight_ref.shape
    out = dot_rows(rows[:, :width], weight_ref[...])
    mixed_ref[...] = (out + rows[:, width : width + part].astype(jnp.float32)).astype(jnp.bfloat16)
    info_ref[...] = rows[:, width + part :]


def row_codes(info, first, parity, per_device):
    where_to = info(first).astype(jnp.int32) - PLANE * parity
    inside = info(first + 8).astype(jnp.int32)
    fits = (where_to >= 0) & (where_to < PLANE)
    return jnp.where(fits, where_to * per_device + inside, -1)


def tables_kernel(parity_ref, info_ref, onehot_ref, mix_ref):
    rows, tokens = onehot_ref.shape
    info = info_ref[...].astype(jnp.float32)
    turned = info.T
    codes = row_codes(lambda at: turned[at : at + 8], 0, parity_ref[0], rows // PLANE)
    row = lax.broadcasted_iota(jnp.int32, (rows, tokens), 0)
    chosen = codes[0:1, :] == row
    for choice in range(1, TOP):
        chosen = chosen | (codes[choice : choice + 1, :] == row)
    onehot_ref[...] = jnp.where(chosen, 1.0, 0.0).astype(jnp.bfloat16)
    column = lax.broadcasted_iota(jnp.int32, mix_ref.shape, 1)
    mix = jnp.zeros(mix_ref.shape, jnp.float32)
    for choice in range(TOP):
        code = row_codes(lambda at: info[:, at : at + 1], choice, parity_ref[0], rows // PLANE)
        mix = jnp.where(code == column, info[:, 16 + choice : 17 + choice], mix)
    mix_ref[...] = mix.astype(jnp.bfloat16)


def pick_kernel(z_ref, onehot_ref, gain_ref, *refs):
    parts = refs[:Z_SIZE]
    normed_ref, own_ref, out_hbm, mixed_ref, out_ref, sems = refs[Z_SIZE:]
    for step, part_ref in enumerate(parts):
        mixed_ref[source_z(z_ref, step)] = part_ref[...]
    columns = mixed_ref.shape[2]
    tokens = own_ref.shape[0]
    own = pl.ds(pl.multiple_of(z_ref[0] * tokens, tokens), tokens)
    for z in range(Z_SIZE):
        own_ref[:, z * columns : (z + 1) * columns] = mixed_ref[z, own, :].astype(jnp.float32)
    mixed = jnp.concatenate([mixed_ref[z] for z in range(Z_SIZE)], axis=1).astype(jnp.float32)
    mean_square = jnp.mean(mixed * mixed, axis=-1, keepdims=True)
    normed = (mixed * lax.rsqrt(mean_square + EPSILON) * gain_ref[...]).astype(jnp.bfloat16)
    normed_ref[...] = normed
    picked = out_ref.shape[1]
    copies = []
    for p in range(PLANE):
        onehot = onehot_ref[p * picked : (p + 1) * picked]
        out_ref[p] = dot(onehot, normed).astype(jnp.bfloat16)
        copy = pltpu.make_async_copy(out_ref.at[p], out_hbm.at[p], sems.at[p])
        copy.start()
        copies.append(copy)
    for copy in copies:
        copy.wait()


def shared_kernel(rows_ref, weight_ref, out_ref):
    parts, units, _ = weight_ref.shape
    units = units // 3
    gate_weight, up_weight, down_weight = [
        jnp.concatenate([weight_ref[p, at * units : (at + 1) * units] for p in range(parts)], axis=0)
        for at in range(3)
    ]
    rows = rows_ref[...]
    act = silu_times(dot_rows(rows, gate_weight), dot_rows(rows, up_weight))
    out_ref[...] = dot(act, down_weight)


def experts_kernel(
    rows_ref, gate_up_hbm, down_hbm, out_hbm, gate_up_ref, down_ref, out_ref, in_sems, out_sems
):
    halves = gate_up_ref.shape[0]
    fetches = []
    for half in range(halves):
        gate_up = pltpu.make_async_copy(
            gate_up_hbm.at[half], gate_up_ref.at[half], in_sems.at[0, half]
        )
        down = pltpu.make_async_copy(down_hbm.at[half], down_ref.at[half], in_sems.at[1, half])
        gate_up.start()
        down.start()
        fetches.append((gate_up, down))
    sources, rows, width = rows_ref.shape
    per_half = rows // halves
    copies = []
    for pair in range(halves // 2):
        both = pl.ds(2 * pair * per_half, 2 * per_half)
        arrived = rows_ref[:, both, :].astype(jnp.float32)
        results = []
        for member in range(2):
            half = 2 * pair + member
            own = arrived[:, member * per_half : (member + 1) * per_half]
            own = own.reshape(sources * per_half, width).astype(jnp.bfloat16)
            fetches[half][0].wait()
            act = silu_times(dot(own, gate_up_ref[half, 0]), dot(own, gate_up_ref[half, 1]))
            fetches[half][1].wait()
            results.append(dot(act, down_ref[half]).reshape(sources, per_half, width))
        out_ref[:, both, :] = jnp.concatenate(results, axis=1).astype(jnp.bfloat16)
        copy = pltpu.make_async_copy(out_ref.at[:, both], out_hbm.at[:, both], out_sems.at[pair])
        copy.start()
        copies.append(copy)
    for copy in copies:
        copy.wait()


def combine_kernel(z_ref, mix_ref, rows_ref, shared_ref, *refs):
    outs, sum_ref = refs[:Z_SIZE], refs[Z_SIZE]
    tokens = outs[0].shape[0]
    sum_ref[...] = dot(mix_ref[...], rows_ref[...]) + shared_ref[...]
    for step, out_ref in enumerate(outs):
        z = lax.rem(z_ref[0] + step, Z_SIZE)
        rows = pl.ds(pl.multiple_of(z * tokens, tokens), tokens)
        out_ref[...] = sum_ref[rows, :].astype(jnp.bfloat16)


def final_kernel(mixed_ref, *refs):
    total = mixed_ref[...]
    for part_ref in refs[:Z_SIZE]:
        total = total + part_ref[...].astype(jnp.float32)
    refs[Z_SIZE][...] = total.astype(jnp.bfloat16)


def reorder_kernel(me_ref, table_ref, from_ref, to_ref):
    me = me_ref[0]
    for block in range(to_ref.shape[0]):
        source = table_ref[block]
        z_steps = lax.rem(lax.div(me, PLANE) - lax.div(source, PLANE) + Z_SIZE, Z_SIZE)
        steps = lax.rem(lax.rem(me, PLANE) - lax.rem(source, PLANE) + PLANE, PLANE)
        to_ref[block] = from_ref[z_steps * PLANE + steps]


def params(mib=16):
    return pltpu.CompilerParams(vmem_limit_bytes=mib * MIB)


def cost(flops, moved):
    return pl.CostEstimate(flops=int(flops), bytes_accessed=int(moved), transcendentals=0)


def shards(
    queries,
    key_vectors,
    value_vectors,
    lengths,
    out_weight,
    residual,
    norm_gain,
    route_ids,
    route_logits,
    shared_gate_up,
    shared_down,
    expert_gate_up,
    expert_down,
    cache_blocks,
    block_table,
):
    tokens, width = residual.shape
    devices = lax.axis_size("seq")
    me = lax.axis_index("seq")
    z_index, plane_index = lax.div(me, PLANE), lax.rem(me, PLANE)
    planes = [[p + PLANE * z for p in range(PLANE)] for z in range(Z_SIZE)]
    bf16, f32 = jnp.bfloat16, jnp.float32
    shape = jax.ShapeDtypeStruct
    scalar = lambda value: jnp.reshape(value, (1,)).astype(jnp.int32)
    all_tokens = Z_SIZE * tokens
    part = width // Z_SIZE

    def exchange(array, groups):
        return lax.all_to_all(
            array, "seq", split_axis=0, concat_axis=0, tiled=True, axis_index_groups=groups
        )

    own_kv = jnp.concatenate([key_vectors, value_vectors], axis=1)
    behind = [from_behind(own_kv, "seq", offset) for offset in range(REACH, 0, -1)]

    turned_weight = lax.all_gather(
        out_weight.T, "seq", axis=0, tiled=True, axis_index_groups=planes
    )
    info = pl.pallas_call(
        route_kernel,
        out_shape=shape((tokens, 128), bf16),
        in_specs=[SMEM] + [VMEM] * 2,
        out_specs=VMEM,
        scratch_shapes=[pltpu.VMEM((128, 128), f32)],
        compiler_params=params(),
        cost_estimate=cost(MIB, MIB),
        name="route",
    )(scalar(z_index), route_ids.T, route_logits.T)

    def along_z(arrays):
        return [arrays[0]] + [
            lax.ppermute(arrays[step], "seq", z_pairs[step]) for step in range(1, Z_SIZE)
        ]

    z_pairs = [
        [
            (z * PLANE + p, (z + step) % Z_SIZE * PLANE + p)
            for z in range(Z_SIZE)
            for p in range(PLANE)
        ]
        for step in range(Z_SIZE)
    ]
    z_scalar = scalar(z_index)
    gain = norm_gain.reshape(1, width)
    own_shared = jnp.concatenate(
        [jnp.transpose(shared_gate_up, (1, 2, 0)).reshape(-1, width), shared_down], axis=0
    )
    info, own_shared = lax.optimization_barrier((info, own_shared))
    shared_weight = lax.all_gather(own_shared, "seq", axis=0, axis_index_groups=planes)

    sent_width = width + part + info.shape[1]
    sent = pl.pallas_call(
        attention_kernel,
        out_shape=[shape((tokens, sent_width), bf16)] * Z_SIZE,
        in_specs=[SMEM] * 3 + [VMEM] * 8,
        out_specs=[VMEM] * Z_SIZE,
        compiler_params=params(),
        cost_estimate=cost(4 * tokens * 5 * tokens * width, 3 * MIB),
        name="attention",
    )(z_scalar, scalar(me * tokens), lengths, queries, *behind, own_kv, residual, info)

    gathered = along_z(sent)
    gathered, cache_blocks, expert_gate_up = lax.optimization_barrier(
        (gathered, cache_blocks, expert_gate_up)
    )

    _, block_tokens, layers, kv_heads, head_size = cache_blocks.shape
    per_device = block_tokens // devices
    cache_view = cache_blocks.reshape(Z_SIZE, PLANE, per_device * layers, kv_heads, head_size)
    in_plane = []
    for step in range(PLANE):
        piece = lax.dynamic_index_in_dim(
            cache_view, lax.rem(plane_index + step, PLANE), axis=1, keepdims=False
        )
        if step:
            pairs = [
                (z * PLANE + p, z * PLANE + (p + step) % PLANE)
                for z in range(Z_SIZE)
                for p in range(PLANE)
            ]
            piece = lax.ppermute(piece, "seq", pairs)
        in_plane.append(piece)
    gate_up = jnp.transpose(expert_gate_up, (0, 2, 1, 3))

    mixed_part, info = pl.pallas_call(
        project_kernel,
        out_shape=[shape((all_tokens, part), bf16), shape((all_tokens, 128), bf16)],
        in_specs=[SMEM] + [VMEM] * (Z_SIZE + 1),
        out_specs=[VMEM] * 2,
        scratch_shapes=[pltpu.VMEM((Z_SIZE, tokens, sent_width), bf16)],
        compiler_params=params(),
        cost_estimate=cost(2 * all_tokens * width * part, 3 * MIB),
        name="project",
    )(z_scalar, *gathered, turned_weight)
    mixed = along_z([mixed_part] * Z_SIZE)

    local_halves, _, _, half_ff = expert_gate_up.shape
    per_half = Z_SIZE * CAP
    picked = local_halves * per_half
    onehot, mix = pl.pallas_call(
        tables_kernel,
        out_shape=[
            shape((PLANE * picked, all_tokens), bf16),
            shape((all_tokens, PLANE * picked), bf16),
        ],
        in_specs=[SMEM, VMEM],
        out_specs=[VMEM] * 2,
        compiler_params=params(),
        cost_estimate=cost(20 * PLANE * picked * all_tokens, MIB),
        name="tables",
    )(scalar(lax.rem(z_index, 2)), info)
    normed, own_mixed, outgoing = pl.pallas_call(
        pick_kernel,
        out_shape=[
            shape((all_tokens, width), bf16),
            shape((tokens, width), f32),
            shape((PLANE, picked, width), bf16),
        ],
        in_specs=[SMEM] + [VMEM] * (2 + Z_SIZE),
        out_specs=[VMEM, VMEM, HBM],
        scratch_shapes=[
            pltpu.VMEM((Z_SIZE, all_tokens, part), bf16),
            pltpu.VMEM((PLANE, picked, width), bf16),
            pltpu.SemaphoreType.DMA((PLANE,)),
        ],
        compiler_params=params(20),
        cost_estimate=cost(2 * PLANE * picked * all_tokens * width, 5 * MIB),
        name="pick",
    )(z_scalar, onehot, gain, *mixed)

    outgoing, in_plane = lax.optimization_barrier((outgoing, in_plane))
    arrived = exchange(outgoing, planes)
    grouped = pl.pallas_call(
        regroup_kernel,
        out_shape=[shape((PLANE,) + in_plane[0].shape[1:], bf16)] * Z_SIZE,
        in_specs=[SMEM] + [VMEM] * PLANE,
        out_specs=[VMEM] * Z_SIZE,
        compiler_params=params(),
        cost_estimate=cost(0, 2 * MIB),
        name="regroup",
    )(z_scalar, *in_plane)
    arrived_cache = [grouped[0]]
    for step in range(1, Z_SIZE):
        arrived_cache.append(lax.ppermute(grouped[step], "seq", z_pairs[step]))

    arrived, shared_weight = lax.optimization_barrier((arrived, shared_weight))
    shared_part = pl.pallas_call(
        shared_kernel,
        out_shape=shape((all_tokens, width), f32),
        in_specs=[VMEM] * 2,
        out_specs=VMEM,
        compiler_params=params(24),
        cost_estimate=cost(6 * all_tokens * 256 * width, 5 * MIB),
        name="shared_expert",
    )(normed, shared_weight)

    returning = pl.pallas_call(
        experts_kernel,
        out_shape=shape((PLANE, picked, width), bf16),
        in_specs=[VMEM, HBM, HBM],
        out_specs=HBM,
        scratch_shapes=[
            pltpu.VMEM((local_halves, 2, width, half_ff), bf16),
            pltpu.VMEM((local_halves, half_ff, width), bf16),
            pltpu.VMEM((PLANE, picked, width), bf16),
            pltpu.SemaphoreType.DMA((2, local_halves)),
            pltpu.SemaphoreType.DMA((local_halves // 2,)),
        ],
        compiler_params=params(40),
        cost_estimate=cost(6 * PLANE * picked * half_ff * width, 14 * MIB),
        name="experts",
    )(arrived, gate_up, expert_down)
    returning, arrived_cache = lax.optimization_barrier((returning, arrived_cache))
    returned = exchange(returning, planes).reshape(PLANE * picked, width)

    arrived_cache = jnp.concatenate(arrived_cache)
    cache_out = pl.pallas_call(
        reorder_kernel,
        out_shape=shape(arrived_cache.shape, bf16),
        in_specs=[SMEM, SMEM, VMEM],
        out_specs=VMEM,
        compiler_params=params(),
        cost_estimate=cost(0, 2 * arrived_cache.size * 2),
        name="reorder",
    )(scalar(me), block_table, arrived_cache)
    cache_out = cache_out.reshape(devices, per_device, layers, kv_heads, head_size)

    sums = pl.pallas_call(
        combine_kernel,
        out_shape=[shape((tokens, width), bf16)] * Z_SIZE,
        in_specs=[SMEM] + [VMEM] * 3,
        out_specs=[VMEM] * Z_SIZE,
        scratch_shapes=[pltpu.VMEM((all_tokens, width), f32)],
        compiler_params=params(24),
        cost_estimate=cost(2 * all_tokens * PLANE * picked * width, 3 * MIB),
        name="combine",
    )(z_scalar, mix, returned, shared_part)
    layer_out = pl.pallas_call(
        final_kernel,
        out_shape=shape((tokens, width), bf16),
        in_specs=[VMEM] * (1 + Z_SIZE),
        out_specs=VMEM,
        compiler_params=params(),
        cost_estimate=cost(5 * tokens * width, 2 * MIB),
        name="final",
    )(own_mixed, *along_z(sums))
    return (layer_out, cache_out)


def solution(mesh):
    in_specs = (
        P("seq", "head"),
        P("seq", "head"),
        P("seq", "head"),
        P(),
        P("head", "seq"),
        P(("seq", "head"), None),
        P(),
        P(("seq", "head"), None),
        P(("seq", "head"), None),
        P(None, None, ("seq", "head")),
        P(("seq", "head"), None),
        P("seq", None, None, None),
        P("seq", None, None),
        P("seq", None, None, "head", None),
        P(),
    )
    out_specs = (P(("seq", "head"), None), P(None, "seq", None, "head", None))
    planes_fit = mesh.shape["seq"] == Z_SIZE * PLANE and mesh.shape["head"] == 1
    body = shards if planes_fit else general_shards
    return jax.shard_map(body, mesh=mesh, in_specs=in_specs, out_specs=out_specs, check_vma=False)
```

```python
import math

import jax
import jax.numpy as jnp
from jax import lax
from jax.experimental import pallas as pl
from jax.experimental.pallas import tpu as pltpu
from jax.sharding import PartitionSpec as P

HD = 128
EXPERTS = 64
TOP = 6
REACH = 4
HALVES = 128
CAP = 6
Z_SIZE = 4
PLANE = 8
MIB = 1024 * 1024


NEGATIVE = -1e30
EPSILON = 1e-05


def from_behind(shard, axis, by):
    devices = lax.axis_size(axis)
    pairs = [(i, i + by) for i in range(devices) if 0 <= i + by < devices]
    return lax.ppermute(shard, axis, pairs)


def segment_of(positions, lengths):
    request_ends = jnp.cumsum(lengths)
    passed = (request_ends[None, :] <= positions[:, None]).astype(jnp.int32)
    return jnp.sum(passed, axis=1)


def shared_ffn(rows_in, gate_up_part, down_part):
    shared_both = jnp.einsum(
        "td,dcf->tcf", rows_in, gate_up_part, preferred_element_type=jnp.float32
    )
    shared_act = (jax.nn.silu(shared_both[:, 0]) * shared_both[:, 1]).astype(jnp.bfloat16)
    return jnp.dot(shared_act, down_part, preferred_element_type=jnp.float32)


def general_shards(
    queries,
    key_vectors,
    value_vectors,
    lengths,
    out_weight,
    residual,
    norm_gain,
    route_ids,
    route_logits,
    shared_gate_up,
    shared_down,
    expert_gate_up,
    expert_down,
    cache_blocks,
    block_table,
):
    handed = lax.all_to_all(cache_blocks, "seq", split_axis=1, concat_axis=0, tiled=True)
    cache_out = jnp.take(handed, block_table, axis=0)
    tok_rows = queries.shape[0]
    seq_index = lax.axis_index("seq")
    earlier = [
        from_behind((key_vectors, value_vectors), "seq", offset) for offset in range(REACH, 0, -1)
    ]
    window_keys = jnp.concatenate([member[0] for member in earlier] + [key_vectors], axis=0)
    window_values = jnp.concatenate([member[1] for member in earlier] + [value_vectors], axis=0)
    key_count = window_keys.shape[0]
    kv_heads = key_vectors.shape[1] // HD
    query_heads = queries.shape[1] // HD
    group_size = query_heads // kv_heads
    query_pos = seq_index * tok_rows + jnp.arange(tok_rows, dtype=jnp.int32)
    key_pos = (seq_index - REACH) * tok_rows + jnp.arange(key_count, dtype=jnp.int32)
    visible = (key_pos[None, :] >= 0) & (key_pos[None, :] <= query_pos[:, None])
    visible = visible & (
        segment_of(key_pos, lengths)[None, :] == segment_of(query_pos, lengths)[:, None]
    )
    query_part = queries.reshape(tok_rows, kv_heads, group_size, HD)
    key_part = window_keys.reshape(key_count, kv_heads, HD)
    value_part = window_values.reshape(key_count, kv_heads, HD)
    scores = jnp.einsum(
        "tkgd,wkd->kgtw", query_part, key_part, preferred_element_type=jnp.float32
    ) * (1.0 / math.sqrt(HD))
    scores = jnp.where(visible[None, None], scores, NEGATIVE)
    row_max = jnp.max(scores, axis=-1, keepdims=True)
    weights = jnp.exp(scores - row_max)
    row_total = jnp.sum(weights, axis=-1)
    weighted = jnp.einsum(
        "kgtw,wkd->tkgd",
        weights.astype(jnp.bfloat16),
        value_part,
        preferred_element_type=jnp.float32,
    )
    heads = (weighted / jnp.transpose(row_total, (2, 0, 1))[..., None]).astype(jnp.bfloat16)
    heads = heads.reshape(tok_rows, query_heads * HD)
    partial_out = jnp.dot(
        heads,
        lax.all_gather(out_weight, "seq", axis=1, tiled=True),
        preferred_element_type=jnp.float32,
    )
    attn_out = lax.psum_scatter(partial_out, "head", scatter_dimension=0, tiled=True)
    mixed = residual.astype(jnp.float32) + attn_out
    mean_square = jnp.mean(mixed * mixed, axis=-1, keepdims=True)
    normed = (mixed * lax.rsqrt(mean_square + EPSILON) * norm_gain).astype(jnp.bfloat16)
    gate_up_all, down_all = (
        lax.all_gather(shared_gate_up, ("seq", "head"), axis=2, tiled=True),
        lax.all_gather(shared_down, ("seq", "head"), axis=0, tiled=True),
    )
    shared_part = shared_ffn(normed, gate_up_all, down_all)
    own_tokens = normed.shape[0]
    width_model = normed.shape[1]
    flat_ids = route_ids.reshape(-1)
    onehot = (flat_ids[:, None] == jnp.arange(EXPERTS, dtype=jnp.int32)[None, :]).astype(jnp.int32)
    slot_rank = jnp.sum((jnp.cumsum(onehot, axis=0) - 1) * onehot, axis=1)
    first_slot = flat_ids * CAP + slot_rank
    second_slot = (flat_ids + EXPERTS) * CAP + slot_rank
    token_of = jnp.arange(flat_ids.shape[0], dtype=jnp.int32) // TOP
    routed_rows = normed[token_of]
    outgoing = jnp.zeros((HALVES * CAP, width_model), jnp.bfloat16)
    outgoing = outgoing.at[jnp.concatenate([first_slot, second_slot])].set(
        jnp.concatenate([routed_rows, routed_rows], axis=0)
    )
    local_halves = expert_gate_up.shape[0]
    outgoing = outgoing.reshape(HALVES // local_halves, local_halves, CAP, width_model)
    gate_up = jnp.einsum(
        "nsjd,sdcf->nsjcf",
        lax.all_to_all(outgoing, "seq", split_axis=0, concat_axis=0, tiled=True),
        expert_gate_up,
        preferred_element_type=jnp.float32,
    )
    expert_act = (jax.nn.silu(gate_up[:, :, :, 0]) * gate_up[:, :, :, 1]).astype(jnp.bfloat16)
    half_out = jnp.einsum(
        "nsjf,sfd->nsjd", expert_act, expert_down, preferred_element_type=jnp.float32
    ).astype(jnp.bfloat16)
    returned = lax.all_to_all(half_out, "seq", split_axis=0, concat_axis=0, tiled=True)
    returned = returned.reshape(HALVES * CAP, width_model)
    pair_sum = returned[first_slot].astype(jnp.float32) + returned[second_slot].astype(jnp.float32)
    route_probs = jax.nn.softmax(route_logits, axis=-1)
    routed = jnp.sum(
        route_probs[:, :, None] * pair_sum.reshape(own_tokens, TOP, width_model), axis=1
    )
    layer_out = (mixed + shared_part + routed).astype(jnp.bfloat16)
    return (layer_out, cache_out)


VMEM = pl.BlockSpec(memory_space=pltpu.VMEM)
SMEM = pl.BlockSpec(memory_space=pltpu.SMEM)
HBM = pl.BlockSpec(memory_space=pltpu.HBM)


def dot_rows(left, right):
    return lax.dot_general(left, right, (((1,), (1,)), ((), ())), preferred_element_type=jnp.float32)


def dot(left, right):
    return jnp.dot(left, right, preferred_element_type=jnp.float32)


def silu_times(gate, up):
    return (gate / (1.0 + jnp.exp(-gate)) * up).astype(jnp.bfloat16)


def attention_kernel(
    z_ref,
    first_ref,
    lengths_ref,
    q_ref,
    k4_ref,
    k3_ref,
    k2_ref,
    k1_ref,
    own_ref,
    residual_ref,
    info_ref,
    *out_refs,
):
    tokens, width = q_ref.shape
    part = width // Z_SIZE
    kv_width = own_ref.shape[1] // 2
    kv_heads = kv_width // HD
    group = width // HD // kv_heads
    blocks = [k4_ref, k3_ref, k2_ref, k1_ref, own_ref]
    keys = len(blocks) * tokens
    first = first_ref[0]
    query_pos = first + lax.broadcasted_iota(jnp.int32, (tokens, keys), 0)
    key_pos = first - (keys - tokens) + lax.broadcasted_iota(jnp.int32, (tokens, keys), 1)
    start = jnp.zeros((tokens, keys), jnp.int32)
    end = jnp.int32(0)
    for request in range(lengths_ref.shape[0]):
        end = end + lengths_ref[request]
        start = jnp.maximum(start, jnp.where(query_pos >= end, end, 0))
    hidden = jnp.where((key_pos >= start) & (key_pos <= query_pos), 0.0, NEGATIVE)
    hidden = jnp.concatenate([hidden] * group, axis=0)
    scale = 1.0 / math.sqrt(HD)
    for step, out_ref in enumerate(out_refs):
        z = lax.rem(z_ref[0] + step, Z_SIZE)
        for column in range(Z_SIZE):

            @pl.when(z == column)
            def _(column=column, out_ref=out_ref):
                columns = slice(column * part, (column + 1) * part)
                out_ref[:, width : width + part] = residual_ref[:, columns]

        out_ref[:, width + part :] = info_ref[...]
    for kv in range(kv_heads):
        at = slice(kv * HD, (kv + 1) * HD)
        value_at = slice(kv_width + kv * HD, kv_width + (kv + 1) * HD)
        key = jnp.concatenate([block[:, at] for block in blocks], axis=0)
        value = jnp.concatenate([block[:, value_at] for block in blocks], axis=0)
        heads = [kv * group + member for member in range(group)]
        query = jnp.concatenate([q_ref[:, h * HD : (h + 1) * HD] for h in heads], axis=0)
        scores = dot_rows(query, key) * scale + hidden
        weights = jnp.exp(scores - jnp.max(scores, axis=-1, keepdims=True))
        total = jnp.sum(weights, axis=-1, keepdims=True)
        result = (dot(weights.astype(jnp.bfloat16), value) / total).astype(jnp.bfloat16)
        for member, h in enumerate(heads):
            for out_ref in out_refs:
                out_ref[:, h * HD : (h + 1) * HD] = result[member * tokens : (member + 1) * tokens]


def route_kernel(z_ref, ids_ref, logits_ref, out_ref, turned_ref):
    choices, tokens = ids_ref.shape
    turned_ref[...] = jnp.zeros(turned_ref.shape, jnp.float32)
    turned_ref[:choices, :tokens] = ids_ref[...].astype(jnp.float32)
    turned_ref[8 : 8 + choices, :tokens] = logits_ref[...]
    table = turned_ref[...].T[:tokens]
    lane = lax.broadcasted_iota(jnp.int32, table.shape, 1)
    ids = [table[:, c : c + 1].astype(jnp.int32) for c in range(choices)]
    logits = [table[:, 8 + c : 9 + c] for c in range(choices)]
    member = jnp.zeros(table.shape, jnp.float32)
    for one in ids:
        member = jnp.where(lane == one, 1.0, member)
    row = lax.broadcasted_iota(jnp.int32, (tokens, tokens), 0)
    earlier = jnp.where(lax.broadcasted_iota(jnp.int32, (tokens, tokens), 1) < row, 1.0, 0.0)
    ahead = dot(earlier.astype(jnp.bfloat16), member.astype(jnp.bfloat16))
    top = logits[0]
    for one in logits[1:]:
        top = jnp.maximum(top, one)
    powers = [jnp.exp(one - top) for one in logits]
    total = sum(powers[1:], powers[0])
    per_device = EXPERTS // 2 // PLANE
    out = jnp.zeros(table.shape, jnp.float32)
    for c, one in enumerate(ids):
        rank = jnp.sum(jnp.where(lane == one, ahead, 0.0), axis=1, keepdims=True)
        where_to = lax.div(one, per_device).astype(jnp.float32)
        first = (lax.rem(one, per_device) * Z_SIZE + z_ref[0]) * CAP
        out = jnp.where(lane == c, where_to, out)
        out = jnp.where(lane == 8 + c, first.astype(jnp.float32) + rank, out)
        out = jnp.where(lane == 16 + c, powers[c] / total, out)
    out_ref[...] = out.astype(jnp.bfloat16)


def regroup_kernel(z_ref, *refs):
    pieces, outs = refs[:PLANE], refs[PLANE:]
    for step, out in enumerate(outs):
        z = lax.rem(z_ref[0] + step, Z_SIZE)
        for at, piece in enumerate(pieces):
            out[at] = piece[z]


def source_z(z_ref, step):
    return lax.rem(z_ref[0] + Z_SIZE - step, Z_SIZE)


def project_kernel(z_ref, *refs):
    sent = refs[:Z_SIZE]
    weight_ref, mixed_ref, info_ref, rows_ref = refs[Z_SIZE:]
    for step, sent_ref in enumerate(sent):
        rows_ref[source_z(z_ref, step)] = sent_ref[...]
    rows = jnp.concatenate([rows_ref[z] for z in range(Z_SIZE)], axis=0)
    part, width = weight_ref.shape
    out = dot_rows(rows[:, :width], weight_ref[...])
    mixed_ref[...] = (out + rows[:, width : width + part].astype(jnp.float32)).astype(jnp.bfloat16)
    info_ref[...] = rows[:, width + part :]


def row_codes(info, first, parity, per_device):
    where_to = info(first).astype(jnp.int32) - PLANE * parity
    inside = info(first + 8).astype(jnp.int32)
    fits = (where_to >= 0) & (where_to < PLANE)
    return jnp.where(fits, where_to * per_device + inside, -1)


def tables_kernel(parity_ref, info_ref, onehot_ref, mix_ref):
    rows, tokens = onehot_ref.shape
    info = info_ref[...].astype(jnp.float32)
    turned = info.T
    codes = row_codes(lambda at: turned[at : at + 8], 0, parity_ref[0], rows // PLANE)
    row = lax.broadcasted_iota(jnp.int32, (rows, tokens), 0)
    chosen = codes[0:1, :] == row
    for choice in range(1, TOP):
        chosen = chosen | (codes[choice : choice + 1, :] == row)
    onehot_ref[...] = jnp.where(chosen, 1.0, 0.0).astype(jnp.bfloat16)
    column = lax.broadcasted_iota(jnp.int32, mix_ref.shape, 1)
    mix = jnp.zeros(mix_ref.shape, jnp.float32)
    for choice in range(TOP):
        code = row_codes(lambda at: info[:, at : at + 1], choice, parity_ref[0], rows // PLANE)
        mix = jnp.where(code == column, info[:, 16 + choice : 17 + choice], mix)
    mix_ref[...] = mix.astype(jnp.bfloat16)


def pick_kernel(z_ref, onehot_ref, gain_ref, *refs):
    parts = refs[:Z_SIZE]
    normed_ref, own_ref, out_hbm, mixed_ref, out_ref, sems = refs[Z_SIZE:]
    for step, part_ref in enumerate(parts):
        mixed_ref[source_z(z_ref, step)] = part_ref[...]
    columns = mixed_ref.shape[2]
    tokens = own_ref.shape[0]
    own = pl.ds(pl.multiple_of(z_ref[0] * tokens, tokens), tokens)
    for z in range(Z_SIZE):
        own_ref[:, z * columns : (z + 1) * columns] = mixed_ref[z, own, :].astype(jnp.float32)
    mixed = jnp.concatenate([mixed_ref[z] for z in range(Z_SIZE)], axis=1).astype(jnp.float32)
    mean_square = jnp.mean(mixed * mixed, axis=-1, keepdims=True)
    normed = (mixed * lax.rsqrt(mean_square + EPSILON) * gain_ref[...]).astype(jnp.bfloat16)
    normed_ref[...] = normed
    picked = out_ref.shape[1]
    copies = []
    for p in range(PLANE):
        onehot = onehot_ref[p * picked : (p + 1) * picked]
        out_ref[p] = dot(onehot, normed).astype(jnp.bfloat16)
        copy = pltpu.make_async_copy(out_ref.at[p], out_hbm.at[p], sems.at[p])
        copy.start()
        copies.append(copy)
    for copy in copies:
        copy.wait()


def shared_kernel(rows_ref, weight_ref, out_ref):
    parts, units, _ = weight_ref.shape
    units = units // 3
    gate_weight, up_weight, down_weight = [
        jnp.concatenate([weight_ref[p, at * units : (at + 1) * units] for p in range(parts)], axis=0)
        for at in range(3)
    ]
    rows = rows_ref[...]
    act = silu_times(dot_rows(rows, gate_weight), dot_rows(rows, up_weight))
    out_ref[...] = dot(act, down_weight).astype(jnp.bfloat16)


def experts_kernel(
    rows_hbm,
    gate_up_hbm,
    down_hbm,
    out_hbm,
    rows_ref,
    gate_up_ref,
    down_ref,
    out_ref,
    in_sems,
    row_sems,
    out_sems,
):
    halves = gate_up_ref.shape[0]
    sources, rows, width = rows_ref.shape
    per_half = rows // halves
    fetches, row_fetches = [], []
    for half in range(halves):
        if half % 2 == 0:
            both = pl.ds(half * per_half, 2 * per_half)
            fetch = pltpu.make_async_copy(
                rows_hbm.at[:, both], rows_ref.at[:, both], row_sems.at[half // 2]
            )
            fetch.start()
            row_fetches.append(fetch)
        gate_up = pltpu.make_async_copy(
            gate_up_hbm.at[half], gate_up_ref.at[half], in_sems.at[0, half]
        )
        down = pltpu.make_async_copy(down_hbm.at[half], down_ref.at[half], in_sems.at[1, half])
        gate_up.start()
        down.start()
        fetches.append((gate_up, down))
    copies = []
    for pair in range(halves // 2):
        both = pl.ds(2 * pair * per_half, 2 * per_half)
        row_fetches[pair].wait()
        arrived = rows_ref[:, both, :].astype(jnp.float32)
        results = []
        for member in range(2):
            half = 2 * pair + member
            own = arrived[:, member * per_half : (member + 1) * per_half]
            own = own.reshape(sources * per_half, width).astype(jnp.bfloat16)
            fetches[half][0].wait()
            act = silu_times(dot(own, gate_up_ref[half, 0]), dot(own, gate_up_ref[half, 1]))
            fetches[half][1].wait()
            results.append(dot(act, down_ref[half]).reshape(sources, per_half, width))
        out_ref[:, both, :] = jnp.concatenate(results, axis=1).astype(jnp.bfloat16)
        copy = pltpu.make_async_copy(out_ref.at[:, both], out_hbm.at[:, both], out_sems.at[pair])
        copy.start()
        copies.append(copy)
    for copy in copies:
        copy.wait()


def combine_kernel(z_ref, mix_ref, rows_ref, shared_ref, *refs):
    outs, sum_ref = refs[:Z_SIZE], refs[Z_SIZE]
    tokens = outs[0].shape[0]
    sum_ref[...] = dot(mix_ref[...], rows_ref[...]) + shared_ref[...].astype(jnp.float32)
    for step, out_ref in enumerate(outs):
        z = lax.rem(z_ref[0] + step, Z_SIZE)
        rows = pl.ds(pl.multiple_of(z * tokens, tokens), tokens)
        out_ref[...] = sum_ref[rows, :].astype(jnp.bfloat16)


def final_kernel(mixed_ref, *refs):
    total = mixed_ref[...]
    for part_ref in refs[:Z_SIZE]:
        total = total + part_ref[...].astype(jnp.float32)
    refs[Z_SIZE][...] = total.astype(jnp.bfloat16)


def reorder_kernel(me_ref, table_ref, from_ref, to_ref):
    me = me_ref[0]
    for block in range(to_ref.shape[0]):
        source = table_ref[block]
        z_steps = lax.rem(lax.div(me, PLANE) - lax.div(source, PLANE) + Z_SIZE, Z_SIZE)
        steps = lax.rem(lax.rem(me, PLANE) - lax.rem(source, PLANE) + PLANE, PLANE)
        to_ref[block] = from_ref[z_steps * PLANE + steps]


def params(mib=16):
    return pltpu.CompilerParams(vmem_limit_bytes=mib * MIB)


def cost(flops, moved):
    return pl.CostEstimate(flops=int(flops), bytes_accessed=int(moved), transcendentals=0)


def shards(
    queries,
    key_vectors,
    value_vectors,
    lengths,
    out_weight,
    residual,
    norm_gain,
    route_ids,
    route_logits,
    shared_gate_up,
    shared_down,
    expert_gate_up,
    expert_down,
    cache_blocks,
    block_table,
):
    tokens, width = residual.shape
    devices = lax.axis_size("seq")
    me = lax.axis_index("seq")
    z_index, plane_index = lax.div(me, PLANE), lax.rem(me, PLANE)
    planes = [[p + PLANE * z for p in range(PLANE)] for z in range(Z_SIZE)]
    bf16, f32 = jnp.bfloat16, jnp.float32
    shape = jax.ShapeDtypeStruct
    scalar = lambda value: jnp.reshape(value, (1,)).astype(jnp.int32)
    all_tokens = Z_SIZE * tokens
    part = width // Z_SIZE

    def exchange(array, groups):
        return lax.all_to_all(
            array, "seq", split_axis=0, concat_axis=0, tiled=True, axis_index_groups=groups
        )

    own_kv = jnp.concatenate([key_vectors, value_vectors], axis=1)
    behind = [from_behind(own_kv, "seq", offset) for offset in range(REACH, 0, -1)]

    behind[-1], route_ids, route_logits, shared_gate_up, shared_down = lax.optimization_barrier(
        (behind[-1], route_ids, route_logits, shared_gate_up, shared_down)
    )

    turned_weight = lax.all_gather(
        out_weight.T, "seq", axis=0, tiled=True, axis_index_groups=planes
    )
    info = pl.pallas_call(
        route_kernel,
        out_shape=shape((tokens, 128), bf16),
        in_specs=[SMEM] + [VMEM] * 2,
        out_specs=VMEM,
        scratch_shapes=[pltpu.VMEM((128, 128), f32)],
        compiler_params=params(),
        cost_estimate=cost(MIB, MIB),
        name="route",
    )(scalar(z_index), route_ids.T, route_logits.T)

    def along_z(arrays):
        return [arrays[0]] + [
            lax.ppermute(arrays[step], "seq", z_pairs[step]) for step in range(1, Z_SIZE)
        ]

    z_pairs = [
        [
            (z * PLANE + p, (z + step) % Z_SIZE * PLANE + p)
            for z in range(Z_SIZE)
            for p in range(PLANE)
        ]
        for step in range(Z_SIZE)
    ]
    z_scalar = scalar(z_index)
    gain = norm_gain.reshape(1, width)
    own_shared = jnp.concatenate(
        [jnp.transpose(shared_gate_up, (1, 2, 0)).reshape(-1, width), shared_down], axis=0
    )
    info, own_shared = lax.optimization_barrier((info, own_shared))
    shared_weight = lax.all_gather(own_shared, "seq", axis=0, axis_index_groups=planes)

    sent_width = width + part + info.shape[1]
    sent = pl.pallas_call(
        attention_kernel,
        out_shape=[shape((tokens, sent_width), bf16)] * Z_SIZE,
        in_specs=[SMEM] * 3 + [VMEM] * 8,
        out_specs=[VMEM] * Z_SIZE,
        compiler_params=params(58),
        cost_estimate=cost(4 * tokens * 5 * tokens * width, 3 * MIB),
        name="attention",
    )(z_scalar, scalar(me * tokens), lengths, queries, *behind, own_kv, residual, info)

    gathered = along_z(sent)

    mixed_part, info = pl.pallas_call(
        project_kernel,
        out_shape=[shape((all_tokens, part), bf16), shape((all_tokens, 128), bf16)],
        in_specs=[SMEM] + [VMEM] * (Z_SIZE + 1),
        out_specs=[VMEM] * 2,
        scratch_shapes=[pltpu.VMEM((Z_SIZE, tokens, sent_width), bf16)],
        compiler_params=params(),
        cost_estimate=cost(2 * all_tokens * width * part, 3 * MIB),
        name="project",
    )(z_scalar, *gathered, turned_weight)
    mixed = along_z([mixed_part] * Z_SIZE)

    local_halves, _, _, half_ff = expert_gate_up.shape
    per_half = Z_SIZE * CAP
    picked = local_halves * per_half
    onehot, mix = pl.pallas_call(
        tables_kernel,
        out_shape=[
            shape((PLANE * picked, all_tokens), bf16),
            shape((all_tokens, PLANE * picked), bf16),
        ],
        in_specs=[SMEM, VMEM],
        out_specs=[VMEM] * 2,
        compiler_params=params(),
        cost_estimate=cost(20 * PLANE * picked * all_tokens, MIB),
        name="tables",
    )(scalar(lax.rem(z_index, 2)), info)
    onehot, cache_blocks, expert_gate_up = lax.optimization_barrier(
        (onehot, cache_blocks, expert_gate_up)
    )

    _, block_tokens, layers, kv_heads, head_size = cache_blocks.shape
    per_device = block_tokens // devices
    cache_view = cache_blocks.reshape(Z_SIZE, PLANE, per_device * layers, kv_heads, head_size)
    in_plane = []
    for step in range(PLANE):
        piece = lax.dynamic_index_in_dim(
            cache_view, lax.rem(plane_index + step, PLANE), axis=1, keepdims=False
        )
        if step:
            pairs = [
                (z * PLANE + p, z * PLANE + (p + step) % PLANE)
                for z in range(Z_SIZE)
                for p in range(PLANE)
            ]
            piece = lax.ppermute(piece, "seq", pairs)
        in_plane.append(piece)
    gate_up = jnp.transpose(expert_gate_up, (0, 2, 1, 3))

    normed, own_mixed, outgoing = pl.pallas_call(
        pick_kernel,
        out_shape=[
            shape((all_tokens, width), bf16),
            shape((tokens, width), f32),
            shape((PLANE, picked, width), bf16),
        ],
        in_specs=[SMEM] + [VMEM] * (2 + Z_SIZE),
        out_specs=[VMEM, VMEM, HBM],
        scratch_shapes=[
            pltpu.VMEM((Z_SIZE, all_tokens, part), bf16),
            pltpu.VMEM((PLANE, picked, width), bf16),
            pltpu.SemaphoreType.DMA((PLANE,)),
        ],
        compiler_params=params(58),
        cost_estimate=cost(2 * PLANE * picked * all_tokens * width, 5 * MIB),
        name="pick",
    )(z_scalar, onehot, gain, *mixed)

    arrived = exchange(outgoing, planes)
    grouped = pl.pallas_call(
        regroup_kernel,
        out_shape=[shape((PLANE,) + in_plane[0].shape[1:], bf16)] * Z_SIZE,
        in_specs=[SMEM] + [VMEM] * PLANE,
        out_specs=[VMEM] * Z_SIZE,
        compiler_params=params(),
        cost_estimate=cost(0, 2 * MIB),
        name="regroup",
    )(z_scalar, *in_plane)
    arrived_cache = [grouped[0]]
    for step in range(1, Z_SIZE):
        arrived_cache.append(lax.ppermute(grouped[step], "seq", z_pairs[step]))

    arrived, shared_weight = lax.optimization_barrier((arrived, shared_weight))
    shared_part = pl.pallas_call(
        shared_kernel,
        out_shape=shape((all_tokens, width), bf16),
        in_specs=[VMEM] * 2,
        out_specs=VMEM,
        compiler_params=params(24),
        cost_estimate=cost(6 * all_tokens * 256 * width, 5 * MIB),
        name="shared_expert",
    )(normed, shared_weight)

    returning = pl.pallas_call(
        experts_kernel,
        out_shape=shape((PLANE, picked, width), bf16),
        in_specs=[HBM, HBM, HBM],
        out_specs=HBM,
        scratch_shapes=[
            pltpu.VMEM((PLANE, picked, width), bf16),
            pltpu.VMEM((local_halves, 2, width, half_ff), bf16),
            pltpu.VMEM((local_halves, half_ff, width), bf16),
            pltpu.VMEM((PLANE, picked, width), bf16),
            pltpu.SemaphoreType.DMA((2, local_halves)),
            pltpu.SemaphoreType.DMA((local_halves // 2,)),
            pltpu.SemaphoreType.DMA((local_halves // 2,)),
        ],
        compiler_params=params(58),
        cost_estimate=cost(6 * PLANE * picked * half_ff * width, 14 * MIB),
        name="experts",
    )(arrived, gate_up, expert_down)
    returning, arrived_cache = lax.optimization_barrier((returning, arrived_cache))
    returned = exchange(returning, planes).reshape(PLANE * picked, width)

    arrived_cache = jnp.concatenate(arrived_cache)
    cache_out = pl.pallas_call(
        reorder_kernel,
        out_shape=shape(arrived_cache.shape, bf16),
        in_specs=[SMEM, SMEM, VMEM],
        out_specs=VMEM,
        compiler_params=params(),
        cost_estimate=cost(0, 2 * arrived_cache.size * 2),
        name="reorder",
    )(scalar(me), block_table, arrived_cache)
    cache_out = cache_out.reshape(devices, per_device, layers, kv_heads, head_size)

    sums = pl.pallas_call(
        combine_kernel,
        out_shape=[shape((tokens, width), bf16)] * Z_SIZE,
        in_specs=[SMEM] + [VMEM] * 3,
        out_specs=[VMEM] * Z_SIZE,
        scratch_shapes=[pltpu.VMEM((all_tokens, width), f32)],
        compiler_params=params(24),
        cost_estimate=cost(2 * all_tokens * PLANE * picked * width, 3 * MIB),
        name="combine",
    )(z_scalar, mix, returned, shared_part)
    layer_out = pl.pallas_call(
        final_kernel,
        out_shape=shape((tokens, width), bf16),
        in_specs=[VMEM] * (1 + Z_SIZE),
        out_specs=VMEM,
        compiler_params=params(),
        cost_estimate=cost(5 * tokens * width, 2 * MIB),
        name="final",
    )(own_mixed, *along_z(sums))
    return (layer_out, cache_out)


def solution(mesh):
    in_specs = (
        P("seq", "head"),
        P("seq", "head"),
        P("seq", "head"),
        P(),
        P("head", "seq"),
        P(("seq", "head"), None),
        P(),
        P(("seq", "head"), None),
        P(("seq", "head"), None),
        P(None, None, ("seq", "head")),
        P(("seq", "head"), None),
        P("seq", None, None, None),
        P("seq", None, None),
        P("seq", None, None, "head", None),
        P(),
    )
    out_specs = (P(("seq", "head"), None), P(None, "seq", None, "head", None))
    planes_fit = mesh.shape["seq"] == Z_SIZE * PLANE and mesh.shape["head"] == 1
    body = shards if planes_fit else general_shards
    return jax.shard_map(body, mesh=mesh, in_specs=in_specs, out_specs=out_specs, check_vma=False)
```

```python
import math

import jax
import jax.numpy as jnp
from jax import lax
from jax.experimental import pallas as pl
from jax.experimental.pallas import tpu as pltpu
from jax.sharding import PartitionSpec as P

HD = 128
EXPERTS = 64
TOP = 6
REACH = 4
HALVES = 128
CAP = 6
Z_SIZE = 4
PLANE = 8
MIB = 1024 * 1024


NEGATIVE = -1e30
EPSILON = 1e-05


def from_behind(shard, axis, by):
    devices = lax.axis_size(axis)
    pairs = [(i, i + by) for i in range(devices) if 0 <= i + by < devices]
    return lax.ppermute(shard, axis, pairs)


def segment_of(positions, lengths):
    request_ends = jnp.cumsum(lengths)
    passed = (request_ends[None, :] <= positions[:, None]).astype(jnp.int32)
    return jnp.sum(passed, axis=1)


def shared_ffn(rows_in, gate_up_part, down_part):
    shared_both = jnp.einsum(
        "td,dcf->tcf", rows_in, gate_up_part, preferred_element_type=jnp.float32
    )
    shared_act = (jax.nn.silu(shared_both[:, 0]) * shared_both[:, 1]).astype(jnp.bfloat16)
    return jnp.dot(shared_act, down_part, preferred_element_type=jnp.float32)


def general_shards(
    queries,
    key_vectors,
    value_vectors,
    lengths,
    out_weight,
    residual,
    norm_gain,
    route_ids,
    route_logits,
    shared_gate_up,
    shared_down,
    expert_gate_up,
    expert_down,
    cache_blocks,
    block_table,
):
    handed = lax.all_to_all(cache_blocks, "seq", split_axis=1, concat_axis=0, tiled=True)
    cache_out = jnp.take(handed, block_table, axis=0)
    tok_rows = queries.shape[0]
    seq_index = lax.axis_index("seq")
    earlier = [
        from_behind((key_vectors, value_vectors), "seq", offset) for offset in range(REACH, 0, -1)
    ]
    window_keys = jnp.concatenate([member[0] for member in earlier] + [key_vectors], axis=0)
    window_values = jnp.concatenate([member[1] for member in earlier] + [value_vectors], axis=0)
    key_count = window_keys.shape[0]
    kv_heads = key_vectors.shape[1] // HD
    query_heads = queries.shape[1] // HD
    group_size = query_heads // kv_heads
    query_pos = seq_index * tok_rows + jnp.arange(tok_rows, dtype=jnp.int32)
    key_pos = (seq_index - REACH) * tok_rows + jnp.arange(key_count, dtype=jnp.int32)
    visible = (key_pos[None, :] >= 0) & (key_pos[None, :] <= query_pos[:, None])
    visible = visible & (
        segment_of(key_pos, lengths)[None, :] == segment_of(query_pos, lengths)[:, None]
    )
    query_part = queries.reshape(tok_rows, kv_heads, group_size, HD)
    key_part = window_keys.reshape(key_count, kv_heads, HD)
    value_part = window_values.reshape(key_count, kv_heads, HD)
    scores = jnp.einsum(
        "tkgd,wkd->kgtw", query_part, key_part, preferred_element_type=jnp.float32
    ) * (1.0 / math.sqrt(HD))
    scores = jnp.where(visible[None, None], scores, NEGATIVE)
    row_max = jnp.max(scores, axis=-1, keepdims=True)
    weights = jnp.exp(scores - row_max)
    row_total = jnp.sum(weights, axis=-1)
    weighted = jnp.einsum(
        "kgtw,wkd->tkgd",
        weights.astype(jnp.bfloat16),
        value_part,
        preferred_element_type=jnp.float32,
    )
    heads = (weighted / jnp.transpose(row_total, (2, 0, 1))[..., None]).astype(jnp.bfloat16)
    heads = heads.reshape(tok_rows, query_heads * HD)
    partial_out = jnp.dot(
        heads,
        lax.all_gather(out_weight, "seq", axis=1, tiled=True),
        preferred_element_type=jnp.float32,
    )
    attn_out = lax.psum_scatter(partial_out, "head", scatter_dimension=0, tiled=True)
    mixed = residual.astype(jnp.float32) + attn_out
    mean_square = jnp.mean(mixed * mixed, axis=-1, keepdims=True)
    normed = (mixed * lax.rsqrt(mean_square + EPSILON) * norm_gain).astype(jnp.bfloat16)
    gate_up_all, down_all = (
        lax.all_gather(shared_gate_up, ("seq", "head"), axis=2, tiled=True),
        lax.all_gather(shared_down, ("seq", "head"), axis=0, tiled=True),
    )
    shared_part = shared_ffn(normed, gate_up_all, down_all)
    own_tokens = normed.shape[0]
    width_model = normed.shape[1]
    flat_ids = route_ids.reshape(-1)
    onehot = (flat_ids[:, None] == jnp.arange(EXPERTS, dtype=jnp.int32)[None, :]).astype(jnp.int32)
    slot_rank = jnp.sum((jnp.cumsum(onehot, axis=0) - 1) * onehot, axis=1)
    first_slot = flat_ids * CAP + slot_rank
    second_slot = (flat_ids + EXPERTS) * CAP + slot_rank
    token_of = jnp.arange(flat_ids.shape[0], dtype=jnp.int32) // TOP
    routed_rows = normed[token_of]
    outgoing = jnp.zeros((HALVES * CAP, width_model), jnp.bfloat16)
    outgoing = outgoing.at[jnp.concatenate([first_slot, second_slot])].set(
        jnp.concatenate([routed_rows, routed_rows], axis=0)
    )
    local_halves = expert_gate_up.shape[0]
    outgoing = outgoing.reshape(HALVES // local_halves, local_halves, CAP, width_model)
    gate_up = jnp.einsum(
        "nsjd,sdcf->nsjcf",
        lax.all_to_all(outgoing, "seq", split_axis=0, concat_axis=0, tiled=True),
        expert_gate_up,
        preferred_element_type=jnp.float32,
    )
    expert_act = (jax.nn.silu(gate_up[:, :, :, 0]) * gate_up[:, :, :, 1]).astype(jnp.bfloat16)
    half_out = jnp.einsum(
        "nsjf,sfd->nsjd", expert_act, expert_down, preferred_element_type=jnp.float32
    ).astype(jnp.bfloat16)
    returned = lax.all_to_all(half_out, "seq", split_axis=0, concat_axis=0, tiled=True)
    returned = returned.reshape(HALVES * CAP, width_model)
    pair_sum = returned[first_slot].astype(jnp.float32) + returned[second_slot].astype(jnp.float32)
    route_probs = jax.nn.softmax(route_logits, axis=-1)
    routed = jnp.sum(
        route_probs[:, :, None] * pair_sum.reshape(own_tokens, TOP, width_model), axis=1
    )
    layer_out = (mixed + shared_part + routed).astype(jnp.bfloat16)
    return (layer_out, cache_out)


VMEM = pl.BlockSpec(memory_space=pltpu.VMEM)
SMEM = pl.BlockSpec(memory_space=pltpu.SMEM)
HBM = pl.BlockSpec(memory_space=pltpu.HBM)


def dot_rows(left, right):
    return lax.dot_general(left, right, (((1,), (1,)), ((), ())), preferred_element_type=jnp.float32)


def dot(left, right):
    return jnp.dot(left, right, preferred_element_type=jnp.float32)


def silu_times(gate, up):
    return (gate / (1.0 + jnp.exp(-gate)) * up).astype(jnp.bfloat16)


def attention_kernel(
    z_ref,
    first_ref,
    lengths_ref,
    q_ref,
    k4_ref,
    k3_ref,
    k2_ref,
    k1_ref,
    own_ref,
    residual_ref,
    info_ref,
    *out_refs,
):
    tokens, width = q_ref.shape
    part = width // Z_SIZE
    kv_width = own_ref.shape[1] // 2
    kv_heads = kv_width // HD
    group = width // HD // kv_heads
    blocks = [k4_ref, k3_ref, k2_ref, k1_ref, own_ref]
    keys = len(blocks) * tokens
    first = first_ref[0]
    query_pos = first + lax.broadcasted_iota(jnp.int32, (tokens, keys), 0)
    key_pos = first - (keys - tokens) + lax.broadcasted_iota(jnp.int32, (tokens, keys), 1)
    start = jnp.zeros((tokens, keys), jnp.int32)
    end = jnp.int32(0)
    for request in range(lengths_ref.shape[0]):
        end = end + lengths_ref[request]
        start = jnp.maximum(start, jnp.where(query_pos >= end, end, 0))
    hidden = jnp.where((key_pos >= start) & (key_pos <= query_pos), 0.0, NEGATIVE)
    hidden = jnp.concatenate([hidden] * group, axis=0)
    scale = 1.0 / math.sqrt(HD)
    for step, out_ref in enumerate(out_refs):
        z = lax.rem(z_ref[0] + step, Z_SIZE)
        for column in range(Z_SIZE):

            @pl.when(z == column)
            def _(column=column, out_ref=out_ref):
                columns = slice(column * part, (column + 1) * part)
                out_ref[:, width : width + part] = residual_ref[:, columns]

        out_ref[:, width + part :] = info_ref[...]
    for kv in range(kv_heads):
        at = slice(kv * HD, (kv + 1) * HD)
        value_at = slice(kv_width + kv * HD, kv_width + (kv + 1) * HD)
        key = jnp.concatenate([block[:, at] for block in blocks], axis=0)
        value = jnp.concatenate([block[:, value_at] for block in blocks], axis=0)
        heads = [kv * group + member for member in range(group)]
        query = jnp.concatenate([q_ref[:, h * HD : (h + 1) * HD] for h in heads], axis=0)
        scores = dot_rows(query, key) * scale + hidden
        weights = jnp.exp(scores - jnp.max(scores, axis=-1, keepdims=True))
        total = jnp.sum(weights, axis=-1, keepdims=True)
        result = (dot(weights.astype(jnp.bfloat16), value) / total).astype(jnp.bfloat16)
        for member, h in enumerate(heads):
            for out_ref in out_refs:
                out_ref[:, h * HD : (h + 1) * HD] = result[member * tokens : (member + 1) * tokens]


def route_kernel(z_ref, ids_ref, logits_ref, out_ref, turned_ref):
    choices, tokens = ids_ref.shape
    turned_ref[...] = jnp.zeros(turned_ref.shape, jnp.float32)
    turned_ref[:choices, :tokens] = ids_ref[...].astype(jnp.float32)
    turned_ref[8 : 8 + choices, :tokens] = logits_ref[...]
    table = turned_ref[...].T[:tokens]
    lane = lax.broadcasted_iota(jnp.int32, table.shape, 1)
    ids = [table[:, c : c + 1].astype(jnp.int32) for c in range(choices)]
    logits = [table[:, 8 + c : 9 + c] for c in range(choices)]
    member = jnp.zeros(table.shape, jnp.float32)
    for one in ids:
        member = jnp.where(lane == one, 1.0, member)
    row = lax.broadcasted_iota(jnp.int32, (tokens, tokens), 0)
    earlier = jnp.where(lax.broadcasted_iota(jnp.int32, (tokens, tokens), 1) < row, 1.0, 0.0)
    ahead = dot(earlier.astype(jnp.bfloat16), member.astype(jnp.bfloat16))
    top = logits[0]
    for one in logits[1:]:
        top = jnp.maximum(top, one)
    powers = [jnp.exp(one - top) for one in logits]
    total = sum(powers[1:], powers[0])
    per_device = EXPERTS // 2 // PLANE
    out = jnp.zeros(table.shape, jnp.float32)
    for c, one in enumerate(ids):
        rank = jnp.sum(jnp.where(lane == one, ahead, 0.0), axis=1, keepdims=True)
        where_to = lax.div(one, per_device).astype(jnp.float32)
        first = (lax.rem(one, per_device) * Z_SIZE + z_ref[0]) * CAP
        out = jnp.where(lane == c, where_to, out)
        out = jnp.where(lane == 8 + c, first.astype(jnp.float32) + rank, out)
        out = jnp.where(lane == 16 + c, powers[c] / total, out)
    out_ref[...] = out.astype(jnp.bfloat16)


def regroup_kernel(z_ref, pieces_ref, *outs):
    for step, out in enumerate(outs):
        z = lax.rem(z_ref[0] + step, Z_SIZE)
        for at in range(PLANE):
            out[at] = pieces_ref[at, z]


def source_z(z_ref, step):
    return lax.rem(z_ref[0] + Z_SIZE - step, Z_SIZE)


def project_kernel(z_ref, *refs):
    sent = refs[:Z_SIZE]
    weight_ref, mixed_ref, info_ref, rows_ref = refs[Z_SIZE:]
    for step, sent_ref in enumerate(sent):
        rows_ref[source_z(z_ref, step)] = sent_ref[...]
    rows = jnp.concatenate([rows_ref[z] for z in range(Z_SIZE)], axis=0)
    part, width = weight_ref.shape
    out = dot_rows(rows[:, :width], weight_ref[...])
    mixed_ref[...] = (out + rows[:, width : width + part].astype(jnp.float32)).astype(jnp.bfloat16)
    info_ref[...] = rows[:, width + part :]


def row_codes(info, first, parity, per_device):
    where_to = info(first).astype(jnp.int32) - PLANE * parity
    inside = info(first + 8).astype(jnp.int32)
    fits = (where_to >= 0) & (where_to < PLANE)
    return jnp.where(fits, where_to * per_device + inside, -1)


def tables_kernel(parity_ref, info_ref, onehot_ref, mix_ref):
    rows, tokens = onehot_ref.shape
    info = info_ref[...].astype(jnp.float32)
    turned = info.T
    codes = row_codes(lambda at: turned[at : at + 8], 0, parity_ref[0], rows // PLANE)
    row = lax.broadcasted_iota(jnp.int32, (rows, tokens), 0)
    chosen = codes[0:1, :] == row
    for choice in range(1, TOP):
        chosen = chosen | (codes[choice : choice + 1, :] == row)
    onehot_ref[...] = jnp.where(chosen, 1.0, 0.0).astype(jnp.bfloat16)
    column = lax.broadcasted_iota(jnp.int32, mix_ref.shape, 1)
    mix = jnp.zeros(mix_ref.shape, jnp.float32)
    for choice in range(TOP):
        code = row_codes(lambda at: info[:, at : at + 1], choice, parity_ref[0], rows // PLANE)
        mix = jnp.where(code == column, info[:, 16 + choice : 17 + choice], mix)
    mix_ref[...] = mix.astype(jnp.bfloat16)


def pick_kernel(z_ref, onehot_ref, gain_ref, *refs):
    parts = refs[:Z_SIZE]
    normed_ref, own_ref, out_hbm, mixed_ref, out_ref, sems = refs[Z_SIZE:]
    for step, part_ref in enumerate(parts):
        mixed_ref[source_z(z_ref, step)] = part_ref[...]
    columns = mixed_ref.shape[2]
    tokens = own_ref.shape[0]
    own = pl.ds(pl.multiple_of(z_ref[0] * tokens, tokens), tokens)
    for z in range(Z_SIZE):
        own_ref[:, z * columns : (z + 1) * columns] = mixed_ref[z, own, :].astype(jnp.float32)
    mixed = jnp.concatenate([mixed_ref[z] for z in range(Z_SIZE)], axis=1).astype(jnp.float32)
    mean_square = jnp.mean(mixed * mixed, axis=-1, keepdims=True)
    normed = (mixed * lax.rsqrt(mean_square + EPSILON) * gain_ref[...]).astype(jnp.bfloat16)
    normed_ref[...] = normed
    picked = out_ref.shape[1]
    copies = []
    for p in range(PLANE):
        onehot = onehot_ref[p * picked : (p + 1) * picked]
        out_ref[p] = dot(onehot, normed).astype(jnp.bfloat16)
        copy = pltpu.make_async_copy(out_ref.at[p], out_hbm.at[p], sems.at[p])
        copy.start()
        copies.append(copy)
    for copy in copies:
        copy.wait()


def shared_kernel(rows_ref, weight_ref, out_ref):
    parts, units, _ = weight_ref.shape
    units = units // 3
    gate_weight, up_weight, down_weight = [
        jnp.concatenate([weight_ref[p, at * units : (at + 1) * units] for p in range(parts)], axis=0)
        for at in range(3)
    ]
    rows = rows_ref[...]
    act = silu_times(dot_rows(rows, gate_weight), dot_rows(rows, up_weight))
    out_ref[...] = dot(act, down_weight).astype(jnp.bfloat16)


def experts_kernel(
    rows_hbm,
    gate_up_hbm,
    down_hbm,
    out_hbm,
    rows_ref,
    gate_up_ref,
    down_ref,
    out_ref,
    in_sems,
    row_sems,
    out_sems,
):
    halves = gate_up_ref.shape[0]
    sources, rows, width = rows_ref.shape
    per_half = rows // halves
    fetches, row_fetches = [], []
    for half in range(halves):
        if half % 2 == 0:
            both = pl.ds(half * per_half, 2 * per_half)
            fetch = pltpu.make_async_copy(
                rows_hbm.at[:, both], rows_ref.at[:, both], row_sems.at[half // 2]
            )
            fetch.start()
            row_fetches.append(fetch)
        gate_up = pltpu.make_async_copy(
            gate_up_hbm.at[half], gate_up_ref.at[half], in_sems.at[0, half]
        )
        down = pltpu.make_async_copy(down_hbm.at[half], down_ref.at[half], in_sems.at[1, half])
        gate_up.start()
        down.start()
        fetches.append((gate_up, down))
    copies = []
    for pair in range(halves // 2):
        both = pl.ds(2 * pair * per_half, 2 * per_half)
        row_fetches[pair].wait()
        arrived = rows_ref[:, both, :].astype(jnp.float32)
        results = []
        for member in range(2):
            half = 2 * pair + member
            own = arrived[:, member * per_half : (member + 1) * per_half]
            own = own.reshape(sources * per_half, width).astype(jnp.bfloat16)
            fetches[half][0].wait()
            act = silu_times(dot(own, gate_up_ref[half, 0]), dot(own, gate_up_ref[half, 1]))
            fetches[half][1].wait()
            results.append(dot(act, down_ref[half]).reshape(sources, per_half, width))
        out_ref[:, both, :] = jnp.concatenate(results, axis=1).astype(jnp.bfloat16)
        copy = pltpu.make_async_copy(out_ref.at[:, both], out_hbm.at[:, both], out_sems.at[pair])
        copy.start()
        copies.append(copy)
    for copy in copies:
        copy.wait()


def combine_kernel(z_ref, mix_ref, rows_ref, shared_ref, *refs):
    outs, sum_ref = refs[:Z_SIZE], refs[Z_SIZE]
    tokens = outs[0].shape[0]
    sum_ref[...] = dot(mix_ref[...], rows_ref[...]) + shared_ref[...].astype(jnp.float32)
    for step, out_ref in enumerate(outs):
        z = lax.rem(z_ref[0] + step, Z_SIZE)
        rows = pl.ds(pl.multiple_of(z * tokens, tokens), tokens)
        out_ref[...] = sum_ref[rows, :].astype(jnp.bfloat16)


def final_kernel(mixed_ref, *refs):
    total = mixed_ref[...]
    for part_ref in refs[:Z_SIZE]:
        total = total + part_ref[...].astype(jnp.float32)
    refs[Z_SIZE][...] = total.astype(jnp.bfloat16)


def reorder_kernel(me_ref, table_ref, from_ref, to_ref):
    me = me_ref[0]
    for block in range(to_ref.shape[0]):
        source = table_ref[block]
        z_steps = lax.rem(lax.div(me, PLANE) - lax.div(source, PLANE) + Z_SIZE, Z_SIZE)
        to_ref[block] = from_ref[z_steps * PLANE + lax.rem(source, PLANE)]


def params(mib=16):
    return pltpu.CompilerParams(vmem_limit_bytes=mib * MIB)


def cost(flops, moved):
    return pl.CostEstimate(flops=int(flops), bytes_accessed=int(moved), transcendentals=0)


def shards(
    queries,
    key_vectors,
    value_vectors,
    lengths,
    out_weight,
    residual,
    norm_gain,
    route_ids,
    route_logits,
    shared_gate_up,
    shared_down,
    expert_gate_up,
    expert_down,
    cache_blocks,
    block_table,
):
    tokens, width = residual.shape
    devices = lax.axis_size("seq")
    me = lax.axis_index("seq")
    z_index = lax.div(me, PLANE)
    planes = [[p + PLANE * z for p in range(PLANE)] for z in range(Z_SIZE)]
    bf16, f32 = jnp.bfloat16, jnp.float32
    shape = jax.ShapeDtypeStruct
    scalar = lambda value: jnp.reshape(value, (1,)).astype(jnp.int32)
    all_tokens = Z_SIZE * tokens
    part = width // Z_SIZE

    def exchange(array, groups):
        return lax.all_to_all(
            array, "seq", split_axis=0, concat_axis=0, tiled=True, axis_index_groups=groups
        )

    own_kv = jnp.concatenate([key_vectors, value_vectors], axis=1)
    behind = [from_behind(own_kv, "seq", offset) for offset in range(REACH, 0, -1)]

    turned_weight = lax.all_gather(
        out_weight.T, "seq", axis=0, tiled=True, axis_index_groups=planes
    )
    info = pl.pallas_call(
        route_kernel,
        out_shape=shape((tokens, 128), bf16),
        in_specs=[SMEM] + [VMEM] * 2,
        out_specs=VMEM,
        scratch_shapes=[pltpu.VMEM((128, 128), f32)],
        compiler_params=params(),
        cost_estimate=cost(MIB, MIB),
        name="route",
    )(scalar(z_index), route_ids.T, route_logits.T)

    def along_z(arrays):
        return [arrays[0]] + [
            lax.ppermute(arrays[step], "seq", z_pairs[step]) for step in range(1, Z_SIZE)
        ]

    z_pairs = [
        [
            (z * PLANE + p, (z + step) % Z_SIZE * PLANE + p)
            for z in range(Z_SIZE)
            for p in range(PLANE)
        ]
        for step in range(Z_SIZE)
    ]
    z_scalar = scalar(z_index)
    gain = norm_gain.reshape(1, width)
    own_shared = jnp.concatenate(
        [jnp.transpose(shared_gate_up, (1, 2, 0)).reshape(-1, width), shared_down], axis=0
    )

    sent_width = width + part + info.shape[1]
    sent = pl.pallas_call(
        attention_kernel,
        out_shape=[shape((tokens, sent_width), bf16)] * Z_SIZE,
        in_specs=[SMEM] * 3 + [VMEM] * 8,
        out_specs=[VMEM] * Z_SIZE,
        compiler_params=params(58),
        cost_estimate=cost(4 * tokens * 5 * tokens * width, 3 * MIB),
        name="attention",
    )(z_scalar, scalar(me * tokens), lengths, queries, *behind, own_kv, residual, info)

    sent, own_shared = lax.optimization_barrier((sent, own_shared))
    shared_weight = lax.all_gather(own_shared, "seq", axis=0, axis_index_groups=planes)
    gathered = along_z(sent)

    mixed_part, info = pl.pallas_call(
        project_kernel,
        out_shape=[shape((all_tokens, part), bf16), shape((all_tokens, 128), bf16)],
        in_specs=[SMEM] + [VMEM] * (Z_SIZE + 1),
        out_specs=[VMEM] * 2,
        scratch_shapes=[pltpu.VMEM((Z_SIZE, tokens, sent_width), bf16)],
        compiler_params=params(),
        cost_estimate=cost(2 * all_tokens * width * part, 3 * MIB),
        name="project",
    )(z_scalar, *gathered, turned_weight)
    mixed = along_z([mixed_part] * Z_SIZE)

    local_halves, _, _, half_ff = expert_gate_up.shape
    per_half = Z_SIZE * CAP
    picked = local_halves * per_half
    onehot, mix = pl.pallas_call(
        tables_kernel,
        out_shape=[
            shape((PLANE * picked, all_tokens), bf16),
            shape((all_tokens, PLANE * picked), bf16),
        ],
        in_specs=[SMEM, VMEM],
        out_specs=[VMEM] * 2,
        compiler_params=params(),
        cost_estimate=cost(20 * PLANE * picked * all_tokens, MIB),
        name="tables",
    )(scalar(lax.rem(z_index, 2)), info)
    onehot, cache_blocks, expert_gate_up = lax.optimization_barrier(
        (onehot, cache_blocks, expert_gate_up)
    )

    _, block_tokens, layers, kv_heads, head_size = cache_blocks.shape
    per_device = block_tokens // devices
    cache_view = cache_blocks.reshape(Z_SIZE, PLANE, per_device * layers, kv_heads, head_size)
    in_plane = exchange(jnp.transpose(cache_view, (1, 0, 2, 3, 4)), planes)
    gate_up = jnp.transpose(expert_gate_up, (0, 2, 1, 3))

    normed, own_mixed, outgoing = pl.pallas_call(
        pick_kernel,
        out_shape=[
            shape((all_tokens, width), bf16),
            shape((tokens, width), f32),
            shape((PLANE, picked, width), bf16),
        ],
        in_specs=[SMEM] + [VMEM] * (2 + Z_SIZE),
        out_specs=[VMEM, VMEM, HBM],
        scratch_shapes=[
            pltpu.VMEM((Z_SIZE, all_tokens, part), bf16),
            pltpu.VMEM((PLANE, picked, width), bf16),
            pltpu.SemaphoreType.DMA((PLANE,)),
        ],
        compiler_params=params(58),
        cost_estimate=cost(2 * PLANE * picked * all_tokens * width, 5 * MIB),
        name="pick",
    )(z_scalar, onehot, gain, *mixed)

    arrived = exchange(outgoing, planes)
    grouped = pl.pallas_call(
        regroup_kernel,
        out_shape=[shape((PLANE,) + in_plane.shape[2:], bf16)] * Z_SIZE,
        in_specs=[SMEM, VMEM],
        out_specs=[VMEM] * Z_SIZE,
        compiler_params=params(),
        cost_estimate=cost(0, 2 * MIB),
        name="regroup",
    )(z_scalar, in_plane)
    arrived_cache = [grouped[0]]
    for step in range(1, Z_SIZE):
        arrived_cache.append(lax.ppermute(grouped[step], "seq", z_pairs[step]))

    arrived, shared_weight = lax.optimization_barrier((arrived, shared_weight))
    shared_part = pl.pallas_call(
        shared_kernel,
        out_shape=shape((all_tokens, width), bf16),
        in_specs=[VMEM] * 2,
        out_specs=VMEM,
        compiler_params=params(24),
        cost_estimate=cost(6 * all_tokens * 256 * width, 5 * MIB),
        name="shared_expert",
    )(normed, shared_weight)

    returning = pl.pallas_call(
        experts_kernel,
        out_shape=shape((PLANE, picked, width), bf16),
        in_specs=[HBM, HBM, HBM],
        out_specs=HBM,
        scratch_shapes=[
            pltpu.VMEM((PLANE, picked, width), bf16),
            pltpu.VMEM((local_halves, 2, width, half_ff), bf16),
            pltpu.VMEM((local_halves, half_ff, width), bf16),
            pltpu.VMEM((PLANE, picked, width), bf16),
            pltpu.SemaphoreType.DMA((2, local_halves)),
            pltpu.SemaphoreType.DMA((local_halves // 2,)),
            pltpu.SemaphoreType.DMA((local_halves // 2,)),
        ],
        compiler_params=params(58),
        cost_estimate=cost(6 * PLANE * picked * half_ff * width, 14 * MIB),
        name="experts",
    )(arrived, gate_up, expert_down)
    returning, arrived_cache = lax.optimization_barrier((returning, arrived_cache))
    returned = exchange(returning, planes).reshape(PLANE * picked, width)

    arrived_cache = jnp.concatenate(arrived_cache)
    cache_out = pl.pallas_call(
        reorder_kernel,
        out_shape=shape(arrived_cache.shape, bf16),
        in_specs=[SMEM, SMEM, VMEM],
        out_specs=VMEM,
        compiler_params=params(),
        cost_estimate=cost(0, 2 * arrived_cache.size * 2),
        name="reorder",
    )(scalar(me), block_table, arrived_cache)
    cache_out = cache_out.reshape(devices, per_device, layers, kv_heads, head_size)

    sums = pl.pallas_call(
        combine_kernel,
        out_shape=[shape((tokens, width), bf16)] * Z_SIZE,
        in_specs=[SMEM] + [VMEM] * 3,
        out_specs=[VMEM] * Z_SIZE,
        scratch_shapes=[pltpu.VMEM((all_tokens, width), f32)],
        compiler_params=params(24),
        cost_estimate=cost(2 * all_tokens * PLANE * picked * width, 3 * MIB),
        name="combine",
    )(z_scalar, mix, returned, shared_part)
    layer_out = pl.pallas_call(
        final_kernel,
        out_shape=shape((tokens, width), bf16),
        in_specs=[VMEM] * (1 + Z_SIZE),
        out_specs=VMEM,
        compiler_params=params(),
        cost_estimate=cost(5 * tokens * width, 2 * MIB),
        name="final",
    )(own_mixed, *along_z(sums))
    return (layer_out, cache_out)


def solution(mesh):
    in_specs = (
        P("seq", "head"),
        P("seq", "head"),
        P("seq", "head"),
        P(),
        P("head", "seq"),
        P(("seq", "head"), None),
        P(),
        P(("seq", "head"), None),
        P(("seq", "head"), None),
        P(None, None, ("seq", "head")),
        P(("seq", "head"), None),
        P("seq", None, None, None),
        P("seq", None, None),
        P("seq", None, None, "head", None),
        P(),
    )
    out_specs = (P(("seq", "head"), None), P(None, "seq", None, "head", None))
    planes_fit = mesh.shape["seq"] == Z_SIZE * PLANE and mesh.shape["head"] == 1
    body = shards if planes_fit else general_shards
    return jax.shard_map(body, mesh=mesh, in_specs=in_specs, out_specs=out_specs, check_vma=False)
```

```python
import math

import jax
import jax.numpy as jnp
from jax import lax
from jax.experimental import pallas as pl
from jax.experimental.pallas import tpu as pltpu
from jax.sharding import PartitionSpec as P

HD = 128
EXPERTS = 64
TOP = 6
REACH = 4
HALVES = 128
CAP = 6
Z_SIZE = 4
PLANE = 8
MIB = 1024 * 1024


NEGATIVE = -1e30
EPSILON = 1e-05


def from_behind(shard, axis, by):
    devices = lax.axis_size(axis)
    pairs = [(i, i + by) for i in range(devices) if 0 <= i + by < devices]
    return lax.ppermute(shard, axis, pairs)


def segment_of(positions, lengths):
    request_ends = jnp.cumsum(lengths)
    passed = (request_ends[None, :] <= positions[:, None]).astype(jnp.int32)
    return jnp.sum(passed, axis=1)


def shared_ffn(rows_in, gate_up_part, down_part):
    shared_both = jnp.einsum(
        "td,dcf->tcf", rows_in, gate_up_part, preferred_element_type=jnp.float32
    )
    shared_act = (jax.nn.silu(shared_both[:, 0]) * shared_both[:, 1]).astype(jnp.bfloat16)
    return jnp.dot(shared_act, down_part, preferred_element_type=jnp.float32)


def general_shards(
    queries,
    key_vectors,
    value_vectors,
    lengths,
    out_weight,
    residual,
    norm_gain,
    route_ids,
    route_logits,
    shared_gate_up,
    shared_down,
    expert_gate_up,
    expert_down,
    cache_blocks,
    block_table,
):
    handed = lax.all_to_all(cache_blocks, "seq", split_axis=1, concat_axis=0, tiled=True)
    cache_out = jnp.take(handed, block_table, axis=0)
    tok_rows = queries.shape[0]
    seq_index = lax.axis_index("seq")
    earlier = [
        from_behind((key_vectors, value_vectors), "seq", offset) for offset in range(REACH, 0, -1)
    ]
    window_keys = jnp.concatenate([member[0] for member in earlier] + [key_vectors], axis=0)
    window_values = jnp.concatenate([member[1] for member in earlier] + [value_vectors], axis=0)
    key_count = window_keys.shape[0]
    kv_heads = key_vectors.shape[1] // HD
    query_heads = queries.shape[1] // HD
    group_size = query_heads // kv_heads
    query_pos = seq_index * tok_rows + jnp.arange(tok_rows, dtype=jnp.int32)
    key_pos = (seq_index - REACH) * tok_rows + jnp.arange(key_count, dtype=jnp.int32)
    visible = (key_pos[None, :] >= 0) & (key_pos[None, :] <= query_pos[:, None])
    visible = visible & (
        segment_of(key_pos, lengths)[None, :] == segment_of(query_pos, lengths)[:, None]
    )
    query_part = queries.reshape(tok_rows, kv_heads, group_size, HD)
    key_part = window_keys.reshape(key_count, kv_heads, HD)
    value_part = window_values.reshape(key_count, kv_heads, HD)
    scores = jnp.einsum(
        "tkgd,wkd->kgtw", query_part, key_part, preferred_element_type=jnp.float32
    ) * (1.0 / math.sqrt(HD))
    scores = jnp.where(visible[None, None], scores, NEGATIVE)
    row_max = jnp.max(scores, axis=-1, keepdims=True)
    weights = jnp.exp(scores - row_max)
    row_total = jnp.sum(weights, axis=-1)
    weighted = jnp.einsum(
        "kgtw,wkd->tkgd",
        weights.astype(jnp.bfloat16),
        value_part,
        preferred_element_type=jnp.float32,
    )
    heads = (weighted / jnp.transpose(row_total, (2, 0, 1))[..., None]).astype(jnp.bfloat16)
    heads = heads.reshape(tok_rows, query_heads * HD)
    partial_out = jnp.dot(
        heads,
        lax.all_gather(out_weight, "seq", axis=1, tiled=True),
        preferred_element_type=jnp.float32,
    )
    attn_out = lax.psum_scatter(partial_out, "head", scatter_dimension=0, tiled=True)
    mixed = residual.astype(jnp.float32) + attn_out
    mean_square = jnp.mean(mixed * mixed, axis=-1, keepdims=True)
    normed = (mixed * lax.rsqrt(mean_square + EPSILON) * norm_gain).astype(jnp.bfloat16)
    gate_up_all, down_all = (
        lax.all_gather(shared_gate_up, ("seq", "head"), axis=2, tiled=True),
        lax.all_gather(shared_down, ("seq", "head"), axis=0, tiled=True),
    )
    shared_part = shared_ffn(normed, gate_up_all, down_all)
    own_tokens = normed.shape[0]
    width_model = normed.shape[1]
    flat_ids = route_ids.reshape(-1)
    onehot = (flat_ids[:, None] == jnp.arange(EXPERTS, dtype=jnp.int32)[None, :]).astype(jnp.int32)
    slot_rank = jnp.sum((jnp.cumsum(onehot, axis=0) - 1) * onehot, axis=1)
    first_slot = flat_ids * CAP + slot_rank
    second_slot = (flat_ids + EXPERTS) * CAP + slot_rank
    token_of = jnp.arange(flat_ids.shape[0], dtype=jnp.int32) // TOP
    routed_rows = normed[token_of]
    outgoing = jnp.zeros((HALVES * CAP, width_model), jnp.bfloat16)
    outgoing = outgoing.at[jnp.concatenate([first_slot, second_slot])].set(
        jnp.concatenate([routed_rows, routed_rows], axis=0)
    )
    local_halves = expert_gate_up.shape[0]
    outgoing = outgoing.reshape(HALVES // local_halves, local_halves, CAP, width_model)
    gate_up = jnp.einsum(
        "nsjd,sdcf->nsjcf",
        lax.all_to_all(outgoing, "seq", split_axis=0, concat_axis=0, tiled=True),
        expert_gate_up,
        preferred_element_type=jnp.float32,
    )
    expert_act = (jax.nn.silu(gate_up[:, :, :, 0]) * gate_up[:, :, :, 1]).astype(jnp.bfloat16)
    half_out = jnp.einsum(
        "nsjf,sfd->nsjd", expert_act, expert_down, preferred_element_type=jnp.float32
    ).astype(jnp.bfloat16)
    returned = lax.all_to_all(half_out, "seq", split_axis=0, concat_axis=0, tiled=True)
    returned = returned.reshape(HALVES * CAP, width_model)
    pair_sum = returned[first_slot].astype(jnp.float32) + returned[second_slot].astype(jnp.float32)
    route_probs = jax.nn.softmax(route_logits, axis=-1)
    routed = jnp.sum(
        route_probs[:, :, None] * pair_sum.reshape(own_tokens, TOP, width_model), axis=1
    )
    layer_out = (mixed + shared_part + routed).astype(jnp.bfloat16)
    return (layer_out, cache_out)


VMEM = pl.BlockSpec(memory_space=pltpu.VMEM)
SMEM = pl.BlockSpec(memory_space=pltpu.SMEM)
HBM = pl.BlockSpec(memory_space=pltpu.HBM)


def dot_rows(left, right):
    return lax.dot_general(left, right, (((1,), (1,)), ((), ())), preferred_element_type=jnp.float32)


def dot(left, right):
    return jnp.dot(left, right, preferred_element_type=jnp.float32)


def silu_times(gate, up):
    return (gate / (1.0 + jnp.exp(-gate)) * up).astype(jnp.bfloat16)


def attention_kernel(
    z_ref,
    first_ref,
    lengths_ref,
    q_ref,
    k4_ref,
    k3_ref,
    k2_ref,
    k1_ref,
    own_ref,
    residual_ref,
    info_ref,
    *out_refs,
):
    tokens, width = q_ref.shape
    part = width // Z_SIZE
    kv_width = own_ref.shape[1] // 2
    kv_heads = kv_width // HD
    group = width // HD // kv_heads
    blocks = [k4_ref, k3_ref, k2_ref, k1_ref, own_ref]
    keys = len(blocks) * tokens
    first = first_ref[0]
    query_pos = first + lax.broadcasted_iota(jnp.int32, (tokens, keys), 0)
    key_pos = first - (keys - tokens) + lax.broadcasted_iota(jnp.int32, (tokens, keys), 1)
    start = jnp.zeros((tokens, keys), jnp.int32)
    end = jnp.int32(0)
    for request in range(lengths_ref.shape[0]):
        end = end + lengths_ref[request]
        start = jnp.maximum(start, jnp.where(query_pos >= end, end, 0))
    hidden = jnp.where((key_pos >= start) & (key_pos <= query_pos), 0.0, NEGATIVE)
    hidden = jnp.concatenate([hidden] * group, axis=0)
    scale = 1.0 / math.sqrt(HD)
    for step, out_ref in enumerate(out_refs):
        z = lax.rem(z_ref[0] + step, Z_SIZE)
        for column in range(Z_SIZE):

            @pl.when(z == column)
            def _(column=column, out_ref=out_ref):
                columns = slice(column * part, (column + 1) * part)
                out_ref[:, width : width + part] = residual_ref[:, columns]

        out_ref[:, width + part :] = info_ref[...]
    for kv in range(kv_heads):
        at = slice(kv * HD, (kv + 1) * HD)
        value_at = slice(kv_width + kv * HD, kv_width + (kv + 1) * HD)
        key = jnp.concatenate([block[:, at] for block in blocks], axis=0)
        value = jnp.concatenate([block[:, value_at] for block in blocks], axis=0)
        heads = [kv * group + member for member in range(group)]
        query = jnp.concatenate([q_ref[:, h * HD : (h + 1) * HD] for h in heads], axis=0)
        scores = dot_rows(query, key) * scale + hidden
        weights = jnp.exp(scores - jnp.max(scores, axis=-1, keepdims=True))
        total = jnp.sum(weights, axis=-1, keepdims=True)
        result = (dot(weights.astype(jnp.bfloat16), value) / total).astype(jnp.bfloat16)
        for member, h in enumerate(heads):
            for out_ref in out_refs:
                out_ref[:, h * HD : (h + 1) * HD] = result[member * tokens : (member + 1) * tokens]


def route_kernel(z_ref, ids_ref, logits_ref, out_ref, turned_ref):
    choices, tokens = ids_ref.shape
    turned_ref[...] = jnp.zeros(turned_ref.shape, jnp.float32)
    turned_ref[:choices, :tokens] = ids_ref[...].astype(jnp.float32)
    turned_ref[8 : 8 + choices, :tokens] = logits_ref[...]
    table = turned_ref[...].T[:tokens]
    lane = lax.broadcasted_iota(jnp.int32, table.shape, 1)
    ids = [table[:, c : c + 1].astype(jnp.int32) for c in range(choices)]
    logits = [table[:, 8 + c : 9 + c] for c in range(choices)]
    member = jnp.zeros(table.shape, jnp.float32)
    for one in ids:
        member = jnp.where(lane == one, 1.0, member)
    row = lax.broadcasted_iota(jnp.int32, (tokens, tokens), 0)
    earlier = jnp.where(lax.broadcasted_iota(jnp.int32, (tokens, tokens), 1) < row, 1.0, 0.0)
    ahead = dot(earlier.astype(jnp.bfloat16), member.astype(jnp.bfloat16))
    top = logits[0]
    for one in logits[1:]:
        top = jnp.maximum(top, one)
    powers = [jnp.exp(one - top) for one in logits]
    total = sum(powers[1:], powers[0])
    per_device = EXPERTS // 2 // PLANE
    out = jnp.zeros(table.shape, jnp.float32)
    for c, one in enumerate(ids):
        rank = jnp.sum(jnp.where(lane == one, ahead, 0.0), axis=1, keepdims=True)
        where_to = lax.div(one, per_device).astype(jnp.float32)
        first = (lax.rem(one, per_device) * Z_SIZE + z_ref[0]) * CAP
        out = jnp.where(lane == c, where_to, out)
        out = jnp.where(lane == 8 + c, first.astype(jnp.float32) + rank, out)
        out = jnp.where(lane == 16 + c, powers[c] / total, out)
    out_ref[...] = out.astype(jnp.bfloat16)


def regroup_kernel(z_ref, *refs):
    pieces, outs = refs[:PLANE], refs[PLANE:]
    for step, out in enumerate(outs):
        z = lax.rem(z_ref[0] + step, Z_SIZE)
        for at, piece in enumerate(pieces):
            out[at] = piece[z]


def source_z(z_ref, step):
    return lax.rem(z_ref[0] + Z_SIZE - step, Z_SIZE)


def project_kernel(z_ref, *refs):
    sent = refs[:Z_SIZE]
    weight_ref, mixed_ref, info_ref, rows_ref = refs[Z_SIZE:]
    for step, sent_ref in enumerate(sent):
        rows_ref[source_z(z_ref, step)] = sent_ref[...]
    rows = jnp.concatenate([rows_ref[z] for z in range(Z_SIZE)], axis=0)
    part, width = weight_ref.shape
    out = dot_rows(rows[:, :width], weight_ref[...])
    mixed = (out + rows[:, width : width + part].astype(jnp.float32)).astype(jnp.bfloat16)
    for z in range(Z_SIZE):
        mixed_ref[z] = mixed
    info_ref[...] = rows[:, width + part :]


def row_codes(info, first, parity, per_device):
    where_to = info(first).astype(jnp.int32) - PLANE * parity
    inside = info(first + 8).astype(jnp.int32)
    fits = (where_to >= 0) & (where_to < PLANE)
    return jnp.where(fits, where_to * per_device + inside, -1)


def tables_kernel(parity_ref, info_ref, onehot_ref, mix_ref):
    rows, tokens = onehot_ref.shape
    info = info_ref[...].astype(jnp.float32)
    turned = info.T
    codes = row_codes(lambda at: turned[at : at + 8], 0, parity_ref[0], rows // PLANE)
    row = lax.broadcasted_iota(jnp.int32, (rows, tokens), 0)
    chosen = codes[0:1, :] == row
    for choice in range(1, TOP):
        chosen = chosen | (codes[choice : choice + 1, :] == row)
    onehot_ref[...] = jnp.where(chosen, 1.0, 0.0).astype(jnp.bfloat16)
    column = lax.broadcasted_iota(jnp.int32, mix_ref.shape, 1)
    mix = jnp.zeros(mix_ref.shape, jnp.float32)
    for choice in range(TOP):
        code = row_codes(lambda at: info[:, at : at + 1], choice, parity_ref[0], rows // PLANE)
        mix = jnp.where(code == column, info[:, 16 + choice : 17 + choice], mix)
    mix_ref[...] = mix.astype(jnp.bfloat16)


def norm(mixed_ref, gain_ref):
    mixed = jnp.concatenate([mixed_ref[z] for z in range(Z_SIZE)], axis=1).astype(jnp.float32)
    mean_square = jnp.mean(mixed * mixed, axis=-1, keepdims=True)
    return (mixed * lax.rsqrt(mean_square + EPSILON) * gain_ref[...]).astype(jnp.bfloat16)


def pick_kernel(onehot_ref, gain_ref, mixed_ref, out_hbm, out_ref, sems):
    normed = norm(mixed_ref, gain_ref)
    picked = out_ref.shape[1]
    copies = []
    for p in range(PLANE):
        onehot = onehot_ref[p * picked : (p + 1) * picked]
        out_ref[p] = dot(onehot, normed).astype(jnp.bfloat16)
        copy = pltpu.make_async_copy(out_ref.at[p], out_hbm.at[p], sems.at[p])
        copy.start()
        copies.append(copy)
    for copy in copies:
        copy.wait()


def shared_kernel(z_ref, gain_ref, mixed_ref, weight_ref, out_ref, own_ref):
    tokens, columns = own_ref.shape[0], mixed_ref.shape[2]
    own = pl.ds(pl.multiple_of(z_ref[0] * tokens, tokens), tokens)
    for z in range(Z_SIZE):
        own_ref[:, z * columns : (z + 1) * columns] = mixed_ref[z, own, :].astype(jnp.float32)
    parts, units, _ = weight_ref.shape
    units = units // 3
    gate_weight, up_weight, down_weight = [
        jnp.concatenate([weight_ref[p, at * units : (at + 1) * units] for p in range(parts)], axis=0)
        for at in range(3)
    ]
    rows = norm(mixed_ref, gain_ref)
    act = silu_times(dot_rows(rows, gate_weight), dot_rows(rows, up_weight))
    out_ref[...] = dot(act, down_weight).astype(jnp.bfloat16)


def experts_kernel(
    rows_hbm,
    gate_up_hbm,
    down_hbm,
    out_hbm,
    rows_ref,
    gate_up_ref,
    down_ref,
    out_ref,
    in_sems,
    row_sems,
    out_sems,
):
    halves = gate_up_ref.shape[0]
    sources, rows, width = rows_ref.shape
    per_half = rows // halves
    row_fetches = [
        pltpu.make_async_copy(
            rows_hbm.at[:, pl.ds(2 * pair * per_half, 2 * per_half)],
            rows_ref.at[:, pl.ds(2 * pair * per_half, 2 * per_half)],
            row_sems.at[pair],
        )
        for pair in range(halves // 2)
    ]
    gate_up_fetches = [
        pltpu.make_async_copy(gate_up_hbm.at[half], gate_up_ref.at[half], in_sems.at[0, half])
        for half in range(halves)
    ]
    down_fetches = [
        pltpu.make_async_copy(down_hbm.at[half], down_ref.at[half], in_sems.at[1, half])
        for half in range(halves)
    ]
    row_fetches[0].start()
    gate_up_fetches[0].start()
    down_fetches[0].start()
    copies = []
    for pair in range(halves // 2):
        both = pl.ds(2 * pair * per_half, 2 * per_half)
        row_fetches[pair].wait()
        if pair + 1 < halves // 2:
            row_fetches[pair + 1].start()
        arrived = rows_ref[:, both, :].astype(jnp.float32)
        results = []
        for member in range(2):
            half = 2 * pair + member
            own = arrived[:, member * per_half : (member + 1) * per_half]
            own = own.reshape(sources * per_half, width).astype(jnp.bfloat16)
            gate_up_fetches[half].wait()
            if half + 1 < halves:
                gate_up_fetches[half + 1].start()
                down_fetches[half + 1].start()
            act = silu_times(dot(own, gate_up_ref[half, 0]), dot(own, gate_up_ref[half, 1]))
            down_fetches[half].wait()
            results.append(dot(act, down_ref[half]).reshape(sources, per_half, width))
        out_ref[:, both, :] = jnp.concatenate(results, axis=1).astype(jnp.bfloat16)
        copy = pltpu.make_async_copy(out_ref.at[:, both], out_hbm.at[:, both], out_sems.at[pair])
        copy.start()
        copies.append(copy)
    for copy in copies:
        copy.wait()


def combine_kernel(z_ref, mix_ref, rows_ref, shared_ref, *refs):
    outs, sum_ref = refs[:Z_SIZE], refs[Z_SIZE]
    tokens = outs[0].shape[0]
    sum_ref[...] = dot(mix_ref[...], rows_ref[...]) + shared_ref[...].astype(jnp.float32)
    for step, out_ref in enumerate(outs):
        z = lax.rem(z_ref[0] + step, Z_SIZE)
        rows = pl.ds(pl.multiple_of(z * tokens, tokens), tokens)
        out_ref[...] = sum_ref[rows, :].astype(jnp.bfloat16)


def final_kernel(mixed_ref, *refs):
    total = mixed_ref[...]
    for part_ref in refs[:Z_SIZE]:
        total = total + part_ref[...].astype(jnp.float32)
    refs[Z_SIZE][...] = total.astype(jnp.bfloat16)


def reorder_kernel(me_ref, table_ref, from_ref, to_ref):
    me = me_ref[0]
    for block in range(to_ref.shape[0]):
        source = table_ref[block]
        z_steps = lax.rem(lax.div(me, PLANE) - lax.div(source, PLANE) + Z_SIZE, Z_SIZE)
        steps = lax.rem(lax.rem(me, PLANE) - lax.rem(source, PLANE) + PLANE, PLANE)
        to_ref[block] = from_ref[z_steps * PLANE + steps]


def params(mib=16):
    return pltpu.CompilerParams(vmem_limit_bytes=mib * MIB)


def cost(flops, moved):
    return pl.CostEstimate(flops=int(flops), bytes_accessed=int(moved), transcendentals=0)


def shards(
    queries,
    key_vectors,
    value_vectors,
    lengths,
    out_weight,
    residual,
    norm_gain,
    route_ids,
    route_logits,
    shared_gate_up,
    shared_down,
    expert_gate_up,
    expert_down,
    cache_blocks,
    block_table,
):
    tokens, width = residual.shape
    devices = lax.axis_size("seq")
    me = lax.axis_index("seq")
    z_index, plane_index = lax.div(me, PLANE), lax.rem(me, PLANE)
    z_groups = [[p + PLANE * z for z in range(Z_SIZE)] for p in range(PLANE)]
    planes = [[p + PLANE * z for p in range(PLANE)] for z in range(Z_SIZE)]
    bf16, f32 = jnp.bfloat16, jnp.float32
    shape = jax.ShapeDtypeStruct
    scalar = lambda value: jnp.reshape(value, (1,)).astype(jnp.int32)
    all_tokens = Z_SIZE * tokens
    part = width // Z_SIZE

    def exchange(array, groups):
        return lax.all_to_all(
            array, "seq", split_axis=0, concat_axis=0, tiled=True, axis_index_groups=groups
        )

    own_kv = jnp.concatenate([key_vectors, value_vectors], axis=1)
    behind = [from_behind(own_kv, "seq", offset) for offset in range(REACH, 0, -1)]

    turned_weight = lax.all_gather(
        out_weight.T, "seq", axis=0, tiled=True, axis_index_groups=planes
    )
    info = pl.pallas_call(
        route_kernel,
        out_shape=shape((tokens, 128), bf16),
        in_specs=[SMEM] + [VMEM] * 2,
        out_specs=VMEM,
        scratch_shapes=[pltpu.VMEM((128, 128), f32)],
        compiler_params=params(),
        cost_estimate=cost(MIB, MIB),
        name="route",
    )(scalar(z_index), route_ids.T, route_logits.T)

    def along_z(arrays):
        return [arrays[0]] + [
            lax.ppermute(arrays[step], "seq", z_pairs[step]) for step in range(1, Z_SIZE)
        ]

    z_pairs = [
        [
            (z * PLANE + p, (z + step) % Z_SIZE * PLANE + p)
            for z in range(Z_SIZE)
            for p in range(PLANE)
        ]
        for step in range(Z_SIZE)
    ]
    z_scalar = scalar(z_index)
    gain = norm_gain.reshape(1, width)
    own_shared = jnp.concatenate(
        [jnp.transpose(shared_gate_up, (1, 2, 0)).reshape(-1, width), shared_down], axis=0
    )

    sent_width = width + part + info.shape[1]
    sent = pl.pallas_call(
        attention_kernel,
        out_shape=[shape((tokens, sent_width), bf16)] * Z_SIZE,
        in_specs=[SMEM] * 3 + [VMEM] * 8,
        out_specs=[VMEM] * Z_SIZE,
        compiler_params=params(58),
        cost_estimate=cost(4 * tokens * 5 * tokens * width, 3 * MIB),
        name="attention",
    )(z_scalar, scalar(me * tokens), lengths, queries, *behind, own_kv, residual, info)

    sent, own_shared = lax.optimization_barrier((sent, own_shared))
    shared_weight = lax.all_gather(own_shared, "seq", axis=0, axis_index_groups=planes)
    gathered = along_z(sent)
    gathered, cache_blocks, expert_gate_up = lax.optimization_barrier(
        (gathered, cache_blocks, expert_gate_up)
    )

    _, block_tokens, layers, kv_heads, head_size = cache_blocks.shape
    per_device = block_tokens // devices
    cache_view = cache_blocks.reshape(Z_SIZE, PLANE, per_device * layers, kv_heads, head_size)
    in_plane = []
    for step in range(PLANE):
        piece = lax.dynamic_index_in_dim(
            cache_view, lax.rem(plane_index + step, PLANE), axis=1, keepdims=False
        )
        if step:
            pairs = [
                (z * PLANE + p, z * PLANE + (p + step) % PLANE)
                for z in range(Z_SIZE)
                for p in range(PLANE)
            ]
            piece = lax.ppermute(piece, "seq", pairs)
        in_plane.append(piece)
    gate_up = jnp.transpose(expert_gate_up, (0, 2, 1, 3))

    mixed_part, info = pl.pallas_call(
        project_kernel,
        out_shape=[shape((Z_SIZE, all_tokens, part), bf16), shape((all_tokens, 128), bf16)],
        in_specs=[SMEM] + [VMEM] * (Z_SIZE + 1),
        out_specs=[VMEM] * 2,
        scratch_shapes=[pltpu.VMEM((Z_SIZE, tokens, sent_width), bf16)],
        compiler_params=params(58),
        cost_estimate=cost(2 * all_tokens * width * part, 3 * MIB),
        name="project",
    )(z_scalar, *gathered, turned_weight)
    mixed = exchange(mixed_part, z_groups)

    local_halves, _, _, half_ff = expert_gate_up.shape
    per_half = Z_SIZE * CAP
    picked = local_halves * per_half
    onehot, mix = pl.pallas_call(
        tables_kernel,
        out_shape=[
            shape((PLANE * picked, all_tokens), bf16),
            shape((all_tokens, PLANE * picked), bf16),
        ],
        in_specs=[SMEM, VMEM],
        out_specs=[VMEM] * 2,
        compiler_params=params(),
        cost_estimate=cost(20 * PLANE * picked * all_tokens, MIB),
        name="tables",
    )(scalar(lax.rem(z_index, 2)), info)
    outgoing = pl.pallas_call(
        pick_kernel,
        out_shape=shape((PLANE, picked, width), bf16),
        in_specs=[VMEM] * 3,
        out_specs=HBM,
        scratch_shapes=[
            pltpu.VMEM((PLANE, picked, width), bf16),
            pltpu.SemaphoreType.DMA((PLANE,)),
        ],
        compiler_params=params(58),
        cost_estimate=cost(2 * PLANE * picked * all_tokens * width, 4 * MIB),
        name="pick",
    )(onehot, gain, mixed)

    outgoing, in_plane = lax.optimization_barrier((outgoing, in_plane))
    arrived = exchange(outgoing, planes)
    grouped = pl.pallas_call(
        regroup_kernel,
        out_shape=[shape((PLANE,) + in_plane[0].shape[1:], bf16)] * Z_SIZE,
        in_specs=[SMEM] + [VMEM] * PLANE,
        out_specs=[VMEM] * Z_SIZE,
        compiler_params=params(58),
        cost_estimate=cost(0, 2 * MIB),
        name="regroup",
    )(z_scalar, *in_plane)
    arrived_cache = [grouped[0]]
    for step in range(1, Z_SIZE):
        arrived_cache.append(lax.ppermute(grouped[step], "seq", z_pairs[step]))

    arrived, shared_weight = lax.optimization_barrier((arrived, shared_weight))
    shared_part, own_mixed = pl.pallas_call(
        shared_kernel,
        out_shape=[shape((all_tokens, width), bf16), shape((tokens, width), f32)],
        in_specs=[SMEM] + [VMEM] * 3,
        out_specs=[VMEM] * 2,
        compiler_params=params(24),
        cost_estimate=cost(6 * all_tokens * 256 * width, 5 * MIB),
        name="shared_expert",
    )(z_scalar, gain, mixed, shared_weight)

    returning = pl.pallas_call(
        experts_kernel,
        out_shape=shape((PLANE, picked, width), bf16),
        in_specs=[HBM, HBM, HBM],
        out_specs=HBM,
        scratch_shapes=[
            pltpu.VMEM((PLANE, picked, width), bf16),
            pltpu.VMEM((local_halves, 2, width, half_ff), bf16),
            pltpu.VMEM((local_halves, half_ff, width), bf16),
            pltpu.VMEM((PLANE, picked, width), bf16),
            pltpu.SemaphoreType.DMA((2, local_halves)),
            pltpu.SemaphoreType.DMA((local_halves // 2,)),
            pltpu.SemaphoreType.DMA((local_halves // 2,)),
        ],
        compiler_params=params(58),
        cost_estimate=cost(6 * PLANE * picked * half_ff * width, 14 * MIB),
        name="experts",
    )(arrived, gate_up, expert_down)
    returning, arrived_cache = lax.optimization_barrier((returning, arrived_cache))
    returned = exchange(returning, planes).reshape(PLANE * picked, width)

    arrived_cache = jnp.concatenate(arrived_cache)
    cache_out = pl.pallas_call(
        reorder_kernel,
        out_shape=shape(arrived_cache.shape, bf16),
        in_specs=[SMEM, SMEM, VMEM],
        out_specs=VMEM,
        compiler_params=params(),
        cost_estimate=cost(0, 2 * arrived_cache.size * 2),
        name="reorder",
    )(scalar(me), block_table, arrived_cache)
    cache_out = cache_out.reshape(devices, per_device, layers, kv_heads, head_size)

    sums = pl.pallas_call(
        combine_kernel,
        out_shape=[shape((tokens, width), bf16)] * Z_SIZE,
        in_specs=[SMEM] + [VMEM] * 3,
        out_specs=[VMEM] * Z_SIZE,
        scratch_shapes=[pltpu.VMEM((all_tokens, width), f32)],
        compiler_params=params(24),
        cost_estimate=cost(2 * all_tokens * PLANE * picked * width, 3 * MIB),
        name="combine",
    )(z_scalar, mix, returned, shared_part)
    layer_out = pl.pallas_call(
        final_kernel,
        out_shape=shape((tokens, width), bf16),
        in_specs=[VMEM] * (1 + Z_SIZE),
        out_specs=VMEM,
        compiler_params=params(),
        cost_estimate=cost(5 * tokens * width, 2 * MIB),
        name="final",
    )(own_mixed, *along_z(sums))
    return (layer_out, cache_out)


def solution(mesh):
    in_specs = (
        P("seq", "head"),
        P("seq", "head"),
        P("seq", "head"),
        P(),
        P("head", "seq"),
        P(("seq", "head"), None),
        P(),
        P(("seq", "head"), None),
        P(("seq", "head"), None),
        P(None, None, ("seq", "head")),
        P(("seq", "head"), None),
        P("seq", None, None, None),
        P("seq", None, None),
        P("seq", None, None, "head", None),
        P(),
    )
    out_specs = (P(("seq", "head"), None), P(None, "seq", None, "head", None))
    planes_fit = mesh.shape["seq"] == Z_SIZE * PLANE and mesh.shape["head"] == 1
    body = shards if planes_fit else general_shards
    return jax.shard_map(body, mesh=mesh, in_specs=in_specs, out_specs=out_specs, check_vma=False)
```

```python
import math

import jax
import jax.numpy as jnp
from jax import lax
from jax.experimental import pallas as pl
from jax.experimental.pallas import tpu as pltpu
from jax.sharding import PartitionSpec as P

HD = 128
EXPERTS = 64
TOP = 6
REACH = 4
HALVES = 128
CAP = 6
Z_SIZE = 4
PLANE = 8
MIB = 1024 * 1024


NEGATIVE = -1e30
EPSILON = 1e-05


def from_behind(shard, axis, by):
    devices = lax.axis_size(axis)
    pairs = [(i, i + by) for i in range(devices) if 0 <= i + by < devices]
    return lax.ppermute(shard, axis, pairs)


def segment_of(positions, lengths):
    request_ends = jnp.cumsum(lengths)
    passed = (request_ends[None, :] <= positions[:, None]).astype(jnp.int32)
    return jnp.sum(passed, axis=1)


def shared_ffn(rows_in, gate_up_part, down_part):
    shared_both = jnp.einsum(
        "td,dcf->tcf", rows_in, gate_up_part, preferred_element_type=jnp.float32
    )
    shared_act = (jax.nn.silu(shared_both[:, 0]) * shared_both[:, 1]).astype(jnp.bfloat16)
    return jnp.dot(shared_act, down_part, preferred_element_type=jnp.float32)


def general_shards(
    queries,
    key_vectors,
    value_vectors,
    lengths,
    out_weight,
    residual,
    norm_gain,
    route_ids,
    route_logits,
    shared_gate_up,
    shared_down,
    expert_gate_up,
    expert_down,
    cache_blocks,
    block_table,
):
    handed = lax.all_to_all(cache_blocks, "seq", split_axis=1, concat_axis=0, tiled=True)
    cache_out = jnp.take(handed, block_table, axis=0)
    tok_rows = queries.shape[0]
    seq_index = lax.axis_index("seq")
    earlier = [
        from_behind((key_vectors, value_vectors), "seq", offset) for offset in range(REACH, 0, -1)
    ]
    window_keys = jnp.concatenate([member[0] for member in earlier] + [key_vectors], axis=0)
    window_values = jnp.concatenate([member[1] for member in earlier] + [value_vectors], axis=0)
    key_count = window_keys.shape[0]
    kv_heads = key_vectors.shape[1] // HD
    query_heads = queries.shape[1] // HD
    group_size = query_heads // kv_heads
    query_pos = seq_index * tok_rows + jnp.arange(tok_rows, dtype=jnp.int32)
    key_pos = (seq_index - REACH) * tok_rows + jnp.arange(key_count, dtype=jnp.int32)
    visible = (key_pos[None, :] >= 0) & (key_pos[None, :] <= query_pos[:, None])
    visible = visible & (
        segment_of(key_pos, lengths)[None, :] == segment_of(query_pos, lengths)[:, None]
    )
    query_part = queries.reshape(tok_rows, kv_heads, group_size, HD)
    key_part = window_keys.reshape(key_count, kv_heads, HD)
    value_part = window_values.reshape(key_count, kv_heads, HD)
    scores = jnp.einsum(
        "tkgd,wkd->kgtw", query_part, key_part, preferred_element_type=jnp.float32
    ) * (1.0 / math.sqrt(HD))
    scores = jnp.where(visible[None, None], scores, NEGATIVE)
    row_max = jnp.max(scores, axis=-1, keepdims=True)
    weights = jnp.exp(scores - row_max)
    row_total = jnp.sum(weights, axis=-1)
    weighted = jnp.einsum(
        "kgtw,wkd->tkgd",
        weights.astype(jnp.bfloat16),
        value_part,
        preferred_element_type=jnp.float32,
    )
    heads = (weighted / jnp.transpose(row_total, (2, 0, 1))[..., None]).astype(jnp.bfloat16)
    heads = heads.reshape(tok_rows, query_heads * HD)
    partial_out = jnp.dot(
        heads,
        lax.all_gather(out_weight, "seq", axis=1, tiled=True),
        preferred_element_type=jnp.float32,
    )
    attn_out = lax.psum_scatter(partial_out, "head", scatter_dimension=0, tiled=True)
    mixed = residual.astype(jnp.float32) + attn_out
    mean_square = jnp.mean(mixed * mixed, axis=-1, keepdims=True)
    normed = (mixed * lax.rsqrt(mean_square + EPSILON) * norm_gain).astype(jnp.bfloat16)
    gate_up_all, down_all = (
        lax.all_gather(shared_gate_up, ("seq", "head"), axis=2, tiled=True),
        lax.all_gather(shared_down, ("seq", "head"), axis=0, tiled=True),
    )
    shared_part = shared_ffn(normed, gate_up_all, down_all)
    own_tokens = normed.shape[0]
    width_model = normed.shape[1]
    flat_ids = route_ids.reshape(-1)
    onehot = (flat_ids[:, None] == jnp.arange(EXPERTS, dtype=jnp.int32)[None, :]).astype(jnp.int32)
    slot_rank = jnp.sum((jnp.cumsum(onehot, axis=0) - 1) * onehot, axis=1)
    first_slot = flat_ids * CAP + slot_rank
    second_slot = (flat_ids + EXPERTS) * CAP + slot_rank
    token_of = jnp.arange(flat_ids.shape[0], dtype=jnp.int32) // TOP
    routed_rows = normed[token_of]
    outgoing = jnp.zeros((HALVES * CAP, width_model), jnp.bfloat16)
    outgoing = outgoing.at[jnp.concatenate([first_slot, second_slot])].set(
        jnp.concatenate([routed_rows, routed_rows], axis=0)
    )
    local_halves = expert_gate_up.shape[0]
    outgoing = outgoing.reshape(HALVES // local_halves, local_halves, CAP, width_model)
    gate_up = jnp.einsum(
        "nsjd,sdcf->nsjcf",
        lax.all_to_all(outgoing, "seq", split_axis=0, concat_axis=0, tiled=True),
        expert_gate_up,
        preferred_element_type=jnp.float32,
    )
    expert_act = (jax.nn.silu(gate_up[:, :, :, 0]) * gate_up[:, :, :, 1]).astype(jnp.bfloat16)
    half_out = jnp.einsum(
        "nsjf,sfd->nsjd", expert_act, expert_down, preferred_element_type=jnp.float32
    ).astype(jnp.bfloat16)
    returned = lax.all_to_all(half_out, "seq", split_axis=0, concat_axis=0, tiled=True)
    returned = returned.reshape(HALVES * CAP, width_model)
    pair_sum = returned[first_slot].astype(jnp.float32) + returned[second_slot].astype(jnp.float32)
    route_probs = jax.nn.softmax(route_logits, axis=-1)
    routed = jnp.sum(
        route_probs[:, :, None] * pair_sum.reshape(own_tokens, TOP, width_model), axis=1
    )
    layer_out = (mixed + shared_part + routed).astype(jnp.bfloat16)
    return (layer_out, cache_out)


VMEM = pl.BlockSpec(memory_space=pltpu.VMEM)
SMEM = pl.BlockSpec(memory_space=pltpu.SMEM)
HBM = pl.BlockSpec(memory_space=pltpu.HBM)


def dot_rows(left, right):
    return lax.dot_general(left, right, (((1,), (1,)), ((), ())), preferred_element_type=jnp.float32)


def dot(left, right):
    return jnp.dot(left, right, preferred_element_type=jnp.float32)


def silu_times(gate, up):
    return (gate / (1.0 + jnp.exp(-gate)) * up).astype(jnp.bfloat16)


def attention_kernel(
    z_ref,
    first_ref,
    lengths_ref,
    q_ref,
    k4_ref,
    k3_ref,
    k2_ref,
    k1_ref,
    own_ref,
    residual_ref,
    info_ref,
    *out_refs,
):
    tokens, width = q_ref.shape
    part = width // Z_SIZE
    kv_width = own_ref.shape[1] // 2
    kv_heads = kv_width // HD
    group = width // HD // kv_heads
    blocks = [k4_ref, k3_ref, k2_ref, k1_ref, own_ref]
    keys = len(blocks) * tokens
    first = first_ref[0]
    query_pos = first + lax.broadcasted_iota(jnp.int32, (tokens, keys), 0)
    key_pos = first - (keys - tokens) + lax.broadcasted_iota(jnp.int32, (tokens, keys), 1)
    start = jnp.zeros((tokens, keys), jnp.int32)
    end = jnp.int32(0)
    for request in range(lengths_ref.shape[0]):
        end = end + lengths_ref[request]
        start = jnp.maximum(start, jnp.where(query_pos >= end, end, 0))
    hidden = jnp.where((key_pos >= start) & (key_pos <= query_pos), 0.0, NEGATIVE)
    hidden = jnp.concatenate([hidden] * group, axis=0)
    scale = 1.0 / math.sqrt(HD)
    for step, out_ref in enumerate(out_refs):
        z = lax.rem(z_ref[0] + step, Z_SIZE)
        for column in range(Z_SIZE):

            @pl.when(z == column)
            def _(column=column, out_ref=out_ref):
                columns = slice(column * part, (column + 1) * part)
                out_ref[:, width : width + part] = residual_ref[:, columns]

        out_ref[:, width + part :] = info_ref[...]
    for kv in range(kv_heads):
        at = slice(kv * HD, (kv + 1) * HD)
        value_at = slice(kv_width + kv * HD, kv_width + (kv + 1) * HD)
        key = jnp.concatenate([block[:, at] for block in blocks], axis=0)
        value = jnp.concatenate([block[:, value_at] for block in blocks], axis=0)
        heads = [kv * group + member for member in range(group)]
        query = jnp.concatenate([q_ref[:, h * HD : (h + 1) * HD] for h in heads], axis=0)
        scores = dot_rows(query, key) * scale + hidden
        weights = jnp.exp(scores - jnp.max(scores, axis=-1, keepdims=True))
        total = jnp.sum(weights, axis=-1, keepdims=True)
        result = (dot(weights.astype(jnp.bfloat16), value) / total).astype(jnp.bfloat16)
        for member, h in enumerate(heads):
            for out_ref in out_refs:
                out_ref[:, h * HD : (h + 1) * HD] = result[member * tokens : (member + 1) * tokens]


def route_kernel(z_ref, ids_ref, logits_ref, out_ref, turned_ref):
    choices, tokens = ids_ref.shape
    turned_ref[...] = jnp.zeros(turned_ref.shape, jnp.float32)
    turned_ref[:choices, :tokens] = ids_ref[...].astype(jnp.float32)
    turned_ref[8 : 8 + choices, :tokens] = logits_ref[...]
    table = turned_ref[...].T[:tokens]
    lane = lax.broadcasted_iota(jnp.int32, table.shape, 1)
    ids = [table[:, c : c + 1].astype(jnp.int32) for c in range(choices)]
    logits = [table[:, 8 + c : 9 + c] for c in range(choices)]
    member = jnp.zeros(table.shape, jnp.float32)
    for one in ids:
        member = jnp.where(lane == one, 1.0, member)
    row = lax.broadcasted_iota(jnp.int32, (tokens, tokens), 0)
    earlier = jnp.where(lax.broadcasted_iota(jnp.int32, (tokens, tokens), 1) < row, 1.0, 0.0)
    ahead = dot(earlier.astype(jnp.bfloat16), member.astype(jnp.bfloat16))
    top = logits[0]
    for one in logits[1:]:
        top = jnp.maximum(top, one)
    powers = [jnp.exp(one - top) for one in logits]
    total = sum(powers[1:], powers[0])
    per_device = EXPERTS // 2 // PLANE
    out = jnp.zeros(table.shape, jnp.float32)
    for c, one in enumerate(ids):
        rank = jnp.sum(jnp.where(lane == one, ahead, 0.0), axis=1, keepdims=True)
        where_to = lax.div(one, per_device).astype(jnp.float32)
        first = (lax.rem(one, per_device) * Z_SIZE + z_ref[0]) * CAP
        out = jnp.where(lane == c, where_to, out)
        out = jnp.where(lane == 8 + c, first.astype(jnp.float32) + rank, out)
        out = jnp.where(lane == 16 + c, powers[c] / total, out)
    out_ref[...] = out.astype(jnp.bfloat16)


def regroup_kernel(z_ref, *refs):
    pieces, outs = refs[:PLANE], refs[PLANE:]
    for step, out in enumerate(outs):
        z = lax.rem(z_ref[0] + step, Z_SIZE)
        for at, piece in enumerate(pieces):
            out[at] = piece[z]


def source_z(z_ref, step):
    return lax.rem(z_ref[0] + Z_SIZE - step, Z_SIZE)


def project_kernel(z_ref, *refs):
    sent = refs[:Z_SIZE]
    weight_ref, mixed_ref, info_ref, rows_ref = refs[Z_SIZE:]
    for step, sent_ref in enumerate(sent):
        rows_ref[source_z(z_ref, step)] = sent_ref[...]
    rows = jnp.concatenate([rows_ref[z] for z in range(Z_SIZE)], axis=0)
    part, width = weight_ref.shape
    out = dot_rows(rows[:, :width], weight_ref[...])
    mixed = (out + rows[:, width : width + part].astype(jnp.float32)).astype(jnp.bfloat16)
    for z in range(Z_SIZE):
        mixed_ref[z] = mixed
    info_ref[...] = rows[:, width + part :]


def row_codes(info, first, parity, per_device):
    where_to = info(first).astype(jnp.int32) - PLANE * parity
    inside = info(first + 8).astype(jnp.int32)
    fits = (where_to >= 0) & (where_to < PLANE)
    return jnp.where(fits, where_to * per_device + inside, -1)


def tables_kernel(parity_ref, info_ref, onehot_ref, mix_ref):
    rows, tokens = onehot_ref.shape
    info = info_ref[...].astype(jnp.float32)
    turned = info.T
    codes = row_codes(lambda at: turned[at : at + 8], 0, parity_ref[0], rows // PLANE)
    row = lax.broadcasted_iota(jnp.int32, (rows, tokens), 0)
    chosen = codes[0:1, :] == row
    for choice in range(1, TOP):
        chosen = chosen | (codes[choice : choice + 1, :] == row)
    onehot_ref[...] = jnp.where(chosen, 1.0, 0.0).astype(jnp.bfloat16)
    column = lax.broadcasted_iota(jnp.int32, mix_ref.shape, 1)
    mix = jnp.zeros(mix_ref.shape, jnp.float32)
    for choice in range(TOP):
        code = row_codes(lambda at: info[:, at : at + 1], choice, parity_ref[0], rows // PLANE)
        mix = jnp.where(code == column, info[:, 16 + choice : 17 + choice], mix)
    mix_ref[...] = mix.astype(jnp.bfloat16)


def norm(mixed_ref, gain_ref):
    mixed = jnp.concatenate([mixed_ref[z] for z in range(Z_SIZE)], axis=1).astype(jnp.float32)
    mean_square = jnp.mean(mixed * mixed, axis=-1, keepdims=True)
    return (mixed * lax.rsqrt(mean_square + EPSILON) * gain_ref[...]).astype(jnp.bfloat16)


def pick_kernel(onehot_ref, gain_ref, mixed_ref, out_hbm, out_ref, sems):
    normed = norm(mixed_ref, gain_ref)
    picked = out_ref.shape[1]
    copies = []
    for p in range(PLANE):
        onehot = onehot_ref[p * picked : (p + 1) * picked]
        out_ref[p] = dot(onehot, normed).astype(jnp.bfloat16)
        copy = pltpu.make_async_copy(out_ref.at[p], out_hbm.at[p], sems.at[p])
        copy.start()
        copies.append(copy)
    for copy in copies:
        copy.wait()


def shared_kernel(z_ref, gain_ref, mixed_ref, weight_ref, out_ref, own_ref):
    tokens, columns = own_ref.shape[0], mixed_ref.shape[2]
    own = pl.ds(pl.multiple_of(z_ref[0] * tokens, tokens), tokens)
    for z in range(Z_SIZE):
        own_ref[:, z * columns : (z + 1) * columns] = mixed_ref[z, own, :].astype(jnp.float32)
    parts, units, _ = weight_ref.shape
    units = units // 3
    gate_weight, up_weight, down_weight = [
        jnp.concatenate([weight_ref[p, at * units : (at + 1) * units] for p in range(parts)], axis=0)
        for at in range(3)
    ]
    rows = norm(mixed_ref, gain_ref)
    act = silu_times(dot_rows(rows, gate_weight), dot_rows(rows, up_weight))
    out_ref[...] = dot(act, down_weight).astype(jnp.bfloat16)


def hold_kernel(*refs):
    count = (len(refs) + 1) // 2
    copies = []
    for from_ref, to_ref in zip(refs[: count - 1], refs[count - 1 : -1]):
        for at in range(to_ref.shape[0]):
            copy = pltpu.make_async_copy(from_ref.at[at], to_ref.at[at], refs[-1].at[len(copies)])
            copy.start()
            copies.append(copy)
    for copy in copies:
        copy.wait()


def experts_kernel(rows_ref, gate_up_ref, down_ref, out_hbm, out_ref, out_sems):
    halves = gate_up_ref.shape[0]
    sources, rows, width = rows_ref.shape
    per_half = rows // halves
    copies = []
    for pair in range(halves // 2):
        both = pl.ds(2 * pair * per_half, 2 * per_half)
        arrived = rows_ref[:, both, :].astype(jnp.float32)
        results = []
        for member in range(2):
            half = 2 * pair + member
            own = arrived[:, member * per_half : (member + 1) * per_half]
            own = own.reshape(sources * per_half, width).astype(jnp.bfloat16)
            act = silu_times(dot(own, gate_up_ref[half, 0]), dot(own, gate_up_ref[half, 1]))
            results.append(dot(act, down_ref[half]).reshape(sources, per_half, width))
        out_ref[:, both, :] = jnp.concatenate(results, axis=1).astype(jnp.bfloat16)
        copy = pltpu.make_async_copy(out_ref.at[:, both], out_hbm.at[:, both], out_sems.at[pair])
        copy.start()
        copies.append(copy)
    for copy in copies:
        copy.wait()


def combine_kernel(z_ref, mix_ref, rows_ref, shared_ref, *refs):
    outs, sum_ref = refs[:Z_SIZE], refs[Z_SIZE]
    tokens = outs[0].shape[0]
    sum_ref[...] = dot(mix_ref[...], rows_ref[...]) + shared_ref[...].astype(jnp.float32)
    for step, out_ref in enumerate(outs):
        z = lax.rem(z_ref[0] + step, Z_SIZE)
        rows = pl.ds(pl.multiple_of(z * tokens, tokens), tokens)
        out_ref[...] = sum_ref[rows, :].astype(jnp.bfloat16)


def final_kernel(mixed_ref, *refs):
    total = mixed_ref[...]
    for part_ref in refs[:Z_SIZE]:
        total = total + part_ref[...].astype(jnp.float32)
    refs[Z_SIZE][...] = total.astype(jnp.bfloat16)


def reorder_kernel(me_ref, table_ref, from_ref, to_ref):
    me = me_ref[0]
    for block in range(to_ref.shape[0]):
        source = table_ref[block]
        z_steps = lax.rem(lax.div(me, PLANE) - lax.div(source, PLANE) + Z_SIZE, Z_SIZE)
        steps = lax.rem(lax.rem(me, PLANE) - lax.rem(source, PLANE) + PLANE, PLANE)
        to_ref[block] = from_ref[z_steps * PLANE + steps]


def params(mib=16):
    return pltpu.CompilerParams(vmem_limit_bytes=mib * MIB)


def cost(flops, moved):
    return pl.CostEstimate(flops=int(flops), bytes_accessed=int(moved), transcendentals=0)


def shards(
    queries,
    key_vectors,
    value_vectors,
    lengths,
    out_weight,
    residual,
    norm_gain,
    route_ids,
    route_logits,
    shared_gate_up,
    shared_down,
    expert_gate_up,
    expert_down,
    cache_blocks,
    block_table,
):
    tokens, width = residual.shape
    devices = lax.axis_size("seq")
    me = lax.axis_index("seq")
    z_index, plane_index = lax.div(me, PLANE), lax.rem(me, PLANE)
    z_groups = [[p + PLANE * z for z in range(Z_SIZE)] for p in range(PLANE)]
    planes = [[p + PLANE * z for p in range(PLANE)] for z in range(Z_SIZE)]
    bf16, f32 = jnp.bfloat16, jnp.float32
    shape = jax.ShapeDtypeStruct
    scalar = lambda value: jnp.reshape(value, (1,)).astype(jnp.int32)
    all_tokens = Z_SIZE * tokens
    part = width // Z_SIZE

    def exchange(array, groups):
        return lax.all_to_all(
            array, "seq", split_axis=0, concat_axis=0, tiled=True, axis_index_groups=groups
        )

    own_kv = jnp.concatenate([key_vectors, value_vectors], axis=1)
    behind = [from_behind(own_kv, "seq", offset) for offset in range(REACH, 0, -1)]

    turned_weight = lax.all_gather(
        out_weight.T, "seq", axis=0, tiled=True, axis_index_groups=planes
    )
    info = pl.pallas_call(
        route_kernel,
        out_shape=shape((tokens, 128), bf16),
        in_specs=[SMEM] + [VMEM] * 2,
        out_specs=VMEM,
        scratch_shapes=[pltpu.VMEM((128, 128), f32)],
        compiler_params=params(),
        cost_estimate=cost(MIB, MIB),
        name="route",
    )(scalar(z_index), route_ids.T, route_logits.T)

    def along_z(arrays):
        return [arrays[0]] + [
            lax.ppermute(arrays[step], "seq", z_pairs[step]) for step in range(1, Z_SIZE)
        ]

    z_pairs = [
        [
            (z * PLANE + p, (z + step) % Z_SIZE * PLANE + p)
            for z in range(Z_SIZE)
            for p in range(PLANE)
        ]
        for step in range(Z_SIZE)
    ]
    z_scalar = scalar(z_index)
    gain = norm_gain.reshape(1, width)
    own_shared = jnp.concatenate(
        [jnp.transpose(shared_gate_up, (1, 2, 0)).reshape(-1, width), shared_down], axis=0
    )

    sent_width = width + part + info.shape[1]
    sent = pl.pallas_call(
        attention_kernel,
        out_shape=[shape((tokens, sent_width), bf16)] * Z_SIZE,
        in_specs=[SMEM] * 3 + [VMEM] * 8,
        out_specs=[VMEM] * Z_SIZE,
        compiler_params=params(58),
        cost_estimate=cost(4 * tokens * 5 * tokens * width, 3 * MIB),
        name="attention",
    )(z_scalar, scalar(me * tokens), lengths, queries, *behind, own_kv, residual, info)

    sent, own_shared = lax.optimization_barrier((sent, own_shared))
    shared_weight = lax.all_gather(own_shared, "seq", axis=0, axis_index_groups=planes)
    gathered = along_z(sent)
    gathered, cache_blocks, expert_gate_up = lax.optimization_barrier(
        (gathered, cache_blocks, expert_gate_up)
    )

    _, block_tokens, layers, kv_heads, head_size = cache_blocks.shape
    per_device = block_tokens // devices
    cache_view = cache_blocks.reshape(Z_SIZE, PLANE, per_device * layers, kv_heads, head_size)
    in_plane = []
    for step in range(PLANE):
        piece = lax.dynamic_index_in_dim(
            cache_view, lax.rem(plane_index + step, PLANE), axis=1, keepdims=False
        )
        if step:
            pairs = [
                (z * PLANE + p, z * PLANE + (p + step) % PLANE)
                for z in range(Z_SIZE)
                for p in range(PLANE)
            ]
            piece = lax.ppermute(piece, "seq", pairs)
        in_plane.append(piece)
    gate_up = jnp.transpose(expert_gate_up, (0, 2, 1, 3))

    mixed_part, info = pl.pallas_call(
        project_kernel,
        out_shape=[pltpu.HBM((Z_SIZE, all_tokens, part), bf16), shape((all_tokens, 128), bf16)],
        in_specs=[SMEM] + [VMEM] * (Z_SIZE + 1),
        out_specs=[VMEM] * 2,
        scratch_shapes=[pltpu.VMEM((Z_SIZE, tokens, sent_width), bf16)],
        compiler_params=params(),
        cost_estimate=cost(2 * all_tokens * width * part, 3 * MIB),
        name="project",
    )(z_scalar, *gathered, turned_weight)
    mixed = exchange(mixed_part, z_groups)

    local_halves, _, _, half_ff = expert_gate_up.shape
    per_half = Z_SIZE * CAP
    picked = local_halves * per_half
    onehot, mix = pl.pallas_call(
        tables_kernel,
        out_shape=[
            shape((PLANE * picked, all_tokens), bf16),
            shape((all_tokens, PLANE * picked), bf16),
        ],
        in_specs=[SMEM, VMEM],
        out_specs=[VMEM] * 2,
        compiler_params=params(),
        cost_estimate=cost(20 * PLANE * picked * all_tokens, MIB),
        name="tables",
    )(scalar(lax.rem(z_index, 2)), info)
    outgoing = pl.pallas_call(
        pick_kernel,
        out_shape=pltpu.HBM((PLANE, picked, width), bf16),
        in_specs=[VMEM] * 3,
        out_specs=HBM,
        scratch_shapes=[
            pltpu.VMEM((PLANE, picked, width), bf16),
            pltpu.SemaphoreType.DMA((PLANE,)),
        ],
        compiler_params=params(),
        cost_estimate=cost(2 * PLANE * picked * all_tokens * width, 4 * MIB),
        name="pick",
    )(onehot, gain, mixed)

    outgoing, in_plane = lax.optimization_barrier((outgoing, in_plane))
    arrived = exchange(outgoing, planes)
    grouped = pl.pallas_call(
        regroup_kernel,
        out_shape=[shape((PLANE,) + in_plane[0].shape[1:], bf16)] * Z_SIZE,
        in_specs=[SMEM] + [VMEM] * PLANE,
        out_specs=[VMEM] * Z_SIZE,
        compiler_params=params(),
        cost_estimate=cost(0, 2 * MIB),
        name="regroup",
    )(z_scalar, *in_plane)
    grouped, gate_up, expert_down = lax.optimization_barrier((grouped, gate_up, expert_down))
    gate_up, down = pl.pallas_call(
        hold_kernel,
        out_shape=[pltpu.VMEM(gate_up.shape, bf16), pltpu.VMEM(expert_down.shape, bf16)],
        in_specs=[HBM] * 2,
        out_specs=[VMEM] * 2,
        scratch_shapes=[pltpu.SemaphoreType.DMA((2 * local_halves,))],
        compiler_params=params(4),
        cost_estimate=cost(0, 18 * MIB),
        name="hold",
    )(gate_up, expert_down)
    arrived_cache = [grouped[0]]
    for step in range(1, Z_SIZE):
        arrived_cache.append(lax.ppermute(grouped[step], "seq", z_pairs[step]))

    arrived, gate_up, down, shared_weight = lax.optimization_barrier(
        (arrived, gate_up, down, shared_weight)
    )
    shared_part, own_mixed = pl.pallas_call(
        shared_kernel,
        out_shape=[shape((all_tokens, width), bf16), shape((tokens, width), f32)],
        in_specs=[SMEM] + [VMEM] * 3,
        out_specs=[VMEM] * 2,
        compiler_params=params(24),
        cost_estimate=cost(6 * all_tokens * 256 * width, 5 * MIB),
        name="shared_expert",
    )(z_scalar, gain, mixed, shared_weight)

    returning = pl.pallas_call(
        experts_kernel,
        out_shape=pltpu.HBM((PLANE, picked, width), bf16),
        in_specs=[VMEM] * 3,
        out_specs=HBM,
        scratch_shapes=[
            pltpu.VMEM((PLANE, picked, width), bf16),
            pltpu.SemaphoreType.DMA((local_halves // 2,)),
        ],
        compiler_params=params(20),
        cost_estimate=cost(6 * PLANE * picked * half_ff * width, 14 * MIB),
        name="experts",
    )(arrived, gate_up, down)
    returning, arrived_cache = lax.optimization_barrier((returning, arrived_cache))
    returned = exchange(returning, planes).reshape(PLANE * picked, width)

    arrived_cache = jnp.concatenate(arrived_cache)
    cache_out = pl.pallas_call(
        reorder_kernel,
        out_shape=shape(arrived_cache.shape, bf16),
        in_specs=[SMEM, SMEM, VMEM],
        out_specs=VMEM,
        compiler_params=params(),
        cost_estimate=cost(0, 2 * arrived_cache.size * 2),
        name="reorder",
    )(scalar(me), block_table, arrived_cache)
    cache_out = cache_out.reshape(devices, per_device, layers, kv_heads, head_size)

    sums = pl.pallas_call(
        combine_kernel,
        out_shape=[shape((tokens, width), bf16)] * Z_SIZE,
        in_specs=[SMEM] + [VMEM] * 3,
        out_specs=[VMEM] * Z_SIZE,
        scratch_shapes=[pltpu.VMEM((all_tokens, width), f32)],
        compiler_params=params(24),
        cost_estimate=cost(2 * all_tokens * PLANE * picked * width, 3 * MIB),
        name="combine",
    )(z_scalar, mix, returned, shared_part)
    layer_out = pl.pallas_call(
        final_kernel,
        out_shape=shape((tokens, width), bf16),
        in_specs=[VMEM] * (1 + Z_SIZE),
        out_specs=VMEM,
        compiler_params=params(),
        cost_estimate=cost(5 * tokens * width, 2 * MIB),
        name="final",
    )(own_mixed, *along_z(sums))
    return (layer_out, cache_out)


def solution(mesh):
    in_specs = (
        P("seq", "head"),
        P("seq", "head"),
        P("seq", "head"),
        P(),
        P("head", "seq"),
        P(("seq", "head"), None),
        P(),
        P(("seq", "head"), None),
        P(("seq", "head"), None),
        P(None, None, ("seq", "head")),
        P(("seq", "head"), None),
        P("seq", None, None, None),
        P("seq", None, None),
        P("seq", None, None, "head", None),
        P(),
    )
    out_specs = (P(("seq", "head"), None), P(None, "seq", None, "head", None))
    planes_fit = mesh.shape["seq"] == Z_SIZE * PLANE and mesh.shape["head"] == 1
    body = shards if planes_fit else general_shards
    return jax.shard_map(body, mesh=mesh, in_specs=in_specs, out_specs=out_specs, check_vma=False)
```

```python
import math

import jax
import jax.numpy as jnp
from jax import lax
from jax.experimental import pallas as pl
from jax.experimental.pallas import tpu as pltpu
from jax.sharding import PartitionSpec as P

HD = 128
EXPERTS = 64
TOP = 6
REACH = 4
HALVES = 128
CAP = 6
Z_SIZE = 4
PLANE = 8
MIB = 1024 * 1024


NEGATIVE = -1e30
EPSILON = 1e-05


def from_behind(shard, axis, by):
    devices = lax.axis_size(axis)
    pairs = [(i, i + by) for i in range(devices) if 0 <= i + by < devices]
    return lax.ppermute(shard, axis, pairs)


def segment_of(positions, lengths):
    request_ends = jnp.cumsum(lengths)
    passed = (request_ends[None, :] <= positions[:, None]).astype(jnp.int32)
    return jnp.sum(passed, axis=1)


def shared_ffn(rows_in, gate_up_part, down_part):
    shared_both = jnp.einsum(
        "td,dcf->tcf", rows_in, gate_up_part, preferred_element_type=jnp.float32
    )
    shared_act = (jax.nn.silu(shared_both[:, 0]) * shared_both[:, 1]).astype(jnp.bfloat16)
    return jnp.dot(shared_act, down_part, preferred_element_type=jnp.float32)


def general_shards(
    queries,
    key_vectors,
    value_vectors,
    lengths,
    out_weight,
    residual,
    norm_gain,
    route_ids,
    route_logits,
    shared_gate_up,
    shared_down,
    expert_gate_up,
    expert_down,
    cache_blocks,
    block_table,
):
    handed = lax.all_to_all(cache_blocks, "seq", split_axis=1, concat_axis=0, tiled=True)
    cache_out = jnp.take(handed, block_table, axis=0)
    tok_rows = queries.shape[0]
    seq_index = lax.axis_index("seq")
    earlier = [
        from_behind((key_vectors, value_vectors), "seq", offset) for offset in range(REACH, 0, -1)
    ]
    window_keys = jnp.concatenate([member[0] for member in earlier] + [key_vectors], axis=0)
    window_values = jnp.concatenate([member[1] for member in earlier] + [value_vectors], axis=0)
    key_count = window_keys.shape[0]
    kv_heads = key_vectors.shape[1] // HD
    query_heads = queries.shape[1] // HD
    group_size = query_heads // kv_heads
    query_pos = seq_index * tok_rows + jnp.arange(tok_rows, dtype=jnp.int32)
    key_pos = (seq_index - REACH) * tok_rows + jnp.arange(key_count, dtype=jnp.int32)
    visible = (key_pos[None, :] >= 0) & (key_pos[None, :] <= query_pos[:, None])
    visible = visible & (
        segment_of(key_pos, lengths)[None, :] == segment_of(query_pos, lengths)[:, None]
    )
    query_part = queries.reshape(tok_rows, kv_heads, group_size, HD)
    key_part = window_keys.reshape(key_count, kv_heads, HD)
    value_part = window_values.reshape(key_count, kv_heads, HD)
    scores = jnp.einsum(
        "tkgd,wkd->kgtw", query_part, key_part, preferred_element_type=jnp.float32
    ) * (1.0 / math.sqrt(HD))
    scores = jnp.where(visible[None, None], scores, NEGATIVE)
    row_max = jnp.max(scores, axis=-1, keepdims=True)
    weights = jnp.exp(scores - row_max)
    row_total = jnp.sum(weights, axis=-1)
    weighted = jnp.einsum(
        "kgtw,wkd->tkgd",
        weights.astype(jnp.bfloat16),
        value_part,
        preferred_element_type=jnp.float32,
    )
    heads = (weighted / jnp.transpose(row_total, (2, 0, 1))[..., None]).astype(jnp.bfloat16)
    heads = heads.reshape(tok_rows, query_heads * HD)
    partial_out = jnp.dot(
        heads,
        lax.all_gather(out_weight, "seq", axis=1, tiled=True),
        preferred_element_type=jnp.float32,
    )
    attn_out = lax.psum_scatter(partial_out, "head", scatter_dimension=0, tiled=True)
    mixed = residual.astype(jnp.float32) + attn_out
    mean_square = jnp.mean(mixed * mixed, axis=-1, keepdims=True)
    normed = (mixed * lax.rsqrt(mean_square + EPSILON) * norm_gain).astype(jnp.bfloat16)
    gate_up_all, down_all = (
        lax.all_gather(shared_gate_up, ("seq", "head"), axis=2, tiled=True),
        lax.all_gather(shared_down, ("seq", "head"), axis=0, tiled=True),
    )
    shared_part = shared_ffn(normed, gate_up_all, down_all)
    own_tokens = normed.shape[0]
    width_model = normed.shape[1]
    flat_ids = route_ids.reshape(-1)
    onehot = (flat_ids[:, None] == jnp.arange(EXPERTS, dtype=jnp.int32)[None, :]).astype(jnp.int32)
    slot_rank = jnp.sum((jnp.cumsum(onehot, axis=0) - 1) * onehot, axis=1)
    first_slot = flat_ids * CAP + slot_rank
    second_slot = (flat_ids + EXPERTS) * CAP + slot_rank
    token_of = jnp.arange(flat_ids.shape[0], dtype=jnp.int32) // TOP
    routed_rows = normed[token_of]
    outgoing = jnp.zeros((HALVES * CAP, width_model), jnp.bfloat16)
    outgoing = outgoing.at[jnp.concatenate([first_slot, second_slot])].set(
        jnp.concatenate([routed_rows, routed_rows], axis=0)
    )
    local_halves = expert_gate_up.shape[0]
    outgoing = outgoing.reshape(HALVES // local_halves, local_halves, CAP, width_model)
    gate_up = jnp.einsum(
        "nsjd,sdcf->nsjcf",
        lax.all_to_all(outgoing, "seq", split_axis=0, concat_axis=0, tiled=True),
        expert_gate_up,
        preferred_element_type=jnp.float32,
    )
    expert_act = (jax.nn.silu(gate_up[:, :, :, 0]) * gate_up[:, :, :, 1]).astype(jnp.bfloat16)
    half_out = jnp.einsum(
        "nsjf,sfd->nsjd", expert_act, expert_down, preferred_element_type=jnp.float32
    ).astype(jnp.bfloat16)
    returned = lax.all_to_all(half_out, "seq", split_axis=0, concat_axis=0, tiled=True)
    returned = returned.reshape(HALVES * CAP, width_model)
    pair_sum = returned[first_slot].astype(jnp.float32) + returned[second_slot].astype(jnp.float32)
    route_probs = jax.nn.softmax(route_logits, axis=-1)
    routed = jnp.sum(
        route_probs[:, :, None] * pair_sum.reshape(own_tokens, TOP, width_model), axis=1
    )
    layer_out = (mixed + shared_part + routed).astype(jnp.bfloat16)
    return (layer_out, cache_out)


VMEM = pl.BlockSpec(memory_space=pltpu.VMEM)
SMEM = pl.BlockSpec(memory_space=pltpu.SMEM)
HBM = pl.BlockSpec(memory_space=pltpu.HBM)


def dot_rows(left, right):
    return lax.dot_general(left, right, (((1,), (1,)), ((), ())), preferred_element_type=jnp.float32)


def dot(left, right):
    return jnp.dot(left, right, preferred_element_type=jnp.float32)


def silu_times(gate, up):
    return (gate / (1.0 + jnp.exp(-gate)) * up).astype(jnp.bfloat16)


def join_kernel(key_ref, value_ref, out_ref):
    width = key_ref.shape[1]
    out_ref[:, :width] = key_ref[...]
    out_ref[:, width:] = value_ref[...]


def attention_kernel(
    z_ref,
    first_ref,
    lengths_ref,
    q_ref,
    k4_ref,
    k3_ref,
    k2_ref,
    k1_ref,
    own_ref,
    residual_ref,
    info_ref,
    *out_refs,
):
    tokens, width = q_ref.shape
    part = width // Z_SIZE
    kv_width = own_ref.shape[1] // 2
    kv_heads = kv_width // HD
    group = width // HD // kv_heads
    blocks = [k4_ref, k3_ref, k2_ref, k1_ref, own_ref]
    keys = len(blocks) * tokens
    first = first_ref[0]
    query_pos = first + lax.broadcasted_iota(jnp.int32, (tokens, keys), 0)
    key_pos = first - (keys - tokens) + lax.broadcasted_iota(jnp.int32, (tokens, keys), 1)
    start = jnp.zeros((tokens, keys), jnp.int32)
    end = jnp.int32(0)
    for request in range(lengths_ref.shape[0]):
        end = end + lengths_ref[request]
        start = jnp.maximum(start, jnp.where(query_pos >= end, end, 0))
    hidden = jnp.where((key_pos >= start) & (key_pos <= query_pos), 0.0, NEGATIVE)
    hidden = jnp.concatenate([hidden] * group, axis=0)
    scale = 1.0 / math.sqrt(HD)
    for step, out_ref in enumerate(out_refs):
        z = lax.rem(z_ref[0] + step, Z_SIZE)
        for column in range(Z_SIZE):

            @pl.when(z == column)
            def _(column=column, out_ref=out_ref):
                columns = slice(column * part, (column + 1) * part)
                out_ref[:, width : width + part] = residual_ref[:, columns]

        out_ref[:, width + part :] = info_ref[...]
    for kv in range(kv_heads):
        at = slice(kv * HD, (kv + 1) * HD)
        value_at = slice(kv_width + kv * HD, kv_width + (kv + 1) * HD)
        key = jnp.concatenate([block[:, at] for block in blocks], axis=0)
        value = jnp.concatenate([block[:, value_at] for block in blocks], axis=0)
        heads = [kv * group + member for member in range(group)]
        query = jnp.concatenate([q_ref[:, h * HD : (h + 1) * HD] for h in heads], axis=0)
        scores = dot_rows(query, key) * scale + hidden
        weights = jnp.exp(scores - jnp.max(scores, axis=-1, keepdims=True))
        total = jnp.sum(weights, axis=-1, keepdims=True)
        result = (dot(weights.astype(jnp.bfloat16), value) / total).astype(jnp.bfloat16)
        for member, h in enumerate(heads):
            for out_ref in out_refs:
                out_ref[:, h * HD : (h + 1) * HD] = result[member * tokens : (member + 1) * tokens]


def route_kernel(z_ref, ids_ref, logits_ref, out_ref, turned_ref):
    choices, tokens = ids_ref.shape
    turned_ref[...] = jnp.zeros(turned_ref.shape, jnp.float32)
    turned_ref[:choices, :tokens] = ids_ref[...].astype(jnp.float32)
    turned_ref[8 : 8 + choices, :tokens] = logits_ref[...]
    table = turned_ref[...].T[:tokens]
    lane = lax.broadcasted_iota(jnp.int32, table.shape, 1)
    ids = [table[:, c : c + 1].astype(jnp.int32) for c in range(choices)]
    logits = [table[:, 8 + c : 9 + c] for c in range(choices)]
    member = jnp.zeros(table.shape, jnp.float32)
    for one in ids:
        member = jnp.where(lane == one, 1.0, member)
    row = lax.broadcasted_iota(jnp.int32, (tokens, tokens), 0)
    earlier = jnp.where(lax.broadcasted_iota(jnp.int32, (tokens, tokens), 1) < row, 1.0, 0.0)
    ahead = dot(earlier.astype(jnp.bfloat16), member.astype(jnp.bfloat16))
    top = logits[0]
    for one in logits[1:]:
        top = jnp.maximum(top, one)
    powers = [jnp.exp(one - top) for one in logits]
    total = sum(powers[1:], powers[0])
    per_device = EXPERTS // 2 // PLANE
    out = jnp.zeros(table.shape, jnp.float32)
    for c, one in enumerate(ids):
        rank = jnp.sum(jnp.where(lane == one, ahead, 0.0), axis=1, keepdims=True)
        where_to = lax.div(one, per_device).astype(jnp.float32)
        first = (lax.rem(one, per_device) * Z_SIZE + z_ref[0]) * CAP
        out = jnp.where(lane == c, where_to, out)
        out = jnp.where(lane == 8 + c, first.astype(jnp.float32) + rank, out)
        out = jnp.where(lane == 16 + c, powers[c] / total, out)
    out_ref[...] = out.astype(jnp.bfloat16)


def regroup_kernel(z_ref, *refs):
    pieces, outs = refs[:PLANE], refs[PLANE:]
    for step, out in enumerate(outs):
        z = lax.rem(z_ref[0] + step, Z_SIZE)
        for at, piece in enumerate(pieces):
            out[at] = piece[z]


def source_z(z_ref, step):
    return lax.rem(z_ref[0] + Z_SIZE - step, Z_SIZE)


def project_kernel(z_ref, *refs):
    sent = refs[:Z_SIZE]
    weight_ref, mixed_ref, info_ref, rows_ref = refs[Z_SIZE:]
    for step, sent_ref in enumerate(sent):
        rows_ref[source_z(z_ref, step)] = sent_ref[...]
    rows = jnp.concatenate([rows_ref[z] for z in range(Z_SIZE)], axis=0)
    part, width = weight_ref.shape
    out = dot_rows(rows[:, :width], weight_ref[...])
    mixed = (out + rows[:, width : width + part].astype(jnp.float32)).astype(jnp.bfloat16)
    for z in range(Z_SIZE):
        mixed_ref[z] = mixed
    info_ref[...] = rows[:, width + part :]


def row_codes(info, first, parity, per_device):
    where_to = info(first).astype(jnp.int32) - PLANE * parity
    inside = info(first + 8).astype(jnp.int32)
    fits = (where_to >= 0) & (where_to < PLANE)
    return jnp.where(fits, where_to * per_device + inside, -1)


def tables_kernel(parity_ref, info_ref, onehot_ref, mix_ref):
    rows, tokens = onehot_ref.shape
    info = info_ref[...].astype(jnp.float32)
    turned = info.T
    codes = row_codes(lambda at: turned[at : at + 8], 0, parity_ref[0], rows // PLANE)
    row = lax.broadcasted_iota(jnp.int32, (rows, tokens), 0)
    chosen = codes[0:1, :] == row
    for choice in range(1, TOP):
        chosen = chosen | (codes[choice : choice + 1, :] == row)
    onehot_ref[...] = jnp.where(chosen, 1.0, 0.0).astype(jnp.bfloat16)
    column = lax.broadcasted_iota(jnp.int32, mix_ref.shape, 1)
    mix = jnp.zeros(mix_ref.shape, jnp.float32)
    for choice in range(TOP):
        code = row_codes(lambda at: info[:, at : at + 1], choice, parity_ref[0], rows // PLANE)
        mix = jnp.where(code == column, info[:, 16 + choice : 17 + choice], mix)
    mix_ref[...] = mix.astype(jnp.bfloat16)


def norm(mixed_ref, gain_ref):
    mixed = jnp.concatenate([mixed_ref[z] for z in range(Z_SIZE)], axis=1).astype(jnp.float32)
    mean_square = jnp.mean(mixed * mixed, axis=-1, keepdims=True)
    return (mixed * lax.rsqrt(mean_square + EPSILON) * gain_ref[...]).astype(jnp.bfloat16)


def pick_kernel(onehot_ref, gain_ref, mixed_ref, out_hbm, out_ref, sems):
    normed = norm(mixed_ref, gain_ref)
    picked = out_ref.shape[1]
    copies = []
    for p in range(PLANE):
        onehot = onehot_ref[p * picked : (p + 1) * picked]
        out_ref[p] = dot(onehot, normed).astype(jnp.bfloat16)
        copy = pltpu.make_async_copy(out_ref.at[p], out_hbm.at[p], sems.at[p])
        copy.start()
        copies.append(copy)
    for copy in copies:
        copy.wait()


def shared_kernel(z_ref, gain_ref, mixed_ref, weight_ref, out_ref, own_ref):
    tokens, columns = own_ref.shape[0], mixed_ref.shape[2]
    own = pl.ds(pl.multiple_of(z_ref[0] * tokens, tokens), tokens)
    for z in range(Z_SIZE):
        own_ref[:, z * columns : (z + 1) * columns] = mixed_ref[z, own, :].astype(jnp.float32)
    parts, units, _ = weight_ref.shape
    units = units // 3
    gate_weight, up_weight, down_weight = [
        jnp.concatenate([weight_ref[p, at * units : (at + 1) * units] for p in range(parts)], axis=0)
        for at in range(3)
    ]
    rows = norm(mixed_ref, gain_ref)
    act = silu_times(dot_rows(rows, gate_weight), dot_rows(rows, up_weight))
    out_ref[...] = dot(act, down_weight).astype(jnp.bfloat16)


def experts_kernel(
    rows_ref, gate_up_hbm, down_hbm, out_hbm, gate_up_ref, down_ref, out_ref, in_sems, out_sems
):
    halves = gate_up_ref.shape[0]
    sources, rows, width = rows_ref.shape
    per_half = rows // halves
    fetches = []
    for half in range(halves):
        pairs = ((gate_up_hbm, gate_up_ref), (down_hbm, down_ref))
        for at, (from_ref, to_ref) in enumerate(pairs):
            fetch = pltpu.make_async_copy(from_ref.at[half], to_ref.at[half], in_sems.at[at, half])
            fetch.start()
            fetches.append(fetch)
    copies = []
    for pair in range(halves // 2):
        both = pl.ds(2 * pair * per_half, 2 * per_half)
        arrived = rows_ref[:, both, :].astype(jnp.float32)
        results = []
        for member in range(2):
            half = 2 * pair + member
            own = arrived[:, member * per_half : (member + 1) * per_half]
            own = own.reshape(sources * per_half, width).astype(jnp.bfloat16)
            fetches[2 * half].wait()
            act = silu_times(dot(own, gate_up_ref[half, 0]), dot(own, gate_up_ref[half, 1]))
            fetches[2 * half + 1].wait()
            results.append(dot(act, down_ref[half]).reshape(sources, per_half, width))
        out_ref[:, both, :] = jnp.concatenate(results, axis=1).astype(jnp.bfloat16)
        copy = pltpu.make_async_copy(out_ref.at[:, both], out_hbm.at[:, both], out_sems.at[pair])
        copy.start()
        copies.append(copy)
    for copy in copies:
        copy.wait()


def combine_kernel(z_ref, mix_ref, rows_ref, shared_ref, *refs):
    outs, sum_ref = refs[:Z_SIZE], refs[Z_SIZE]
    tokens = outs[0].shape[0]
    sum_ref[...] = dot(mix_ref[...], rows_ref[...]) + shared_ref[...].astype(jnp.float32)
    for step, out_ref in enumerate(outs):
        z = lax.rem(z_ref[0] + step, Z_SIZE)
        rows = pl.ds(pl.multiple_of(z * tokens, tokens), tokens)
        out_ref[...] = sum_ref[rows, :].astype(jnp.bfloat16)


def final_kernel(mixed_ref, *refs):
    total = mixed_ref[...]
    for part_ref in refs[:Z_SIZE]:
        total = total + part_ref[...].astype(jnp.float32)
    refs[Z_SIZE][...] = total.astype(jnp.bfloat16)


def reorder_kernel(me_ref, table_ref, from_ref, to_ref):
    me = me_ref[0]
    for block in range(to_ref.shape[0]):
        source = table_ref[block]
        z_steps = lax.rem(lax.div(me, PLANE) - lax.div(source, PLANE) + Z_SIZE, Z_SIZE)
        steps = lax.rem(lax.rem(me, PLANE) - lax.rem(source, PLANE) + PLANE, PLANE)
        to_ref[block] = from_ref[z_steps * PLANE + steps]


def in_hbm(array):
    return pltpu.with_memory_space_constraint(array, pltpu.HBM)


def params(mib=16):
    return pltpu.CompilerParams(vmem_limit_bytes=mib * MIB)


def cost(flops, moved):
    return pl.CostEstimate(flops=int(flops), bytes_accessed=int(moved), transcendentals=0)


def shards(
    queries,
    key_vectors,
    value_vectors,
    lengths,
    out_weight,
    residual,
    norm_gain,
    route_ids,
    route_logits,
    shared_gate_up,
    shared_down,
    expert_gate_up,
    expert_down,
    cache_blocks,
    block_table,
):
    tokens, width = residual.shape
    devices = lax.axis_size("seq")
    me = lax.axis_index("seq")
    z_index, plane_index = lax.div(me, PLANE), lax.rem(me, PLANE)
    z_groups = [[p + PLANE * z for z in range(Z_SIZE)] for p in range(PLANE)]
    planes = [[p + PLANE * z for p in range(PLANE)] for z in range(Z_SIZE)]
    bf16, f32 = jnp.bfloat16, jnp.float32
    shape = jax.ShapeDtypeStruct
    scalar = lambda value: jnp.reshape(value, (1,)).astype(jnp.int32)
    all_tokens = Z_SIZE * tokens
    part = width // Z_SIZE

    def exchange(array, groups):
        return lax.all_to_all(
            array, "seq", split_axis=0, concat_axis=0, tiled=True, axis_index_groups=groups
        )

    own_kv = pl.pallas_call(
        join_kernel,
        out_shape=pltpu.HBM((tokens, 2 * key_vectors.shape[1]), bf16),
        in_specs=[VMEM] * 2,
        out_specs=VMEM,
        compiler_params=params(),
        name="join",
    )(key_vectors, value_vectors)
    behind = [from_behind(own_kv, "seq", offset) for offset in range(REACH, 0, -1)]

    turned_weight = lax.all_gather(
        out_weight.T, "seq", axis=0, tiled=True, axis_index_groups=planes
    )
    info = pl.pallas_call(
        route_kernel,
        out_shape=shape((tokens, 128), bf16),
        in_specs=[SMEM] + [VMEM] * 2,
        out_specs=VMEM,
        scratch_shapes=[pltpu.VMEM((128, 128), f32)],
        compiler_params=params(),
        cost_estimate=cost(MIB, MIB),
        name="route",
    )(scalar(z_index), route_ids.T, route_logits.T)

    def along_z(arrays):
        return [arrays[0]] + [
            lax.ppermute(arrays[step], "seq", z_pairs[step]) for step in range(1, Z_SIZE)
        ]

    z_pairs = [
        [
            (z * PLANE + p, (z + step) % Z_SIZE * PLANE + p)
            for z in range(Z_SIZE)
            for p in range(PLANE)
        ]
        for step in range(Z_SIZE)
    ]
    z_scalar = scalar(z_index)
    gain = norm_gain.reshape(1, width)
    own_shared = jnp.concatenate(
        [jnp.transpose(shared_gate_up, (1, 2, 0)).reshape(-1, width), shared_down], axis=0
    )

    sent_width = width + part + info.shape[1]
    sent = pl.pallas_call(
        attention_kernel,
        out_shape=[shape((tokens, sent_width), bf16)] * Z_SIZE,
        in_specs=[SMEM] * 3 + [VMEM] * 8,
        out_specs=[VMEM] * Z_SIZE,
        compiler_params=params(58),
        cost_estimate=cost(4 * tokens * 5 * tokens * width, 3 * MIB),
        name="attention",
    )(z_scalar, scalar(me * tokens), lengths, queries, *behind, own_kv, residual, info)

    sent, own_shared = lax.optimization_barrier((sent, own_shared))
    shared_weight = lax.all_gather(own_shared, "seq", axis=0, axis_index_groups=planes)
    gathered = along_z(sent)
    gathered, cache_blocks, expert_gate_up = lax.optimization_barrier(
        (gathered, cache_blocks, expert_gate_up)
    )

    _, block_tokens, layers, kv_heads, head_size = cache_blocks.shape
    per_device = block_tokens // devices
    cache_view = cache_blocks.reshape(Z_SIZE, PLANE, per_device * layers, kv_heads, head_size)
    in_plane = []
    for step in range(PLANE):
        piece = lax.dynamic_index_in_dim(
            cache_view, lax.rem(plane_index + step, PLANE), axis=1, keepdims=False
        )
        if step:
            pairs = [
                (z * PLANE + p, z * PLANE + (p + step) % PLANE)
                for z in range(Z_SIZE)
                for p in range(PLANE)
            ]
            piece = lax.ppermute(piece, "seq", pairs)
        in_plane.append(piece)
    gate_up = jnp.transpose(expert_gate_up, (0, 2, 1, 3))

    mixed_part, info = pl.pallas_call(
        project_kernel,
        out_shape=[pltpu.HBM((Z_SIZE, all_tokens, part), bf16), shape((all_tokens, 128), bf16)],
        in_specs=[SMEM] + [VMEM] * (Z_SIZE + 1),
        out_specs=[VMEM] * 2,
        scratch_shapes=[pltpu.VMEM((Z_SIZE, tokens, sent_width), bf16)],
        compiler_params=params(),
        cost_estimate=cost(2 * all_tokens * width * part, 3 * MIB),
        name="project",
    )(z_scalar, *gathered, turned_weight)
    mixed = exchange(mixed_part, z_groups)

    local_halves, _, _, half_ff = expert_gate_up.shape
    per_half = Z_SIZE * CAP
    picked = local_halves * per_half
    onehot, mix = pl.pallas_call(
        tables_kernel,
        out_shape=[
            shape((PLANE * picked, all_tokens), bf16),
            shape((all_tokens, PLANE * picked), bf16),
        ],
        in_specs=[SMEM, VMEM],
        out_specs=[VMEM] * 2,
        compiler_params=params(),
        cost_estimate=cost(20 * PLANE * picked * all_tokens, MIB),
        name="tables",
    )(scalar(lax.rem(z_index, 2)), info)
    outgoing = pl.pallas_call(
        pick_kernel,
        out_shape=pltpu.HBM((PLANE, picked, width), bf16),
        in_specs=[VMEM] * 3,
        out_specs=HBM,
        scratch_shapes=[
            pltpu.VMEM((PLANE, picked, width), bf16),
            pltpu.SemaphoreType.DMA((PLANE,)),
        ],
        compiler_params=params(),
        cost_estimate=cost(2 * PLANE * picked * all_tokens * width, 4 * MIB),
        name="pick",
    )(onehot, gain, mixed)

    outgoing, in_plane = lax.optimization_barrier((outgoing, in_plane))
    arrived = exchange(outgoing, planes)
    grouped = pl.pallas_call(
        regroup_kernel,
        out_shape=[shape((PLANE,) + in_plane[0].shape[1:], bf16)] * Z_SIZE,
        in_specs=[SMEM] + [VMEM] * PLANE,
        out_specs=[VMEM] * Z_SIZE,
        compiler_params=params(),
        cost_estimate=cost(0, 2 * MIB),
        name="regroup",
    )(z_scalar, *[in_hbm(piece) for piece in in_plane])
    arrived_cache = [grouped[0]]
    for step in range(1, Z_SIZE):
        arrived_cache.append(lax.ppermute(grouped[step], "seq", z_pairs[step]))

    arrived, shared_weight = lax.optimization_barrier((arrived, shared_weight))
    shared_part, own_mixed = pl.pallas_call(
        shared_kernel,
        out_shape=[shape((all_tokens, width), bf16), shape((tokens, width), f32)],
        in_specs=[SMEM] + [VMEM] * 3,
        out_specs=[VMEM] * 2,
        compiler_params=params(24),
        cost_estimate=cost(6 * all_tokens * 256 * width, 5 * MIB),
        name="shared_expert",
    )(z_scalar, gain, mixed, shared_weight)

    returning = pl.pallas_call(
        experts_kernel,
        out_shape=pltpu.HBM((PLANE, picked, width), bf16),
        in_specs=[VMEM, HBM, HBM],
        out_specs=HBM,
        scratch_shapes=[
            pltpu.VMEM((local_halves, 2, width, half_ff), bf16),
            pltpu.VMEM((local_halves, half_ff, width), bf16),
            pltpu.VMEM((PLANE, picked, width), bf16),
            pltpu.SemaphoreType.DMA((2, local_halves)),
            pltpu.SemaphoreType.DMA((local_halves // 2,)),
        ],
        compiler_params=params(32),
        cost_estimate=cost(6 * PLANE * picked * half_ff * width, 14 * MIB),
        name="experts",
    )(arrived, in_hbm(gate_up), in_hbm(expert_down))
    returning, arrived_cache = lax.optimization_barrier((returning, arrived_cache))
    returned = exchange(returning, planes).reshape(PLANE * picked, width)

    arrived_cache = jnp.concatenate(arrived_cache)
    cache_out = pl.pallas_call(
        reorder_kernel,
        out_shape=shape(arrived_cache.shape, bf16),
        in_specs=[SMEM, SMEM, VMEM],
        out_specs=VMEM,
        compiler_params=params(),
        cost_estimate=cost(0, 2 * arrived_cache.size * 2),
        name="reorder",
    )(scalar(me), block_table, arrived_cache)
    cache_out = cache_out.reshape(devices, per_device, layers, kv_heads, head_size)

    sums = pl.pallas_call(
        combine_kernel,
        out_shape=[shape((tokens, width), bf16)] * Z_SIZE,
        in_specs=[SMEM] + [VMEM] * 3,
        out_specs=[VMEM] * Z_SIZE,
        scratch_shapes=[pltpu.VMEM((all_tokens, width), f32)],
        compiler_params=params(24),
        cost_estimate=cost(2 * all_tokens * PLANE * picked * width, 3 * MIB),
        name="combine",
    )(z_scalar, in_hbm(mix), returned, in_hbm(shared_part))
    layer_out = pl.pallas_call(
        final_kernel,
        out_shape=shape((tokens, width), bf16),
        in_specs=[VMEM] * (1 + Z_SIZE),
        out_specs=VMEM,
        compiler_params=params(),
        cost_estimate=cost(5 * tokens * width, 2 * MIB),
        name="final",
    )(own_mixed, *along_z(sums))
    return (layer_out, cache_out)


def solution(mesh):
    in_specs = (
        P("seq", "head"),
        P("seq", "head"),
        P("seq", "head"),
        P(),
        P("head", "seq"),
        P(("seq", "head"), None),
        P(),
        P(("seq", "head"), None),
        P(("seq", "head"), None),
        P(None, None, ("seq", "head")),
        P(("seq", "head"), None),
        P("seq", None, None, None),
        P("seq", None, None),
        P("seq", None, None, "head", None),
        P(),
    )
    out_specs = (P(("seq", "head"), None), P(None, "seq", None, "head", None))
    planes_fit = mesh.shape["seq"] == Z_SIZE * PLANE and mesh.shape["head"] == 1
    body = shards if planes_fit else general_shards
    return jax.shard_map(body, mesh=mesh, in_specs=in_specs, out_specs=out_specs, check_vma=False)
```

```python
import math

import jax
import jax.numpy as jnp
from jax import lax
from jax.experimental import pallas as pl
from jax.experimental.pallas import tpu as pltpu
from jax.sharding import PartitionSpec as P

HD = 128
EXPERTS = 64
TOP = 6
REACH = 4
HALVES = 128
CAP = 6
Z_SIZE = 4
PLANE = 8
MIB = 1024 * 1024


NEGATIVE = -1e30
EPSILON = 1e-05


def from_behind(shard, axis, by):
    devices = lax.axis_size(axis)
    pairs = [(i, i + by) for i in range(devices) if 0 <= i + by < devices]
    return lax.ppermute(shard, axis, pairs)


def segment_of(positions, lengths):
    request_ends = jnp.cumsum(lengths)
    passed = (request_ends[None, :] <= positions[:, None]).astype(jnp.int32)
    return jnp.sum(passed, axis=1)


def shared_ffn(rows_in, gate_up_part, down_part):
    shared_both = jnp.einsum(
        "td,dcf->tcf", rows_in, gate_up_part, preferred_element_type=jnp.float32
    )
    shared_act = (jax.nn.silu(shared_both[:, 0]) * shared_both[:, 1]).astype(jnp.bfloat16)
    return jnp.dot(shared_act, down_part, preferred_element_type=jnp.float32)


def general_shards(
    queries,
    key_vectors,
    value_vectors,
    lengths,
    out_weight,
    residual,
    norm_gain,
    route_ids,
    route_logits,
    shared_gate_up,
    shared_down,
    expert_gate_up,
    expert_down,
    cache_blocks,
    block_table,
):
    handed = lax.all_to_all(cache_blocks, "seq", split_axis=1, concat_axis=0, tiled=True)
    cache_out = jnp.take(handed, block_table, axis=0)
    tok_rows = queries.shape[0]
    seq_index = lax.axis_index("seq")
    earlier = [
        from_behind((key_vectors, value_vectors), "seq", offset) for offset in range(REACH, 0, -1)
    ]
    window_keys = jnp.concatenate([member[0] for member in earlier] + [key_vectors], axis=0)
    window_values = jnp.concatenate([member[1] for member in earlier] + [value_vectors], axis=0)
    key_count = window_keys.shape[0]
    kv_heads = key_vectors.shape[1] // HD
    query_heads = queries.shape[1] // HD
    group_size = query_heads // kv_heads
    query_pos = seq_index * tok_rows + jnp.arange(tok_rows, dtype=jnp.int32)
    key_pos = (seq_index - REACH) * tok_rows + jnp.arange(key_count, dtype=jnp.int32)
    visible = (key_pos[None, :] >= 0) & (key_pos[None, :] <= query_pos[:, None])
    visible = visible & (
        segment_of(key_pos, lengths)[None, :] == segment_of(query_pos, lengths)[:, None]
    )
    query_part = queries.reshape(tok_rows, kv_heads, group_size, HD)
    key_part = window_keys.reshape(key_count, kv_heads, HD)
    value_part = window_values.reshape(key_count, kv_heads, HD)
    scores = jnp.einsum(
        "tkgd,wkd->kgtw", query_part, key_part, preferred_element_type=jnp.float32
    ) * (1.0 / math.sqrt(HD))
    scores = jnp.where(visible[None, None], scores, NEGATIVE)
    row_max = jnp.max(scores, axis=-1, keepdims=True)
    weights = jnp.exp(scores - row_max)
    row_total = jnp.sum(weights, axis=-1)
    weighted = jnp.einsum(
        "kgtw,wkd->tkgd",
        weights.astype(jnp.bfloat16),
        value_part,
        preferred_element_type=jnp.float32,
    )
    heads = (weighted / jnp.transpose(row_total, (2, 0, 1))[..., None]).astype(jnp.bfloat16)
    heads = heads.reshape(tok_rows, query_heads * HD)
    partial_out = jnp.dot(
        heads,
        lax.all_gather(out_weight, "seq", axis=1, tiled=True),
        preferred_element_type=jnp.float32,
    )
    attn_out = lax.psum_scatter(partial_out, "head", scatter_dimension=0, tiled=True)
    mixed = residual.astype(jnp.float32) + attn_out
    mean_square = jnp.mean(mixed * mixed, axis=-1, keepdims=True)
    normed = (mixed * lax.rsqrt(mean_square + EPSILON) * norm_gain).astype(jnp.bfloat16)
    gate_up_all, down_all = (
        lax.all_gather(shared_gate_up, ("seq", "head"), axis=2, tiled=True),
        lax.all_gather(shared_down, ("seq", "head"), axis=0, tiled=True),
    )
    shared_part = shared_ffn(normed, gate_up_all, down_all)
    own_tokens = normed.shape[0]
    width_model = normed.shape[1]
    flat_ids = route_ids.reshape(-1)
    onehot = (flat_ids[:, None] == jnp.arange(EXPERTS, dtype=jnp.int32)[None, :]).astype(jnp.int32)
    slot_rank = jnp.sum((jnp.cumsum(onehot, axis=0) - 1) * onehot, axis=1)
    first_slot = flat_ids * CAP + slot_rank
    second_slot = (flat_ids + EXPERTS) * CAP + slot_rank
    token_of = jnp.arange(flat_ids.shape[0], dtype=jnp.int32) // TOP
    routed_rows = normed[token_of]
    outgoing = jnp.zeros((HALVES * CAP, width_model), jnp.bfloat16)
    outgoing = outgoing.at[jnp.concatenate([first_slot, second_slot])].set(
        jnp.concatenate([routed_rows, routed_rows], axis=0)
    )
    local_halves = expert_gate_up.shape[0]
    outgoing = outgoing.reshape(HALVES // local_halves, local_halves, CAP, width_model)
    gate_up = jnp.einsum(
        "nsjd,sdcf->nsjcf",
        lax.all_to_all(outgoing, "seq", split_axis=0, concat_axis=0, tiled=True),
        expert_gate_up,
        preferred_element_type=jnp.float32,
    )
    expert_act = (jax.nn.silu(gate_up[:, :, :, 0]) * gate_up[:, :, :, 1]).astype(jnp.bfloat16)
    half_out = jnp.einsum(
        "nsjf,sfd->nsjd", expert_act, expert_down, preferred_element_type=jnp.float32
    ).astype(jnp.bfloat16)
    returned = lax.all_to_all(half_out, "seq", split_axis=0, concat_axis=0, tiled=True)
    returned = returned.reshape(HALVES * CAP, width_model)
    pair_sum = returned[first_slot].astype(jnp.float32) + returned[second_slot].astype(jnp.float32)
    route_probs = jax.nn.softmax(route_logits, axis=-1)
    routed = jnp.sum(
        route_probs[:, :, None] * pair_sum.reshape(own_tokens, TOP, width_model), axis=1
    )
    layer_out = (mixed + shared_part + routed).astype(jnp.bfloat16)
    return (layer_out, cache_out)


VMEM = pl.BlockSpec(memory_space=pltpu.VMEM)
SMEM = pl.BlockSpec(memory_space=pltpu.SMEM)
HBM = pl.BlockSpec(memory_space=pltpu.HBM)


def dot_rows(left, right):
    return lax.dot_general(left, right, (((1,), (1,)), ((), ())), preferred_element_type=jnp.float32)


def dot(left, right):
    return jnp.dot(left, right, preferred_element_type=jnp.float32)


def silu_times(gate, up):
    return (gate / (1.0 + jnp.exp(-gate)) * up).astype(jnp.bfloat16)


def join_kernel(key_ref, value_ref, out_ref):
    width = key_ref.shape[1]
    out_ref[:, :width] = key_ref[...]
    out_ref[:, width:] = value_ref[...]


def attention_kernel(
    first_ref, lengths_ref, q_ref, k4_ref, k3_ref, k2_ref, k1_ref, own_ref, info_ref, out_ref
):
    tokens, width = q_ref.shape
    kv_width = own_ref.shape[1] // 2
    kv_heads = kv_width // HD
    group = width // HD // kv_heads
    blocks = [k4_ref, k3_ref, k2_ref, k1_ref, own_ref]
    keys = len(blocks) * tokens
    first = first_ref[0]
    query_pos = first + lax.broadcasted_iota(jnp.int32, (tokens, keys), 0)
    key_pos = first - (keys - tokens) + lax.broadcasted_iota(jnp.int32, (tokens, keys), 1)
    start = jnp.zeros((tokens, keys), jnp.int32)
    end = jnp.int32(0)
    for request in range(lengths_ref.shape[0]):
        end = end + lengths_ref[request]
        start = jnp.maximum(start, jnp.where(query_pos >= end, end, 0))
    hidden = jnp.where((key_pos >= start) & (key_pos <= query_pos), 0.0, NEGATIVE)
    hidden = jnp.concatenate([hidden] * group, axis=0)
    scale = 1.0 / math.sqrt(HD)
    out_ref[:, width:] = info_ref[...]
    for kv in range(kv_heads):
        at = slice(kv * HD, (kv + 1) * HD)
        value_at = slice(kv_width + kv * HD, kv_width + (kv + 1) * HD)
        key = jnp.concatenate([block[:, at] for block in blocks], axis=0)
        value = jnp.concatenate([block[:, value_at] for block in blocks], axis=0)
        heads = [kv * group + member for member in range(group)]
        query = jnp.concatenate([q_ref[:, h * HD : (h + 1) * HD] for h in heads], axis=0)
        scores = dot_rows(query, key) * scale + hidden
        weights = jnp.exp(scores - jnp.max(scores, axis=-1, keepdims=True))
        total = jnp.sum(weights, axis=-1, keepdims=True)
        result = (dot(weights.astype(jnp.bfloat16), value) / total).astype(jnp.bfloat16)
        for member, h in enumerate(heads):
            out_ref[:, h * HD : (h + 1) * HD] = result[member * tokens : (member + 1) * tokens]


def route_kernel(z_ref, ids_ref, logits_ref, out_ref, turned_ref):
    choices, tokens = ids_ref.shape
    turned_ref[...] = jnp.zeros(turned_ref.shape, jnp.float32)
    turned_ref[:choices, :tokens] = ids_ref[...].astype(jnp.float32)
    turned_ref[8 : 8 + choices, :tokens] = logits_ref[...]
    table = turned_ref[...].T[:tokens]
    lane = lax.broadcasted_iota(jnp.int32, table.shape, 1)
    ids = [table[:, c : c + 1].astype(jnp.int32) for c in range(choices)]
    logits = [table[:, 8 + c : 9 + c] for c in range(choices)]
    member = jnp.zeros(table.shape, jnp.float32)
    for one in ids:
        member = jnp.where(lane == one, 1.0, member)
    row = lax.broadcasted_iota(jnp.int32, (tokens, tokens), 0)
    earlier = jnp.where(lax.broadcasted_iota(jnp.int32, (tokens, tokens), 1) < row, 1.0, 0.0)
    ahead = dot(earlier.astype(jnp.bfloat16), member.astype(jnp.bfloat16))
    top = logits[0]
    for one in logits[1:]:
        top = jnp.maximum(top, one)
    powers = [jnp.exp(one - top) for one in logits]
    total = sum(powers[1:], powers[0])
    per_device = EXPERTS // 2 // PLANE
    out = jnp.zeros(table.shape, jnp.float32)
    for c, one in enumerate(ids):
        rank = jnp.sum(jnp.where(lane == one, ahead, 0.0), axis=1, keepdims=True)
        where_to = lax.div(one, per_device).astype(jnp.float32)
        first = (lax.rem(one, per_device) * Z_SIZE + z_ref[0]) * CAP
        out = jnp.where(lane == c, where_to, out)
        out = jnp.where(lane == 8 + c, first.astype(jnp.float32) + rank, out)
        out = jnp.where(lane == 16 + c, powers[c] / total, out)
    out_ref[...] = out.astype(jnp.bfloat16)


def regroup_kernel(z_ref, *refs):
    pieces, outs = refs[:PLANE], refs[PLANE:]
    for step, out in enumerate(outs):
        z = lax.rem(z_ref[0] + step, Z_SIZE)
        for at, piece in enumerate(pieces):
            out[at] = piece[z]


def source_z(z_ref, step):
    return lax.rem(z_ref[0] + Z_SIZE - step, Z_SIZE)


def project_kernel(z_ref, *refs):
    sent = refs[:Z_SIZE]
    weight_ref, out_ref, info_ref, rows_ref = refs[Z_SIZE:]
    for step, sent_ref in enumerate(sent):
        rows_ref[source_z(z_ref, step)] = sent_ref[...]
    rows = jnp.concatenate([rows_ref[z] for z in range(Z_SIZE)], axis=0)
    width = weight_ref.shape[1]
    out = dot_rows(rows[:, :width], weight_ref[...]).astype(jnp.bfloat16)
    for z in range(Z_SIZE):
        out_ref[z] = out
    info_ref[...] = rows[:, width:]


def row_codes(info, first, parity, per_device):
    where_to = info(first).astype(jnp.int32) - PLANE * parity
    inside = info(first + 8).astype(jnp.int32)
    fits = (where_to >= 0) & (where_to < PLANE)
    return jnp.where(fits, where_to * per_device + inside, -1)


def tables_kernel(parity_ref, info_ref, onehot_ref, mix_ref):
    rows, tokens = onehot_ref.shape
    info = info_ref[...].astype(jnp.float32)
    turned = info.T
    codes = row_codes(lambda at: turned[at : at + 8], 0, parity_ref[0], rows // PLANE)
    row = lax.broadcasted_iota(jnp.int32, (rows, tokens), 0)
    chosen = codes[0:1, :] == row
    for choice in range(1, TOP):
        chosen = chosen | (codes[choice : choice + 1, :] == row)
    onehot_ref[...] = jnp.where(chosen, 1.0, 0.0).astype(jnp.bfloat16)
    column = lax.broadcasted_iota(jnp.int32, mix_ref.shape, 1)
    mix = jnp.zeros(mix_ref.shape, jnp.float32)
    for choice in range(TOP):
        code = row_codes(lambda at: info[:, at : at + 1], choice, parity_ref[0], rows // PLANE)
        mix = jnp.where(code == column, info[:, 16 + choice : 17 + choice], mix)
    mix_ref[...] = mix.astype(jnp.bfloat16)


def norm(projected_ref, residual_ref, gain_ref):
    projected = jnp.concatenate([projected_ref[z] for z in range(Z_SIZE)], axis=1)
    mixed = residual_ref[...].astype(jnp.float32) + projected.astype(jnp.float32)
    mean_square = jnp.mean(mixed * mixed, axis=-1, keepdims=True)
    return (mixed * lax.rsqrt(mean_square + EPSILON) * gain_ref[...]).astype(jnp.bfloat16)


def pick_kernel(onehot_ref, gain_ref, projected_ref, residual_ref, out_hbm, out_ref, sems):
    normed = norm(projected_ref, residual_ref, gain_ref)
    picked = out_ref.shape[1]
    copies = []
    for p in range(PLANE):
        onehot = onehot_ref[p * picked : (p + 1) * picked]
        out_ref[p] = dot(onehot, normed).astype(jnp.bfloat16)
        copy = pltpu.make_async_copy(out_ref.at[p], out_hbm.at[p], sems.at[p])
        copy.start()
        copies.append(copy)
    for copy in copies:
        copy.wait()


def shared_kernel(z_ref, gain_ref, projected_ref, residual_ref, weight_ref, out_ref, own_ref):
    tokens, columns = own_ref.shape[0], projected_ref.shape[2]
    own = pl.ds(pl.multiple_of(z_ref[0] * tokens, tokens), tokens)
    for z in range(Z_SIZE):
        at = slice(z * columns, (z + 1) * columns)
        own_residual = residual_ref[own, at].astype(jnp.float32)
        own_ref[:, at] = own_residual + projected_ref[z, own, :].astype(jnp.float32)
    parts, units, _ = weight_ref.shape
    units = units // 3
    gate_weight, up_weight, down_weight = [
        jnp.concatenate([weight_ref[p, at * units : (at + 1) * units] for p in range(parts)], axis=0)
        for at in range(3)
    ]
    rows = norm(projected_ref, residual_ref, gain_ref)
    act = silu_times(dot_rows(rows, gate_weight), dot_rows(rows, up_weight))
    out_ref[...] = dot(act, down_weight).astype(jnp.bfloat16)


def experts_kernel(
    rows_ref, gate_up_hbm, down_hbm, out_hbm, gate_up_ref, down_ref, out_ref, in_sems, out_sems
):
    halves = gate_up_ref.shape[0]
    sources, rows, width = rows_ref.shape
    per_half = rows // halves
    fetches = []
    for half in range(halves):
        pairs = ((gate_up_hbm, gate_up_ref), (down_hbm, down_ref))
        for at, (from_ref, to_ref) in enumerate(pairs):
            fetch = pltpu.make_async_copy(from_ref.at[half], to_ref.at[half], in_sems.at[at, half])
            fetch.start()
            fetches.append(fetch)
    copies = []
    for pair in range(halves // 2):
        both = pl.ds(2 * pair * per_half, 2 * per_half)
        arrived = rows_ref[:, both, :].astype(jnp.float32)
        results = []
        for member in range(2):
            half = 2 * pair + member
            own = arrived[:, member * per_half : (member + 1) * per_half]
            own = own.reshape(sources * per_half, width).astype(jnp.bfloat16)
            fetches[2 * half].wait()
            act = silu_times(dot(own, gate_up_ref[half, 0]), dot(own, gate_up_ref[half, 1]))
            fetches[2 * half + 1].wait()
            results.append(dot(act, down_ref[half]).reshape(sources, per_half, width))
        out_ref[:, both, :] = jnp.concatenate(results, axis=1).astype(jnp.bfloat16)
        copy = pltpu.make_async_copy(out_ref.at[:, both], out_hbm.at[:, both], out_sems.at[pair])
        copy.start()
        copies.append(copy)
    for copy in copies:
        copy.wait()


def combine_kernel(z_ref, mix_ref, rows_ref, shared_ref, *refs):
    outs, sum_ref = refs[:Z_SIZE], refs[Z_SIZE]
    tokens = outs[0].shape[0]
    sum_ref[...] = dot(mix_ref[...], rows_ref[...]) + shared_ref[...].astype(jnp.float32)
    for step, out_ref in enumerate(outs):
        z = lax.rem(z_ref[0] + step, Z_SIZE)
        rows = pl.ds(pl.multiple_of(z * tokens, tokens), tokens)
        out_ref[...] = sum_ref[rows, :].astype(jnp.bfloat16)


def final_kernel(mixed_ref, *refs):
    total = mixed_ref[...]
    for part_ref in refs[:Z_SIZE]:
        total = total + part_ref[...].astype(jnp.float32)
    refs[Z_SIZE][...] = total.astype(jnp.bfloat16)


def reorder_kernel(me_ref, table_ref, from_ref, to_ref):
    me = me_ref[0]
    for block in range(to_ref.shape[0]):
        source = table_ref[block]
        z_steps = lax.rem(lax.div(me, PLANE) - lax.div(source, PLANE) + Z_SIZE, Z_SIZE)
        steps = lax.rem(lax.rem(me, PLANE) - lax.rem(source, PLANE) + PLANE, PLANE)
        to_ref[block] = from_ref[z_steps * PLANE + steps]


def in_hbm(array):
    return pltpu.with_memory_space_constraint(array, pltpu.HBM)


def params(mib=16):
    return pltpu.CompilerParams(vmem_limit_bytes=mib * MIB)


def cost(flops, moved):
    return pl.CostEstimate(flops=int(flops), bytes_accessed=int(moved), transcendentals=0)


def shards(
    queries,
    key_vectors,
    value_vectors,
    lengths,
    out_weight,
    residual,
    norm_gain,
    route_ids,
    route_logits,
    shared_gate_up,
    shared_down,
    expert_gate_up,
    expert_down,
    cache_blocks,
    block_table,
):
    tokens, width = residual.shape
    devices = lax.axis_size("seq")
    me = lax.axis_index("seq")
    z_index, plane_index = lax.div(me, PLANE), lax.rem(me, PLANE)
    z_groups = [[p + PLANE * z for z in range(Z_SIZE)] for p in range(PLANE)]
    planes = [[p + PLANE * z for p in range(PLANE)] for z in range(Z_SIZE)]
    bf16, f32 = jnp.bfloat16, jnp.float32
    shape = jax.ShapeDtypeStruct
    scalar = lambda value: jnp.reshape(value, (1,)).astype(jnp.int32)
    all_tokens = Z_SIZE * tokens
    part = width // Z_SIZE

    def exchange(array, groups):
        return lax.all_to_all(
            array, "seq", split_axis=0, concat_axis=0, tiled=True, axis_index_groups=groups
        )

    line_residual = lax.all_gather(
        residual, "seq", axis=0, tiled=True, axis_index_groups=z_groups
    )
    own_kv = pl.pallas_call(
        join_kernel,
        out_shape=pltpu.HBM((tokens, 2 * key_vectors.shape[1]), bf16),
        in_specs=[VMEM] * 2,
        out_specs=VMEM,
        compiler_params=params(),
        name="join",
    )(in_hbm(key_vectors), in_hbm(value_vectors))
    own_kv, out_weight = lax.optimization_barrier((own_kv, out_weight))
    behind = [from_behind(own_kv, "seq", offset) for offset in range(REACH, 0, -1)]

    turned_weight = lax.all_gather(
        out_weight.T, "seq", axis=0, tiled=True, axis_index_groups=planes
    )
    info = pl.pallas_call(
        route_kernel,
        out_shape=pltpu.HBM((tokens, 128), bf16),
        in_specs=[SMEM] + [VMEM] * 2,
        out_specs=VMEM,
        scratch_shapes=[pltpu.VMEM((128, 128), f32)],
        compiler_params=params(),
        cost_estimate=cost(MIB, MIB),
        name="route",
    )(scalar(z_index), in_hbm(route_ids.T), in_hbm(route_logits.T))

    def along_z(arrays):
        return [arrays[0]] + [
            lax.ppermute(arrays[step], "seq", z_pairs[step]) for step in range(1, Z_SIZE)
        ]

    z_pairs = [
        [
            (z * PLANE + p, (z + step) % Z_SIZE * PLANE + p)
            for z in range(Z_SIZE)
            for p in range(PLANE)
        ]
        for step in range(Z_SIZE)
    ]
    z_scalar = scalar(z_index)
    gain = norm_gain.reshape(1, width)
    own_shared = jnp.concatenate(
        [jnp.transpose(shared_gate_up, (1, 2, 0)).reshape(-1, width), shared_down], axis=0
    )

    sent_width = width + info.shape[1]
    sent = pl.pallas_call(
        attention_kernel,
        out_shape=pltpu.HBM((tokens, sent_width), bf16),
        in_specs=[SMEM] * 2 + [VMEM] * 7,
        out_specs=VMEM,
        compiler_params=params(58),
        cost_estimate=cost(4 * tokens * 5 * tokens * width, 3 * MIB),
        name="attention",
    )(scalar(me * tokens), in_hbm(lengths), queries, *behind, own_kv, info)

    sent, own_shared = lax.optimization_barrier((sent, own_shared))
    shared_weight = lax.all_gather(own_shared, "seq", axis=0, axis_index_groups=planes)
    gathered = along_z([sent] * Z_SIZE)
    gathered, cache_blocks, expert_gate_up = lax.optimization_barrier(
        (gathered, cache_blocks, expert_gate_up)
    )

    _, block_tokens, layers, kv_heads, head_size = cache_blocks.shape
    per_device = block_tokens // devices
    cache_view = cache_blocks.reshape(Z_SIZE, PLANE, per_device * layers, kv_heads, head_size)
    in_plane = []
    for step in range(PLANE):
        piece = lax.dynamic_index_in_dim(
            cache_view, lax.rem(plane_index + step, PLANE), axis=1, keepdims=False
        )
        if step:
            pairs = [
                (z * PLANE + p, z * PLANE + (p + step) % PLANE)
                for z in range(Z_SIZE)
                for p in range(PLANE)
            ]
            piece = lax.ppermute(piece, "seq", pairs)
        in_plane.append(piece)
    gate_up = jnp.transpose(expert_gate_up, (0, 2, 1, 3))

    projected_part, info = pl.pallas_call(
        project_kernel,
        out_shape=[pltpu.HBM((Z_SIZE, all_tokens, part), bf16), shape((all_tokens, 128), bf16)],
        in_specs=[SMEM] + [VMEM] * (Z_SIZE + 1),
        out_specs=[VMEM] * 2,
        scratch_shapes=[pltpu.VMEM((Z_SIZE, tokens, sent_width), bf16)],
        compiler_params=params(),
        cost_estimate=cost(2 * all_tokens * width * part, 3 * MIB),
        name="project",
    )(z_scalar, in_hbm(gathered[0]), *gathered[1:], in_hbm(turned_weight))
    projected = exchange(projected_part, z_groups)

    local_halves, _, _, half_ff = expert_gate_up.shape
    per_half = Z_SIZE * CAP
    picked = local_halves * per_half
    onehot, mix = pl.pallas_call(
        tables_kernel,
        out_shape=[
            shape((PLANE * picked, all_tokens), bf16),
            shape((all_tokens, PLANE * picked), bf16),
        ],
        in_specs=[SMEM, VMEM],
        out_specs=[VMEM] * 2,
        compiler_params=params(),
        cost_estimate=cost(20 * PLANE * picked * all_tokens, MIB),
        name="tables",
    )(scalar(lax.rem(z_index, 2)), info)
    outgoing = pl.pallas_call(
        pick_kernel,
        out_shape=pltpu.HBM((PLANE, picked, width), bf16),
        in_specs=[VMEM] * 4,
        out_specs=HBM,
        scratch_shapes=[
            pltpu.VMEM((PLANE, picked, width), bf16),
            pltpu.SemaphoreType.DMA((PLANE,)),
        ],
        compiler_params=params(),
        cost_estimate=cost(2 * PLANE * picked * all_tokens * width, 4 * MIB),
        name="pick",
    )(onehot, gain, projected, in_hbm(line_residual))

    outgoing, in_plane = lax.optimization_barrier((outgoing, in_plane))
    arrived = exchange(outgoing, planes)
    grouped = pl.pallas_call(
        regroup_kernel,
        out_shape=[shape((PLANE,) + in_plane[0].shape[1:], bf16)] * Z_SIZE,
        in_specs=[SMEM] + [VMEM] * PLANE,
        out_specs=[VMEM] * Z_SIZE,
        compiler_params=params(),
        cost_estimate=cost(0, 2 * MIB),
        name="regroup",
    )(z_scalar, *[in_hbm(piece) for piece in in_plane])
    arrived_cache = [grouped[0]]
    for step in range(1, Z_SIZE):
        arrived_cache.append(lax.ppermute(grouped[step], "seq", z_pairs[step]))

    arrived, shared_weight = lax.optimization_barrier((arrived, shared_weight))
    shared_part, own_mixed = pl.pallas_call(
        shared_kernel,
        out_shape=[shape((all_tokens, width), bf16), shape((tokens, width), f32)],
        in_specs=[SMEM] + [VMEM] * 4,
        out_specs=[VMEM] * 2,
        compiler_params=params(24),
        cost_estimate=cost(6 * all_tokens * 256 * width, 5 * MIB),
        name="shared_expert",
    )(z_scalar, gain, projected, in_hbm(line_residual), shared_weight)

    returning = pl.pallas_call(
        experts_kernel,
        out_shape=pltpu.HBM((PLANE, picked, width), bf16),
        in_specs=[VMEM, HBM, HBM],
        out_specs=HBM,
        scratch_shapes=[
            pltpu.VMEM((local_halves, 2, width, half_ff), bf16),
            pltpu.VMEM((local_halves, half_ff, width), bf16),
            pltpu.VMEM((PLANE, picked, width), bf16),
            pltpu.SemaphoreType.DMA((2, local_halves)),
            pltpu.SemaphoreType.DMA((local_halves // 2,)),
        ],
        compiler_params=params(32),
        cost_estimate=cost(6 * PLANE * picked * half_ff * width, 14 * MIB),
        name="experts",
    )(arrived, in_hbm(gate_up), in_hbm(expert_down))
    returning, arrived_cache = lax.optimization_barrier((returning, arrived_cache))
    returned = exchange(returning, planes).reshape(PLANE * picked, width)

    arrived_cache = jnp.concatenate(arrived_cache)
    cache_out = pl.pallas_call(
        reorder_kernel,
        out_shape=shape(arrived_cache.shape, bf16),
        in_specs=[SMEM, SMEM, VMEM],
        out_specs=VMEM,
        compiler_params=params(),
        cost_estimate=cost(0, 2 * arrived_cache.size * 2),
        name="reorder",
    )(scalar(me), block_table, arrived_cache)
    cache_out = cache_out.reshape(devices, per_device, layers, kv_heads, head_size)

    sums = pl.pallas_call(
        combine_kernel,
        out_shape=[shape((tokens, width), bf16)] * Z_SIZE,
        in_specs=[SMEM] + [VMEM] * 3,
        out_specs=[VMEM] * Z_SIZE,
        scratch_shapes=[pltpu.VMEM((all_tokens, width), f32)],
        compiler_params=params(24),
        cost_estimate=cost(2 * all_tokens * PLANE * picked * width, 3 * MIB),
        name="combine",
    )(z_scalar, in_hbm(mix), returned, in_hbm(shared_part))
    layer_out = pl.pallas_call(
        final_kernel,
        out_shape=shape((tokens, width), bf16),
        in_specs=[VMEM] * (1 + Z_SIZE),
        out_specs=VMEM,
        compiler_params=params(),
        cost_estimate=cost(5 * tokens * width, 2 * MIB),
        name="final",
    )(own_mixed, *along_z(sums))
    return (layer_out, cache_out)


def solution(mesh):
    in_specs = (
        P("seq", "head"),
        P("seq", "head"),
        P("seq", "head"),
        P(),
        P("head", "seq"),
        P(("seq", "head"), None),
        P(),
        P(("seq", "head"), None),
        P(("seq", "head"), None),
        P(None, None, ("seq", "head")),
        P(("seq", "head"), None),
        P("seq", None, None, None),
        P("seq", None, None),
        P("seq", None, None, "head", None),
        P(),
    )
    out_specs = (P(("seq", "head"), None), P(None, "seq", None, "head", None))
    planes_fit = mesh.shape["seq"] == Z_SIZE * PLANE and mesh.shape["head"] == 1
    body = shards if planes_fit else general_shards
    return jax.shard_map(body, mesh=mesh, in_specs=in_specs, out_specs=out_specs, check_vma=False)
```

```python
import math

import jax
import jax.numpy as jnp
from jax import lax
from jax.experimental import pallas as pl
from jax.experimental.pallas import tpu as pltpu
from jax.sharding import PartitionSpec as P

HD = 128
EXPERTS = 64
TOP = 6
REACH = 4
HALVES = 128
CAP = 6
Z_SIZE = 4
PLANE = 8
MIB = 1024 * 1024


NEGATIVE = -1e30
EPSILON = 1e-05


def from_behind(shard, axis, by):
    devices = lax.axis_size(axis)
    pairs = [(i, i + by) for i in range(devices) if 0 <= i + by < devices]
    return lax.ppermute(shard, axis, pairs)


def segment_of(positions, lengths):
    request_ends = jnp.cumsum(lengths)
    passed = (request_ends[None, :] <= positions[:, None]).astype(jnp.int32)
    return jnp.sum(passed, axis=1)


def shared_ffn(rows_in, gate_up_part, down_part):
    shared_both = jnp.einsum(
        "td,dcf->tcf", rows_in, gate_up_part, preferred_element_type=jnp.float32
    )
    shared_act = (jax.nn.silu(shared_both[:, 0]) * shared_both[:, 1]).astype(jnp.bfloat16)
    return jnp.dot(shared_act, down_part, preferred_element_type=jnp.float32)


def general_shards(
    queries,
    key_vectors,
    value_vectors,
    lengths,
    out_weight,
    residual,
    norm_gain,
    route_ids,
    route_logits,
    shared_gate_up,
    shared_down,
    expert_gate_up,
    expert_down,
    cache_blocks,
    block_table,
):
    handed = lax.all_to_all(cache_blocks, "seq", split_axis=1, concat_axis=0, tiled=True)
    cache_out = jnp.take(handed, block_table, axis=0)
    tok_rows = queries.shape[0]
    seq_index = lax.axis_index("seq")
    earlier = [
        from_behind((key_vectors, value_vectors), "seq", offset) for offset in range(REACH, 0, -1)
    ]
    window_keys = jnp.concatenate([member[0] for member in earlier] + [key_vectors], axis=0)
    window_values = jnp.concatenate([member[1] for member in earlier] + [value_vectors], axis=0)
    key_count = window_keys.shape[0]
    kv_heads = key_vectors.shape[1] // HD
    query_heads = queries.shape[1] // HD
    group_size = query_heads // kv_heads
    query_pos = seq_index * tok_rows + jnp.arange(tok_rows, dtype=jnp.int32)
    key_pos = (seq_index - REACH) * tok_rows + jnp.arange(key_count, dtype=jnp.int32)
    visible = (key_pos[None, :] >= 0) & (key_pos[None, :] <= query_pos[:, None])
    visible = visible & (
        segment_of(key_pos, lengths)[None, :] == segment_of(query_pos, lengths)[:, None]
    )
    query_part = queries.reshape(tok_rows, kv_heads, group_size, HD)
    key_part = window_keys.reshape(key_count, kv_heads, HD)
    value_part = window_values.reshape(key_count, kv_heads, HD)
    scores = jnp.einsum(
        "tkgd,wkd->kgtw", query_part, key_part, preferred_element_type=jnp.float32
    ) * (1.0 / math.sqrt(HD))
    scores = jnp.where(visible[None, None], scores, NEGATIVE)
    row_max = jnp.max(scores, axis=-1, keepdims=True)
    weights = jnp.exp(scores - row_max)
    row_total = jnp.sum(weights, axis=-1)
    weighted = jnp.einsum(
        "kgtw,wkd->tkgd",
        weights.astype(jnp.bfloat16),
        value_part,
        preferred_element_type=jnp.float32,
    )
    heads = (weighted / jnp.transpose(row_total, (2, 0, 1))[..., None]).astype(jnp.bfloat16)
    heads = heads.reshape(tok_rows, query_heads * HD)
    partial_out = jnp.dot(
        heads,
        lax.all_gather(out_weight, "seq", axis=1, tiled=True),
        preferred_element_type=jnp.float32,
    )
    attn_out = lax.psum_scatter(partial_out, "head", scatter_dimension=0, tiled=True)
    mixed = residual.astype(jnp.float32) + attn_out
    mean_square = jnp.mean(mixed * mixed, axis=-1, keepdims=True)
    normed = (mixed * lax.rsqrt(mean_square + EPSILON) * norm_gain).astype(jnp.bfloat16)
    gate_up_all, down_all = (
        lax.all_gather(shared_gate_up, ("seq", "head"), axis=2, tiled=True),
        lax.all_gather(shared_down, ("seq", "head"), axis=0, tiled=True),
    )
    shared_part = shared_ffn(normed, gate_up_all, down_all)
    own_tokens = normed.shape[0]
    width_model = normed.shape[1]
    flat_ids = route_ids.reshape(-1)
    onehot = (flat_ids[:, None] == jnp.arange(EXPERTS, dtype=jnp.int32)[None, :]).astype(jnp.int32)
    slot_rank = jnp.sum((jnp.cumsum(onehot, axis=0) - 1) * onehot, axis=1)
    first_slot = flat_ids * CAP + slot_rank
    second_slot = (flat_ids + EXPERTS) * CAP + slot_rank
    token_of = jnp.arange(flat_ids.shape[0], dtype=jnp.int32) // TOP
    routed_rows = normed[token_of]
    outgoing = jnp.zeros((HALVES * CAP, width_model), jnp.bfloat16)
    outgoing = outgoing.at[jnp.concatenate([first_slot, second_slot])].set(
        jnp.concatenate([routed_rows, routed_rows], axis=0)
    )
    local_halves = expert_gate_up.shape[0]
    outgoing = outgoing.reshape(HALVES // local_halves, local_halves, CAP, width_model)
    gate_up = jnp.einsum(
        "nsjd,sdcf->nsjcf",
        lax.all_to_all(outgoing, "seq", split_axis=0, concat_axis=0, tiled=True),
        expert_gate_up,
        preferred_element_type=jnp.float32,
    )
    expert_act = (jax.nn.silu(gate_up[:, :, :, 0]) * gate_up[:, :, :, 1]).astype(jnp.bfloat16)
    half_out = jnp.einsum(
        "nsjf,sfd->nsjd", expert_act, expert_down, preferred_element_type=jnp.float32
    ).astype(jnp.bfloat16)
    returned = lax.all_to_all(half_out, "seq", split_axis=0, concat_axis=0, tiled=True)
    returned = returned.reshape(HALVES * CAP, width_model)
    pair_sum = returned[first_slot].astype(jnp.float32) + returned[second_slot].astype(jnp.float32)
    route_probs = jax.nn.softmax(route_logits, axis=-1)
    routed = jnp.sum(
        route_probs[:, :, None] * pair_sum.reshape(own_tokens, TOP, width_model), axis=1
    )
    layer_out = (mixed + shared_part + routed).astype(jnp.bfloat16)
    return (layer_out, cache_out)


VMEM = pl.BlockSpec(memory_space=pltpu.VMEM)
SMEM = pl.BlockSpec(memory_space=pltpu.SMEM)
HBM = pl.BlockSpec(memory_space=pltpu.HBM)


def dot_rows(left, right):
    return lax.dot_general(left, right, (((1,), (1,)), ((), ())), preferred_element_type=jnp.float32)


def dot(left, right):
    return jnp.dot(left, right, preferred_element_type=jnp.float32)


def silu_times(gate, up):
    return (gate / (1.0 + jnp.exp(-gate)) * up).astype(jnp.bfloat16)


def join_kernel(key_ref, value_ref, out_ref):
    width = key_ref.shape[1]
    out_ref[:, :width] = key_ref[...]
    out_ref[:, width:] = value_ref[...]


def attention_kernel(
    z_ref,
    first_ref,
    lengths_ref,
    q_ref,
    k4_ref,
    k3_ref,
    k2_ref,
    k1_ref,
    own_ref,
    residual_ref,
    info_ref,
    *out_refs,
):
    tokens, width = q_ref.shape
    part = width // Z_SIZE
    kv_width = own_ref.shape[1] // 2
    kv_heads = kv_width // HD
    group = width // HD // kv_heads
    blocks = [k4_ref, k3_ref, k2_ref, k1_ref, own_ref]
    keys = len(blocks) * tokens
    first = first_ref[0]
    query_pos = first + lax.broadcasted_iota(jnp.int32, (tokens, keys), 0)
    key_pos = first - (keys - tokens) + lax.broadcasted_iota(jnp.int32, (tokens, keys), 1)
    start = jnp.zeros((tokens, keys), jnp.int32)
    end = jnp.int32(0)
    for request in range(lengths_ref.shape[0]):
        end = end + lengths_ref[request]
        start = jnp.maximum(start, jnp.where(query_pos >= end, end, 0))
    hidden = jnp.where((key_pos >= start) & (key_pos <= query_pos), 0.0, NEGATIVE)
    hidden = jnp.concatenate([hidden] * group, axis=0)
    scale = 1.0 / math.sqrt(HD)
    for step, out_ref in enumerate(out_refs):
        z = lax.rem(z_ref[0] + step, Z_SIZE)
        for column in range(Z_SIZE):

            @pl.when(z == column)
            def _(column=column, out_ref=out_ref):
                columns = slice(column * part, (column + 1) * part)
                out_ref[:, width : width + part] = residual_ref[:, columns]

        out_ref[:, width + part :] = info_ref[...]
    for kv in range(kv_heads):
        at = slice(kv * HD, (kv + 1) * HD)
        value_at = slice(kv_width + kv * HD, kv_width + (kv + 1) * HD)
        key = jnp.concatenate([block[:, at] for block in blocks], axis=0)
        value = jnp.concatenate([block[:, value_at] for block in blocks], axis=0)
        heads = [kv * group + member for member in range(group)]
        query = jnp.concatenate([q_ref[:, h * HD : (h + 1) * HD] for h in heads], axis=0)
        scores = dot_rows(query, key) * scale + hidden
        weights = jnp.exp(scores - jnp.max(scores, axis=-1, keepdims=True))
        total = jnp.sum(weights, axis=-1, keepdims=True)
        result = (dot(weights.astype(jnp.bfloat16), value) / total).astype(jnp.bfloat16)
        for member, h in enumerate(heads):
            for out_ref in out_refs:
                out_ref[:, h * HD : (h + 1) * HD] = result[member * tokens : (member + 1) * tokens]


def route_kernel(z_ref, ids_ref, logits_ref, out_ref, turned_ref):
    choices, tokens = ids_ref.shape
    turned_ref[...] = jnp.zeros(turned_ref.shape, jnp.float32)
    turned_ref[:choices, :tokens] = ids_ref[...].astype(jnp.float32)
    turned_ref[8 : 8 + choices, :tokens] = logits_ref[...]
    table = turned_ref[...].T[:tokens]
    lane = lax.broadcasted_iota(jnp.int32, table.shape, 1)
    ids = [table[:, c : c + 1].astype(jnp.int32) for c in range(choices)]
    logits = [table[:, 8 + c : 9 + c] for c in range(choices)]
    member = jnp.zeros(table.shape, jnp.float32)
    for one in ids:
        member = jnp.where(lane == one, 1.0, member)
    row = lax.broadcasted_iota(jnp.int32, (tokens, tokens), 0)
    earlier = jnp.where(lax.broadcasted_iota(jnp.int32, (tokens, tokens), 1) < row, 1.0, 0.0)
    ahead = dot(earlier.astype(jnp.bfloat16), member.astype(jnp.bfloat16))
    top = logits[0]
    for one in logits[1:]:
        top = jnp.maximum(top, one)
    powers = [jnp.exp(one - top) for one in logits]
    total = sum(powers[1:], powers[0])
    per_device = EXPERTS // 2 // PLANE
    out = jnp.zeros(table.shape, jnp.float32)
    for c, one in enumerate(ids):
        rank = jnp.sum(jnp.where(lane == one, ahead, 0.0), axis=1, keepdims=True)
        where_to = lax.div(one, per_device).astype(jnp.float32)
        first = (lax.rem(one, per_device) * Z_SIZE + z_ref[0]) * CAP
        out = jnp.where(lane == c, where_to, out)
        out = jnp.where(lane == 8 + c, first.astype(jnp.float32) + rank, out)
        out = jnp.where(lane == 16 + c, powers[c] / total, out)
    out_ref[...] = out.astype(jnp.bfloat16)


def regroup_kernel(z_ref, *refs):
    pieces, outs = refs[:PLANE], refs[PLANE:]
    for step, out in enumerate(outs):
        z = lax.rem(z_ref[0] + step, Z_SIZE)
        for at, piece in enumerate(pieces):
            out[at] = piece[z]


def source_z(z_ref, step):
    return lax.rem(z_ref[0] + Z_SIZE - step, Z_SIZE)


def project_kernel(z_ref, *refs):
    sent = refs[:Z_SIZE]
    weight_ref, mixed_ref, info_ref, rows_ref = refs[Z_SIZE:]
    for step, sent_ref in enumerate(sent):
        rows_ref[source_z(z_ref, step)] = sent_ref[...]
    rows = jnp.concatenate([rows_ref[z] for z in range(Z_SIZE)], axis=0)
    part, width = weight_ref.shape
    out = dot_rows(rows[:, :width], weight_ref[...])
    mixed = (out + rows[:, width : width + part].astype(jnp.float32)).astype(jnp.bfloat16)
    for z in range(Z_SIZE):
        mixed_ref[z] = mixed
    info_ref[...] = rows[:, width + part :]


def row_codes(info, first, parity, per_device):
    where_to = info(first).astype(jnp.int32) - PLANE * parity
    inside = info(first + 8).astype(jnp.int32)
    fits = (where_to >= 0) & (where_to < PLANE)
    return jnp.where(fits, where_to * per_device + inside, -1)


def tables_kernel(parity_ref, info_ref, onehot_ref, mix_ref):
    rows, tokens = onehot_ref.shape
    info = info_ref[...].astype(jnp.float32)
    turned = info.T
    codes = row_codes(lambda at: turned[at : at + 8], 0, parity_ref[0], rows // PLANE)
    row = lax.broadcasted_iota(jnp.int32, (rows, tokens), 0)
    chosen = codes[0:1, :] == row
    for choice in range(1, TOP):
        chosen = chosen | (codes[choice : choice + 1, :] == row)
    onehot_ref[...] = jnp.where(chosen, 1.0, 0.0).astype(jnp.bfloat16)
    column = lax.broadcasted_iota(jnp.int32, mix_ref.shape, 1)
    mix = jnp.zeros(mix_ref.shape, jnp.float32)
    for choice in range(TOP):
        code = row_codes(lambda at: info[:, at : at + 1], choice, parity_ref[0], rows // PLANE)
        mix = jnp.where(code == column, info[:, 16 + choice : 17 + choice], mix)
    mix_ref[...] = mix.astype(jnp.bfloat16)


def norm(mixed_ref, gain_ref):
    mixed = jnp.concatenate([mixed_ref[z] for z in range(Z_SIZE)], axis=1).astype(jnp.float32)
    mean_square = jnp.mean(mixed * mixed, axis=-1, keepdims=True)
    return (mixed * lax.rsqrt(mean_square + EPSILON) * gain_ref[...]).astype(jnp.bfloat16)


def pick_kernel(onehot_ref, gain_ref, mixed_ref, out_hbm, out_ref, sems):
    normed = norm(mixed_ref, gain_ref)
    picked = out_ref.shape[1]
    copies = []
    for p in range(PLANE):
        onehot = onehot_ref[p * picked : (p + 1) * picked]
        out_ref[p] = dot(onehot, normed).astype(jnp.bfloat16)
        copy = pltpu.make_async_copy(out_ref.at[p], out_hbm.at[p], sems.at[p])
        copy.start()
        copies.append(copy)
    for copy in copies:
        copy.wait()


def shared_kernel(z_ref, gain_ref, mixed_ref, weight_ref, out_ref, own_ref):
    tokens, columns = own_ref.shape[0], mixed_ref.shape[2]
    own = pl.ds(pl.multiple_of(z_ref[0] * tokens, tokens), tokens)
    for z in range(Z_SIZE):
        own_ref[:, z * columns : (z + 1) * columns] = mixed_ref[z, own, :].astype(jnp.float32)
    parts, units, _ = weight_ref.shape
    units = units // 3
    gate_weight, up_weight, down_weight = [
        jnp.concatenate([weight_ref[p, at * units : (at + 1) * units] for p in range(parts)], axis=0)
        for at in range(3)
    ]
    rows = norm(mixed_ref, gain_ref)
    act = silu_times(dot_rows(rows, gate_weight), dot_rows(rows, up_weight))
    out_ref[...] = dot(act, down_weight).astype(jnp.bfloat16)


def experts_kernel(
    rows_ref, gate_up_hbm, down_hbm, out_hbm, gate_up_ref, down_ref, out_ref, in_sems, out_sems
):
    halves = gate_up_ref.shape[0]
    sources, rows, width = rows_ref.shape
    per_half = rows // halves
    fetches = []
    for half in range(halves):
        pairs = ((gate_up_hbm, gate_up_ref), (down_hbm, down_ref))
        for at, (from_ref, to_ref) in enumerate(pairs):
            fetch = pltpu.make_async_copy(from_ref.at[half], to_ref.at[half], in_sems.at[at, half])
            fetch.start()
            fetches.append(fetch)
    copies = []
    for pair in range(halves // 2):
        both = pl.ds(2 * pair * per_half, 2 * per_half)
        arrived = rows_ref[:, both, :].astype(jnp.float32)
        results = []
        for member in range(2):
            half = 2 * pair + member
            own = arrived[:, member * per_half : (member + 1) * per_half]
            own = own.reshape(sources * per_half, width).astype(jnp.bfloat16)
            fetches[2 * half].wait()
            act = silu_times(dot(own, gate_up_ref[half, 0]), dot(own, gate_up_ref[half, 1]))
            fetches[2 * half + 1].wait()
            results.append(dot(act, down_ref[half]).reshape(sources, per_half, width))
        out_ref[:, both, :] = jnp.concatenate(results, axis=1).astype(jnp.bfloat16)
        copy = pltpu.make_async_copy(out_ref.at[:, both], out_hbm.at[:, both], out_sems.at[pair])
        copy.start()
        copies.append(copy)
    for copy in copies:
        copy.wait()


def combine_kernel(z_ref, mix_ref, rows_ref, shared_ref, *refs):
    outs, sum_ref = refs[:Z_SIZE], refs[Z_SIZE]
    tokens = outs[0].shape[0]
    sum_ref[...] = dot(mix_ref[...], rows_ref[...]) + shared_ref[...].astype(jnp.float32)
    for step, out_ref in enumerate(outs):
        z = lax.rem(z_ref[0] + step, Z_SIZE)
        rows = pl.ds(pl.multiple_of(z * tokens, tokens), tokens)
        out_ref[...] = sum_ref[rows, :].astype(jnp.bfloat16)


def final_kernel(mixed_ref, *refs):
    total = mixed_ref[...]
    for part_ref in refs[:Z_SIZE]:
        total = total + part_ref[...].astype(jnp.float32)
    refs[Z_SIZE][...] = total.astype(jnp.bfloat16)


def reorder_kernel(me_ref, table_ref, from_ref, to_ref):
    me = me_ref[0]
    for block in range(to_ref.shape[0]):
        source = table_ref[block]
        z_steps = lax.rem(lax.div(me, PLANE) - lax.div(source, PLANE) + Z_SIZE, Z_SIZE)
        steps = lax.rem(lax.rem(me, PLANE) - lax.rem(source, PLANE) + PLANE, PLANE)
        to_ref[block] = from_ref[z_steps * PLANE + steps]


def in_hbm(array):
    return pltpu.with_memory_space_constraint(array, pltpu.HBM)


def params(mib=16):
    return pltpu.CompilerParams(vmem_limit_bytes=mib * MIB)


def cost(flops, moved):
    return pl.CostEstimate(flops=int(flops), bytes_accessed=int(moved), transcendentals=0)


def shards(
    queries,
    key_vectors,
    value_vectors,
    lengths,
    out_weight,
    residual,
    norm_gain,
    route_ids,
    route_logits,
    shared_gate_up,
    shared_down,
    expert_gate_up,
    expert_down,
    cache_blocks,
    block_table,
):
    tokens, width = residual.shape
    devices = lax.axis_size("seq")
    me = lax.axis_index("seq")
    z_index, plane_index = lax.div(me, PLANE), lax.rem(me, PLANE)
    z_groups = [[p + PLANE * z for z in range(Z_SIZE)] for p in range(PLANE)]
    planes = [[p + PLANE * z for p in range(PLANE)] for z in range(Z_SIZE)]
    bf16, f32 = jnp.bfloat16, jnp.float32
    shape = jax.ShapeDtypeStruct
    scalar = lambda value: jnp.reshape(value, (1,)).astype(jnp.int32)
    all_tokens = Z_SIZE * tokens
    part = width // Z_SIZE

    def exchange(array, groups):
        return lax.all_to_all(
            array, "seq", split_axis=0, concat_axis=0, tiled=True, axis_index_groups=groups
        )

    own_kv = pl.pallas_call(
        join_kernel,
        out_shape=pltpu.HBM((tokens, 2 * key_vectors.shape[1]), bf16),
        in_specs=[VMEM] * 2,
        out_specs=VMEM,
        compiler_params=params(),
        name="join",
    )(in_hbm(key_vectors), in_hbm(value_vectors))
    behind = [from_behind(own_kv, "seq", offset) for offset in range(REACH, 0, -1)]

    turned_weight = lax.all_gather(
        out_weight.T, "seq", axis=0, tiled=True, axis_index_groups=planes
    )
    info = pl.pallas_call(
        route_kernel,
        out_shape=pltpu.HBM((tokens, 128), bf16),
        in_specs=[SMEM] + [VMEM] * 2,
        out_specs=VMEM,
        scratch_shapes=[pltpu.VMEM((128, 128), f32)],
        compiler_params=params(),
        cost_estimate=cost(MIB, MIB),
        name="route",
    )(scalar(z_index), in_hbm(route_ids.T), in_hbm(route_logits.T))

    def along_z(arrays):
        return [arrays[0]] + [
            lax.ppermute(arrays[step], "seq", z_pairs[step]) for step in range(1, Z_SIZE)
        ]

    z_pairs = [
        [
            (z * PLANE + p, (z + step) % Z_SIZE * PLANE + p)
            for z in range(Z_SIZE)
            for p in range(PLANE)
        ]
        for step in range(Z_SIZE)
    ]
    z_scalar = scalar(z_index)
    gain = norm_gain.reshape(1, width)
    own_shared = jnp.concatenate(
        [jnp.transpose(shared_gate_up, (1, 2, 0)).reshape(-1, width), shared_down], axis=0
    )

    sent_width = width + part + info.shape[1]
    sent = pl.pallas_call(
        attention_kernel,
        out_shape=[pltpu.HBM((tokens, sent_width), bf16)] * Z_SIZE,
        in_specs=[SMEM] * 3 + [VMEM] * 8,
        out_specs=[VMEM] * Z_SIZE,
        compiler_params=params(58),
        cost_estimate=cost(4 * tokens * 5 * tokens * width, 3 * MIB),
        name="attention",
    )(z_scalar, scalar(me * tokens), in_hbm(lengths), queries, *behind, own_kv, residual, info)

    sent, own_shared = lax.optimization_barrier((sent, own_shared))
    shared_weight = lax.all_gather(own_shared, "seq", axis=0, axis_index_groups=planes)
    gathered = along_z(sent)
    gathered, cache_blocks, expert_gate_up = lax.optimization_barrier(
        (gathered, cache_blocks, expert_gate_up)
    )

    _, block_tokens, layers, kv_heads, head_size = cache_blocks.shape
    per_device = block_tokens // devices
    cache_view = cache_blocks.reshape(Z_SIZE, PLANE, per_device * layers, kv_heads, head_size)
    in_plane = []
    for step in range(PLANE):
        piece = lax.dynamic_index_in_dim(
            cache_view, lax.rem(plane_index + step, PLANE), axis=1, keepdims=False
        )
        if step:
            pairs = [
                (z * PLANE + p, z * PLANE + (p + step) % PLANE)
                for z in range(Z_SIZE)
                for p in range(PLANE)
            ]
            piece = lax.ppermute(piece, "seq", pairs)
        in_plane.append(piece)
    gate_up = jnp.transpose(expert_gate_up, (0, 2, 1, 3))

    mixed_part, info = pl.pallas_call(
        project_kernel,
        out_shape=[pltpu.HBM((Z_SIZE, all_tokens, part), bf16), shape((all_tokens, 128), bf16)],
        in_specs=[SMEM] + [VMEM] * (Z_SIZE + 1),
        out_specs=[VMEM] * 2,
        scratch_shapes=[pltpu.VMEM((Z_SIZE, tokens, sent_width), bf16)],
        compiler_params=params(),
        cost_estimate=cost(2 * all_tokens * width * part, 3 * MIB),
        name="project",
    )(z_scalar, in_hbm(gathered[0]), *gathered[1:], in_hbm(turned_weight))
    mixed = exchange(mixed_part, z_groups)

    local_halves, _, _, half_ff = expert_gate_up.shape
    per_half = Z_SIZE * CAP
    picked = local_halves * per_half
    onehot, mix = pl.pallas_call(
        tables_kernel,
        out_shape=[
            shape((PLANE * picked, all_tokens), bf16),
            shape((all_tokens, PLANE * picked), bf16),
        ],
        in_specs=[SMEM, VMEM],
        out_specs=[VMEM] * 2,
        compiler_params=params(),
        cost_estimate=cost(20 * PLANE * picked * all_tokens, MIB),
        name="tables",
    )(scalar(lax.rem(z_index, 2)), info)
    outgoing = pl.pallas_call(
        pick_kernel,
        out_shape=pltpu.HBM((PLANE, picked, width), bf16),
        in_specs=[VMEM] * 3,
        out_specs=HBM,
        scratch_shapes=[
            pltpu.VMEM((PLANE, picked, width), bf16),
            pltpu.SemaphoreType.DMA((PLANE,)),
        ],
        compiler_params=params(),
        cost_estimate=cost(2 * PLANE * picked * all_tokens * width, 4 * MIB),
        name="pick",
    )(onehot, gain, mixed)

    outgoing, in_plane = lax.optimization_barrier((outgoing, in_plane))
    arrived = exchange(outgoing, planes)
    grouped = pl.pallas_call(
        regroup_kernel,
        out_shape=[shape((PLANE,) + in_plane[0].shape[1:], bf16)] * Z_SIZE,
        in_specs=[SMEM] + [VMEM] * PLANE,
        out_specs=[VMEM] * Z_SIZE,
        compiler_params=params(),
        cost_estimate=cost(0, 2 * MIB),
        name="regroup",
    )(z_scalar, *[in_hbm(piece) for piece in in_plane])
    arrived_cache = [grouped[0]]
    for step in range(1, Z_SIZE):
        arrived_cache.append(lax.ppermute(grouped[step], "seq", z_pairs[step]))

    arrived, shared_weight = lax.optimization_barrier((arrived, shared_weight))
    shared_part, own_mixed = pl.pallas_call(
        shared_kernel,
        out_shape=[shape((all_tokens, width), bf16), shape((tokens, width), f32)],
        in_specs=[SMEM] + [VMEM] * 3,
        out_specs=[VMEM] * 2,
        compiler_params=params(24),
        cost_estimate=cost(6 * all_tokens * 256 * width, 5 * MIB),
        name="shared_expert",
    )(z_scalar, gain, mixed, shared_weight)

    returning = pl.pallas_call(
        experts_kernel,
        out_shape=pltpu.HBM((PLANE, picked, width), bf16),
        in_specs=[VMEM, HBM, HBM],
        out_specs=HBM,
        scratch_shapes=[
            pltpu.VMEM((local_halves, 2, width, half_ff), bf16),
            pltpu.VMEM((local_halves, half_ff, width), bf16),
            pltpu.VMEM((PLANE, picked, width), bf16),
            pltpu.SemaphoreType.DMA((2, local_halves)),
            pltpu.SemaphoreType.DMA((local_halves // 2,)),
        ],
        compiler_params=params(32),
        cost_estimate=cost(6 * PLANE * picked * half_ff * width, 14 * MIB),
        name="experts",
    )(arrived, in_hbm(gate_up), in_hbm(expert_down))
    returning, arrived_cache = lax.optimization_barrier((returning, arrived_cache))
    returned = exchange(returning, planes).reshape(PLANE * picked, width)

    arrived_cache = jnp.concatenate(arrived_cache)
    cache_out = pl.pallas_call(
        reorder_kernel,
        out_shape=shape(arrived_cache.shape, bf16),
        in_specs=[SMEM, SMEM, VMEM],
        out_specs=VMEM,
        compiler_params=params(),
        cost_estimate=cost(0, 2 * arrived_cache.size * 2),
        name="reorder",
    )(scalar(me), block_table, arrived_cache)
    cache_out = cache_out.reshape(devices, per_device, layers, kv_heads, head_size)

    sums = pl.pallas_call(
        combine_kernel,
        out_shape=[shape((tokens, width), bf16)] * Z_SIZE,
        in_specs=[SMEM] + [VMEM] * 3,
        out_specs=[VMEM] * Z_SIZE,
        scratch_shapes=[pltpu.VMEM((all_tokens, width), f32)],
        compiler_params=params(24),
        cost_estimate=cost(2 * all_tokens * PLANE * picked * width, 3 * MIB),
        name="combine",
    )(z_scalar, in_hbm(mix), returned, in_hbm(shared_part))
    layer_out = pl.pallas_call(
        final_kernel,
        out_shape=shape((tokens, width), bf16),
        in_specs=[VMEM] * (1 + Z_SIZE),
        out_specs=VMEM,
        compiler_params=params(),
        cost_estimate=cost(5 * tokens * width, 2 * MIB),
        name="final",
    )(own_mixed, *along_z(sums))
    return (layer_out, cache_out)


def solution(mesh):
    in_specs = (
        P("seq", "head"),
        P("seq", "head"),
        P("seq", "head"),
        P(),
        P("head", "seq"),
        P(("seq", "head"), None),
        P(),
        P(("seq", "head"), None),
        P(("seq", "head"), None),
        P(None, None, ("seq", "head")),
        P(("seq", "head"), None),
        P("seq", None, None, None),
        P("seq", None, None),
        P("seq", None, None, "head", None),
        P(),
    )
    out_specs = (P(("seq", "head"), None), P(None, "seq", None, "head", None))
    planes_fit = mesh.shape["seq"] == Z_SIZE * PLANE and mesh.shape["head"] == 1
    body = shards if planes_fit else general_shards
    return jax.shard_map(body, mesh=mesh, in_specs=in_specs, out_specs=out_specs, check_vma=False)
```

```python
import math

import jax
import jax.numpy as jnp
from jax import lax
from jax.experimental import pallas as pl
from jax.experimental.pallas import tpu as pltpu
from jax.sharding import PartitionSpec as P

HD = 128
EXPERTS = 64
TOP = 6
REACH = 4
HALVES = 128
CAP = 6
Z_SIZE = 4
PLANE = 8
MIB = 1024 * 1024


NEGATIVE = -1e30
EPSILON = 1e-05


def from_behind(shard, axis, by):
    devices = lax.axis_size(axis)
    pairs = [(i, i + by) for i in range(devices) if 0 <= i + by < devices]
    return lax.ppermute(shard, axis, pairs)


def segment_of(positions, lengths):
    request_ends = jnp.cumsum(lengths)
    passed = (request_ends[None, :] <= positions[:, None]).astype(jnp.int32)
    return jnp.sum(passed, axis=1)


def shared_ffn(rows_in, gate_up_part, down_part):
    shared_both = jnp.einsum(
        "td,dcf->tcf", rows_in, gate_up_part, preferred_element_type=jnp.float32
    )
    shared_act = (jax.nn.silu(shared_both[:, 0]) * shared_both[:, 1]).astype(jnp.bfloat16)
    return jnp.dot(shared_act, down_part, preferred_element_type=jnp.float32)


def general_shards(
    queries,
    key_vectors,
    value_vectors,
    lengths,
    out_weight,
    residual,
    norm_gain,
    route_ids,
    route_logits,
    shared_gate_up,
    shared_down,
    expert_gate_up,
    expert_down,
    cache_blocks,
    block_table,
):
    handed = lax.all_to_all(cache_blocks, "seq", split_axis=1, concat_axis=0, tiled=True)
    cache_out = jnp.take(handed, block_table, axis=0)
    tok_rows = queries.shape[0]
    seq_index = lax.axis_index("seq")
    earlier = [
        from_behind((key_vectors, value_vectors), "seq", offset) for offset in range(REACH, 0, -1)
    ]
    window_keys = jnp.concatenate([member[0] for member in earlier] + [key_vectors], axis=0)
    window_values = jnp.concatenate([member[1] for member in earlier] + [value_vectors], axis=0)
    key_count = window_keys.shape[0]
    kv_heads = key_vectors.shape[1] // HD
    query_heads = queries.shape[1] // HD
    group_size = query_heads // kv_heads
    query_pos = seq_index * tok_rows + jnp.arange(tok_rows, dtype=jnp.int32)
    key_pos = (seq_index - REACH) * tok_rows + jnp.arange(key_count, dtype=jnp.int32)
    visible = (key_pos[None, :] >= 0) & (key_pos[None, :] <= query_pos[:, None])
    visible = visible & (
        segment_of(key_pos, lengths)[None, :] == segment_of(query_pos, lengths)[:, None]
    )
    query_part = queries.reshape(tok_rows, kv_heads, group_size, HD)
    key_part = window_keys.reshape(key_count, kv_heads, HD)
    value_part = window_values.reshape(key_count, kv_heads, HD)
    scores = jnp.einsum(
        "tkgd,wkd->kgtw", query_part, key_part, preferred_element_type=jnp.float32
    ) * (1.0 / math.sqrt(HD))
    scores = jnp.where(visible[None, None], scores, NEGATIVE)
    row_max = jnp.max(scores, axis=-1, keepdims=True)
    weights = jnp.exp(scores - row_max)
    row_total = jnp.sum(weights, axis=-1)
    weighted = jnp.einsum(
        "kgtw,wkd->tkgd",
        weights.astype(jnp.bfloat16),
        value_part,
        preferred_element_type=jnp.float32,
    )
    heads = (weighted / jnp.transpose(row_total, (2, 0, 1))[..., None]).astype(jnp.bfloat16)
    heads = heads.reshape(tok_rows, query_heads * HD)
    partial_out = jnp.dot(
        heads,
        lax.all_gather(out_weight, "seq", axis=1, tiled=True),
        preferred_element_type=jnp.float32,
    )
    attn_out = lax.psum_scatter(partial_out, "head", scatter_dimension=0, tiled=True)
    mixed = residual.astype(jnp.float32) + attn_out
    mean_square = jnp.mean(mixed * mixed, axis=-1, keepdims=True)
    normed = (mixed * lax.rsqrt(mean_square + EPSILON) * norm_gain).astype(jnp.bfloat16)
    gate_up_all, down_all = (
        lax.all_gather(shared_gate_up, ("seq", "head"), axis=2, tiled=True),
        lax.all_gather(shared_down, ("seq", "head"), axis=0, tiled=True),
    )
    shared_part = shared_ffn(normed, gate_up_all, down_all)
    own_tokens = normed.shape[0]
    width_model = normed.shape[1]
    flat_ids = route_ids.reshape(-1)
    onehot = (flat_ids[:, None] == jnp.arange(EXPERTS, dtype=jnp.int32)[None, :]).astype(jnp.int32)
    slot_rank = jnp.sum((jnp.cumsum(onehot, axis=0) - 1) * onehot, axis=1)
    first_slot = flat_ids * CAP + slot_rank
    second_slot = (flat_ids + EXPERTS) * CAP + slot_rank
    token_of = jnp.arange(flat_ids.shape[0], dtype=jnp.int32) // TOP
    routed_rows = normed[token_of]
    outgoing = jnp.zeros((HALVES * CAP, width_model), jnp.bfloat16)
    outgoing = outgoing.at[jnp.concatenate([first_slot, second_slot])].set(
        jnp.concatenate([routed_rows, routed_rows], axis=0)
    )
    local_halves = expert_gate_up.shape[0]
    outgoing = outgoing.reshape(HALVES // local_halves, local_halves, CAP, width_model)
    gate_up = jnp.einsum(
        "nsjd,sdcf->nsjcf",
        lax.all_to_all(outgoing, "seq", split_axis=0, concat_axis=0, tiled=True),
        expert_gate_up,
        preferred_element_type=jnp.float32,
    )
    expert_act = (jax.nn.silu(gate_up[:, :, :, 0]) * gate_up[:, :, :, 1]).astype(jnp.bfloat16)
    half_out = jnp.einsum(
        "nsjf,sfd->nsjd", expert_act, expert_down, preferred_element_type=jnp.float32
    ).astype(jnp.bfloat16)
    returned = lax.all_to_all(half_out, "seq", split_axis=0, concat_axis=0, tiled=True)
    returned = returned.reshape(HALVES * CAP, width_model)
    pair_sum = returned[first_slot].astype(jnp.float32) + returned[second_slot].astype(jnp.float32)
    route_probs = jax.nn.softmax(route_logits, axis=-1)
    routed = jnp.sum(
        route_probs[:, :, None] * pair_sum.reshape(own_tokens, TOP, width_model), axis=1
    )
    layer_out = (mixed + shared_part + routed).astype(jnp.bfloat16)
    return (layer_out, cache_out)


VMEM = pl.BlockSpec(memory_space=pltpu.VMEM)
SMEM = pl.BlockSpec(memory_space=pltpu.SMEM)
HBM = pl.BlockSpec(memory_space=pltpu.HBM)


def dot_rows(left, right):
    return lax.dot_general(left, right, (((1,), (1,)), ((), ())), preferred_element_type=jnp.float32)


def dot(left, right):
    return jnp.dot(left, right, preferred_element_type=jnp.float32)


def silu_times(gate, up):
    return (gate / (1.0 + jnp.exp(-gate)) * up).astype(jnp.bfloat16)


def join_kernel(key_ref, value_ref, out_ref):
    width = key_ref.shape[1]
    out_ref[:, :width] = key_ref[...]
    out_ref[:, width:] = value_ref[...]


def attention_kernel(
    z_ref,
    first_ref,
    lengths_ref,
    q_ref,
    k4_ref,
    k3_ref,
    k2_ref,
    k1_ref,
    own_ref,
    residual_ref,
    info_ref,
    *out_refs,
):
    tokens, width = q_ref.shape
    part = width // Z_SIZE
    kv_width = own_ref.shape[1] // 2
    kv_heads = kv_width // HD
    group = width // HD // kv_heads
    blocks = [k4_ref, k3_ref, k2_ref, k1_ref, own_ref]
    keys = len(blocks) * tokens
    first = first_ref[0]
    query_pos = first + lax.broadcasted_iota(jnp.int32, (tokens, keys), 0)
    key_pos = first - (keys - tokens) + lax.broadcasted_iota(jnp.int32, (tokens, keys), 1)
    start = jnp.zeros((tokens, keys), jnp.int32)
    end = jnp.int32(0)
    for request in range(lengths_ref.shape[0]):
        end = end + lengths_ref[request]
        start = jnp.maximum(start, jnp.where(query_pos >= end, end, 0))
    hidden = jnp.where((key_pos >= start) & (key_pos <= query_pos), 0.0, NEGATIVE)
    hidden = jnp.concatenate([hidden] * group, axis=0)
    scale = 1.0 / math.sqrt(HD)
    for flip in range(Z_SIZE):
        z = lax.bitwise_xor(z_ref[0], flip)
        out_ref = out_refs[min(flip, 2)]
        first_column = width if flip < 3 else width + part + HD
        for column in range(Z_SIZE):

            @pl.when(z == column)
            def _(column=column, out_ref=out_ref, first_column=first_column):
                columns = slice(column * part, (column + 1) * part)
                out_ref[:, first_column : first_column + part] = residual_ref[:, columns]

    for out_ref in out_refs:
        out_ref[:, width + part : width + part + HD] = info_ref[...]
    for kv in range(kv_heads):
        at = slice(kv * HD, (kv + 1) * HD)
        value_at = slice(kv_width + kv * HD, kv_width + (kv + 1) * HD)
        key = jnp.concatenate([block[:, at] for block in blocks], axis=0)
        value = jnp.concatenate([block[:, value_at] for block in blocks], axis=0)
        heads = [kv * group + member for member in range(group)]
        query = jnp.concatenate([q_ref[:, h * HD : (h + 1) * HD] for h in heads], axis=0)
        scores = dot_rows(query, key) * scale + hidden
        weights = jnp.exp(scores - jnp.max(scores, axis=-1, keepdims=True))
        total = jnp.sum(weights, axis=-1, keepdims=True)
        result = (dot(weights.astype(jnp.bfloat16), value) / total).astype(jnp.bfloat16)
        for member, h in enumerate(heads):
            for out_ref in out_refs:
                out_ref[:, h * HD : (h + 1) * HD] = result[member * tokens : (member + 1) * tokens]


def route_kernel(z_ref, ids_ref, logits_ref, out_ref, turned_ref):
    choices, tokens = ids_ref.shape
    turned_ref[...] = jnp.zeros(turned_ref.shape, jnp.float32)
    turned_ref[:choices, :tokens] = ids_ref[...].astype(jnp.float32)
    turned_ref[8 : 8 + choices, :tokens] = logits_ref[...]
    table = turned_ref[...].T[:tokens]
    lane = lax.broadcasted_iota(jnp.int32, table.shape, 1)
    ids = [table[:, c : c + 1].astype(jnp.int32) for c in range(choices)]
    logits = [table[:, 8 + c : 9 + c] for c in range(choices)]
    member = jnp.zeros(table.shape, jnp.float32)
    for one in ids:
        member = jnp.where(lane == one, 1.0, member)
    row = lax.broadcasted_iota(jnp.int32, (tokens, tokens), 0)
    earlier = jnp.where(lax.broadcasted_iota(jnp.int32, (tokens, tokens), 1) < row, 1.0, 0.0)
    ahead = dot(earlier.astype(jnp.bfloat16), member.astype(jnp.bfloat16))
    top = logits[0]
    for one in logits[1:]:
        top = jnp.maximum(top, one)
    powers = [jnp.exp(one - top) for one in logits]
    total = sum(powers[1:], powers[0])
    per_device = EXPERTS // 2 // PLANE
    out = jnp.zeros(table.shape, jnp.float32)
    for c, one in enumerate(ids):
        rank = jnp.sum(jnp.where(lane == one, ahead, 0.0), axis=1, keepdims=True)
        where_to = lax.div(one, per_device).astype(jnp.float32)
        first = (lax.rem(one, per_device) * Z_SIZE + z_ref[0]) * CAP
        out = jnp.where(lane == c, where_to, out)
        out = jnp.where(lane == 8 + c, first.astype(jnp.float32) + rank, out)
        out = jnp.where(lane == 16 + c, powers[c] / total, out)
    out_ref[...] = out.astype(jnp.bfloat16)


def regroup_kernel(z_ref, *refs):
    pieces, outs = refs[:PLANE], refs[PLANE:]
    for step, out in enumerate(outs):
        z = lax.rem(z_ref[0] + step, Z_SIZE)
        for at, piece in enumerate(pieces):
            out[at] = piece[z]


def project_kernel(z_ref, *refs):
    sent = refs[:Z_SIZE]
    weight_ref, mixed_ref, info_ref, rows_ref = refs[Z_SIZE:]
    part, width = weight_ref.shape
    for flip, sent_ref in enumerate(sent):
        z = lax.bitwise_xor(z_ref[0], flip)
        if flip < 3:
            rows_ref[z] = sent_ref[:, : rows_ref.shape[2]]
        else:
            rows_ref[z, :, :width] = sent_ref[:, :width]
            rows_ref[z, :, width : width + part] = sent_ref[:, width + part + HD :]
            rows_ref[z, :, width + part :] = sent_ref[:, width + part : width + part + HD]
    rows = jnp.concatenate([rows_ref[z] for z in range(Z_SIZE)], axis=0)
    out = dot_rows(rows[:, :width], weight_ref[...])
    mixed = (out + rows[:, width : width + part].astype(jnp.float32)).astype(jnp.bfloat16)
    for z in range(Z_SIZE):
        mixed_ref[z] = mixed
    info_ref[...] = rows[:, width + part :]


def row_codes(info, first, parity, per_device):
    where_to = info(first).astype(jnp.int32) - PLANE * parity
    inside = info(first + 8).astype(jnp.int32)
    fits = (where_to >= 0) & (where_to < PLANE)
    return jnp.where(fits, where_to * per_device + inside, -1)


def tables_kernel(parity_ref, info_ref, onehot_ref, mix_ref):
    rows, tokens = onehot_ref.shape
    info = info_ref[...].astype(jnp.float32)
    turned = info.T
    codes = row_codes(lambda at: turned[at : at + 8], 0, parity_ref[0], rows // PLANE)
    row = lax.broadcasted_iota(jnp.int32, (rows, tokens), 0)
    chosen = codes[0:1, :] == row
    for choice in range(1, TOP):
        chosen = chosen | (codes[choice : choice + 1, :] == row)
    onehot_ref[...] = jnp.where(chosen, 1.0, 0.0).astype(jnp.bfloat16)
    column = lax.broadcasted_iota(jnp.int32, mix_ref.shape, 1)
    mix = jnp.zeros(mix_ref.shape, jnp.float32)
    for choice in range(TOP):
        code = row_codes(lambda at: info[:, at : at + 1], choice, parity_ref[0], rows // PLANE)
        mix = jnp.where(code == column, info[:, 16 + choice : 17 + choice], mix)
    mix_ref[...] = mix.astype(jnp.bfloat16)


def norm(mixed_ref, gain_ref):
    mixed = jnp.concatenate([mixed_ref[z] for z in range(Z_SIZE)], axis=1).astype(jnp.float32)
    mean_square = jnp.mean(mixed * mixed, axis=-1, keepdims=True)
    return (mixed * lax.rsqrt(mean_square + EPSILON) * gain_ref[...]).astype(jnp.bfloat16)


def pick_kernel(onehot_ref, gain_ref, mixed_ref, out_hbm, out_ref, sems):
    normed = norm(mixed_ref, gain_ref)
    picked = out_ref.shape[1]
    copies = []
    for p in range(PLANE):
        onehot = onehot_ref[p * picked : (p + 1) * picked]
        out_ref[p] = dot(onehot, normed).astype(jnp.bfloat16)
        copy = pltpu.make_async_copy(out_ref.at[p], out_hbm.at[p], sems.at[p])
        copy.start()
        copies.append(copy)
    for copy in copies:
        copy.wait()


def shared_kernel(z_ref, gain_ref, mixed_ref, weight_ref, out_ref, own_ref):
    tokens, columns = own_ref.shape[0], mixed_ref.shape[2]
    own = pl.ds(pl.multiple_of(z_ref[0] * tokens, tokens), tokens)
    for z in range(Z_SIZE):
        own_ref[:, z * columns : (z + 1) * columns] = mixed_ref[z, own, :].astype(jnp.float32)
    parts, units, _ = weight_ref.shape
    units = units // 3
    gate_weight, up_weight, down_weight = [
        jnp.concatenate([weight_ref[p, at * units : (at + 1) * units] for p in range(parts)], axis=0)
        for at in range(3)
    ]
    rows = norm(mixed_ref, gain_ref)
    act = silu_times(dot_rows(rows, gate_weight), dot_rows(rows, up_weight))
    out_ref[...] = dot(act, down_weight).astype(jnp.bfloat16)


def experts_kernel(
    rows_ref, gate_up_hbm, down_hbm, out_hbm, gate_up_ref, down_ref, out_ref, in_sems, out_sems
):
    halves = gate_up_ref.shape[0]
    sources, rows, width = rows_ref.shape
    per_half = rows // halves
    fetches = []
    for half in range(halves):
        pairs = ((gate_up_hbm, gate_up_ref), (down_hbm, down_ref))
        for at, (from_ref, to_ref) in enumerate(pairs):
            fetch = pltpu.make_async_copy(from_ref.at[half], to_ref.at[half], in_sems.at[at, half])
            fetch.start()
            fetches.append(fetch)
    copies = []
    for pair in range(halves // 2):
        both = pl.ds(2 * pair * per_half, 2 * per_half)
        arrived = rows_ref[:, both, :].astype(jnp.float32)
        results = []
        for member in range(2):
            half = 2 * pair + member
            own = arrived[:, member * per_half : (member + 1) * per_half]
            own = own.reshape(sources * per_half, width).astype(jnp.bfloat16)
            fetches[2 * half].wait()
            act = silu_times(dot(own, gate_up_ref[half, 0]), dot(own, gate_up_ref[half, 1]))
            fetches[2 * half + 1].wait()
            results.append(dot(act, down_ref[half]).reshape(sources, per_half, width))
        out_ref[:, both, :] = jnp.concatenate(results, axis=1).astype(jnp.bfloat16)
        copy = pltpu.make_async_copy(out_ref.at[:, both], out_hbm.at[:, both], out_sems.at[pair])
        copy.start()
        copies.append(copy)
    for copy in copies:
        copy.wait()


def combine_kernel(z_ref, mix_ref, rows_ref, shared_ref, *refs):
    outs, sum_ref = refs[:Z_SIZE], refs[Z_SIZE]
    tokens = outs[0].shape[0]
    sum_ref[...] = dot(mix_ref[...], rows_ref[...]) + shared_ref[...].astype(jnp.float32)
    for step, out_ref in enumerate(outs):
        z = lax.rem(z_ref[0] + step, Z_SIZE)
        rows = pl.ds(pl.multiple_of(z * tokens, tokens), tokens)
        out_ref[...] = sum_ref[rows, :].astype(jnp.bfloat16)


def final_kernel(mixed_ref, *refs):
    total = mixed_ref[...]
    for part_ref in refs[:Z_SIZE]:
        total = total + part_ref[...].astype(jnp.float32)
    refs[Z_SIZE][...] = total.astype(jnp.bfloat16)


def reorder_kernel(me_ref, table_ref, from_ref, to_ref):
    me = me_ref[0]
    for block in range(to_ref.shape[0]):
        source = table_ref[block]
        z_steps = lax.rem(lax.div(me, PLANE) - lax.div(source, PLANE) + Z_SIZE, Z_SIZE)
        steps = lax.rem(lax.rem(me, PLANE) - lax.rem(source, PLANE) + PLANE, PLANE)
        to_ref[block] = from_ref[z_steps * PLANE + steps]


def in_hbm(array):
    return pltpu.with_memory_space_constraint(array, pltpu.HBM)


def params(mib=16):
    return pltpu.CompilerParams(vmem_limit_bytes=mib * MIB)


def cost(flops, moved):
    return pl.CostEstimate(flops=int(flops), bytes_accessed=int(moved), transcendentals=0)


def shards(
    queries,
    key_vectors,
    value_vectors,
    lengths,
    out_weight,
    residual,
    norm_gain,
    route_ids,
    route_logits,
    shared_gate_up,
    shared_down,
    expert_gate_up,
    expert_down,
    cache_blocks,
    block_table,
):
    tokens, width = residual.shape
    devices = lax.axis_size("seq")
    me = lax.axis_index("seq")
    z_index, plane_index = lax.div(me, PLANE), lax.rem(me, PLANE)
    z_groups = [[p + PLANE * z for z in range(Z_SIZE)] for p in range(PLANE)]
    planes = [[p + PLANE * z for p in range(PLANE)] for z in range(Z_SIZE)]
    bf16, f32 = jnp.bfloat16, jnp.float32
    shape = jax.ShapeDtypeStruct
    scalar = lambda value: jnp.reshape(value, (1,)).astype(jnp.int32)
    all_tokens = Z_SIZE * tokens
    part = width // Z_SIZE

    def exchange(array, groups):
        return lax.all_to_all(
            array, "seq", split_axis=0, concat_axis=0, tiled=True, axis_index_groups=groups
        )

    own_kv = pl.pallas_call(
        join_kernel,
        out_shape=pltpu.HBM((tokens, 2 * key_vectors.shape[1]), bf16),
        in_specs=[VMEM] * 2,
        out_specs=VMEM,
        compiler_params=params(),
        name="join",
    )(in_hbm(key_vectors), in_hbm(value_vectors))
    behind = [from_behind(own_kv, "seq", offset) for offset in range(REACH, 0, -1)]

    turned_weight = lax.all_gather(
        out_weight.T, "seq", axis=0, tiled=True, axis_index_groups=planes
    )
    info = pl.pallas_call(
        route_kernel,
        out_shape=pltpu.HBM((tokens, 128), bf16),
        in_specs=[SMEM] + [VMEM] * 2,
        out_specs=VMEM,
        scratch_shapes=[pltpu.VMEM((128, 128), f32)],
        compiler_params=params(),
        cost_estimate=cost(MIB, MIB),
        name="route",
    )(scalar(z_index), in_hbm(route_ids.T), in_hbm(route_logits.T))

    def along_z(arrays):
        return [arrays[0]] + [
            lax.ppermute(arrays[step], "seq", z_pairs[step]) for step in range(1, Z_SIZE)
        ]

    z_pairs = [
        [
            (z * PLANE + p, (z + step) % Z_SIZE * PLANE + p)
            for z in range(Z_SIZE)
            for p in range(PLANE)
        ]
        for step in range(Z_SIZE)
    ]
    z_scalar = scalar(z_index)
    gain = norm_gain.reshape(1, width)
    own_shared = jnp.concatenate(
        [jnp.transpose(shared_gate_up, (1, 2, 0)).reshape(-1, width), shared_down], axis=0
    )

    sent_width = width + part + info.shape[1]
    sent = pl.pallas_call(
        attention_kernel,
        out_shape=[
            pltpu.HBM((tokens, sent_width), bf16),
            pltpu.HBM((tokens, sent_width), bf16),
            pltpu.HBM((tokens, sent_width + part), bf16),
        ],
        in_specs=[SMEM] * 3 + [VMEM] * 8,
        out_specs=[VMEM] * 3,
        compiler_params=params(58),
        cost_estimate=cost(4 * tokens * 5 * tokens * width, 3 * MIB),
        name="attention",
    )(z_scalar, scalar(me * tokens), in_hbm(lengths), queries, *behind, own_kv, residual, info)

    sent, own_shared = lax.optimization_barrier((sent, own_shared))
    shared_weight = lax.all_gather(own_shared, "seq", axis=0, axis_index_groups=planes)
    z_swaps = [
        [(z * PLANE + p, (z ^ flip) * PLANE + p) for z in range(Z_SIZE) for p in range(PLANE)]
        for flip in range(Z_SIZE)
    ]
    far = lax.ppermute(sent[2], "seq", z_swaps[2])
    near = lax.ppermute(sent[1], "seq", z_swaps[1])
    passed_on = lax.ppermute(far, "seq", z_swaps[1])
    gathered = [sent[0], near, far, passed_on]
    gathered, cache_blocks, expert_gate_up = lax.optimization_barrier(
        (gathered, cache_blocks, expert_gate_up)
    )

    _, block_tokens, layers, kv_heads, head_size = cache_blocks.shape
    per_device = block_tokens // devices
    cache_view = cache_blocks.reshape(Z_SIZE, PLANE, per_device * layers, kv_heads, head_size)
    in_plane = []
    for step in range(PLANE):
        piece = lax.dynamic_index_in_dim(
            cache_view, lax.rem(plane_index + step, PLANE), axis=1, keepdims=False
        )
        if step:
            pairs = [
                (z * PLANE + p, z * PLANE + (p + step) % PLANE)
                for z in range(Z_SIZE)
                for p in range(PLANE)
            ]
            piece = lax.ppermute(piece, "seq", pairs)
        in_plane.append(piece)
    gate_up = jnp.transpose(expert_gate_up, (0, 2, 1, 3))

    mixed_part, info = pl.pallas_call(
        project_kernel,
        out_shape=[pltpu.HBM((Z_SIZE, all_tokens, part), bf16), shape((all_tokens, 128), bf16)],
        in_specs=[SMEM] + [VMEM] * (Z_SIZE + 1),
        out_specs=[VMEM] * 2,
        scratch_shapes=[pltpu.VMEM((Z_SIZE, tokens, sent_width), bf16)],
        compiler_params=params(),
        cost_estimate=cost(2 * all_tokens * width * part, 3 * MIB),
        name="project",
    )(z_scalar, in_hbm(gathered[0]), *gathered[1:], in_hbm(turned_weight))
    mixed = exchange(mixed_part, z_groups)

    local_halves, _, _, half_ff = expert_gate_up.shape
    per_half = Z_SIZE * CAP
    picked = local_halves * per_half
    onehot, mix = pl.pallas_call(
        tables_kernel,
        out_shape=[
            shape((PLANE * picked, all_tokens), bf16),
            shape((all_tokens, PLANE * picked), bf16),
        ],
        in_specs=[SMEM, VMEM],
        out_specs=[VMEM] * 2,
        compiler_params=params(),
        cost_estimate=cost(20 * PLANE * picked * all_tokens, MIB),
        name="tables",
    )(scalar(lax.rem(z_index, 2)), info)
    outgoing = pl.pallas_call(
        pick_kernel,
        out_shape=pltpu.HBM((PLANE, picked, width), bf16),
        in_specs=[VMEM] * 3,
        out_specs=HBM,
        scratch_shapes=[
            pltpu.VMEM((PLANE, picked, width), bf16),
            pltpu.SemaphoreType.DMA((PLANE,)),
        ],
        compiler_params=params(),
        cost_estimate=cost(2 * PLANE * picked * all_tokens * width, 4 * MIB),
        name="pick",
    )(onehot, gain, mixed)

    outgoing, in_plane = lax.optimization_barrier((outgoing, in_plane))
    arrived = exchange(outgoing, planes)
    grouped = pl.pallas_call(
        regroup_kernel,
        out_shape=[shape((PLANE,) + in_plane[0].shape[1:], bf16)] * Z_SIZE,
        in_specs=[SMEM] + [VMEM] * PLANE,
        out_specs=[VMEM] * Z_SIZE,
        compiler_params=params(),
        cost_estimate=cost(0, 2 * MIB),
        name="regroup",
    )(z_scalar, *[in_hbm(piece) for piece in in_plane])
    arrived_cache = [grouped[0]]
    for step in range(1, Z_SIZE):
        arrived_cache.append(lax.ppermute(grouped[step], "seq", z_pairs[step]))

    arrived, shared_weight = lax.optimization_barrier((arrived, shared_weight))
    shared_part, own_mixed = pl.pallas_call(
        shared_kernel,
        out_shape=[shape((all_tokens, width), bf16), shape((tokens, width), f32)],
        in_specs=[SMEM] + [VMEM] * 3,
        out_specs=[VMEM] * 2,
        compiler_params=params(24),
        cost_estimate=cost(6 * all_tokens * 256 * width, 5 * MIB),
        name="shared_expert",
    )(z_scalar, gain, mixed, shared_weight)

    returning = pl.pallas_call(
        experts_kernel,
        out_shape=pltpu.HBM((PLANE, picked, width), bf16),
        in_specs=[VMEM, HBM, HBM],
        out_specs=HBM,
        scratch_shapes=[
            pltpu.VMEM((local_halves, 2, width, half_ff), bf16),
            pltpu.VMEM((local_halves, half_ff, width), bf16),
            pltpu.VMEM((PLANE, picked, width), bf16),
            pltpu.SemaphoreType.DMA((2, local_halves)),
            pltpu.SemaphoreType.DMA((local_halves // 2,)),
        ],
        compiler_params=params(32),
        cost_estimate=cost(6 * PLANE * picked * half_ff * width, 14 * MIB),
        name="experts",
    )(arrived, in_hbm(gate_up), in_hbm(expert_down))
    returning, arrived_cache = lax.optimization_barrier((returning, arrived_cache))
    returned = exchange(returning, planes).reshape(PLANE * picked, width)

    arrived_cache = jnp.concatenate(arrived_cache)
    cache_out = pl.pallas_call(
        reorder_kernel,
        out_shape=shape(arrived_cache.shape, bf16),
        in_specs=[SMEM, SMEM, VMEM],
        out_specs=VMEM,
        compiler_params=params(),
        cost_estimate=cost(0, 2 * arrived_cache.size * 2),
        name="reorder",
    )(scalar(me), block_table, arrived_cache)
    cache_out = cache_out.reshape(devices, per_device, layers, kv_heads, head_size)

    sums = pl.pallas_call(
        combine_kernel,
        out_shape=[shape((tokens, width), bf16)] * Z_SIZE,
        in_specs=[SMEM] + [VMEM] * 3,
        out_specs=[VMEM] * Z_SIZE,
        scratch_shapes=[pltpu.VMEM((all_tokens, width), f32)],
        compiler_params=params(24),
        cost_estimate=cost(2 * all_tokens * PLANE * picked * width, 3 * MIB),
        name="combine",
    )(z_scalar, in_hbm(mix), returned, in_hbm(shared_part))
    layer_out = pl.pallas_call(
        final_kernel,
        out_shape=shape((tokens, width), bf16),
        in_specs=[VMEM] * (1 + Z_SIZE),
        out_specs=VMEM,
        compiler_params=params(),
        cost_estimate=cost(5 * tokens * width, 2 * MIB),
        name="final",
    )(own_mixed, *along_z(sums))
    return (layer_out, cache_out)


def solution(mesh):
    in_specs = (
        P("seq", "head"),
        P("seq", "head"),
        P("seq", "head"),
        P(),
        P("head", "seq"),
        P(("seq", "head"), None),
        P(),
        P(("seq", "head"), None),
        P(("seq", "head"), None),
        P(None, None, ("seq", "head")),
        P(("seq", "head"), None),
        P("seq", None, None, None),
        P("seq", None, None),
        P("seq", None, None, "head", None),
        P(),
    )
    out_specs = (P(("seq", "head"), None), P(None, "seq", None, "head", None))
    planes_fit = mesh.shape["seq"] == Z_SIZE * PLANE and mesh.shape["head"] == 1
    body = shards if planes_fit else general_shards
    return jax.shard_map(body, mesh=mesh, in_specs=in_specs, out_specs=out_specs, check_vma=False)
```

```python
import math

import jax
import jax.numpy as jnp
from jax import lax
from jax.experimental import pallas as pl
from jax.experimental.pallas import tpu as pltpu
from jax.sharding import PartitionSpec as P

HD = 128
EXPERTS = 64
TOP = 6
REACH = 4
HALVES = 128
CAP = 6
Z_SIZE = 4
PLANE = 8
MIB = 1024 * 1024


NEGATIVE = -1e30
EPSILON = 1e-05


def from_behind(shard, axis, by):
    devices = lax.axis_size(axis)
    pairs = [(i, i + by) for i in range(devices) if 0 <= i + by < devices]
    return lax.ppermute(shard, axis, pairs)


def segment_of(positions, lengths):
    request_ends = jnp.cumsum(lengths)
    passed = (request_ends[None, :] <= positions[:, None]).astype(jnp.int32)
    return jnp.sum(passed, axis=1)


def shared_ffn(rows_in, gate_up_part, down_part):
    shared_both = jnp.einsum(
        "td,dcf->tcf", rows_in, gate_up_part, preferred_element_type=jnp.float32
    )
    shared_act = (jax.nn.silu(shared_both[:, 0]) * shared_both[:, 1]).astype(jnp.bfloat16)
    return jnp.dot(shared_act, down_part, preferred_element_type=jnp.float32)


def general_shards(
    queries,
    key_vectors,
    value_vectors,
    lengths,
    out_weight,
    residual,
    norm_gain,
    route_ids,
    route_logits,
    shared_gate_up,
    shared_down,
    expert_gate_up,
    expert_down,
    cache_blocks,
    block_table,
):
    handed = lax.all_to_all(cache_blocks, "seq", split_axis=1, concat_axis=0, tiled=True)
    cache_out = jnp.take(handed, block_table, axis=0)
    tok_rows = queries.shape[0]
    seq_index = lax.axis_index("seq")
    earlier = [
        from_behind((key_vectors, value_vectors), "seq", offset) for offset in range(REACH, 0, -1)
    ]
    window_keys = jnp.concatenate([member[0] for member in earlier] + [key_vectors], axis=0)
    window_values = jnp.concatenate([member[1] for member in earlier] + [value_vectors], axis=0)
    key_count = window_keys.shape[0]
    kv_heads = key_vectors.shape[1] // HD
    query_heads = queries.shape[1] // HD
    group_size = query_heads // kv_heads
    query_pos = seq_index * tok_rows + jnp.arange(tok_rows, dtype=jnp.int32)
    key_pos = (seq_index - REACH) * tok_rows + jnp.arange(key_count, dtype=jnp.int32)
    visible = (key_pos[None, :] >= 0) & (key_pos[None, :] <= query_pos[:, None])
    visible = visible & (
        segment_of(key_pos, lengths)[None, :] == segment_of(query_pos, lengths)[:, None]
    )
    query_part = queries.reshape(tok_rows, kv_heads, group_size, HD)
    key_part = window_keys.reshape(key_count, kv_heads, HD)
    value_part = window_values.reshape(key_count, kv_heads, HD)
    scores = jnp.einsum(
        "tkgd,wkd->kgtw", query_part, key_part, preferred_element_type=jnp.float32
    ) * (1.0 / math.sqrt(HD))
    scores = jnp.where(visible[None, None], scores, NEGATIVE)
    row_max = jnp.max(scores, axis=-1, keepdims=True)
    weights = jnp.exp(scores - row_max)
    row_total = jnp.sum(weights, axis=-1)
    weighted = jnp.einsum(
        "kgtw,wkd->tkgd",
        weights.astype(jnp.bfloat16),
        value_part,
        preferred_element_type=jnp.float32,
    )
    heads = (weighted / jnp.transpose(row_total, (2, 0, 1))[..., None]).astype(jnp.bfloat16)
    heads = heads.reshape(tok_rows, query_heads * HD)
    partial_out = jnp.dot(
        heads,
        lax.all_gather(out_weight, "seq", axis=1, tiled=True),
        preferred_element_type=jnp.float32,
    )
    attn_out = lax.psum_scatter(partial_out, "head", scatter_dimension=0, tiled=True)
    mixed = residual.astype(jnp.float32) + attn_out
    mean_square = jnp.mean(mixed * mixed, axis=-1, keepdims=True)
    normed = (mixed * lax.rsqrt(mean_square + EPSILON) * norm_gain).astype(jnp.bfloat16)
    gate_up_all, down_all = (
        lax.all_gather(shared_gate_up, ("seq", "head"), axis=2, tiled=True),
        lax.all_gather(shared_down, ("seq", "head"), axis=0, tiled=True),
    )
    shared_part = shared_ffn(normed, gate_up_all, down_all)
    own_tokens = normed.shape[0]
    width_model = normed.shape[1]
    flat_ids = route_ids.reshape(-1)
    onehot = (flat_ids[:, None] == jnp.arange(EXPERTS, dtype=jnp.int32)[None, :]).astype(jnp.int32)
    slot_rank = jnp.sum((jnp.cumsum(onehot, axis=0) - 1) * onehot, axis=1)
    first_slot = flat_ids * CAP + slot_rank
    second_slot = (flat_ids + EXPERTS) * CAP + slot_rank
    token_of = jnp.arange(flat_ids.shape[0], dtype=jnp.int32) // TOP
    routed_rows = normed[token_of]
    outgoing = jnp.zeros((HALVES * CAP, width_model), jnp.bfloat16)
    outgoing = outgoing.at[jnp.concatenate([first_slot, second_slot])].set(
        jnp.concatenate([routed_rows, routed_rows], axis=0)
    )
    local_halves = expert_gate_up.shape[0]
    outgoing = outgoing.reshape(HALVES // local_halves, local_halves, CAP, width_model)
    gate_up = jnp.einsum(
        "nsjd,sdcf->nsjcf",
        lax.all_to_all(outgoing, "seq", split_axis=0, concat_axis=0, tiled=True),
        expert_gate_up,
        preferred_element_type=jnp.float32,
    )
    expert_act = (jax.nn.silu(gate_up[:, :, :, 0]) * gate_up[:, :, :, 1]).astype(jnp.bfloat16)
    half_out = jnp.einsum(
        "nsjf,sfd->nsjd", expert_act, expert_down, preferred_element_type=jnp.float32
    ).astype(jnp.bfloat16)
    returned = lax.all_to_all(half_out, "seq", split_axis=0, concat_axis=0, tiled=True)
    returned = returned.reshape(HALVES * CAP, width_model)
    pair_sum = returned[first_slot].astype(jnp.float32) + returned[second_slot].astype(jnp.float32)
    route_probs = jax.nn.softmax(route_logits, axis=-1)
    routed = jnp.sum(
        route_probs[:, :, None] * pair_sum.reshape(own_tokens, TOP, width_model), axis=1
    )
    layer_out = (mixed + shared_part + routed).astype(jnp.bfloat16)
    return (layer_out, cache_out)


VMEM = pl.BlockSpec(memory_space=pltpu.VMEM)
SMEM = pl.BlockSpec(memory_space=pltpu.SMEM)
HBM = pl.BlockSpec(memory_space=pltpu.HBM)


def dot_rows(left, right):
    return lax.dot_general(left, right, (((1,), (1,)), ((), ())), preferred_element_type=jnp.float32)


def dot(left, right):
    return jnp.dot(left, right, preferred_element_type=jnp.float32)


def silu_times(gate, up):
    return (gate / (1.0 + jnp.exp(-gate)) * up).astype(jnp.bfloat16)


def join_kernel(key_ref, value_ref, out_ref):
    width = key_ref.shape[1]
    out_ref[:, :width] = key_ref[...]
    out_ref[:, width:] = value_ref[...]


def attention_kernel(
    z_ref,
    first_ref,
    lengths_ref,
    q_ref,
    k4_ref,
    k3_ref,
    k2_ref,
    k1_ref,
    own_ref,
    residual_ref,
    info_ref,
    *out_refs,
):
    tokens, width = q_ref.shape
    part = width // Z_SIZE
    kv_width = own_ref.shape[1] // 2
    kv_heads = kv_width // HD
    group = width // HD // kv_heads
    blocks = [k4_ref, k3_ref, k2_ref, k1_ref, own_ref]
    keys = len(blocks) * tokens
    first = first_ref[0]
    query_pos = first + lax.broadcasted_iota(jnp.int32, (tokens, keys), 0)
    key_pos = first - (keys - tokens) + lax.broadcasted_iota(jnp.int32, (tokens, keys), 1)
    start = jnp.zeros((tokens, keys), jnp.int32)
    end = jnp.int32(0)
    for request in range(lengths_ref.shape[0]):
        end = end + lengths_ref[request]
        start = jnp.maximum(start, jnp.where(query_pos >= end, end, 0))
    hidden = jnp.where((key_pos >= start) & (key_pos <= query_pos), 0.0, NEGATIVE)
    hidden = jnp.concatenate([hidden] * group, axis=0)
    scale = 1.0 / math.sqrt(HD)
    for step, out_ref in enumerate(out_refs):
        z = lax.rem(z_ref[0] + step, Z_SIZE)
        for column in range(Z_SIZE):

            @pl.when(z == column)
            def _(column=column, out_ref=out_ref):
                columns = slice(column * part, (column + 1) * part)
                out_ref[:, width : width + part] = residual_ref[:, columns]

        out_ref[:, width + part :] = info_ref[...]
    for kv in range(kv_heads):
        at = slice(kv * HD, (kv + 1) * HD)
        value_at = slice(kv_width + kv * HD, kv_width + (kv + 1) * HD)
        key = jnp.concatenate([block[:, at] for block in blocks], axis=0)
        value = jnp.concatenate([block[:, value_at] for block in blocks], axis=0)
        heads = [kv * group + member for member in range(group)]
        query = jnp.concatenate([q_ref[:, h * HD : (h + 1) * HD] for h in heads], axis=0)
        scores = dot_rows(query, key) * scale + hidden
        weights = jnp.exp(scores - jnp.max(scores, axis=-1, keepdims=True))
        total = jnp.sum(weights, axis=-1, keepdims=True)
        result = (dot(weights.astype(jnp.bfloat16), value) / total).astype(jnp.bfloat16)
        for member, h in enumerate(heads):
            for out_ref in out_refs:
                out_ref[:, h * HD : (h + 1) * HD] = result[member * tokens : (member + 1) * tokens]


def route_kernel(z_ref, ids_ref, logits_ref, out_ref, turned_ref):
    choices, tokens = ids_ref.shape
    turned_ref[...] = jnp.zeros(turned_ref.shape, jnp.float32)
    turned_ref[:choices, :tokens] = ids_ref[...].astype(jnp.float32)
    turned_ref[8 : 8 + choices, :tokens] = logits_ref[...]
    table = turned_ref[...].T[:tokens]
    lane = lax.broadcasted_iota(jnp.int32, table.shape, 1)
    ids = [table[:, c : c + 1].astype(jnp.int32) for c in range(choices)]
    logits = [table[:, 8 + c : 9 + c] for c in range(choices)]
    member = jnp.zeros(table.shape, jnp.float32)
    for one in ids:
        member = jnp.where(lane == one, 1.0, member)
    row = lax.broadcasted_iota(jnp.int32, (tokens, tokens), 0)
    earlier = jnp.where(lax.broadcasted_iota(jnp.int32, (tokens, tokens), 1) < row, 1.0, 0.0)
    ahead = dot(earlier.astype(jnp.bfloat16), member.astype(jnp.bfloat16))
    top = logits[0]
    for one in logits[1:]:
        top = jnp.maximum(top, one)
    powers = [jnp.exp(one - top) for one in logits]
    total = sum(powers[1:], powers[0])
    per_device = EXPERTS // 2 // PLANE
    out = jnp.zeros(table.shape, jnp.float32)
    for c, one in enumerate(ids):
        rank = jnp.sum(jnp.where(lane == one, ahead, 0.0), axis=1, keepdims=True)
        where_to = lax.div(one, per_device).astype(jnp.float32)
        first = (lax.rem(one, per_device) * Z_SIZE + z_ref[0]) * CAP
        out = jnp.where(lane == c, where_to, out)
        out = jnp.where(lane == 8 + c, first.astype(jnp.float32) + rank, out)
        out = jnp.where(lane == 16 + c, powers[c] / total, out)
    out_ref[...] = out.astype(jnp.bfloat16)


def regroup_kernel(z_ref, *refs):
    pieces, outs = refs[:PLANE], refs[PLANE:]
    for step, out in enumerate(outs):
        z = lax.rem(z_ref[0] + step, Z_SIZE)
        for at, piece in enumerate(pieces):
            out[at] = piece[z]


def source_z(z_ref, step):
    return lax.rem(z_ref[0] + Z_SIZE - step, Z_SIZE)


def project_kernel(z_ref, *refs):
    sent = refs[:Z_SIZE]
    weight_ref, mixed_ref, info_ref, rows_ref = refs[Z_SIZE:]
    for step, sent_ref in enumerate(sent):
        rows_ref[source_z(z_ref, step)] = sent_ref[...]
    rows = jnp.concatenate([rows_ref[z] for z in range(Z_SIZE)], axis=0)
    part, width = weight_ref.shape
    out = dot_rows(rows[:, :width], weight_ref[...])
    mixed = (out + rows[:, width : width + part].astype(jnp.float32)).astype(jnp.bfloat16)
    for z in range(Z_SIZE):
        mixed_ref[z] = mixed
    info_ref[...] = rows[:, width + part :]


def row_codes(info, first, parity, per_device):
    where_to = info(first).astype(jnp.int32) - PLANE * parity
    inside = info(first + 8).astype(jnp.int32)
    fits = (where_to >= 0) & (where_to < PLANE)
    return jnp.where(fits, where_to * per_device + inside, -1)


def tables_kernel(parity_ref, info_ref, onehot_ref, mix_ref):
    rows, tokens = onehot_ref.shape
    info = info_ref[...].astype(jnp.float32)
    turned = info.T
    codes = row_codes(lambda at: turned[at : at + 8], 0, parity_ref[0], rows // PLANE)
    row = lax.broadcasted_iota(jnp.int32, (rows, tokens), 0)
    chosen = codes[0:1, :] == row
    for choice in range(1, TOP):
        chosen = chosen | (codes[choice : choice + 1, :] == row)
    onehot_ref[...] = jnp.where(chosen, 1.0, 0.0).astype(jnp.bfloat16)
    column = lax.broadcasted_iota(jnp.int32, mix_ref.shape, 1)
    mix = jnp.zeros(mix_ref.shape, jnp.float32)
    for choice in range(TOP):
        code = row_codes(lambda at: info[:, at : at + 1], choice, parity_ref[0], rows // PLANE)
        mix = jnp.where(code == column, info[:, 16 + choice : 17 + choice], mix)
    mix_ref[...] = mix.astype(jnp.bfloat16)


def norm(mixed_ref, gain_ref):
    mixed = jnp.concatenate([mixed_ref[z] for z in range(Z_SIZE)], axis=1).astype(jnp.float32)
    mean_square = jnp.mean(mixed * mixed, axis=-1, keepdims=True)
    return (mixed * lax.rsqrt(mean_square + EPSILON) * gain_ref[...]).astype(jnp.bfloat16)


def pick_kernel(onehot_ref, gain_ref, mixed_ref, out_hbm, out_ref, sems):
    normed = norm(mixed_ref, gain_ref)
    picked = out_ref.shape[1]
    copies = []
    for p in range(PLANE):
        onehot = onehot_ref[p * picked : (p + 1) * picked]
        out_ref[p] = dot(onehot, normed).astype(jnp.bfloat16)
        copy = pltpu.make_async_copy(out_ref.at[p], out_hbm.at[p], sems.at[p])
        copy.start()
        copies.append(copy)
    for copy in copies:
        copy.wait()


def shared_kernel(z_ref, gain_ref, mixed_ref, weight_ref, out_ref, own_ref):
    tokens, columns = own_ref.shape[0], mixed_ref.shape[2]
    own = pl.ds(pl.multiple_of(z_ref[0] * tokens, tokens), tokens)
    for z in range(Z_SIZE):
        own_ref[:, z * columns : (z + 1) * columns] = mixed_ref[z, own, :].astype(jnp.float32)
    parts, units, _ = weight_ref.shape
    units = units // 3
    gate_weight, up_weight, down_weight = [
        jnp.concatenate([weight_ref[p, at * units : (at + 1) * units] for p in range(parts)], axis=0)
        for at in range(3)
    ]
    rows = norm(mixed_ref, gain_ref)
    act = silu_times(dot_rows(rows, gate_weight), dot_rows(rows, up_weight))
    out_ref[...] = dot(act, down_weight).astype(jnp.bfloat16)


def experts_kernel(
    rows_ref, gate_up_hbm, down_hbm, out_hbm, gate_up_ref, down_ref, out_ref, in_sems, out_sems
):
    halves = gate_up_ref.shape[0]
    sources, rows, width = rows_ref.shape
    per_half = rows // halves
    fetches = []
    for half in range(halves):
        pairs = ((gate_up_hbm, gate_up_ref), (down_hbm, down_ref))
        for at, (from_ref, to_ref) in enumerate(pairs):
            fetch = pltpu.make_async_copy(from_ref.at[half], to_ref.at[half], in_sems.at[at, half])
            fetch.start()
            fetches.append(fetch)
    copies = []
    for pair in range(halves // 2):
        both = pl.ds(2 * pair * per_half, 2 * per_half)
        arrived = rows_ref[:, both, :].astype(jnp.float32)
        results = []
        for member in range(2):
            half = 2 * pair + member
            own = arrived[:, member * per_half : (member + 1) * per_half]
            own = own.reshape(sources * per_half, width).astype(jnp.bfloat16)
            fetches[2 * half].wait()
            act = silu_times(dot(own, gate_up_ref[half, 0]), dot(own, gate_up_ref[half, 1]))
            fetches[2 * half + 1].wait()
            results.append(dot(act, down_ref[half]).reshape(sources, per_half, width))
        out_ref[:, both, :] = jnp.concatenate(results, axis=1).astype(jnp.bfloat16)
        copy = pltpu.make_async_copy(out_ref.at[:, both], out_hbm.at[:, both], out_sems.at[pair])
        copy.start()
        copies.append(copy)
    for copy in copies:
        copy.wait()


def combine_kernel(z_ref, mix_ref, rows_ref, shared_ref, *refs):
    outs, sum_ref = refs[:Z_SIZE], refs[Z_SIZE]
    tokens = outs[0].shape[0]
    sum_ref[...] = dot(mix_ref[...], rows_ref[...]) + shared_ref[...].astype(jnp.float32)
    for step, out_ref in enumerate(outs):
        z = lax.rem(z_ref[0] + step, Z_SIZE)
        rows = pl.ds(pl.multiple_of(z * tokens, tokens), tokens)
        out_ref[...] = sum_ref[rows, :].astype(jnp.bfloat16)


def final_kernel(mixed_ref, *refs):
    total = mixed_ref[...]
    for part_ref in refs[:Z_SIZE]:
        total = total + part_ref[...].astype(jnp.float32)
    refs[Z_SIZE][...] = total.astype(jnp.bfloat16)


def reorder_kernel(me_ref, table_ref, from_ref, to_ref):
    me = me_ref[0]
    for block in range(to_ref.shape[0]):
        source = table_ref[block]
        z_steps = lax.rem(lax.div(me, PLANE) - lax.div(source, PLANE) + Z_SIZE, Z_SIZE)
        steps = lax.rem(lax.rem(me, PLANE) - lax.rem(source, PLANE) + PLANE, PLANE)
        to_ref[block] = from_ref[z_steps * PLANE + steps]


def in_hbm(array):
    return pltpu.with_memory_space_constraint(array, pltpu.HBM)


def params(mib=16):
    return pltpu.CompilerParams(vmem_limit_bytes=mib * MIB)


def cost(flops, moved):
    return pl.CostEstimate(flops=int(flops), bytes_accessed=int(moved), transcendentals=0)


def shards(
    queries,
    key_vectors,
    value_vectors,
    lengths,
    out_weight,
    residual,
    norm_gain,
    route_ids,
    route_logits,
    shared_gate_up,
    shared_down,
    expert_gate_up,
    expert_down,
    cache_blocks,
    block_table,
):
    tokens, width = residual.shape
    devices = lax.axis_size("seq")
    me = lax.axis_index("seq")
    z_index, plane_index = lax.div(me, PLANE), lax.rem(me, PLANE)
    z_groups = [[p + PLANE * z for z in range(Z_SIZE)] for p in range(PLANE)]
    planes = [[p + PLANE * z for p in range(PLANE)] for z in range(Z_SIZE)]
    bf16, f32 = jnp.bfloat16, jnp.float32
    shape = jax.ShapeDtypeStruct
    scalar = lambda value: jnp.reshape(value, (1,)).astype(jnp.int32)
    all_tokens = Z_SIZE * tokens
    part = width // Z_SIZE

    def exchange(array, groups):
        return lax.all_to_all(
            array, "seq", split_axis=0, concat_axis=0, tiled=True, axis_index_groups=groups
        )

    own_kv = pl.pallas_call(
        join_kernel,
        out_shape=pltpu.HBM((tokens, 2 * key_vectors.shape[1]), bf16),
        in_specs=[VMEM] * 2,
        out_specs=VMEM,
        compiler_params=params(),
        name="join",
    )(in_hbm(key_vectors), in_hbm(value_vectors))
    behind = [from_behind(own_kv, "seq", offset) for offset in range(REACH, 0, -1)]

    info = pl.pallas_call(
        route_kernel,
        out_shape=pltpu.HBM((tokens, 128), bf16),
        in_specs=[SMEM] + [VMEM] * 2,
        out_specs=VMEM,
        scratch_shapes=[pltpu.VMEM((128, 128), f32)],
        compiler_params=params(),
        cost_estimate=cost(MIB, MIB),
        name="route",
    )(scalar(z_index), in_hbm(route_ids.T), in_hbm(route_logits.T))

    info, out_weight = lax.optimization_barrier((info, out_weight))
    turned_weight = lax.all_gather(
        out_weight.T, "seq", axis=0, tiled=True, axis_index_groups=planes
    )

    def along_z(arrays):
        return [arrays[0]] + [
            lax.ppermute(arrays[step], "seq", z_pairs[step]) for step in range(1, Z_SIZE)
        ]

    z_pairs = [
        [
            (z * PLANE + p, (z + step) % Z_SIZE * PLANE + p)
            for z in range(Z_SIZE)
            for p in range(PLANE)
        ]
        for step in range(Z_SIZE)
    ]
    z_scalar = scalar(z_index)
    gain = norm_gain.reshape(1, width)
    own_shared = jnp.concatenate(
        [jnp.transpose(shared_gate_up, (1, 2, 0)).reshape(-1, width), shared_down], axis=0
    )

    sent_width = width + part + info.shape[1]
    sent = pl.pallas_call(
        attention_kernel,
        out_shape=[pltpu.HBM((tokens, sent_width), bf16)] * Z_SIZE,
        in_specs=[SMEM] * 3 + [VMEM] * 8,
        out_specs=[VMEM] * Z_SIZE,
        compiler_params=params(58),
        cost_estimate=cost(4 * tokens * 5 * tokens * width, 3 * MIB),
        name="attention",
    )(z_scalar, scalar(me * tokens), in_hbm(lengths), queries, *behind, own_kv, residual, info)

    sent, own_shared = lax.optimization_barrier((sent, own_shared))
    shared_weight = lax.all_gather(own_shared, "seq", axis=0, axis_index_groups=planes)
    gathered = along_z(sent)
    gathered, cache_blocks, expert_gate_up = lax.optimization_barrier(
        (gathered, cache_blocks, expert_gate_up)
    )

    _, block_tokens, layers, kv_heads, head_size = cache_blocks.shape
    per_device = block_tokens // devices
    cache_view = cache_blocks.reshape(Z_SIZE, PLANE, per_device * layers, kv_heads, head_size)
    in_plane = []
    for step in range(PLANE):
        piece = lax.dynamic_index_in_dim(
            cache_view, lax.rem(plane_index + step, PLANE), axis=1, keepdims=False
        )
        if step:
            pairs = [
                (z * PLANE + p, z * PLANE + (p + step) % PLANE)
                for z in range(Z_SIZE)
                for p in range(PLANE)
            ]
            piece = lax.ppermute(piece, "seq", pairs)
        in_plane.append(piece)
    gate_up = jnp.transpose(expert_gate_up, (0, 2, 1, 3))

    mixed_part, info = pl.pallas_call(
        project_kernel,
        out_shape=[pltpu.HBM((Z_SIZE, all_tokens, part), bf16), shape((all_tokens, 128), bf16)],
        in_specs=[SMEM] + [VMEM] * (Z_SIZE + 1),
        out_specs=[VMEM] * 2,
        scratch_shapes=[pltpu.VMEM((Z_SIZE, tokens, sent_width), bf16)],
        compiler_params=params(),
        cost_estimate=cost(2 * all_tokens * width * part, 3 * MIB),
        name="project",
    )(z_scalar, in_hbm(gathered[0]), *gathered[1:], in_hbm(turned_weight))
    mixed = exchange(mixed_part, z_groups)

    local_halves, _, _, half_ff = expert_gate_up.shape
    per_half = Z_SIZE * CAP
    picked = local_halves * per_half
    onehot, mix = pl.pallas_call(
        tables_kernel,
        out_shape=[
            shape((PLANE * picked, all_tokens), bf16),
            shape((all_tokens, PLANE * picked), bf16),
        ],
        in_specs=[SMEM, VMEM],
        out_specs=[VMEM] * 2,
        compiler_params=params(),
        cost_estimate=cost(20 * PLANE * picked * all_tokens, MIB),
        name="tables",
    )(scalar(lax.rem(z_index, 2)), info)
    outgoing = pl.pallas_call(
        pick_kernel,
        out_shape=pltpu.HBM((PLANE, picked, width), bf16),
        in_specs=[VMEM] * 3,
        out_specs=HBM,
        scratch_shapes=[
            pltpu.VMEM((PLANE, picked, width), bf16),
            pltpu.SemaphoreType.DMA((PLANE,)),
        ],
        compiler_params=params(),
        cost_estimate=cost(2 * PLANE * picked * all_tokens * width, 4 * MIB),
        name="pick",
    )(onehot, gain, mixed)

    outgoing, in_plane = lax.optimization_barrier((outgoing, in_plane))
    arrived = exchange(outgoing, planes)
    grouped = pl.pallas_call(
        regroup_kernel,
        out_shape=[shape((PLANE,) + in_plane[0].shape[1:], bf16)] * Z_SIZE,
        in_specs=[SMEM] + [VMEM] * PLANE,
        out_specs=[VMEM] * Z_SIZE,
        compiler_params=params(),
        cost_estimate=cost(0, 2 * MIB),
        name="regroup",
    )(z_scalar, *[in_hbm(piece) for piece in in_plane])
    arrived_cache = [grouped[0]]
    for step in range(1, Z_SIZE):
        arrived_cache.append(lax.ppermute(grouped[step], "seq", z_pairs[step]))

    arrived, shared_weight = lax.optimization_barrier((arrived, shared_weight))
    shared_part, own_mixed = pl.pallas_call(
        shared_kernel,
        out_shape=[shape((all_tokens, width), bf16), shape((tokens, width), f32)],
        in_specs=[SMEM] + [VMEM] * 3,
        out_specs=[VMEM] * 2,
        compiler_params=params(24),
        cost_estimate=cost(6 * all_tokens * 256 * width, 5 * MIB),
        name="shared_expert",
    )(z_scalar, gain, mixed, shared_weight)

    returning = pl.pallas_call(
        experts_kernel,
        out_shape=pltpu.HBM((PLANE, picked, width), bf16),
        in_specs=[VMEM, HBM, HBM],
        out_specs=HBM,
        scratch_shapes=[
            pltpu.VMEM((local_halves, 2, width, half_ff), bf16),
            pltpu.VMEM((local_halves, half_ff, width), bf16),
            pltpu.VMEM((PLANE, picked, width), bf16),
            pltpu.SemaphoreType.DMA((2, local_halves)),
            pltpu.SemaphoreType.DMA((local_halves // 2,)),
        ],
        compiler_params=params(32),
        cost_estimate=cost(6 * PLANE * picked * half_ff * width, 14 * MIB),
        name="experts",
    )(arrived, in_hbm(gate_up), in_hbm(expert_down))
    returning, arrived_cache = lax.optimization_barrier((returning, arrived_cache))
    returned = exchange(returning, planes).reshape(PLANE * picked, width)

    arrived_cache = jnp.concatenate(arrived_cache)
    cache_out = pl.pallas_call(
        reorder_kernel,
        out_shape=shape(arrived_cache.shape, bf16),
        in_specs=[SMEM, SMEM, VMEM],
        out_specs=VMEM,
        compiler_params=params(),
        cost_estimate=cost(0, 2 * arrived_cache.size * 2),
        name="reorder",
    )(scalar(me), block_table, arrived_cache)
    cache_out = cache_out.reshape(devices, per_device, layers, kv_heads, head_size)

    sums = pl.pallas_call(
        combine_kernel,
        out_shape=[shape((tokens, width), bf16)] * Z_SIZE,
        in_specs=[SMEM] + [VMEM] * 3,
        out_specs=[VMEM] * Z_SIZE,
        scratch_shapes=[pltpu.VMEM((all_tokens, width), f32)],
        compiler_params=params(24),
        cost_estimate=cost(2 * all_tokens * PLANE * picked * width, 3 * MIB),
        name="combine",
    )(z_scalar, in_hbm(mix), returned, in_hbm(shared_part))
    layer_out = pl.pallas_call(
        final_kernel,
        out_shape=shape((tokens, width), bf16),
        in_specs=[VMEM] * (1 + Z_SIZE),
        out_specs=VMEM,
        compiler_params=params(),
        cost_estimate=cost(5 * tokens * width, 2 * MIB),
        name="final",
    )(own_mixed, *along_z(sums))
    return (layer_out, cache_out)


def solution(mesh):
    in_specs = (
        P("seq", "head"),
        P("seq", "head"),
        P("seq", "head"),
        P(),
        P("head", "seq"),
        P(("seq", "head"), None),
        P(),
        P(("seq", "head"), None),
        P(("seq", "head"), None),
        P(None, None, ("seq", "head")),
        P(("seq", "head"), None),
        P("seq", None, None, None),
        P("seq", None, None),
        P("seq", None, None, "head", None),
        P(),
    )
    out_specs = (P(("seq", "head"), None), P(None, "seq", None, "head", None))
    planes_fit = mesh.shape["seq"] == Z_SIZE * PLANE and mesh.shape["head"] == 1
    body = shards if planes_fit else general_shards
    return jax.shard_map(body, mesh=mesh, in_specs=in_specs, out_specs=out_specs, check_vma=False)
```

```python
import math

import jax
import jax.numpy as jnp
from jax import lax
from jax.experimental import pallas as pl
from jax.experimental.pallas import tpu as pltpu
from jax.sharding import PartitionSpec as P

HD = 128
EXPERTS = 64
TOP = 6
REACH = 4
HALVES = 128
CAP = 6
Z_SIZE = 4
PLANE = 8
MIB = 1024 * 1024


NEGATIVE = -1e30
EPSILON = 1e-05


def from_behind(shard, axis, by):
    devices = lax.axis_size(axis)
    pairs = [(i, i + by) for i in range(devices) if 0 <= i + by < devices]
    return lax.ppermute(shard, axis, pairs)


def segment_of(positions, lengths):
    request_ends = jnp.cumsum(lengths)
    passed = (request_ends[None, :] <= positions[:, None]).astype(jnp.int32)
    return jnp.sum(passed, axis=1)


def shared_ffn(rows_in, gate_up_part, down_part):
    shared_both = jnp.einsum(
        "td,dcf->tcf", rows_in, gate_up_part, preferred_element_type=jnp.float32
    )
    shared_act = (jax.nn.silu(shared_both[:, 0]) * shared_both[:, 1]).astype(jnp.bfloat16)
    return jnp.dot(shared_act, down_part, preferred_element_type=jnp.float32)


def general_shards(
    queries,
    key_vectors,
    value_vectors,
    lengths,
    out_weight,
    residual,
    norm_gain,
    route_ids,
    route_logits,
    shared_gate_up,
    shared_down,
    expert_gate_up,
    expert_down,
    cache_blocks,
    block_table,
):
    handed = lax.all_to_all(cache_blocks, "seq", split_axis=1, concat_axis=0, tiled=True)
    cache_out = jnp.take(handed, block_table, axis=0)
    tok_rows = queries.shape[0]
    seq_index = lax.axis_index("seq")
    earlier = [
        from_behind((key_vectors, value_vectors), "seq", offset) for offset in range(REACH, 0, -1)
    ]
    window_keys = jnp.concatenate([member[0] for member in earlier] + [key_vectors], axis=0)
    window_values = jnp.concatenate([member[1] for member in earlier] + [value_vectors], axis=0)
    key_count = window_keys.shape[0]
    kv_heads = key_vectors.shape[1] // HD
    query_heads = queries.shape[1] // HD
    group_size = query_heads // kv_heads
    query_pos = seq_index * tok_rows + jnp.arange(tok_rows, dtype=jnp.int32)
    key_pos = (seq_index - REACH) * tok_rows + jnp.arange(key_count, dtype=jnp.int32)
    visible = (key_pos[None, :] >= 0) & (key_pos[None, :] <= query_pos[:, None])
    visible = visible & (
        segment_of(key_pos, lengths)[None, :] == segment_of(query_pos, lengths)[:, None]
    )
    query_part = queries.reshape(tok_rows, kv_heads, group_size, HD)
    key_part = window_keys.reshape(key_count, kv_heads, HD)
    value_part = window_values.reshape(key_count, kv_heads, HD)
    scores = jnp.einsum(
        "tkgd,wkd->kgtw", query_part, key_part, preferred_element_type=jnp.float32
    ) * (1.0 / math.sqrt(HD))
    scores = jnp.where(visible[None, None], scores, NEGATIVE)
    row_max = jnp.max(scores, axis=-1, keepdims=True)
    weights = jnp.exp(scores - row_max)
    row_total = jnp.sum(weights, axis=-1)
    weighted = jnp.einsum(
        "kgtw,wkd->tkgd",
        weights.astype(jnp.bfloat16),
        value_part,
        preferred_element_type=jnp.float32,
    )
    heads = (weighted / jnp.transpose(row_total, (2, 0, 1))[..., None]).astype(jnp.bfloat16)
    heads = heads.reshape(tok_rows, query_heads * HD)
    partial_out = jnp.dot(
        heads,
        lax.all_gather(out_weight, "seq", axis=1, tiled=True),
        preferred_element_type=jnp.float32,
    )
    attn_out = lax.psum_scatter(partial_out, "head", scatter_dimension=0, tiled=True)
    mixed = residual.astype(jnp.float32) + attn_out
    mean_square = jnp.mean(mixed * mixed, axis=-1, keepdims=True)
    normed = (mixed * lax.rsqrt(mean_square + EPSILON) * norm_gain).astype(jnp.bfloat16)
    gate_up_all, down_all = (
        lax.all_gather(shared_gate_up, ("seq", "head"), axis=2, tiled=True),
        lax.all_gather(shared_down, ("seq", "head"), axis=0, tiled=True),
    )
    shared_part = shared_ffn(normed, gate_up_all, down_all)
    own_tokens = normed.shape[0]
    width_model = normed.shape[1]
    flat_ids = route_ids.reshape(-1)
    onehot = (flat_ids[:, None] == jnp.arange(EXPERTS, dtype=jnp.int32)[None, :]).astype(jnp.int32)
    slot_rank = jnp.sum((jnp.cumsum(onehot, axis=0) - 1) * onehot, axis=1)
    first_slot = flat_ids * CAP + slot_rank
    second_slot = (flat_ids + EXPERTS) * CAP + slot_rank
    token_of = jnp.arange(flat_ids.shape[0], dtype=jnp.int32) // TOP
    routed_rows = normed[token_of]
    outgoing = jnp.zeros((HALVES * CAP, width_model), jnp.bfloat16)
    outgoing = outgoing.at[jnp.concatenate([first_slot, second_slot])].set(
        jnp.concatenate([routed_rows, routed_rows], axis=0)
    )
    local_halves = expert_gate_up.shape[0]
    outgoing = outgoing.reshape(HALVES // local_halves, local_halves, CAP, width_model)
    gate_up = jnp.einsum(
        "nsjd,sdcf->nsjcf",
        lax.all_to_all(outgoing, "seq", split_axis=0, concat_axis=0, tiled=True),
        expert_gate_up,
        preferred_element_type=jnp.float32,
    )
    expert_act = (jax.nn.silu(gate_up[:, :, :, 0]) * gate_up[:, :, :, 1]).astype(jnp.bfloat16)
    half_out = jnp.einsum(
        "nsjf,sfd->nsjd", expert_act, expert_down, preferred_element_type=jnp.float32
    ).astype(jnp.bfloat16)
    returned = lax.all_to_all(half_out, "seq", split_axis=0, concat_axis=0, tiled=True)
    returned = returned.reshape(HALVES * CAP, width_model)
    pair_sum = returned[first_slot].astype(jnp.float32) + returned[second_slot].astype(jnp.float32)
    route_probs = jax.nn.softmax(route_logits, axis=-1)
    routed = jnp.sum(
        route_probs[:, :, None] * pair_sum.reshape(own_tokens, TOP, width_model), axis=1
    )
    layer_out = (mixed + shared_part + routed).astype(jnp.bfloat16)
    return (layer_out, cache_out)


VMEM = pl.BlockSpec(memory_space=pltpu.VMEM)
SMEM = pl.BlockSpec(memory_space=pltpu.SMEM)
HBM = pl.BlockSpec(memory_space=pltpu.HBM)


def dot_rows(left, right):
    return lax.dot_general(left, right, (((1,), (1,)), ((), ())), preferred_element_type=jnp.float32)


def dot(left, right):
    return jnp.dot(left, right, preferred_element_type=jnp.float32)


def silu_times(gate, up):
    return (gate / (1.0 + jnp.exp(-gate)) * up).astype(jnp.bfloat16)


def join_kernel(key_ref, value_ref, out_ref):
    width = key_ref.shape[1]
    out_ref[:, :width] = key_ref[...]
    out_ref[:, width:] = value_ref[...]


def attention_kernel(
    z_ref,
    first_ref,
    lengths_ref,
    q_ref,
    k4_ref,
    k3_ref,
    k2_ref,
    k1_ref,
    own_ref,
    residual_ref,
    info_ref,
    *out_refs,
):
    tokens, width = q_ref.shape
    part = width // Z_SIZE
    kv_width = own_ref.shape[1] // 2
    kv_heads = kv_width // HD
    group = width // HD // kv_heads
    blocks = [k4_ref, k3_ref, k2_ref, k1_ref, own_ref]
    keys = len(blocks) * tokens
    first = first_ref[0]
    query_pos = first + lax.broadcasted_iota(jnp.int32, (tokens, keys), 0)
    key_pos = first - (keys - tokens) + lax.broadcasted_iota(jnp.int32, (tokens, keys), 1)
    start = jnp.zeros((tokens, keys), jnp.int32)
    end = jnp.int32(0)
    for request in range(lengths_ref.shape[0]):
        end = end + lengths_ref[request]
        start = jnp.maximum(start, jnp.where(query_pos >= end, end, 0))
    hidden = jnp.where((key_pos >= start) & (key_pos <= query_pos), 0.0, NEGATIVE)
    hidden = jnp.concatenate([hidden] * group, axis=0)
    scale = 1.0 / math.sqrt(HD)
    for step, out_ref in enumerate(out_refs):
        z = lax.rem(z_ref[0] + step, Z_SIZE)
        for column in range(Z_SIZE):

            @pl.when(z == column)
            def _(column=column, out_ref=out_ref):
                columns = slice(column * part, (column + 1) * part)
                out_ref[:, width : width + part] = residual_ref[:, columns]

        out_ref[:, width + part :] = info_ref[...]
    for kv in range(kv_heads):
        at = slice(kv * HD, (kv + 1) * HD)
        value_at = slice(kv_width + kv * HD, kv_width + (kv + 1) * HD)
        key = jnp.concatenate([block[:, at] for block in blocks], axis=0)
        value = jnp.concatenate([block[:, value_at] for block in blocks], axis=0)
        heads = [kv * group + member for member in range(group)]
        query = jnp.concatenate([q_ref[:, h * HD : (h + 1) * HD] for h in heads], axis=0)
        scores = dot_rows(query, key) * scale + hidden
        weights = jnp.exp(scores - jnp.max(scores, axis=-1, keepdims=True))
        total = jnp.sum(weights, axis=-1, keepdims=True)
        result = (dot(weights.astype(jnp.bfloat16), value) / total).astype(jnp.bfloat16)
        for member, h in enumerate(heads):
            for out_ref in out_refs:
                out_ref[:, h * HD : (h + 1) * HD] = result[member * tokens : (member + 1) * tokens]


def route_kernel(z_ref, ids_ref, logits_ref, out_ref, turned_ref):
    choices, tokens = ids_ref.shape
    turned_ref[...] = jnp.zeros(turned_ref.shape, jnp.float32)
    turned_ref[:choices, :tokens] = ids_ref[...].astype(jnp.float32)
    turned_ref[8 : 8 + choices, :tokens] = logits_ref[...]
    table = turned_ref[...].T[:tokens]
    lane = lax.broadcasted_iota(jnp.int32, table.shape, 1)
    ids = [table[:, c : c + 1].astype(jnp.int32) for c in range(choices)]
    logits = [table[:, 8 + c : 9 + c] for c in range(choices)]
    member = jnp.zeros(table.shape, jnp.float32)
    for one in ids:
        member = jnp.where(lane == one, 1.0, member)
    row = lax.broadcasted_iota(jnp.int32, (tokens, tokens), 0)
    earlier = jnp.where(lax.broadcasted_iota(jnp.int32, (tokens, tokens), 1) < row, 1.0, 0.0)
    ahead = dot(earlier.astype(jnp.bfloat16), member.astype(jnp.bfloat16))
    top = logits[0]
    for one in logits[1:]:
        top = jnp.maximum(top, one)
    powers = [jnp.exp(one - top) for one in logits]
    total = sum(powers[1:], powers[0])
    per_device = EXPERTS // 2 // PLANE
    out = jnp.zeros(table.shape, jnp.float32)
    for c, one in enumerate(ids):
        rank = jnp.sum(jnp.where(lane == one, ahead, 0.0), axis=1, keepdims=True)
        where_to = lax.div(one, per_device).astype(jnp.float32)
        first = (lax.rem(one, per_device) * Z_SIZE + z_ref[0]) * CAP
        out = jnp.where(lane == c, where_to, out)
        out = jnp.where(lane == 8 + c, first.astype(jnp.float32) + rank, out)
        out = jnp.where(lane == 16 + c, powers[c] / total, out)
    out_ref[...] = out.astype(jnp.bfloat16)


def regroup_kernel(z_ref, *refs):
    pieces, outs = refs[:PLANE], refs[PLANE:]
    for step, out in enumerate(outs):
        z = lax.rem(z_ref[0] + step, Z_SIZE)
        for at, piece in enumerate(pieces):
            out[at] = piece[z]


def source_z(z_ref, step):
    return lax.rem(z_ref[0] + Z_SIZE - step, Z_SIZE)


def project_kernel(z_ref, *refs):
    sent = refs[:Z_SIZE]
    weight_ref, mixed_ref, info_ref, rows_ref = refs[Z_SIZE:]
    for step, sent_ref in enumerate(sent):
        rows_ref[source_z(z_ref, step)] = sent_ref[...]
    rows = jnp.concatenate([rows_ref[z] for z in range(Z_SIZE)], axis=0)
    part, width = weight_ref.shape
    out = dot_rows(rows[:, :width], weight_ref[...])
    mixed = (out + rows[:, width : width + part].astype(jnp.float32)).astype(jnp.bfloat16)
    for z in range(Z_SIZE):
        mixed_ref[z] = mixed
    info_ref[...] = rows[:, width + part :]


def row_codes(info, first, parity, per_device):
    where_to = info(first).astype(jnp.int32) - PLANE * parity
    inside = info(first + 8).astype(jnp.int32)
    fits = (where_to >= 0) & (where_to < PLANE)
    return jnp.where(fits, where_to * per_device + inside, -1)


def tables_kernel(parity_ref, info_ref, onehot_ref, mix_ref):
    rows, tokens = onehot_ref.shape
    info = info_ref[...].astype(jnp.float32)
    turned = info.T
    codes = row_codes(lambda at: turned[at : at + 8], 0, parity_ref[0], rows // PLANE)
    row = lax.broadcasted_iota(jnp.int32, (rows, tokens), 0)
    chosen = codes[0:1, :] == row
    for choice in range(1, TOP):
        chosen = chosen | (codes[choice : choice + 1, :] == row)
    onehot_ref[...] = jnp.where(chosen, 1.0, 0.0).astype(jnp.bfloat16)
    column = lax.broadcasted_iota(jnp.int32, mix_ref.shape, 1)
    mix = jnp.zeros(mix_ref.shape, jnp.float32)
    for choice in range(TOP):
        code = row_codes(lambda at: info[:, at : at + 1], choice, parity_ref[0], rows // PLANE)
        mix = jnp.where(code == column, info[:, 16 + choice : 17 + choice], mix)
    mix_ref[...] = mix.astype(jnp.bfloat16)


def norm(mixed_ref, gain_ref):
    mixed = jnp.concatenate([mixed_ref[z] for z in range(Z_SIZE)], axis=1).astype(jnp.float32)
    mean_square = jnp.mean(mixed * mixed, axis=-1, keepdims=True)
    return (mixed * lax.rsqrt(mean_square + EPSILON) * gain_ref[...]).astype(jnp.bfloat16)


def pick_kernel(onehot_ref, gain_ref, mixed_ref, out_hbm, out_ref, sems):
    normed = norm(mixed_ref, gain_ref)
    picked = out_ref.shape[1]
    copies = []
    for p in range(PLANE):
        onehot = onehot_ref[p * picked : (p + 1) * picked]
        out_ref[p] = dot(onehot, normed).astype(jnp.bfloat16)
        copy = pltpu.make_async_copy(out_ref.at[p], out_hbm.at[p], sems.at[p])
        copy.start()
        copies.append(copy)
    for copy in copies:
        copy.wait()


def shared_kernel(z_ref, gain_ref, mixed_ref, weight_ref, out_ref, own_ref):
    tokens, columns = own_ref.shape[0], mixed_ref.shape[2]
    own = pl.ds(pl.multiple_of(z_ref[0] * tokens, tokens), tokens)
    for z in range(Z_SIZE):
        own_ref[:, z * columns : (z + 1) * columns] = mixed_ref[z, own, :].astype(jnp.float32)
    parts, units, _ = weight_ref.shape
    units = units // 3
    gate_weight, up_weight, down_weight = [
        jnp.concatenate([weight_ref[p, at * units : (at + 1) * units] for p in range(parts)], axis=0)
        for at in range(3)
    ]
    rows = norm(mixed_ref, gain_ref)
    act = silu_times(dot_rows(rows, gate_weight), dot_rows(rows, up_weight))
    out_ref[...] = dot(act, down_weight).astype(jnp.bfloat16)


def experts_kernel(
    rows_ref, gate_up_hbm, down_hbm, out_hbm, gate_up_ref, down_ref, out_ref, in_sems, out_sems
):
    halves = gate_up_ref.shape[0]
    sources, rows, width = rows_ref.shape
    per_half = rows // halves
    fetches = []
    for half in range(halves):
        pairs = ((gate_up_hbm, gate_up_ref), (down_hbm, down_ref))
        for at, (from_ref, to_ref) in enumerate(pairs):
            fetch = pltpu.make_async_copy(from_ref.at[half], to_ref.at[half], in_sems.at[at, half])
            fetch.start()
            fetches.append(fetch)
    copies = []
    for pair in range(halves // 2):
        both = pl.ds(2 * pair * per_half, 2 * per_half)
        arrived = rows_ref[:, both, :].astype(jnp.float32)
        results = []
        for member in range(2):
            half = 2 * pair + member
            own = arrived[:, member * per_half : (member + 1) * per_half]
            own = own.reshape(sources * per_half, width).astype(jnp.bfloat16)
            fetches[2 * half].wait()
            act = silu_times(dot(own, gate_up_ref[half, 0]), dot(own, gate_up_ref[half, 1]))
            fetches[2 * half + 1].wait()
            results.append(dot(act, down_ref[half]).reshape(sources, per_half, width))
        out_ref[:, both, :] = jnp.concatenate(results, axis=1).astype(jnp.bfloat16)
        copy = pltpu.make_async_copy(out_ref.at[:, both], out_hbm.at[:, both], out_sems.at[pair])
        copy.start()
        copies.append(copy)
    for copy in copies:
        copy.wait()


def combine_kernel(z_ref, mix_ref, rows_ref, shared_ref, *refs):
    outs, sum_ref = refs[:Z_SIZE], refs[Z_SIZE]
    tokens = outs[0].shape[0]
    sum_ref[...] = dot(mix_ref[...], rows_ref[...]) + shared_ref[...].astype(jnp.float32)
    for step, out_ref in enumerate(outs):
        z = lax.rem(z_ref[0] + step, Z_SIZE)
        rows = pl.ds(pl.multiple_of(z * tokens, tokens), tokens)
        out_ref[...] = sum_ref[rows, :].astype(jnp.bfloat16)


def final_kernel(mixed_ref, *refs):
    total = mixed_ref[...]
    for part_ref in refs[:Z_SIZE]:
        total = total + part_ref[...].astype(jnp.float32)
    refs[Z_SIZE][...] = total.astype(jnp.bfloat16)


def reorder_kernel(me_ref, table_ref, from_ref, to_ref):
    me = me_ref[0]
    for block in range(to_ref.shape[0]):
        source = table_ref[block]
        z_steps = lax.rem(lax.div(me, PLANE) - lax.div(source, PLANE) + Z_SIZE, Z_SIZE)
        steps = lax.rem(lax.rem(me, PLANE) - lax.rem(source, PLANE) + PLANE, PLANE)
        to_ref[block] = from_ref[z_steps * PLANE + steps]


def in_hbm(array):
    return pltpu.with_memory_space_constraint(array, pltpu.HBM)


def params(mib=16):
    return pltpu.CompilerParams(vmem_limit_bytes=mib * MIB)


def cost(flops, moved):
    return pl.CostEstimate(flops=int(flops), bytes_accessed=int(moved), transcendentals=0)


def shards(
    queries,
    key_vectors,
    value_vectors,
    lengths,
    out_weight,
    residual,
    norm_gain,
    route_ids,
    route_logits,
    shared_gate_up,
    shared_down,
    expert_gate_up,
    expert_down,
    cache_blocks,
    block_table,
):
    tokens, width = residual.shape
    devices = lax.axis_size("seq")
    me = lax.axis_index("seq")
    z_index, plane_index = lax.div(me, PLANE), lax.rem(me, PLANE)
    z_groups = [[p + PLANE * z for z in range(Z_SIZE)] for p in range(PLANE)]
    planes = [[p + PLANE * z for p in range(PLANE)] for z in range(Z_SIZE)]
    bf16, f32 = jnp.bfloat16, jnp.float32
    shape = jax.ShapeDtypeStruct
    scalar = lambda value: jnp.reshape(value, (1,)).astype(jnp.int32)
    all_tokens = Z_SIZE * tokens
    part = width // Z_SIZE

    def exchange(array, groups):
        return lax.all_to_all(
            array, "seq", split_axis=0, concat_axis=0, tiled=True, axis_index_groups=groups
        )

    own_kv = pl.pallas_call(
        join_kernel,
        out_shape=pltpu.HBM((tokens, 2 * key_vectors.shape[1]), bf16),
        in_specs=[VMEM] * 2,
        out_specs=VMEM,
        compiler_params=params(),
        name="join",
    )(in_hbm(key_vectors), in_hbm(value_vectors))
    behind = [from_behind(own_kv, "seq", offset) for offset in range(REACH, 0, -1)]

    turned_weight = lax.all_gather(
        out_weight.T, "seq", axis=0, tiled=True, axis_index_groups=planes
    )
    info = pl.pallas_call(
        route_kernel,
        out_shape=pltpu.HBM((tokens, 128), bf16),
        in_specs=[SMEM] + [VMEM] * 2,
        out_specs=VMEM,
        scratch_shapes=[pltpu.VMEM((128, 128), f32)],
        compiler_params=params(),
        cost_estimate=cost(MIB, MIB),
        name="route",
    )(scalar(z_index), in_hbm(route_ids.T), in_hbm(route_logits.T))

    def along_z(arrays):
        return [arrays[0]] + [
            lax.ppermute(arrays[step], "seq", z_pairs[step]) for step in range(1, Z_SIZE)
        ]

    z_pairs = [
        [
            (z * PLANE + p, (z + step) % Z_SIZE * PLANE + p)
            for z in range(Z_SIZE)
            for p in range(PLANE)
        ]
        for step in range(Z_SIZE)
    ]
    z_scalar = scalar(z_index)
    gain = norm_gain.reshape(1, width)
    own_shared = jnp.concatenate(
        [jnp.transpose(shared_gate_up, (1, 2, 0)).reshape(-1, width), shared_down], axis=0
    )

    sent_width = width + part + info.shape[1]
    sent = pl.pallas_call(
        attention_kernel,
        out_shape=[pltpu.HBM((tokens, sent_width), bf16)] * Z_SIZE,
        in_specs=[SMEM] * 3 + [VMEM] * 8,
        out_specs=[VMEM] * Z_SIZE,
        compiler_params=params(),
        cost_estimate=cost(4 * tokens * 5 * tokens * width, 3 * MIB),
        name="attention",
    )(z_scalar, scalar(me * tokens), in_hbm(lengths), in_hbm(queries), *behind, own_kv, in_hbm(residual), info)

    sent, own_shared = lax.optimization_barrier((sent, own_shared))
    shared_weight = lax.all_gather(own_shared, "seq", axis=0, axis_index_groups=planes)
    gathered = along_z(sent)
    gathered, cache_blocks, expert_gate_up = lax.optimization_barrier(
        (gathered, cache_blocks, expert_gate_up)
    )

    _, block_tokens, layers, kv_heads, head_size = cache_blocks.shape
    per_device = block_tokens // devices
    cache_view = cache_blocks.reshape(Z_SIZE, PLANE, per_device * layers, kv_heads, head_size)
    in_plane = []
    for step in range(PLANE):
        piece = lax.dynamic_index_in_dim(
            cache_view, lax.rem(plane_index + step, PLANE), axis=1, keepdims=False
        )
        if step:
            pairs = [
                (z * PLANE + p, z * PLANE + (p + step) % PLANE)
                for z in range(Z_SIZE)
                for p in range(PLANE)
            ]
            piece = lax.ppermute(piece, "seq", pairs)
        in_plane.append(piece)
    gate_up = jnp.transpose(expert_gate_up, (0, 2, 1, 3))

    mixed_part, info = pl.pallas_call(
        project_kernel,
        out_shape=[pltpu.HBM((Z_SIZE, all_tokens, part), bf16), shape((all_tokens, 128), bf16)],
        in_specs=[SMEM] + [VMEM] * (Z_SIZE + 1),
        out_specs=[VMEM] * 2,
        scratch_shapes=[pltpu.VMEM((Z_SIZE, tokens, sent_width), bf16)],
        compiler_params=params(),
        cost_estimate=cost(2 * all_tokens * width * part, 3 * MIB),
        name="project",
    )(z_scalar, in_hbm(gathered[0]), *gathered[1:], in_hbm(turned_weight))
    mixed = exchange(mixed_part, z_groups)

    local_halves, _, _, half_ff = expert_gate_up.shape
    per_half = Z_SIZE * CAP
    picked = local_halves * per_half
    onehot, mix = pl.pallas_call(
        tables_kernel,
        out_shape=[
            shape((PLANE * picked, all_tokens), bf16),
            shape((all_tokens, PLANE * picked), bf16),
        ],
        in_specs=[SMEM, VMEM],
        out_specs=[VMEM] * 2,
        compiler_params=params(),
        cost_estimate=cost(20 * PLANE * picked * all_tokens, MIB),
        name="tables",
    )(scalar(lax.rem(z_index, 2)), info)
    outgoing = pl.pallas_call(
        pick_kernel,
        out_shape=pltpu.HBM((PLANE, picked, width), bf16),
        in_specs=[VMEM] * 3,
        out_specs=HBM,
        scratch_shapes=[
            pltpu.VMEM((PLANE, picked, width), bf16),
            pltpu.SemaphoreType.DMA((PLANE,)),
        ],
        compiler_params=params(),
        cost_estimate=cost(2 * PLANE * picked * all_tokens * width, 4 * MIB),
        name="pick",
    )(onehot, gain, mixed)

    outgoing, in_plane = lax.optimization_barrier((outgoing, in_plane))
    arrived = exchange(outgoing, planes)
    grouped = pl.pallas_call(
        regroup_kernel,
        out_shape=[shape((PLANE,) + in_plane[0].shape[1:], bf16)] * Z_SIZE,
        in_specs=[SMEM] + [VMEM] * PLANE,
        out_specs=[VMEM] * Z_SIZE,
        compiler_params=params(),
        cost_estimate=cost(0, 2 * MIB),
        name="regroup",
    )(z_scalar, *[in_hbm(piece) for piece in in_plane])
    arrived_cache = [grouped[0]]
    for step in range(1, Z_SIZE):
        arrived_cache.append(lax.ppermute(grouped[step], "seq", z_pairs[step]))

    arrived, shared_weight = lax.optimization_barrier((arrived, shared_weight))
    shared_part, own_mixed = pl.pallas_call(
        shared_kernel,
        out_shape=[shape((all_tokens, width), bf16), shape((tokens, width), f32)],
        in_specs=[SMEM] + [VMEM] * 3,
        out_specs=[VMEM] * 2,
        compiler_params=params(24),
        cost_estimate=cost(6 * all_tokens * 256 * width, 5 * MIB),
        name="shared_expert",
    )(z_scalar, gain, mixed, shared_weight)

    returning = pl.pallas_call(
        experts_kernel,
        out_shape=pltpu.HBM((PLANE, picked, width), bf16),
        in_specs=[VMEM, HBM, HBM],
        out_specs=HBM,
        scratch_shapes=[
            pltpu.VMEM((local_halves, 2, width, half_ff), bf16),
            pltpu.VMEM((local_halves, half_ff, width), bf16),
            pltpu.VMEM((PLANE, picked, width), bf16),
            pltpu.SemaphoreType.DMA((2, local_halves)),
            pltpu.SemaphoreType.DMA((local_halves // 2,)),
        ],
        compiler_params=params(32),
        cost_estimate=cost(6 * PLANE * picked * half_ff * width, 14 * MIB),
        name="experts",
    )(arrived, in_hbm(gate_up), in_hbm(expert_down))
    returning, arrived_cache = lax.optimization_barrier((returning, arrived_cache))
    returned = exchange(returning, planes).reshape(PLANE * picked, width)

    arrived_cache = jnp.concatenate(arrived_cache)
    cache_out = pl.pallas_call(
        reorder_kernel,
        out_shape=shape(arrived_cache.shape, bf16),
        in_specs=[SMEM, SMEM, VMEM],
        out_specs=VMEM,
        compiler_params=params(),
        cost_estimate=cost(0, 2 * arrived_cache.size * 2),
        name="reorder",
    )(scalar(me), block_table, arrived_cache)
    cache_out = cache_out.reshape(devices, per_device, layers, kv_heads, head_size)

    sums = pl.pallas_call(
        combine_kernel,
        out_shape=[shape((tokens, width), bf16)] * Z_SIZE,
        in_specs=[SMEM] + [VMEM] * 3,
        out_specs=[VMEM] * Z_SIZE,
        scratch_shapes=[pltpu.VMEM((all_tokens, width), f32)],
        compiler_params=params(24),
        cost_estimate=cost(2 * all_tokens * PLANE * picked * width, 3 * MIB),
        name="combine",
    )(z_scalar, in_hbm(mix), returned, in_hbm(shared_part))
    layer_out = pl.pallas_call(
        final_kernel,
        out_shape=shape((tokens, width), bf16),
        in_specs=[VMEM] * (1 + Z_SIZE),
        out_specs=VMEM,
        compiler_params=params(),
        cost_estimate=cost(5 * tokens * width, 2 * MIB),
        name="final",
    )(own_mixed, *along_z(sums))
    return (layer_out, cache_out)


def solution(mesh):
    in_specs = (
        P("seq", "head"),
        P("seq", "head"),
        P("seq", "head"),
        P(),
        P("head", "seq"),
        P(("seq", "head"), None),
        P(),
        P(("seq", "head"), None),
        P(("seq", "head"), None),
        P(None, None, ("seq", "head")),
        P(("seq", "head"), None),
        P("seq", None, None, None),
        P("seq", None, None),
        P("seq", None, None, "head", None),
        P(),
    )
    out_specs = (P(("seq", "head"), None), P(None, "seq", None, "head", None))
    planes_fit = mesh.shape["seq"] == Z_SIZE * PLANE and mesh.shape["head"] == 1
    body = shards if planes_fit else general_shards
    return jax.shard_map(body, mesh=mesh, in_specs=in_specs, out_specs=out_specs, check_vma=False)
```

```python
import math

import jax
import jax.numpy as jnp
from jax import lax
from jax.experimental import pallas as pl
from jax.experimental.pallas import tpu as pltpu
from jax.sharding import PartitionSpec as P

HD = 128
EXPERTS = 64
TOP = 6
REACH = 4
HALVES = 128
CAP = 6
Z_SIZE = 4
PLANE = 8
MIB = 1024 * 1024


NEGATIVE = -1e30
EPSILON = 1e-05


def from_behind(shard, axis, by):
    devices = lax.axis_size(axis)
    pairs = [(i, i + by) for i in range(devices) if 0 <= i + by < devices]
    return lax.ppermute(shard, axis, pairs)


def segment_of(positions, lengths):
    request_ends = jnp.cumsum(lengths)
    passed = (request_ends[None, :] <= positions[:, None]).astype(jnp.int32)
    return jnp.sum(passed, axis=1)


def shared_ffn(rows_in, gate_up_part, down_part):
    shared_both = jnp.einsum(
        "td,dcf->tcf", rows_in, gate_up_part, preferred_element_type=jnp.float32
    )
    shared_act = (jax.nn.silu(shared_both[:, 0]) * shared_both[:, 1]).astype(jnp.bfloat16)
    return jnp.dot(shared_act, down_part, preferred_element_type=jnp.float32)


def general_shards(
    queries,
    key_vectors,
    value_vectors,
    lengths,
    out_weight,
    residual,
    norm_gain,
    route_ids,
    route_logits,
    shared_gate_up,
    shared_down,
    expert_gate_up,
    expert_down,
    cache_blocks,
    block_table,
):
    handed = lax.all_to_all(cache_blocks, "seq", split_axis=1, concat_axis=0, tiled=True)
    cache_out = jnp.take(handed, block_table, axis=0)
    tok_rows = queries.shape[0]
    seq_index = lax.axis_index("seq")
    earlier = [
        from_behind((key_vectors, value_vectors), "seq", offset) for offset in range(REACH, 0, -1)
    ]
    window_keys = jnp.concatenate([member[0] for member in earlier] + [key_vectors], axis=0)
    window_values = jnp.concatenate([member[1] for member in earlier] + [value_vectors], axis=0)
    key_count = window_keys.shape[0]
    kv_heads = key_vectors.shape[1] // HD
    query_heads = queries.shape[1] // HD
    group_size = query_heads // kv_heads
    query_pos = seq_index * tok_rows + jnp.arange(tok_rows, dtype=jnp.int32)
    key_pos = (seq_index - REACH) * tok_rows + jnp.arange(key_count, dtype=jnp.int32)
    visible = (key_pos[None, :] >= 0) & (key_pos[None, :] <= query_pos[:, None])
    visible = visible & (
        segment_of(key_pos, lengths)[None, :] == segment_of(query_pos, lengths)[:, None]
    )
    query_part = queries.reshape(tok_rows, kv_heads, group_size, HD)
    key_part = window_keys.reshape(key_count, kv_heads, HD)
    value_part = window_values.reshape(key_count, kv_heads, HD)
    scores = jnp.einsum(
        "tkgd,wkd->kgtw", query_part, key_part, preferred_element_type=jnp.float32
    ) * (1.0 / math.sqrt(HD))
    scores = jnp.where(visible[None, None], scores, NEGATIVE)
    row_max = jnp.max(scores, axis=-1, keepdims=True)
    weights = jnp.exp(scores - row_max)
    row_total = jnp.sum(weights, axis=-1)
    weighted = jnp.einsum(
        "kgtw,wkd->tkgd",
        weights.astype(jnp.bfloat16),
        value_part,
        preferred_element_type=jnp.float32,
    )
    heads = (weighted / jnp.transpose(row_total, (2, 0, 1))[..., None]).astype(jnp.bfloat16)
    heads = heads.reshape(tok_rows, query_heads * HD)
    partial_out = jnp.dot(
        heads,
        lax.all_gather(out_weight, "seq", axis=1, tiled=True),
        preferred_element_type=jnp.float32,
    )
    attn_out = lax.psum_scatter(partial_out, "head", scatter_dimension=0, tiled=True)
    mixed = residual.astype(jnp.float32) + attn_out
    mean_square = jnp.mean(mixed * mixed, axis=-1, keepdims=True)
    normed = (mixed * lax.rsqrt(mean_square + EPSILON) * norm_gain).astype(jnp.bfloat16)
    gate_up_all, down_all = (
        lax.all_gather(shared_gate_up, ("seq", "head"), axis=2, tiled=True),
        lax.all_gather(shared_down, ("seq", "head"), axis=0, tiled=True),
    )
    shared_part = shared_ffn(normed, gate_up_all, down_all)
    own_tokens = normed.shape[0]
    width_model = normed.shape[1]
    flat_ids = route_ids.reshape(-1)
    onehot = (flat_ids[:, None] == jnp.arange(EXPERTS, dtype=jnp.int32)[None, :]).astype(jnp.int32)
    slot_rank = jnp.sum((jnp.cumsum(onehot, axis=0) - 1) * onehot, axis=1)
    first_slot = flat_ids * CAP + slot_rank
    second_slot = (flat_ids + EXPERTS) * CAP + slot_rank
    token_of = jnp.arange(flat_ids.shape[0], dtype=jnp.int32) // TOP
    routed_rows = normed[token_of]
    outgoing = jnp.zeros((HALVES * CAP, width_model), jnp.bfloat16)
    outgoing = outgoing.at[jnp.concatenate([first_slot, second_slot])].set(
        jnp.concatenate([routed_rows, routed_rows], axis=0)
    )
    local_halves = expert_gate_up.shape[0]
    outgoing = outgoing.reshape(HALVES // local_halves, local_halves, CAP, width_model)
    gate_up = jnp.einsum(
        "nsjd,sdcf->nsjcf",
        lax.all_to_all(outgoing, "seq", split_axis=0, concat_axis=0, tiled=True),
        expert_gate_up,
        preferred_element_type=jnp.float32,
    )
    expert_act = (jax.nn.silu(gate_up[:, :, :, 0]) * gate_up[:, :, :, 1]).astype(jnp.bfloat16)
    half_out = jnp.einsum(
        "nsjf,sfd->nsjd", expert_act, expert_down, preferred_element_type=jnp.float32
    ).astype(jnp.bfloat16)
    returned = lax.all_to_all(half_out, "seq", split_axis=0, concat_axis=0, tiled=True)
    returned = returned.reshape(HALVES * CAP, width_model)
    pair_sum = returned[first_slot].astype(jnp.float32) + returned[second_slot].astype(jnp.float32)
    route_probs = jax.nn.softmax(route_logits, axis=-1)
    routed = jnp.sum(
        route_probs[:, :, None] * pair_sum.reshape(own_tokens, TOP, width_model), axis=1
    )
    layer_out = (mixed + shared_part + routed).astype(jnp.bfloat16)
    return (layer_out, cache_out)


VMEM = pl.BlockSpec(memory_space=pltpu.VMEM)
SMEM = pl.BlockSpec(memory_space=pltpu.SMEM)
HBM = pl.BlockSpec(memory_space=pltpu.HBM)


def dot_rows(left, right):
    return lax.dot_general(left, right, (((1,), (1,)), ((), ())), preferred_element_type=jnp.float32)


def dot(left, right):
    return jnp.dot(left, right, preferred_element_type=jnp.float32)


def silu_times(gate, up):
    return (gate / (1.0 + jnp.exp(-gate)) * up).astype(jnp.bfloat16)


def join_kernel(key_ref, value_ref, out_ref):
    width = key_ref.shape[1]
    out_ref[:, :width] = key_ref[...]
    out_ref[:, width:] = value_ref[...]


def attention_kernel(
    z_ref,
    first_ref,
    lengths_ref,
    q_ref,
    k1_ref,
    k2_ref,
    k3_ref,
    k4_ref,
    own_ref,
    residual_ref,
    info_ref,
    *out_refs,
):
    tokens, width = q_ref.shape
    part = width // Z_SIZE
    kv_width = own_ref.shape[1] // 2
    kv_heads = kv_width // HD
    group = width // HD // kv_heads
    blocks = [k4_ref, k3_ref, k2_ref, k1_ref, own_ref]
    keys = len(blocks) * tokens
    first = first_ref[0]
    query_pos = first + lax.broadcasted_iota(jnp.int32, (tokens, keys), 0)
    key_pos = first - (keys - tokens) + lax.broadcasted_iota(jnp.int32, (tokens, keys), 1)
    start = jnp.zeros((tokens, keys), jnp.int32)
    end = jnp.int32(0)
    for request in range(lengths_ref.shape[0]):
        end = end + lengths_ref[request]
        start = jnp.maximum(start, jnp.where(query_pos >= end, end, 0))
    hidden = jnp.where((key_pos >= start) & (key_pos <= query_pos), 0.0, NEGATIVE)
    hidden = jnp.concatenate([hidden] * group, axis=0)
    scale = 1.0 / math.sqrt(HD)
    for step, out_ref in enumerate(out_refs):
        z = lax.rem(z_ref[0] + step, Z_SIZE)
        for column in range(Z_SIZE):

            @pl.when(z == column)
            def _(column=column, out_ref=out_ref):
                columns = slice(column * part, (column + 1) * part)
                out_ref[:, width : width + part] = residual_ref[:, columns]

        out_ref[:, width + part :] = info_ref[...]
    for kv in range(kv_heads):
        at = slice(kv * HD, (kv + 1) * HD)
        value_at = slice(kv_width + kv * HD, kv_width + (kv + 1) * HD)
        key = jnp.concatenate([block[:, at] for block in blocks], axis=0)
        value = jnp.concatenate([block[:, value_at] for block in blocks], axis=0)
        heads = [kv * group + member for member in range(group)]
        query = jnp.concatenate([q_ref[:, h * HD : (h + 1) * HD] for h in heads], axis=0)
        scores = dot_rows(query, key) * scale + hidden
        weights = jnp.exp(scores - jnp.max(scores, axis=-1, keepdims=True))
        total = jnp.sum(weights, axis=-1, keepdims=True)
        result = (dot(weights.astype(jnp.bfloat16), value) / total).astype(jnp.bfloat16)
        for member, h in enumerate(heads):
            for out_ref in out_refs:
                out_ref[:, h * HD : (h + 1) * HD] = result[member * tokens : (member + 1) * tokens]


def route_kernel(z_ref, ids_ref, logits_ref, out_ref, turned_ref):
    choices, tokens = ids_ref.shape
    turned_ref[...] = jnp.zeros(turned_ref.shape, jnp.float32)
    turned_ref[:choices, :tokens] = ids_ref[...].astype(jnp.float32)
    turned_ref[8 : 8 + choices, :tokens] = logits_ref[...]
    table = turned_ref[...].T[:tokens]
    lane = lax.broadcasted_iota(jnp.int32, table.shape, 1)
    ids = [table[:, c : c + 1].astype(jnp.int32) for c in range(choices)]
    logits = [table[:, 8 + c : 9 + c] for c in range(choices)]
    member = jnp.zeros(table.shape, jnp.float32)
    for one in ids:
        member = jnp.where(lane == one, 1.0, member)
    row = lax.broadcasted_iota(jnp.int32, (tokens, tokens), 0)
    earlier = jnp.where(lax.broadcasted_iota(jnp.int32, (tokens, tokens), 1) < row, 1.0, 0.0)
    ahead = dot(earlier.astype(jnp.bfloat16), member.astype(jnp.bfloat16))
    top = logits[0]
    for one in logits[1:]:
        top = jnp.maximum(top, one)
    powers = [jnp.exp(one - top) for one in logits]
    total = sum(powers[1:], powers[0])
    per_device = EXPERTS // 2 // PLANE
    out = jnp.zeros(table.shape, jnp.float32)
    for c, one in enumerate(ids):
        rank = jnp.sum(jnp.where(lane == one, ahead, 0.0), axis=1, keepdims=True)
        where_to = lax.div(one, per_device).astype(jnp.float32)
        first = (lax.rem(one, per_device) * Z_SIZE + z_ref[0]) * CAP
        out = jnp.where(lane == c, where_to, out)
        out = jnp.where(lane == 8 + c, first.astype(jnp.float32) + rank, out)
        out = jnp.where(lane == 16 + c, powers[c] / total, out)
    out_ref[...] = out.astype(jnp.bfloat16)


def regroup_kernel(z_ref, *refs):
    pieces, outs = refs[:PLANE], refs[PLANE:]
    for step, out in enumerate(outs):
        z = lax.rem(z_ref[0] + step, Z_SIZE)
        for at, piece in enumerate(pieces):
            out[at] = piece[z]


def source_z(z_ref, step):
    return lax.rem(z_ref[0] + Z_SIZE - step, Z_SIZE)


def project_kernel(z_ref, *refs):
    sent = refs[:Z_SIZE]
    weight_ref, mixed_ref, info_ref, rows_ref = refs[Z_SIZE:]
    for step, sent_ref in enumerate(sent):
        rows_ref[source_z(z_ref, step)] = sent_ref[...]
    rows = jnp.concatenate([rows_ref[z] for z in range(Z_SIZE)], axis=0)
    part, width = weight_ref.shape
    out = dot_rows(rows[:, :width], weight_ref[...])
    mixed = (out + rows[:, width : width + part].astype(jnp.float32)).astype(jnp.bfloat16)
    for z in range(Z_SIZE):
        mixed_ref[z] = mixed
    info_ref[...] = rows[:, width + part :]


def row_codes(info, first, parity, per_device):
    where_to = info(first).astype(jnp.int32) - PLANE * parity
    inside = info(first + 8).astype(jnp.int32)
    fits = (where_to >= 0) & (where_to < PLANE)
    return jnp.where(fits, where_to * per_device + inside, -1)


def tables_kernel(parity_ref, info_ref, onehot_ref, mix_ref):
    rows, tokens = onehot_ref.shape
    info = info_ref[...].astype(jnp.float32)
    turned = info.T
    codes = row_codes(lambda at: turned[at : at + 8], 0, parity_ref[0], rows // PLANE)
    row = lax.broadcasted_iota(jnp.int32, (rows, tokens), 0)
    chosen = codes[0:1, :] == row
    for choice in range(1, TOP):
        chosen = chosen | (codes[choice : choice + 1, :] == row)
    onehot_ref[...] = jnp.where(chosen, 1.0, 0.0).astype(jnp.bfloat16)
    column = lax.broadcasted_iota(jnp.int32, mix_ref.shape, 1)
    mix = jnp.zeros(mix_ref.shape, jnp.float32)
    for choice in range(TOP):
        code = row_codes(lambda at: info[:, at : at + 1], choice, parity_ref[0], rows // PLANE)
        mix = jnp.where(code == column, info[:, 16 + choice : 17 + choice], mix)
    mix_ref[...] = mix.astype(jnp.bfloat16)


def norm(mixed_ref, gain_ref):
    mixed = jnp.concatenate([mixed_ref[z] for z in range(Z_SIZE)], axis=1).astype(jnp.float32)
    mean_square = jnp.mean(mixed * mixed, axis=-1, keepdims=True)
    return (mixed * lax.rsqrt(mean_square + EPSILON) * gain_ref[...]).astype(jnp.bfloat16)


def pick_kernel(onehot_ref, gain_ref, mixed_ref, out_hbm, out_ref, sems):
    normed = norm(mixed_ref, gain_ref)
    picked = out_ref.shape[1]
    copies = []
    for p in range(PLANE):
        onehot = onehot_ref[p * picked : (p + 1) * picked]
        out_ref[p] = dot(onehot, normed).astype(jnp.bfloat16)
        copy = pltpu.make_async_copy(out_ref.at[p], out_hbm.at[p], sems.at[p])
        copy.start()
        copies.append(copy)
    for copy in copies:
        copy.wait()


def shared_kernel(z_ref, gain_ref, mixed_ref, weight_ref, out_ref, own_ref):
    tokens, columns = own_ref.shape[0], mixed_ref.shape[2]
    own = pl.ds(pl.multiple_of(z_ref[0] * tokens, tokens), tokens)
    for z in range(Z_SIZE):
        own_ref[:, z * columns : (z + 1) * columns] = mixed_ref[z, own, :].astype(jnp.float32)
    parts, units, _ = weight_ref.shape
    units = units // 3
    gate_weight, up_weight, down_weight = [
        jnp.concatenate([weight_ref[p, at * units : (at + 1) * units] for p in range(parts)], axis=0)
        for at in range(3)
    ]
    rows = norm(mixed_ref, gain_ref)
    act = silu_times(dot_rows(rows, gate_weight), dot_rows(rows, up_weight))
    out_ref[...] = dot(act, down_weight).astype(jnp.bfloat16)


def experts_kernel(
    rows_ref, gate_up_hbm, down_hbm, out_hbm, gate_up_ref, down_ref, out_ref, in_sems, out_sems
):
    halves = gate_up_ref.shape[0]
    sources, rows, width = rows_ref.shape
    per_half = rows // halves
    fetches = []
    for half in range(halves):
        pairs = ((gate_up_hbm, gate_up_ref), (down_hbm, down_ref))
        for at, (from_ref, to_ref) in enumerate(pairs):
            fetch = pltpu.make_async_copy(from_ref.at[half], to_ref.at[half], in_sems.at[at, half])
            fetch.start()
            fetches.append(fetch)
    copies = []
    for pair in range(halves // 2):
        both = pl.ds(2 * pair * per_half, 2 * per_half)
        arrived = rows_ref[:, both, :].astype(jnp.float32)
        results = []
        for member in range(2):
            half = 2 * pair + member
            own = arrived[:, member * per_half : (member + 1) * per_half]
            own = own.reshape(sources * per_half, width).astype(jnp.bfloat16)
            fetches[2 * half].wait()
            act = silu_times(dot(own, gate_up_ref[half, 0]), dot(own, gate_up_ref[half, 1]))
            fetches[2 * half + 1].wait()
            results.append(dot(act, down_ref[half]).reshape(sources, per_half, width))
        out_ref[:, both, :] = jnp.concatenate(results, axis=1).astype(jnp.bfloat16)
        copy = pltpu.make_async_copy(out_ref.at[:, both], out_hbm.at[:, both], out_sems.at[pair])
        copy.start()
        copies.append(copy)
    for copy in copies:
        copy.wait()


def combine_kernel(z_ref, mix_ref, rows_ref, shared_ref, *refs):
    outs, sum_ref = refs[:Z_SIZE], refs[Z_SIZE]
    tokens = outs[0].shape[0]
    sum_ref[...] = dot(mix_ref[...], rows_ref[...]) + shared_ref[...].astype(jnp.float32)
    for step, out_ref in enumerate(outs):
        z = lax.rem(z_ref[0] + step, Z_SIZE)
        rows = pl.ds(pl.multiple_of(z * tokens, tokens), tokens)
        out_ref[...] = sum_ref[rows, :].astype(jnp.bfloat16)


def final_kernel(mixed_ref, *refs):
    total = mixed_ref[...]
    for part_ref in refs[:Z_SIZE]:
        total = total + part_ref[...].astype(jnp.float32)
    refs[Z_SIZE][...] = total.astype(jnp.bfloat16)


def reorder_kernel(me_ref, table_ref, from_ref, to_ref):
    me = me_ref[0]
    for block in range(to_ref.shape[0]):
        source = table_ref[block]
        z_steps = lax.rem(lax.div(me, PLANE) - lax.div(source, PLANE) + Z_SIZE, Z_SIZE)
        steps = lax.rem(lax.rem(me, PLANE) - lax.rem(source, PLANE) + PLANE, PLANE)
        to_ref[block] = from_ref[z_steps * PLANE + steps]


def in_hbm(array):
    return pltpu.with_memory_space_constraint(array, pltpu.HBM)


def params(mib=16):
    return pltpu.CompilerParams(vmem_limit_bytes=mib * MIB)


def cost(flops, moved):
    return pl.CostEstimate(flops=int(flops), bytes_accessed=int(moved), transcendentals=0)


def shards(
    queries,
    key_vectors,
    value_vectors,
    lengths,
    out_weight,
    residual,
    norm_gain,
    route_ids,
    route_logits,
    shared_gate_up,
    shared_down,
    expert_gate_up,
    expert_down,
    cache_blocks,
    block_table,
):
    tokens, width = residual.shape
    devices = lax.axis_size("seq")
    me = lax.axis_index("seq")
    z_index, plane_index = lax.div(me, PLANE), lax.rem(me, PLANE)
    z_groups = [[p + PLANE * z for z in range(Z_SIZE)] for p in range(PLANE)]
    planes = [[p + PLANE * z for p in range(PLANE)] for z in range(Z_SIZE)]
    bf16, f32 = jnp.bfloat16, jnp.float32
    shape = jax.ShapeDtypeStruct
    scalar = lambda value: jnp.reshape(value, (1,)).astype(jnp.int32)
    all_tokens = Z_SIZE * tokens
    part = width // Z_SIZE

    def exchange(array, groups):
        return lax.all_to_all(
            array, "seq", split_axis=0, concat_axis=0, tiled=True, axis_index_groups=groups
        )

    own_kv = pl.pallas_call(
        join_kernel,
        out_shape=pltpu.HBM((tokens, 2 * key_vectors.shape[1]), bf16),
        in_specs=[VMEM] * 2,
        out_specs=VMEM,
        compiler_params=params(),
        name="join",
    )(in_hbm(key_vectors), in_hbm(value_vectors))
    behind = [from_behind(own_kv, "seq", offset) for offset in range(1, REACH + 1)]

    turned_weight = lax.all_gather(
        out_weight.T, "seq", axis=0, tiled=True, axis_index_groups=planes
    )
    info = pl.pallas_call(
        route_kernel,
        out_shape=pltpu.HBM((tokens, 128), bf16),
        in_specs=[SMEM] + [VMEM] * 2,
        out_specs=VMEM,
        scratch_shapes=[pltpu.VMEM((128, 128), f32)],
        compiler_params=params(),
        cost_estimate=cost(MIB, MIB),
        name="route",
    )(scalar(z_index), in_hbm(route_ids.T), in_hbm(route_logits.T))

    def along_z(arrays):
        return [arrays[0]] + [
            lax.ppermute(arrays[step], "seq", z_pairs[step]) for step in range(1, Z_SIZE)
        ]

    z_pairs = [
        [
            (z * PLANE + p, (z + step) % Z_SIZE * PLANE + p)
            for z in range(Z_SIZE)
            for p in range(PLANE)
        ]
        for step in range(Z_SIZE)
    ]
    z_scalar = scalar(z_index)
    gain = norm_gain.reshape(1, width)
    own_shared = jnp.concatenate(
        [jnp.transpose(shared_gate_up, (1, 2, 0)).reshape(-1, width), shared_down], axis=0
    )

    sent_width = width + part + info.shape[1]
    sent = pl.pallas_call(
        attention_kernel,
        out_shape=[pltpu.HBM((tokens, sent_width), bf16)] * Z_SIZE,
        in_specs=[SMEM] * 3 + [VMEM] * 8,
        out_specs=[VMEM] * Z_SIZE,
        compiler_params=params(58),
        cost_estimate=cost(4 * tokens * 5 * tokens * width, 3 * MIB),
        name="attention",
    )(z_scalar, scalar(me * tokens), in_hbm(lengths), queries, *behind, own_kv, residual, info)

    sent, own_shared = lax.optimization_barrier((sent, own_shared))
    shared_weight = lax.all_gather(own_shared, "seq", axis=0, axis_index_groups=planes)
    gathered = along_z(sent)
    gathered, cache_blocks, expert_gate_up = lax.optimization_barrier(
        (gathered, cache_blocks, expert_gate_up)
    )

    _, block_tokens, layers, kv_heads, head_size = cache_blocks.shape
    per_device = block_tokens // devices
    cache_view = cache_blocks.reshape(Z_SIZE, PLANE, per_device * layers, kv_heads, head_size)
    in_plane = []
    for step in range(PLANE):
        piece = lax.dynamic_index_in_dim(
            cache_view, lax.rem(plane_index + step, PLANE), axis=1, keepdims=False
        )
        if step:
            pairs = [
                (z * PLANE + p, z * PLANE + (p + step) % PLANE)
                for z in range(Z_SIZE)
                for p in range(PLANE)
            ]
            piece = lax.ppermute(piece, "seq", pairs)
        in_plane.append(piece)
    gate_up = jnp.transpose(expert_gate_up, (0, 2, 1, 3))

    mixed_part, info = pl.pallas_call(
        project_kernel,
        out_shape=[pltpu.HBM((Z_SIZE, all_tokens, part), bf16), shape((all_tokens, 128), bf16)],
        in_specs=[SMEM] + [VMEM] * (Z_SIZE + 1),
        out_specs=[VMEM] * 2,
        scratch_shapes=[pltpu.VMEM((Z_SIZE, tokens, sent_width), bf16)],
        compiler_params=params(),
        cost_estimate=cost(2 * all_tokens * width * part, 3 * MIB),
        name="project",
    )(z_scalar, in_hbm(gathered[0]), *gathered[1:], in_hbm(turned_weight))
    mixed = exchange(mixed_part, z_groups)

    local_halves, _, _, half_ff = expert_gate_up.shape
    per_half = Z_SIZE * CAP
    picked = local_halves * per_half
    onehot, mix = pl.pallas_call(
        tables_kernel,
        out_shape=[
            shape((PLANE * picked, all_tokens), bf16),
            shape((all_tokens, PLANE * picked), bf16),
        ],
        in_specs=[SMEM, VMEM],
        out_specs=[VMEM] * 2,
        compiler_params=params(),
        cost_estimate=cost(20 * PLANE * picked * all_tokens, MIB),
        name="tables",
    )(scalar(lax.rem(z_index, 2)), info)
    outgoing = pl.pallas_call(
        pick_kernel,
        out_shape=pltpu.HBM((PLANE, picked, width), bf16),
        in_specs=[VMEM] * 3,
        out_specs=HBM,
        scratch_shapes=[
            pltpu.VMEM((PLANE, picked, width), bf16),
            pltpu.SemaphoreType.DMA((PLANE,)),
        ],
        compiler_params=params(),
        cost_estimate=cost(2 * PLANE * picked * all_tokens * width, 4 * MIB),
        name="pick",
    )(onehot, gain, mixed)

    outgoing, in_plane = lax.optimization_barrier((outgoing, in_plane))
    arrived = exchange(outgoing, planes)
    grouped = pl.pallas_call(
        regroup_kernel,
        out_shape=[shape((PLANE,) + in_plane[0].shape[1:], bf16)] * Z_SIZE,
        in_specs=[SMEM] + [VMEM] * PLANE,
        out_specs=[VMEM] * Z_SIZE,
        compiler_params=params(),
        cost_estimate=cost(0, 2 * MIB),
        name="regroup",
    )(z_scalar, *[in_hbm(piece) for piece in in_plane])
    arrived_cache = [grouped[0]]
    for step in range(1, Z_SIZE):
        arrived_cache.append(lax.ppermute(grouped[step], "seq", z_pairs[step]))

    arrived, shared_weight = lax.optimization_barrier((arrived, shared_weight))
    shared_part, own_mixed = pl.pallas_call(
        shared_kernel,
        out_shape=[shape((all_tokens, width), bf16), shape((tokens, width), f32)],
        in_specs=[SMEM] + [VMEM] * 3,
        out_specs=[VMEM] * 2,
        compiler_params=params(24),
        cost_estimate=cost(6 * all_tokens * 256 * width, 5 * MIB),
        name="shared_expert",
    )(z_scalar, gain, mixed, shared_weight)

    returning = pl.pallas_call(
        experts_kernel,
        out_shape=pltpu.HBM((PLANE, picked, width), bf16),
        in_specs=[VMEM, HBM, HBM],
        out_specs=HBM,
        scratch_shapes=[
            pltpu.VMEM((local_halves, 2, width, half_ff), bf16),
            pltpu.VMEM((local_halves, half_ff, width), bf16),
            pltpu.VMEM((PLANE, picked, width), bf16),
            pltpu.SemaphoreType.DMA((2, local_halves)),
            pltpu.SemaphoreType.DMA((local_halves // 2,)),
        ],
        compiler_params=params(32),
        cost_estimate=cost(6 * PLANE * picked * half_ff * width, 14 * MIB),
        name="experts",
    )(arrived, in_hbm(gate_up), in_hbm(expert_down))
    returning, arrived_cache = lax.optimization_barrier((returning, arrived_cache))
    returned = exchange(returning, planes).reshape(PLANE * picked, width)

    arrived_cache = jnp.concatenate(arrived_cache)
    cache_out = pl.pallas_call(
        reorder_kernel,
        out_shape=shape(arrived_cache.shape, bf16),
        in_specs=[SMEM, SMEM, VMEM],
        out_specs=VMEM,
        compiler_params=params(),
        cost_estimate=cost(0, 2 * arrived_cache.size * 2),
        name="reorder",
    )(scalar(me), block_table, arrived_cache)
    cache_out = cache_out.reshape(devices, per_device, layers, kv_heads, head_size)

    sums = pl.pallas_call(
        combine_kernel,
        out_shape=[shape((tokens, width), bf16)] * Z_SIZE,
        in_specs=[SMEM] + [VMEM] * 3,
        out_specs=[VMEM] * Z_SIZE,
        scratch_shapes=[pltpu.VMEM((all_tokens, width), f32)],
        compiler_params=params(24),
        cost_estimate=cost(2 * all_tokens * PLANE * picked * width, 3 * MIB),
        name="combine",
    )(z_scalar, in_hbm(mix), returned, in_hbm(shared_part))
    layer_out = pl.pallas_call(
        final_kernel,
        out_shape=shape((tokens, width), bf16),
        in_specs=[VMEM] * (1 + Z_SIZE),
        out_specs=VMEM,
        compiler_params=params(),
        cost_estimate=cost(5 * tokens * width, 2 * MIB),
        name="final",
    )(own_mixed, *along_z(sums))
    return (layer_out, cache_out)


def solution(mesh):
    in_specs = (
        P("seq", "head"),
        P("seq", "head"),
        P("seq", "head"),
        P(),
        P("head", "seq"),
        P(("seq", "head"), None),
        P(),
        P(("seq", "head"), None),
        P(("seq", "head"), None),
        P(None, None, ("seq", "head")),
        P(("seq", "head"), None),
        P("seq", None, None, None),
        P("seq", None, None),
        P("seq", None, None, "head", None),
        P(),
    )
    out_specs = (P(("seq", "head"), None), P(None, "seq", None, "head", None))
    planes_fit = mesh.shape["seq"] == Z_SIZE * PLANE and mesh.shape["head"] == 1
    body = shards if planes_fit else general_shards
    return jax.shard_map(body, mesh=mesh, in_specs=in_specs, out_specs=out_specs, check_vma=False)
```
